32 devices in a mesh: dp: 8 (over z, core), row: 2 (over y), col: 2 (over x).
Axes of the slice: x: 2, y: 2, z: 4, core: 2. Of those that a mesh axis runs over, the one named last changes fastest.
Arguments:
- tokens_in: bfloat16 [16384, 1024], P(('dp', 'col'), 'row'), may hold values from -6 to 6
- lengths: int32 [16, 6], P('dp'), may hold values from 1 to 800, 1024 in all within a row
- first_gain: float32 [1024], P('row'), may hold values from 0.25 to 1.75
- joined_weight: bfloat16 [1024, 3, 1024], P('row', None, 'col'), may hold values from -0.1875 to 0.1875
- mixer_weight: bfloat16 [1024, 1024], P('col', 'row'), may hold values from -2 to 2
- second_gain: float32 [1024], P('row'), may hold values from 0.25 to 1.75
- expand_weight: bfloat16 [1024, 2, 2624], P('row', None, 'col'), may hold values from -0.1875 to 0.1875
- shrink_weight: bfloat16 [2624, 1024], P('col', 'row'), may hold values from -0.125 to 0.125
- cotangent: bfloat16 [16384, 1024], P(('dp', 'col'), 'row'), may hold values from -6 to 6
Outputs:
- block_output: bfloat16 [16384, 1024], P(('dp', 'col'), 'row')
- input_grad: float32 [16384, 1024], P(('dp', 'col'), 'row')
- joined_grad: float32 [1024, 3, 1024], P('row', None, 'col')
- mixer_grad: float32 [1024, 1024], P('col', 'row')
- expand_grad: float32 [1024, 2, 2624], P('row', None, 'col')
- shrink_grad: float32 [2624, 1024], P('col', 'row')
- first_gain_grad: float32 [1024], P('row')
- second_gain_grad: float32 [1024], P('row')
The draws below stay inside these ranges and needn't reach their ends.
Inputs may be any that keep to these rules, and one draw needn't show every extreme that they name: Each row lists the document lengths of one sequence in order and sums to 1024; its last entry is the padded tail; one entry of each row is 800.
All inputs are finite; a program needn't handle non-finite values.
Results may differ from the reference program's by a relative error of at most 0.018.
Values may be sent and summed in bfloat16 or wider, within the bound.
A program may use at most 320 MiB of HBM per device.

```python
import math
import jax
import jax.numpy as jnp
import numpy as np
from jax import lax

D = 1024
HEADS = 16
HD = 64
FF = 2624
LEN = 1024
DOCS = 6
MOST = 800
SEQS = 16
TOKENS = 16384


def level_of(rng, dims, cuts, low, largest):
    def one(axis_at, shards_of):
        heights = jax.random.uniform(jax.random.fold_in(jax.random.fold_in(rng, 6), axis_at), (shards_of,), jnp.float32, low / len(cuts), largest / len(cuts))
        return jnp.repeat(jnp.exp(heights), dims[axis_at] // shards_of).reshape((-1,) + (1,) * (len(dims) - axis_at - 1))

    loudness = one(*cuts[0])
    for cut in cuts[1:]:
        loudness = loudness * one(*cut)
    return loudness


def profile(count, total, most, skew):
    portions = [(1 << 20) // math.isqrt(rank ** skew) + 1 for rank in range(2, count + 1)]
    spare, given = total - most - (count - 1), [1] * (count - 1)
    while spare > 0:
        free = [i for i in range(count - 1) if given[i] < most]
        whole, budget = sum([portions[i] for i in free]), spare
        for i in free:
            addition = min(most - given[i], max(1, budget * portions[i] // whole), spare)
            given[i] = given[i] + addition
            spare = spare - addition
    return np.array([most] + given)


def ragged_sizes(key, count, total, limit, lean):
    if count == 2:
        one = jax.random.randint(key, (), max(1, total - limit), min(limit, total - 1) + 1)
        return jnp.stack([one, total - one])
    tallies = jnp.asarray(profile(count, total, limit, lean), jnp.int32)
    couples = (count - 1) // 2
    donor, sink = tallies[1:1 + 2 * couples:2], tallies[2:2 + 2 * couples:2]
    slack = jnp.minimum(donor - 1, limit - sink)
    shifted = jax.random.randint(jax.random.fold_in(key, 1), (couples,), 0, 1 << 20) % (slack + 1)
    tallies = tallies.at[1:1 + 2 * couples:2].set(donor - shifted).at[2:2 + 2 * couples:2].set(sink + shifted)
    return tallies[jax.random.permutation(jax.random.fold_in(key, 2), count)]


def noise(own_key, dims, deviation, most, cuts=(), kind=jnp.bfloat16):
    level = level_of(own_key, dims, cuts, -0.22, 0.18) if cuts else 1.0
    entries = jax.random.normal(own_key, dims, jnp.float32) * deviation * level
    return jnp.minimum(jnp.maximum(entries, -most), most).astype(kind)


def setup_inputs(seed: int = 0) -> dict:
    keys = jax.random.split(jax.random.key(seed), 10)
    return {
        "tokens_in": noise(keys[0], (TOKENS, D), 1.0, 6.0, ((0, 16), (1, 2))),
        "lengths": jax.vmap(lambda own: ragged_sizes(own, DOCS, LEN, MOST, 1))(jax.random.split(keys[1], SEQS)).reshape((SEQS, DOCS)).astype(jnp.int32),
        "first_gain": jnp.clip(1.0 + 0.15 * jax.random.normal(keys[2], (D,), jnp.float32), 0.25, 1.75),
        "joined_weight": noise(keys[3], (D, 3, D), D ** -0.5, 0.1875, ((0, 2), (2, 2))),
        "mixer_weight": noise(keys[4], (D, D), (max(1, D // 128)) ** -0.5, 2.0, ((0, 2), (1, 2))),
        "second_gain": jnp.clip(1.0 + 0.15 * jax.random.normal(keys[5], (D,), jnp.float32), 0.25, 1.75),
        "expand_weight": noise(keys[6], (D, 2, FF), D ** -0.5, 0.1875, ((0, 2), (2, 2))),
        "shrink_weight": noise(keys[7], (FF, D), FF ** -0.5, 0.125, ((0, 2), (1, 2))),
        "cotangent": noise(keys[8], (TOKENS, D), 1.0, 6.0, ((0, 16), (1, 2))),
    }


@jax.custom_vjp
def low(v):
    return lax.optimization_barrier(v.astype(jnp.bfloat16)).astype(jnp.float32)

@jax.custom_vjp
def low_back(v):
    return v

def low_keep(v):
    return (low(v), None)

def low_pass(kept, grad):
    return (grad,)

def back_keep(v):
    return (v, None)

def back_low(kept, grad):
    return (low(grad),)
low.defvjp(low_keep, low_pass)
low_back.defvjp(back_keep, back_low)
rope_base = 160000.0
norm_eps = 1e-05
masked_value = -1000000000.0

def doc_layout(lengths):
    ends = jnp.cumsum(lengths, axis=-1).astype(jnp.int32)
    places = jnp.arange(LEN, dtype=jnp.int32)
    segment = lax.optimization_barrier(jnp.sum((places[None, :, None] >= ends[:, None, :]).astype(jnp.int32), axis=-1)).astype(jnp.int32)
    starts = ends - lengths
    chosen = (segment[:, :, None] == jnp.arange(DOCS, dtype=jnp.int32)[None, None, :]).astype(jnp.int32)
    offset = lax.optimization_barrier(jnp.sum(chosen * starts[:, None, :], axis=-1)).astype(jnp.int32)
    position = places[None, :] - offset
    valid = segment < DOCS - 1
    return (segment, position, valid)

def rotate(values, position):
    half = HD // 2
    freq = rope_base ** (-2.0 * jnp.arange(half, dtype=jnp.float32) / HD)
    angle_val = position[..., None].astype(jnp.float32) * freq
    cosine = jnp.cos(angle_val)[:, :, None, :]
    sine = jnp.sin(angle_val)[:, :, None, :]
    first_half = values[..., :half]
    second_half = values[..., half:]
    return jnp.concatenate([first_half * cosine - second_half * sine, second_half * cosine + first_half * sine], axis=-1)

def normalize(values, gain):
    center = lax.optimization_barrier(jnp.mean(values, axis=-1, keepdims=True))
    spread = lax.optimization_barrier(jnp.mean((values - center) ** 2, axis=-1, keepdims=True))
    return (values - center) * lax.rsqrt(spread + norm_eps) * gain

def attend_one(parts):
    query, key_rot, value, segment = parts
    scale = 1.0 / math.sqrt(HD)
    scores = jnp.einsum('qhd,khd->hqk', query, key_rot, precision=lax.Precision.HIGHEST) * scale
    scores = low_back(scores)
    same_doc = segment[:, None] == segment[None, :]
    scores = jnp.where(same_doc[None], scores, masked_value)
    row_top = lax.optimization_barrier(jnp.max(scores, axis=-1, keepdims=True))
    exp_scores = jnp.exp(scores - row_top)
    probs = exp_scores / lax.optimization_barrier(jnp.sum(exp_scores, axis=-1, keepdims=True))
    probs = low(probs)
    return jnp.einsum('hqk,khd->qhd', probs, value, precision=lax.Precision.HIGHEST)

def layer(inputs, segment, position, gain_a, joined_w, mixer_w, gain_b, expand_w, shrink_w):
    seq_count = inputs.shape[0]
    flat = inputs.reshape(-1, D)
    first = low(normalize(flat, gain_a))
    joined = low_back(jnp.einsum('td,dke->tke', first, joined_w, precision=lax.Precision.HIGHEST))
    joined = joined.reshape(seq_count, LEN, 3, HEADS, HD)
    queries = low(rotate(joined[:, :, 0], position))
    keys_rot = low(rotate(joined[:, :, 1], position))
    values = low(joined[:, :, 2])
    mixed = lax.map(jax.checkpoint(attend_one), (queries, keys_rot, values, segment))
    mixed = low_back(low(mixed.reshape(-1, D)))
    attn_part = low_back(jnp.dot(mixed, mixer_w, precision=lax.Precision.HIGHEST))
    middle = flat + attn_part
    second = low(normalize(middle, gain_b))
    expanded = low_back(jnp.einsum('td,dkf->tkf', second, expand_w, precision=lax.Precision.HIGHEST))
    hidden = low_back(low(jax.nn.gelu(expanded[:, 0], approximate=False) * expanded[:, 1]))
    shrunk = low_back(jnp.dot(hidden, shrink_w, precision=lax.Precision.HIGHEST))
    return (middle + shrunk).reshape(inputs.shape)

def reference(tokens_in, lengths, first_gain, joined_weight, mixer_weight, second_gain, expand_weight, shrink_weight, cotangent):
    group = math.gcd(SEQS, max(1, 4096 // LEN))
    count = SEQS // group
    params = (first_gain.astype(jnp.float32), joined_weight.astype(jnp.float32), mixer_weight.astype(jnp.float32), second_gain.astype(jnp.float32), expand_weight.astype(jnp.float32), shrink_weight.astype(jnp.float32))
    inputs = tokens_in.astype(jnp.float32).reshape(count, group, LEN, D)
    cots = cotangent.astype(jnp.float32).reshape(count, group, LEN, D)
    lens = lengths.reshape(count, group, DOCS)

    def step(totals, pieces):
        x_grp, lens_grp, cot_grp = pieces
        segment, position, valid = doc_layout(lens_grp)

        def forward(x_val, gain_a, joined_w, mixer_w, gain_b, expand_w, shrink_w):
            return layer(x_val, segment, position, gain_a, joined_w, mixer_w, gain_b, expand_w, shrink_w)
        result, pull = jax.vjp(forward, x_grp, *params)
        grads = pull(cot_grp * valid[..., None].astype(jnp.float32))
        new_totals = tuple((old + new for old, new in zip(totals, grads[1:])))
        return (new_totals, (result.astype(jnp.bfloat16), grads[0]))
    init = tuple((jnp.zeros_like(p) for p in params))
    totals, (results, input_grads) = lax.scan(step, init, (inputs, lens, cots))
    return (results.reshape(TOKENS, D), input_grads.reshape(TOKENS, D), totals[1], totals[2], totals[4], totals[5], totals[0], totals[3])
```

```python
import functools
import math

import jax
import jax.numpy as jnp
from jax import lax
from jax.experimental import pallas as pl
from jax.experimental.pallas import tpu as pltpu
from jax.sharding import PartitionSpec as P

D = 1024
HEADS = 16
HD = 64
FF = 2624
LEN = 1024
DOCS = 6
MOST = 800
CORES = 2

rope_base = 160000.0
norm_eps = 1e-05
masked_value = -1000000000.0

PAIR = 2 * HD
WIDE = 256
SOLID = MOST // WIDE * WIDE
REST = LEN - MOST
TO_EXP2 = math.log2(math.e) / math.sqrt(HD)

NT = (((1,), (1,)), ((), ()))
TN = (((0,), (0,)), ((), ()))
MESH_AXES = ("dp", "row", "col")


def lanes_of(shape):
    return lax.broadcasted_iota(jnp.int32, shape, len(shape) - 1)


def swap_halves(u):
    low_half = lanes_of(u.shape) % HD < HD // 2
    return jnp.where(low_half, pltpu.roll(u, PAIR - HD // 2, 1), pltpu.roll(u, HD // 2, 1))


def dot(left, right, dims=(((1,), (0,)), ((), ())), **more):
    return lax.dot_general(left, right, dims, preferred_element_type=jnp.float32, **more)


def only_head(values, head):
    return jnp.where(lanes_of(values.shape) // HD == head, values, jnp.zeros_like(values))


def attend_kernel(
    q_raw, k_raw, v_raw, cos_ref, sin_ref, segc_ref, segr_ref, mixed_ref, q_ref, k_ref, v_ref, lse_ref, out_t
):
    cosine, sine = cos_ref[...], sin_ref[...]
    qs = q_raw[...]
    queries = (qs * cosine + swap_halves(qs) * sine).astype(jnp.bfloat16)
    ks = k_raw[...]
    keys = (ks * cosine + swap_halves(ks) * sine).astype(jnp.bfloat16)
    vs = v_raw[...]
    q_ref[...] = queries
    k_ref[...] = keys
    v_ref[...] = vs.astype(jnp.bfloat16)
    v_t = vs.T.astype(jnp.bfloat16)
    same = segc_ref[MOST:, :] == segr_ref[:, SOLID:]

    def one(q_part, k_part, v_part, mask):
        scores = dot(k_part, q_part, NT)
        if mask is not None:
            scores = jnp.where(mask, scores, masked_value)
        top = jnp.max(scores, axis=0, keepdims=True)
        weights = jnp.exp2((scores - top) * TO_EXP2)
        total = jnp.sum(weights, axis=0, keepdims=True)
        out = dot(v_part, weights.astype(jnp.bfloat16)) / total
        return out, top * TO_EXP2 + jnp.log2(total)

    for head in range(2):
        q_head = only_head(queries, head)
        rows = slice(head * HD, (head + 1) * HD)
        v_head = v_t[rows]
        for at in range(0, SOLID, WIDE):
            out, lse = one(q_head[at : at + WIDE], keys[:MOST], v_head[:, :MOST], None)
            out_t[rows, at : at + WIDE] = out
            lse_ref[0, head : head + 1, at : at + WIDE] = lse
        out_a, lse_a = one(q_head[SOLID : SOLID + 128], keys[:MOST], v_head[:, :MOST], None)
        out_b, lse_b = one(q_head[SOLID:], keys[MOST:], v_head[:, MOST:], same)
        out_t[rows, SOLID:] = out_b
        lse_ref[0, head : head + 1, SOLID:] = lse_b
        inside = lanes_of((1, 128)) < MOST - SOLID
        out_t[rows, SOLID : SOLID + 128] = jnp.where(inside, out_a, out_b[:, :128])
        lse_ref[0, head : head + 1, SOLID : SOLID + 128] = jnp.where(inside, lse_a, lse_b[:, :128])
    mixed_ref[...] = out_t[...].T.astype(jnp.bfloat16)


def attend(joined_raw, cosine, sine, segment):
    wide = joined_raw.shape[1] // 3
    pairs = wide // PAIR
    whole = lambda shape: pl.BlockSpec(shape, lambda i: (0,) * len(shape))
    part = lambda j: pl.BlockSpec((LEN, PAIR), lambda i: (0, j * pairs + i))
    flat = jax.ShapeDtypeStruct((LEN, wide), jnp.bfloat16)
    return pl.pallas_call(
        attend_kernel,
        grid=(pairs,),
        in_specs=[part(0), part(1), part(2), whole((LEN, PAIR)), whole((LEN, PAIR)), whole((LEN, 1)), whole((1, LEN))],
        out_specs=[part(0)] * 4 + [pl.BlockSpec((1, 2, LEN), lambda i: (i, 0, 0))],
        out_shape=[flat] * 4 + [jax.ShapeDtypeStruct((pairs, 2, LEN), jnp.float32)],
        scratch_shapes=[pltpu.VMEM((PAIR, LEN), jnp.float32)],
        compiler_params=pltpu.CompilerParams(vmem_limit_bytes=40 * 1024 * 1024),
        cost_estimate=pl.CostEstimate(
            flops=4 * wide * MOST * MOST * 4, bytes_accessed=20 * LEN * wide, transcendentals=wide // HD * MOST * MOST
        ),
        name="attend_forward",
    )(joined_raw, joined_raw, joined_raw, cosine, sine, segment[:, None], segment[None, :])


def attend_back_kernel(
    q_ref, k_ref, v_ref, o_ref, g_ref, lse_ref, cos_ref, sin_ref, segc_ref, segr_ref, back_ref, dk, dv, dq_t
):
    queries, keys, values, grads = q_ref[...], k_ref[...], v_ref[...], g_ref[...]
    product = o_ref[...].astype(jnp.float32) * grads.astype(jnp.float32)
    chooser = lax.broadcasted_iota(jnp.int32, (8, PAIR), 0) == lanes_of((8, PAIR)) // HD
    delta = dot(chooser.astype(jnp.float32), product, NT, precision=lax.Precision.HIGHEST)
    k_t = keys.astype(jnp.float32).T.astype(jnp.bfloat16)
    same = segc_ref[MOST:, :] == segr_ref[:, SOLID:]
    dk[...] = jnp.zeros_like(dk)
    dv[...] = jnp.zeros_like(dv)

    def one(q_part, g_part, lse, dlt, lo, hi, k_t_part, mask):
        scores = dot(keys[lo:hi], q_part, NT)
        probs = jnp.exp2(scores * TO_EXP2 - lse)
        if mask is not None:
            probs = jnp.where(mask, probs, 0.0)
        probs_grad = dot(values[lo:hi], g_part, NT)
        scores_grad = (probs * (probs_grad - dlt)).astype(jnp.bfloat16)
        dv[lo:hi, :] += dot(probs.astype(jnp.bfloat16), g_part)
        dk[lo:hi, :] += dot(scores_grad, q_part)
        return dot(k_t_part, scores_grad)

    for head in range(2):
        q_head, g_head = only_head(queries, head), only_head(grads, head)
        rows = slice(head * HD, (head + 1) * HD)
        k_t_head = k_t[rows]
        lse = lse_ref[0, head : head + 1, :]
        dlt = delta[head : head + 1, :]
        for at in range(0, SOLID, WIDE):
            cut = slice(at, at + WIDE)
            dq_t[rows, cut] = one(q_head[cut], g_head[cut], lse[:, cut], dlt[:, cut], 0, MOST, k_t_head[:, :MOST], None)
        cut = slice(SOLID, SOLID + 128)
        inside = lanes_of((1, 128)) < MOST - SOLID
        part_a = one(
            q_head[cut], g_head[cut], jnp.where(inside, lse[:, cut], 1e30), dlt[:, cut], 0, MOST, k_t_head[:, :MOST], None
        )
        cut = slice(SOLID, LEN)
        part_b = one(q_head[cut], g_head[cut], lse[:, cut], dlt[:, cut], MOST, LEN, k_t_head[:, MOST:], same)
        dq_t[rows, SOLID:] = part_b
        dq_t[rows, SOLID : SOLID + 128] = part_a + part_b[:, :128]
    cosine, sine = cos_ref[...], sin_ref[...]
    scale = 1.0 / math.sqrt(HD)
    dqs = dq_t[...].T * scale
    back_ref[0] = (dqs * cosine - swap_halves(dqs) * sine).astype(jnp.bfloat16)
    dks = dk[...] * scale
    back_ref[1] = (dks * cosine - swap_halves(dks) * sine).astype(jnp.bfloat16)
    back_ref[2] = dv[...].astype(jnp.bfloat16)


def attend_back(queries, keys, values, mixed, grad, lse, cosine, sine, segment):
    wide = queries.shape[1]
    pairs = wide // PAIR
    whole = lambda shape: pl.BlockSpec(shape, lambda i: (0,) * len(shape))
    part = pl.BlockSpec((LEN, PAIR), lambda i: (0, i))
    return pl.pallas_call(
        attend_back_kernel,
        grid=(pairs,),
        in_specs=[part] * 5
        + [pl.BlockSpec((1, 2, LEN), lambda i: (i, 0, 0))]
        + [whole((LEN, PAIR)), whole((LEN, PAIR)), whole((LEN, 1)), whole((1, LEN))],
        out_specs=pl.BlockSpec((3, LEN, PAIR), lambda i: (0, 0, i)),
        out_shape=jax.ShapeDtypeStruct((3, LEN, wide), jnp.bfloat16),
        scratch_shapes=[
            pltpu.VMEM((LEN, PAIR), jnp.float32),
            pltpu.VMEM((LEN, PAIR), jnp.float32),
            pltpu.VMEM((PAIR, LEN), jnp.float32),
        ],
        compiler_params=pltpu.CompilerParams(vmem_limit_bytes=40 * 1024 * 1024),
        cost_estimate=pl.CostEstimate(
            flops=10 * wide * MOST * MOST * 4, bytes_accessed=20 * LEN * wide, transcendentals=wide // HD * MOST * MOST
        ),
        name="attend_backward",
    )(queries, keys, values, mixed, grad, lse, cosine, sine, segment[:, None], segment[None, :])


class Grid:
    def __init__(self):
        self.rows, self.cols = lax.axis_size("row"), lax.axis_size("col")
        self.planes = lax.axis_size("dp") // CORES
        dp = lax.axis_index("dp")
        self.z, self.core = dp // CORES, dp % CORES
        self.row, self.col = lax.axis_index("row"), lax.axis_index("col")
        self.matched = self.core == self.col

    def move(self, value, route):
        pairs = []
        for z in range(self.planes):
            for core in range(CORES):
                for row in range(self.rows):
                    for col in range(self.cols):
                        to = route(z, core, row, col)
                        if to is not None:
                            pairs.append((self.flat(z, core, row, col), self.flat(*to)))
        return lax.ppermute(value, MESH_AXES, pairs)

    def flat(self, z, core, row, col):
        return ((z * CORES + core) * self.rows + row) * self.cols + col

    def swap_cores(self, value):
        return self.move(value, lambda z, k, r, c: (z, 1 - k, r, c))

    def next_row(self, value, step, matched=False):
        return self.move(
            value, lambda z, k, r, c: (z, k, (r + step) % self.rows, c) if k == c or not matched else None
        )

    def next_plane(self, value, step):
        return self.move(value, lambda z, k, r, c: ((z + step) % self.planes, k, r, c) if k == c else None)

    def by_row(self, own_first):
        if self.rows == 2:
            first = self.row == 0
            a, b = own_first
            return [jnp.where(first, a, b), jnp.where(first, b, a)]
        stacked = jnp.stack(own_first)
        return [
            lax.dynamic_index_in_dim(stacked, (self.row - at) % self.rows, 0, keepdims=False)
            for at in range(self.rows)
        ]


def cut_of(rows):
    return rows * 5 // 16 // 16 * 16


def gather_weight(grid, block, axis):
    cut = cut_of(block.shape[0])
    own_a, own_b = block[:cut], block[cut:]
    crossed = grid.move(own_a, lambda z, k, r, c: (z, 1 - k, r, 1 - c) if k != c else None)
    mine = jnp.where(grid.matched, own_a, crossed)
    part_a = grid.by_row([mine] + [grid.next_row(mine, j) for j in range(1, grid.rows)])
    part_b = grid.by_row([own_b] + [grid.next_row(own_b, j, True) for j in range(1, grid.rows)])
    part_b = jnp.stack(part_b)
    crossed = grid.move(part_b, lambda z, k, r, c: (z, k, r, 1 - c) if k == c else None)
    part_b = jnp.where(grid.matched, part_b, crossed)
    return jnp.concatenate([jnp.concatenate([part_a[i], part_b[i]], axis=0) for i in range(grid.rows)], axis=axis)


def low(value):
    return value.astype(jnp.bfloat16)


def wide(value):
    return value.astype(jnp.float32)


def sum_rows(grid, blocks, matched):
    own = wide(lax.dynamic_index_in_dim(blocks, grid.row, 0, keepdims=False))
    for j in range(1, grid.rows):
        away = lax.dynamic_index_in_dim(blocks, (grid.row + j) % grid.rows, 0, keepdims=False)
        own = own + wide(grid.next_row(away, j, matched))
    return low(own)


def sum_planes(grid, block):
    count = grid.planes
    width = block.shape[1] // count
    piece = lambda at: lax.dynamic_slice_in_dim(block, at % count * width, width, 1)
    own = wide(piece(grid.z))
    for j in range(1, count):
        own = own + wide(grid.next_plane(piece(grid.z + j), j))
    own = low(own)
    parts = jnp.stack([own] + [grid.next_plane(own, j) for j in range(1, count)])
    return jnp.concatenate(
        [lax.dynamic_index_in_dim(parts, (grid.z - at) % count, 0, keepdims=False) for at in range(count)], axis=1
    )


def scatter_grad(grid, blocks):
    cut = cut_of(blocks.shape[1])
    over = lambda z, k, r, c: (z, k, r, 1 - c) if k != c else None
    part_a = sum_rows(grid, blocks[:, :cut], False)
    part_a = low(wide(part_a) + wide(grid.move(part_a, over)))
    part_b = blocks[:, cut:]
    part_b = low(wide(part_b) + wide(grid.move(part_b, over)))
    part_b = sum_rows(grid, part_b, True)
    block = sum_planes(grid, jnp.concatenate([part_a, part_b], axis=0))
    other = grid.move(block, lambda z, k, r, c: (z, 1 - k, r, c) if k == c else None)
    return wide(jnp.where(grid.matched, block, other))


def roll_rows(values, start):
    return lax.dynamic_slice_in_dim(jnp.concatenate([values, values], axis=0), start, values.shape[0], 0)


def large_start(lengths):
    starts = jnp.cumsum(lengths, axis=-1) - lengths
    return jnp.sum(jnp.where(lengths == MOST, starts, 0), axis=-1)


def doc_layout(lengths, places):
    ends = jnp.cumsum(lengths)
    segment = jnp.sum((places[:, None] >= ends[None, :]).astype(jnp.int32), axis=-1)
    chosen = (segment[:, None] == jnp.arange(DOCS, dtype=jnp.int32)[None, :]).astype(jnp.int32)
    position = places - jnp.sum(chosen * (ends - lengths)[None, :], axis=-1)
    return segment, position, segment < DOCS - 1


def to_chips(grid, values, seqs):
    got = []
    for t in range(seqs):
        piece = lax.dynamic_index_in_dim(values, (t + grid.row) % seqs, 0, keepdims=False) if seqs > 1 else values[0]
        got.append(grid.move(piece, lambda z, k, r, c: (z, r // seqs, k * seqs + (t + r) % seqs, c)))
    if seqs == 1:
        return got[0]
    stacked = jnp.stack(got)
    return jnp.concatenate(
        [lax.dynamic_index_in_dim(stacked, (grid.row - j) % seqs, 0, keepdims=False) for j in range(seqs)], axis=1
    )


def from_chips(grid, half, seqs):
    width = half.shape[1] // seqs
    got = []
    for t in range(seqs):
        at = (grid.row - t) % seqs
        piece = lax.dynamic_slice_in_dim(half, at * width, width, 1) if seqs > 1 else half
        back = {}
        for k in range(CORES):
            for r in range(grid.rows):
                back[(r // seqs, k * seqs + (t + r) % seqs)] = (k, r)

        def route(z, k, r, c, back=back):
            core, row = back[(k, r)]
            return (z, core, row, c)

        got.append(grid.move(piece, route))
    if seqs == 1:
        return got[0][None]
    stacked = jnp.stack(got)
    return jnp.stack(
        [lax.dynamic_index_in_dim(stacked, (s - grid.row) % seqs, 0, keepdims=False) for s in range(seqs)]
    )


def both_halves(grid, half):
    other = grid.swap_cores(half)
    return jnp.where(
        grid.core == 0, jnp.concatenate([half, other], axis=1), jnp.concatenate([other, half], axis=1)
    )


def own_half(grid, values):
    width = values.shape[1] // CORES
    return jnp.where(grid.core == 0, values[:, :width], values[:, width:])


def norm_forward(values, gain):
    center = jnp.mean(values, axis=-1, keepdims=True)
    spread = jnp.mean((values - center) ** 2, axis=-1, keepdims=True)
    inv_scale = lax.rsqrt(spread + norm_eps)
    normed = (values - center) * inv_scale
    return normed, inv_scale, low(normed * gain)


def norm_backward(grad_norm, normed, inv_scale, gain):
    scaled = grad_norm * gain
    mean_a = jnp.mean(scaled, axis=-1, keepdims=True)
    mean_b = jnp.mean(scaled * normed, axis=-1, keepdims=True)
    return inv_scale * (scaled - mean_a - normed * mean_b), jnp.sum(grad_norm * normed, axis=0)


def gelu_product(gate_part, up_part):
    return jax.nn.gelu(gate_part, approximate=False) * up_part


def shards(
    tokens_in, lengths, first_gain, joined_weight, mixer_weight, second_gain, expand_weight, shrink_weight, cotangent
):
    grid = Grid()
    rows = grid.rows
    width_here = tokens_in.shape[1]
    wide_here = joined_weight.shape[2]
    hidden_here = shrink_weight.shape[0]
    seqs = tokens_in.shape[0] // LEN
    assert rows == CORES * seqs and grid.cols == CORES

    mine = lax.dynamic_slice_in_dim(lengths, grid.col * seqs, seqs, 0)
    starts_here = large_start(mine)
    other = grid.swap_cores(lengths)
    chip_core, chip_seq = grid.row // seqs, grid.row % seqs
    lens = lax.dynamic_index_in_dim(
        jnp.where(chip_core == grid.core, lengths, other), grid.col * seqs + chip_seq, 0, keepdims=False
    )
    places = (jnp.arange(LEN, dtype=jnp.int32) + large_start(lens)) % LEN
    segment, position, valid = doc_layout(lens, places)
    freq = rope_base ** (-2.0 * jnp.arange(HD // 2, dtype=jnp.float32) / HD)
    angle = position[:, None].astype(jnp.float32) * freq
    cosine, sine = jnp.cos(angle), jnp.sin(angle)
    cosine = jnp.concatenate([cosine] * 4, axis=1)
    sine = jnp.concatenate([-sine, sine] * 2, axis=1)

    def enter(values):
        values = values.reshape(seqs, LEN, width_here)
        return to_chips(grid, jnp.stack([roll_rows(values[s], starts_here[s]) for s in range(seqs)]), seqs)

    def leave(half):
        values = from_chips(grid, half, seqs)
        return jnp.concatenate([roll_rows(values[s], (LEN - starts_here[s]) % LEN) for s in range(seqs)], axis=0)

    gains = lax.all_gather(jnp.stack([first_gain, second_gain]), "row", axis=1, tiled=True)
    gain_a, gain_b = gains[0], gains[1]

    joined_full = gather_weight(grid, joined_weight.reshape(width_here, 3 * wide_here), 0)
    inputs = wide(both_halves(grid, enter(tokens_in)))
    normed_a, inv_a, first = norm_forward(inputs, gain_a)
    joined_raw = dot(first, joined_full)
    mixed, queries, keys, values, lse = attend(joined_raw, cosine, sine, segment)
    mixer_half = gather_weight(grid, mixer_weight, 1)
    mixer_full = jnp.where(
        grid.core == 0,
        jnp.concatenate([mixer_half, grid.swap_cores(mixer_half)], axis=0),
        jnp.concatenate([grid.swap_cores(mixer_half), mixer_half], axis=0),
    )
    middle = inputs + dot(both_halves(grid, mixed), mixer_full)
    normed_b, inv_b, second = norm_forward(middle, gain_b)
    top = jnp.where(valid[:, None], both_halves(grid, enter(cotangent)), 0)

    gate_full = gather_weight(grid, expand_weight[:, 0], 0)
    up_full = gather_weight(grid, expand_weight[:, 1], 0)
    shrink_full = gather_weight(grid, shrink_weight, 1)
    gate_part, up_part = dot(second, gate_full), dot(second, up_full)
    hidden = low(gelu_product(gate_part, up_part))
    shrunk = dot(hidden, shrink_full)
    sent = jnp.where(grid.core == 0, shrunk[:, D // 2 :], shrunk[:, : D // 2])
    block_half = own_half(grid, middle + shrunk) + wide(grid.swap_cores(low(sent)))
    block_output = leave(low(block_half))

    by_rows = lambda g: g.reshape(rows, g.shape[0] // rows, g.shape[1])
    by_cols = lambda g: jnp.stack(jnp.split(g, rows, axis=1))
    shrink_grad = scatter_grad(grid, by_cols(low(dot(hidden, top, TN))))
    hidden_grad = wide(low(dot(top, shrink_full, NT)))
    pull = jax.vjp(gelu_product, gate_part, up_part)[1]
    gate_grad, up_grad = (low(g) for g in pull(hidden_grad))
    gate_weight_grad = scatter_grad(grid, by_rows(low(dot(second, gate_grad, TN))))
    up_weight_grad = scatter_grad(grid, by_rows(low(dot(second, up_grad, TN))))
    expand_grad = jnp.stack([gate_weight_grad, up_weight_grad], axis=1)
    second_back = dot(gate_grad, gate_full, NT) + dot(up_grad, up_full, NT)
    second_back = second_back + wide(grid.swap_cores(low(second_back)))
    middle_part, second_gain_part = norm_backward(second_back, normed_b, inv_b, gain_b)
    middle_grad = wide(top) + middle_part
    middle_low = low(middle_grad)
    mixer_grad = scatter_grad(grid, by_cols(low(dot(mixed, middle_low, TN))))
    mixed_grad = low(dot(middle_low, mixer_half, NT))
    back = attend_back(queries, keys, values, mixed, mixed_grad, lse, cosine, sine, segment)
    joined_grad = scatter_grad(
        grid, by_rows(low(jnp.concatenate([dot(first, back[j], TN) for j in range(3)], axis=1)))
    ).reshape(width_here, 3, wide_here)
    joined_back = jnp.concatenate([back[0], back[1], back[2]], axis=1)
    first_back = dot(joined_back, joined_full, NT)
    first_back = first_back + wide(grid.swap_cores(low(first_back)))
    input_part, first_gain_part = norm_backward(first_back, normed_a, inv_a, gain_a)
    input_grad = wide(leave(low(own_half(grid, middle_grad + input_part))))

    sums = lax.psum(jnp.stack([first_gain_part, second_gain_part]) * (1.0 / CORES), MESH_AXES)
    sums = lax.dynamic_slice_in_dim(sums, grid.row * width_here, width_here, 1)
    return (block_output, input_grad, joined_grad, mixer_grad, expand_grad, shrink_grad, sums[0], sums[1])


def solution(mesh):
    placed = (
        P(("dp", "col"), "row"),
        P("dp", None),
        P("row"),
        P("row", None, "col"),
        P("col", "row"),
        P("row"),
        P("row", None, "col"),
        P("col", "row"),
        P(("dp", "col"), "row"),
    )
    return jax.shard_map(
        shards,
        mesh=mesh,
        in_specs=placed,
        out_specs=(
            P(("dp", "col"), "row"),
            P(("dp", "col"), "row"),
            P("row", None, "col"),
            P("col", "row"),
            P("row", None, "col"),
            P("col", "row"),
            P("row"),
            P("row"),
        ),
        check_vma=False,
    )
```

```python
import functools
import math

import jax
import jax.numpy as jnp
from jax import lax
from jax.experimental import pallas as pl
from jax.experimental.pallas import tpu as pltpu
from jax.sharding import PartitionSpec as P

D = 1024
HEADS = 16
HD = 64
FF = 2624
LEN = 1024
DOCS = 6
MOST = 800
CORES = 2

rope_base = 160000.0
norm_eps = 1e-05
masked_value = -1000000000.0

PAIR = 2 * HD
WIDE = 256
SOLID = MOST // WIDE * WIDE
REST = LEN - MOST
TO_EXP2 = math.log2(math.e) / math.sqrt(HD)

NT = (((1,), (1,)), ((), ()))
TN = (((0,), (0,)), ((), ()))
MESH_AXES = ("dp", "row", "col")


def lanes_of(shape):
    return lax.broadcasted_iota(jnp.int32, shape, len(shape) - 1)


def swap_halves(u):
    low_half = lanes_of(u.shape) % HD < HD // 2
    return jnp.where(low_half, pltpu.roll(u, PAIR - HD // 2, 1), pltpu.roll(u, HD // 2, 1))


def dot(left, right, dims=(((1,), (0,)), ((), ())), **more):
    return lax.dot_general(left, right, dims, preferred_element_type=jnp.float32, **more)


def only_head(values, head):
    return jnp.where(lanes_of(values.shape) // HD == head, values, jnp.zeros_like(values))


def attend_back_kernel(
    q_ref, k_ref, v_ref, o_ref, g_ref, lse_ref, cos_ref, sin_ref, segc_ref, segr_ref, back_ref, dk, dv, dq_t
):
    product = o_ref[...].astype(jnp.float32) * g_ref[...].astype(jnp.float32)
    chooser = lax.broadcasted_iota(jnp.int32, (8, PAIR), 0) == lanes_of((8, PAIR)) // HD
    delta = dot(chooser.astype(jnp.float32), product, NT, precision=lax.Precision.HIGHEST)
    keys, values = k_ref[...], v_ref[...]
    k_t = keys.astype(jnp.float32).T.astype(jnp.bfloat16)
    dk[...] = jnp.zeros_like(dk)
    dv[...] = jnp.zeros_like(dv)
    for head in range(2):
        rows = slice(head * HD, (head + 1) * HD)
        for at in range(0, LEN, WIDE):
            cut = slice(at, at + WIDE)
            q_part, g_part = only_head(q_ref[cut, :], head), only_head(g_ref[cut, :], head)
            scores = dot(keys, q_part, NT)
            probs = jnp.exp2(scores * TO_EXP2 - lse_ref[0, head : head + 1, cut])
            probs = jnp.where(segc_ref[...] == segr_ref[:, cut], probs, 0.0)
            probs_grad = dot(values, g_part, NT)
            scores_grad = (probs * (probs_grad - delta[head : head + 1, cut])).astype(jnp.bfloat16)
            dv[...] += dot(probs.astype(jnp.bfloat16), g_part)
            dk[...] += dot(scores_grad, q_part)
            dq_t[rows, cut] = dot(k_t[rows], scores_grad)
    cosine, sine = cos_ref[...], sin_ref[...]
    scale = 1.0 / math.sqrt(HD)
    dqs = dq_t[...].T * scale
    back_ref[0] = (dqs * cosine - swap_halves(dqs) * sine).astype(jnp.bfloat16)
    dks = dk[...] * scale
    back_ref[1] = (dks * cosine - swap_halves(dks) * sine).astype(jnp.bfloat16)
    back_ref[2] = dv[...].astype(jnp.bfloat16)


def attend_back(queries, keys, values, mixed, grad, lse, cosine, sine, segment):
    wide = queries.shape[1]
    pairs = wide // PAIR
    whole = lambda shape: pl.BlockSpec(shape, lambda i: (0,) * len(shape))
    part = pl.BlockSpec((LEN, PAIR), lambda i: (0, i))
    return pl.pallas_call(
        attend_back_kernel,
        grid=(pairs,),
        in_specs=[part] * 5
        + [pl.BlockSpec((1, 2, LEN), lambda i: (i, 0, 0))]
        + [whole((LEN, PAIR)), whole((LEN, PAIR)), whole((LEN, 1)), whole((1, LEN))],
        out_specs=pl.BlockSpec((3, LEN, PAIR), lambda i: (0, 0, i)),
        out_shape=jax.ShapeDtypeStruct((3, LEN, wide), jnp.bfloat16),
        scratch_shapes=[
            pltpu.VMEM((LEN, PAIR), jnp.float32),
            pltpu.VMEM((LEN, PAIR), jnp.float32),
            pltpu.VMEM((PAIR, LEN), jnp.float32),
        ],
        compiler_params=pltpu.CompilerParams(vmem_limit_bytes=40 * 1024 * 1024),
        cost_estimate=pl.CostEstimate(
            flops=10 * wide * MOST * MOST * 4, bytes_accessed=20 * LEN * wide, transcendentals=wide // HD * MOST * MOST
        ),
        name="attend_backward",
    )(queries, keys, values, mixed, grad, lse, cosine, sine, segment[:, None], segment[None, :])


MESH_ID = pl.DeviceIdType.MESH
BLOCK = 256
HALF_ROWS = LEN // 2


class Place:
    def __init__(self):
        self.rows, self.cols = lax.axis_size("row"), lax.axis_size("col")
        self.planes = lax.axis_size("dp") // CORES
        dp = lax.axis_index("dp")
        self.z, self.core = dp // CORES, dp % CORES
        self.row, self.col = lax.axis_index("row"), lax.axis_index("col")
        self.matched = self.core == self.col
        self.parity = self.z % 2
        self.seqs = self.rows // CORES

    def at(self, z=None, core=None, row=None, col=None):
        z = self.z if z is None else z
        core = self.core if core is None else core
        return (z * CORES + core, self.row if row is None else row, self.col if col is None else col)

    def sibling(self):
        return self.at(core=1 - self.core)

    def across(self):
        return self.at(col=1 - self.col)

    def pair(self):
        return self.at(z=self.z + 1 - 2 * self.parity)

    def row_after(self, step):
        return lax.rem(self.row + step, self.rows)

    def row_before(self, step):
        return lax.rem(self.row + self.rows - step, self.rows)

    def barrier(self):
        sem = pltpu.get_barrier_semaphore()
        count = CORES * self.rows
        partners = [self.across(), self.pair()]
        for step in range(1, count):
            flat = lax.rem(self.core * self.rows + self.row + step, count)
            partners.append(self.at(core=flat // self.rows, row=lax.rem(flat, self.rows)))
        for partner in partners:
            pl.semaphore_signal(sem, inc=1, device_id=partner, device_id_type=MESH_ID)
        pl.semaphore_wait(sem, len(partners))


def remote(src, dst, send, recv, target):
    return pltpu.make_async_remote_copy(
        src_ref=src, dst_ref=dst, send_sem=send, recv_sem=recv, device_id=target, device_id_type=MESH_ID
    )


def shares(count):
    one = count * 2 // 5 // 16 * 16
    return count - 2 * one, one


class Weight:
    def __init__(self, place, source, slot, count, sems, index):
        self.place, self.source, self.slot = place, source, slot
        self.both, self.one = shares(count)
        self.sems = sems
        self.index = index
        self.local = sems[5].at[index]

    def sem(self, kind, row):
        return self.sems[kind].at[self.index, row]

    def plane_part(self):
        return self.place.parity * self.one, self.one + self.both

    def pair_part(self):
        return self.place.parity * (self.one + self.both), self.one

    def other_part(self):
        return (1 - self.place.parity) * (self.one + self.both), self.one

    def start_own(self):
        p = self.place
        start, size = self.plane_part()

        @pl.when(p.matched)
        def _():
            pltpu.make_async_copy(
                self.source(0, 2 * self.one + self.both), self.slot(p.row, 0, 2 * self.one + self.both), self.local
            ).start()
            for step in range(1, p.rows):
                remote(
                    self.source(start, size),
                    self.slot(p.row, start, size),
                    self.sem(0, step),
                    self.sem(3, p.row),
                    p.at(row=p.row_after(step)),
                ).start()
            remote(
                self.source(start, size), self.slot(p.row, start, size), self.sem(1, 0), self.sem(3, p.row), p.across()
            ).start()

    def wait_plane(self, row):
        p = self.place
        start, size = self.plane_part()
        piece = self.slot(row, start, size)
        remote(piece, piece, self.sem(0, 0), self.sem(3, row), p.across()).wait_recv()

    def send_pair(self, row, step):
        start, size = self.pair_part()
        piece = self.slot(row, start, size)
        return remote(piece, piece, self.sem(2, step), self.sem(4, row), self.place.pair())

    def send_across(self, row, step):
        start, size = self.plane_part()
        piece = self.slot(row, start, size)
        return remote(piece, piece, self.sem(1, step), self.sem(3, row), self.place.across())

    def forward_first(self):
        p = self.place

        @pl.when(p.matched)
        def _():
            for step in range(1, p.rows):
                row = p.row_before(step)
                self.wait_plane(row)
                self.send_across(row, step).start()
                self.send_pair(row, step).start()

        @pl.when(jnp.logical_not(p.matched))
        def _():
            self.wait_plane(p.row)
            self.send_pair(p.row, 0).start()

    def forward_second(self):
        p = self.place

        @pl.when(jnp.logical_not(p.matched))
        def _():
            for step in range(1, p.rows):
                row = p.row_before(step)
                self.wait_plane(row)
                self.send_pair(row, step).start()

    def finish(self):
        p = self.place
        start, size = self.other_part()

        def wait_other(row):
            piece = self.slot(row, start, size)
            remote(piece, piece, self.sem(2, 0), self.sem(4, row), p.pair()).wait_recv()

        for step in range(1, p.rows):
            wait_other(p.row_before(step))

        @pl.when(p.matched)
        def _():
            whole = self.slot(p.row, 0, 2 * self.one + self.both)
            pltpu.make_async_copy(whole, whole, self.local).wait()

        @pl.when(jnp.logical_not(p.matched))
        def _():
            wait_other(p.row)

    def drain(self):
        p = self.place
        start, size = self.plane_part()
        piece = self.slot(p.row, start, size)
        for step in range(1, p.rows):
            self.send_pair(p.row, step).wait_send()

        @pl.when(p.matched)
        def _():
            for step in range(1, p.rows):
                remote(piece, piece, self.sem(0, step), self.sem(3, p.row), p.across()).wait_send()
            for step in range(p.rows):
                self.send_across(p.row, step).wait_send()

        @pl.when(jnp.logical_not(p.matched))
        def _():
            self.send_pair(p.row, 0).wait_send()


def block_rows(i, size=BLOCK):
    return pl.ds(pl.multiple_of(i * size, size), size)


def gelu_parts(gate):
    phi = 0.5 * (1.0 + lax.erf(gate * (1.0 / math.sqrt(2.0))))
    return phi, jnp.exp(gate * gate * -0.5) * (1.0 / math.sqrt(2.0 * math.pi))


def forward_kernel(
    chunks,
    tokens_ref, cot_ref, lengths_ref, gains_ref, freq_ref, joined_ref, mixer_ref, gate_ref, up_ref, shrink_ref,
    *rest,
):
    n_chunks = len(chunks)
    outs, scratch = rest[:17], rest[17:]
    (o_tokens, o_first, o_q, o_k, o_v, o_mixed, o_lse, o_middle, o_top, o_shrunk, o_back,
     o_gate, o_up, o_shrink, o_joined, o_mixer, o_small) = outs
    (tok, cot, meta_src, meta, gains, table, first, wj, wm, wg, wu, ws, q_s, k_s, v_s, v_t, out_t, lse, mixed, middle, second,
     top, shrunk, back, hid, dgate, dup, g_gate, g_up, g_shrink,
     tok_send, tok_recv, cot_send, cot_recv, swap_send, meta_send, meta_recv, gain_send, gain_recv,
     w_y, w_x, w_z, w_recv, w_recv_z, w_local, mix_send, mix_recv, mixed_send, mixed_recv, out_sem) = scratch
    p = Place()
    rows, seqs = p.rows, p.seqs
    width = tokens_ref.shape[1]
    wide = q_s.shape[1]
    pairs = wide // PAIR
    sems = (w_y, w_x, w_z, w_recv, w_recv_z, w_local)

    def down(ref, buf, count, col, size):
        source = lambda start, n: ref.at[pl.ds(start, n), pl.ds(col, size)]
        slot = lambda row, start, n: buf.at[pl.ds(row * count + start, n), :]
        return source, slot

    def along(ref, buf, at):
        source = lambda start, n: ref.at[pl.ds(at + start, n), :]
        slot = lambda row, start, n: buf.at[pl.ds(start, n), pl.ds(pl.multiple_of(row * width, width), width)]
        return source, slot

    joined = Weight(p, *down(joined_ref, wj, width, 0, 3 * wide), width, sems, 0)
    mixer = Weight(p, *along(mixer_ref, wm.at[p.core], 0), wide, sems, 1)
    gates, ups, shrinks = [], [], []
    at = 0
    for i, (count, lanes) in enumerate(chunks):
        gates.append(Weight(p, *down(gate_ref, wg[i], width, at, lanes), width, sems, 2 + 3 * i))
        ups.append(Weight(p, *down(up_ref, wu[i], width, at, lanes), width, sems, 3 + 3 * i))
        shrinks.append(Weight(p, *along(shrink_ref, ws[i], at), count, sems, 4 + 3 * i))
        at += count

    def group(i):
        return (gates[i], ups[i], shrinks[i])

    p.barrier()

    is_here = p.core == p.row // seqs

    def send_seq(ref, buf, send, recv):
        for t in range(seqs):
            seq = lax.rem(p.row + t, seqs)
            piece = ref.at[pl.ds(pl.multiple_of(seq * LEN, LEN), LEN), :]
            target = p.at(core=p.row // seqs, row=p.core * seqs + seq)

            def away():
                remote(piece, buf.at[p.row], send.at[t], recv.at[p.row], target).start()

            if t:
                away()
            else:
                pl.when(jnp.logical_not(is_here))(away)

                @pl.when(is_here)
                def _():
                    pltpu.make_async_copy(piece, buf.at[p.row], recv.at[p.row]).start()

    def take_seq(buf, send, recv, swap):
        for u in range(seqs):
            slot = p.core * seqs + u
            pltpu.make_async_copy(buf.at[slot], buf.at[slot], recv.at[slot]).wait()
            remote(buf.at[slot], buf.at[slot], swap.at[u], recv.at[slot], p.sibling()).start()

    def finish_seq(buf, send, recv, swap):
        for u in range(seqs):
            slot = (1 - p.core) * seqs + u
            remote(buf.at[slot], buf.at[slot], swap.at[u], recv.at[slot], p.sibling()).wait_recv()

    def drain_seq(ref, buf, send, recv, swap):
        for u in range(seqs):
            remote(buf.at[0], buf.at[0], swap.at[u], recv.at[0], p.sibling()).wait_send()
            if u:
                remote(buf.at[0], buf.at[0], send.at[u], recv.at[0], p.sibling()).wait_send()

        @pl.when(jnp.logical_not(is_here))
        def _():
            remote(buf.at[0], buf.at[0], send.at[0], recv.at[0], p.sibling()).wait_send()

    send_seq(tokens_ref, tok, tok_send, tok_recv)
    joined.start_own()
    for step in range(1, rows):
        remote(gains_ref, gains.at[p.row], gain_send.at[step], gain_recv.at[p.row], p.at(row=p.row_after(step))).start()
    pltpu.make_async_copy(gains_ref, gains.at[p.row], gain_recv.at[p.row]).start()

    place_row = lanes_of((1, LEN))
    for s in range(seqs):
        base = [lengths_ref[p.col * seqs + s, d] for d in range(DOCS)]
        segment = jnp.zeros((1, LEN), jnp.int32)
        start = jnp.zeros((1, LEN), jnp.int32)
        end = jnp.int32(0)
        for d in range(DOCS):
            end = end + base[d]
            past = place_row >= end
            segment = segment + past.astype(jnp.int32)
            start = jnp.where(past, end, start)
        meta_src[s, 0:1, :] = (place_row - start).astype(jnp.float32)
        meta_src[s, 1:2, :] = segment.astype(jnp.float32)
        meta_src[s, 2:3, :] = (segment < DOCS - 1).astype(jnp.float32)
        meta_src[s, 3:8, :] = jnp.zeros((5, LEN), jnp.float32)

    sends_meta = lax.rem(p.row, seqs) == 0

    @pl.when(sends_meta)
    def _():
        for t in range(seqs):
            target = p.at(core=p.row // seqs, row=p.core * seqs + t)

            def away():
                remote(meta_src.at[t], meta, meta_send.at[t], meta_recv, target).start()

            if t:
                away()
            else:
                pl.when(jnp.logical_not(is_here))(away)

                @pl.when(is_here)
                def _():
                    pltpu.make_async_copy(meta_src.at[t], meta, meta_recv).start()

    mixer.start_own()
    for weight in group(0):
        weight.start_own()
    send_seq(cot_ref, cot, cot_send, cot_recv)
    for i in range(1, n_chunks):
        for weight in group(i):
            weight.start_own()

    count, lanes = chunks[-1]
    if lanes != count:
        ws[-1][count:, :] = jnp.zeros((lanes - count, ws[-1].shape[1]), jnp.bfloat16)

    pltpu.make_async_copy(meta, meta, meta_recv).wait()
    columns = meta[...].T
    angle = columns[:, 0:1] * freq_ref[0:1, :]
    sign = jnp.where(lanes_of((1, PAIR)) % HD < HD // 2, -1.0, 1.0)
    table[0] = jnp.cos(angle)
    table[1] = jnp.sin(angle) * sign
    segment_col, valid_col = columns[:, 1:2], columns[:, 2:3]

    joined.forward_first()
    take_seq(tok, tok_send, tok_recv, swap_send.at[0])
    mixer.forward_first()
    for step in range(1, rows):
        row = p.row_before(step)
        remote(gains.at[row], gains.at[row], gain_send.at[step], gain_recv.at[row], p.sibling()).wait_recv()
    pltpu.make_async_copy(gains.at[p.row], gains.at[p.row], gain_recv.at[p.row]).wait()
    joined.forward_second()
    finish_seq(tok, tok_send, tok_recv, swap_send.at[0])

    def gain_of(kind):
        return jnp.concatenate([gains[j, kind : kind + 1, :] for j in range(rows)], axis=1)

    def norm(values, gain):
        center = jnp.mean(values, axis=-1, keepdims=True)
        values = values - center
        spread = jnp.mean(values * values, axis=-1, keepdims=True)
        return (values * lax.rsqrt(spread + norm_eps) * gain).astype(jnp.bfloat16)

    def tokens_at(cut):
        return jnp.concatenate([tok[j, cut, :] for j in range(rows)], axis=1).astype(jnp.float32)

    gain_a, gain_b = gain_of(0), gain_of(1)

    @pl.loop(0, LEN // BLOCK)
    def _(i):
        cut = block_rows(i)
        first[cut, :] = norm(tokens_at(cut), gain_a)

    for weight in group(0):
        weight.forward_first()
    mixer.forward_second()
    joined.finish()

    def attention(pair):
        cols = slice(pair * PAIR, (pair + 1) * PAIR)

        @pl.loop(0, LEN // BLOCK)
        def _(i):
            cut = block_rows(i)
            part = first[cut, :]
            cosine, sine = table[0, cut, :], table[1, cut, :]
            for j, dst in ((0, q_s), (1, k_s)):
                raw = dot(part, wj[:, j * wide + pair * PAIR : j * wide + (pair + 1) * PAIR])
                dst[cut, cols] = (raw * cosine + swap_halves(raw) * sine).astype(jnp.bfloat16)
            v_s[cut, cols] = dot(part, wj[:, 2 * wide + pair * PAIR : 2 * wide + (pair + 1) * PAIR]).astype(jnp.bfloat16)

        v_t[...] = v_s[:, cols].astype(jnp.float32).T.astype(jnp.bfloat16)
        for head in range(2):
            lanes = slice(head * HD, (head + 1) * HD)

            @pl.loop(0, LEN // BLOCK)
            def _(i):
                cut = block_rows(i)
                scores = dot(k_s[:, cols], only_head(q_s[cut, cols], head), NT)
                scores = jnp.where(segment_col == meta[1:2, cut], scores, masked_value)
                peak = jnp.max(scores, axis=0, keepdims=True)
                weights = jnp.exp2((scores - peak) * TO_EXP2)
                total = jnp.sum(weights, axis=0, keepdims=True)
                out_t[lanes, cut] = dot(v_t[lanes, :], weights.astype(jnp.bfloat16)) / total
                lse[pair, head : head + 1, cut] = peak * TO_EXP2 + jnp.log2(total)

        mixed[p.core, :, cols] = out_t[...].T.astype(jnp.bfloat16)
        piece = mixed.at[p.core, :, cols]
        remote(piece, piece, mixed_send.at[pair], mixed_recv.at[pair], p.sibling()).start()

    steps = [[] for _ in range(pairs)]
    plan = [lambda i=i, half=half: [getattr(w, half)() for w in group(i)]
            for i in range(n_chunks) for half in (("forward_second",) if i == 0 else ("forward_first", "forward_second"))]
    plan.insert(1, lambda: take_seq(cot, cot_send, cot_recv, swap_send.at[1]))

    def share_mixer():
        mixer.finish()
        piece = wm.at[p.core]
        remote(piece, piece, mix_send, mix_recv, p.sibling()).start()

    plan.insert(1, share_mixer)
    for i, step in enumerate(plan):
        steps[i * pairs // len(plan)].append(step)
    for pair in range(pairs):
        attention(pair)
        for step in steps[pair]:
            step()

    for pair in range(pairs):
        piece = mixed.at[p.core, :, pair * PAIR : (pair + 1) * PAIR]
        remote(piece, piece, mixed_send.at[pair], mixed_recv.at[pair], p.sibling()).wait_recv()
    piece = wm.at[p.core]
    remote(piece, piece, mix_send, mix_recv, p.sibling()).wait_recv()
    finish_seq(cot, cot_send, cot_recv, swap_send.at[1])

    @pl.loop(0, LEN // BLOCK)
    def _(i):
        cut = block_rows(i)
        value = tokens_at(cut) + dot(mixed[0, cut, :], wm[0]) + dot(mixed[1, cut, :], wm[1])
        middle[cut, :] = value
        second[cut, :] = norm(value, gain_b)
        shrunk[cut, :] = jnp.zeros((BLOCK, D), jnp.float32)
        back[cut, :] = jnp.zeros((BLOCK, D), jnp.float32)

    valid_16 = valid_col > 0.5
    top[...] = jnp.where(valid_16, jnp.concatenate([cot[j] for j in range(rows)], axis=1), jnp.zeros((), jnp.bfloat16))

    keep = []

    def store(src, dst):
        copy = pltpu.make_async_copy(src, dst, out_sem.at[len(keep)])
        keep.append(copy)
        copy.start()

    for j in range(rows):
        store(tok.at[j], o_tokens.at[j])
    for src, dst in ((first, o_first), (q_s, o_q), (k_s, o_k), (v_s, o_v), (mixed.at[p.core], o_mixed), (lse, o_lse),
                     (middle, o_middle), (top, o_top), (wj, o_joined), (wm.at[p.core], o_mixer)):
        store(src, dst)
    for j in range(rows):
        store(gains.at[j], o_small.at[:, pl.ds(j * width, width)])
    store(meta, o_small.at[:, pl.ds(D, LEN)])

    at = 0
    for i, (count, lanes) in enumerate(chunks):
        for weight in group(i):
            weight.finish()

        @pl.loop(0, LEN // BLOCK)
        def _(t):
            cut = block_rows(t)
            part, grad = second[cut, :], top[cut, :]
            gate = dot(part, wg[i][...])
            up = dot(part, wu[i][...])
            hidden_grad = dot(grad, ws[i][...], NT).astype(jnp.bfloat16).astype(jnp.float32)
            phi, density = gelu_parts(gate)
            act = gate * phi
            hidden = (act * up).astype(jnp.bfloat16)
            d_gate = (hidden_grad * up * (phi + gate * density)).astype(jnp.bfloat16)
            d_up = (hidden_grad * act).astype(jnp.bfloat16)
            hid[cut, :lanes] = hidden
            dgate[cut, :lanes] = d_gate
            dup[cut, :lanes] = d_up
            shrunk[cut, :] += dot(hidden, ws[i][...])
            back[cut, :] += dot(d_gate, wg[i][...], NT) + dot(d_up, wu[i][...], NT)

        @pl.loop(0, D // BLOCK)
        def _(d):
            cut = block_rows(d)
            g_gate[i][cut, :] = dot(second[:, cut], dgate[:, :lanes], TN).astype(jnp.bfloat16)
            g_up[i][cut, :] = dot(second[:, cut], dup[:, :lanes], TN).astype(jnp.bfloat16)
            g_shrink[i][:, cut] = dot(hid[:, :lanes], top[:, cut], TN).astype(jnp.bfloat16)

        store(g_gate[i], o_gate.at[:, pl.ds(at, lanes)])
        store(g_up[i], o_up.at[:, pl.ds(at, lanes)])
        store(g_shrink[i], o_shrink.at[pl.ds(at, lanes), :])
        at += lanes

    store(shrunk, o_shrunk)
    store(back, o_back)

    drain_seq(tokens_ref, tok, tok_send, tok_recv, swap_send.at[0])
    drain_seq(cot_ref, cot, cot_send, cot_recv, swap_send.at[1])
    for step in range(1, rows):
        remote(gains_ref, gains.at[p.row], gain_send.at[step], gain_recv.at[p.row], p.sibling()).wait_send()

    @pl.when(sends_meta)
    def _():
        for t in range(1, seqs):
            remote(meta_src.at[t], meta, meta_send.at[t], meta_recv, p.sibling()).wait_send()

        @pl.when(jnp.logical_not(is_here))
        def _():
            remote(meta_src.at[0], meta, meta_send.at[0], meta_recv, p.sibling()).wait_send()

    for pair in range(pairs):
        piece = mixed.at[p.core, :, pair * PAIR : (pair + 1) * PAIR]
        remote(piece, piece, mixed_send.at[pair], mixed_recv.at[pair], p.sibling()).wait_send()
    piece = wm.at[p.core]
    remote(piece, piece, mix_send, mix_recv, p.sibling()).wait_send()
    for weight in [joined, mixer] + gates + ups + shrinks:
        weight.drain()
    for copy in keep:
        copy.wait()


def forward(tokens, cot, lengths, gains, joined, mixer, gate, up, shrink, chunks):
    rows = lax.axis_size("row")
    seqs = rows // CORES
    width = tokens.shape[1]
    wide = mixer.shape[0]
    pairs = wide // PAIR
    n_chunks = len(chunks)
    padded = sum(lanes for _, lanes in chunks)
    weights = 2 + 3 * n_chunks
    bf16, f32 = jnp.bfloat16, jnp.float32
    freq = rope_base ** (-2.0 * jnp.arange(HD // 2, dtype=f32) / HD)
    freq = jnp.broadcast_to(jnp.concatenate([freq] * 4)[None, :], (8, PAIR))
    outs = [
        ((rows, LEN, width), bf16), ((LEN, D), bf16), ((LEN, wide), bf16), ((LEN, wide), bf16), ((LEN, wide), bf16),
        ((LEN, wide), bf16), ((pairs, 2, LEN), f32), ((LEN, D), f32), ((LEN, D), bf16), ((LEN, D), f32), ((LEN, D), f32),
        ((D, padded), bf16), ((D, padded), bf16), ((padded, D), bf16), ((D, 3 * wide), bf16), ((wide, D), bf16),
        ((8, D + LEN), f32),
    ]
    V, dma = pltpu.VMEM, pltpu.SemaphoreType.DMA
    widest = max(lanes for _, lanes in chunks)
    scratch = [
        V((rows, LEN, width), bf16), V((rows, LEN, width), bf16), V((seqs, 8, LEN), f32), V((8, LEN), f32),
        V((rows, 8, width), f32), V((2, LEN, PAIR), f32), V((LEN, D), bf16), V((D, 3 * wide), bf16), V((CORES, wide, D), bf16),
        [V((D, lanes), bf16) for _, lanes in chunks], [V((D, lanes), bf16) for _, lanes in chunks],
        [V((lanes, D), bf16) for _, lanes in chunks],
        V((LEN, wide), bf16), V((LEN, wide), bf16), V((LEN, wide), bf16), V((PAIR, LEN), bf16), V((PAIR, LEN), f32),
        V((pairs, 2, LEN), f32), V((CORES, LEN, wide), bf16), V((LEN, D), f32), V((LEN, D), bf16), V((LEN, D), bf16),
        V((LEN, D), f32), V((LEN, D), f32), V((LEN, widest), bf16), V((LEN, widest), bf16), V((LEN, widest), bf16),
        [V((D, lanes), bf16) for _, lanes in chunks], [V((D, lanes), bf16) for _, lanes in chunks],
        [V((lanes, D), bf16) for _, lanes in chunks],
        dma((seqs,)), dma((rows,)), dma((seqs,)), dma((rows,)), dma((2, seqs)), dma((seqs,)), dma, dma((rows,)), dma((rows,)),
        dma((weights, rows)), dma((weights, rows)), dma((weights, rows)), dma((weights, rows)), dma((weights, rows)),
        dma((weights,)), dma, dma, dma((pairs,)), dma((pairs,)), dma((2 * rows + 13 + 3 * n_chunks,)),
    ]
    anywhere = pl.BlockSpec(memory_space=pl.ANY)
    in_specs = [anywhere] * 10
    in_specs[2] = pl.BlockSpec(memory_space=pltpu.SMEM)
    in_specs[4] = pl.BlockSpec(memory_space=pltpu.VMEM)
    return pl.pallas_call(
        functools.partial(forward_kernel, chunks),
        in_specs=in_specs,
        out_specs=[anywhere] * len(outs),
        out_shape=[jax.ShapeDtypeStruct(*o) for o in outs],
        scratch_shapes=scratch,
        compiler_params=pltpu.CompilerParams(
            collective_id=0, has_side_effects=True, vmem_limit_bytes=62 * 1024 * 1024
        ),
        name="layer_forward",
    )(tokens, cot, lengths, gains, freq, joined, mixer, gate, up, shrink)


class Grid:
    def __init__(self):
        self.rows, self.cols = lax.axis_size("row"), lax.axis_size("col")
        self.planes = lax.axis_size("dp") // CORES
        dp = lax.axis_index("dp")
        self.z, self.core = dp // CORES, dp % CORES
        self.row, self.col = lax.axis_index("row"), lax.axis_index("col")
        self.matched = self.core == self.col

    def move(self, value, route):
        pairs = []
        for z in range(self.planes):
            for core in range(CORES):
                for row in range(self.rows):
                    for col in range(self.cols):
                        to = route(z, core, row, col)
                        if to is not None:
                            pairs.append((self.flat(z, core, row, col), self.flat(*to)))
        return lax.ppermute(value, MESH_AXES, pairs)

    def flat(self, z, core, row, col):
        return ((z * CORES + core) * self.rows + row) * self.cols + col

    def swap_cores(self, value):
        return self.move(value, lambda z, k, r, c: (z, 1 - k, r, c))

    def next_row(self, value, step, matched=False):
        return self.move(
            value, lambda z, k, r, c: (z, k, (r + step) % self.rows, c) if k == c or not matched else None
        )

    def next_plane(self, value, step):
        return self.move(value, lambda z, k, r, c: ((z + step) % self.planes, k, r, c) if k == c else None)

    def by_row(self, own_first):
        if self.rows == 2:
            first = self.row == 0
            a, b = own_first
            return [jnp.where(first, a, b), jnp.where(first, b, a)]
        stacked = jnp.stack(own_first)
        return [
            lax.dynamic_index_in_dim(stacked, (self.row - at) % self.rows, 0, keepdims=False)
            for at in range(self.rows)
        ]


def cut_of(rows):
    return rows * 5 // 16 // 16 * 16


def gather_weight(grid, block, axis):
    cut = cut_of(block.shape[0])
    own_a, own_b = block[:cut], block[cut:]
    crossed = grid.move(own_a, lambda z, k, r, c: (z, 1 - k, r, 1 - c) if k != c else None)
    mine = jnp.where(grid.matched, own_a, crossed)
    part_a = grid.by_row([mine] + [grid.next_row(mine, j) for j in range(1, grid.rows)])
    part_b = grid.by_row([own_b] + [grid.next_row(own_b, j, True) for j in range(1, grid.rows)])
    part_b = jnp.stack(part_b)
    crossed = grid.move(part_b, lambda z, k, r, c: (z, k, r, 1 - c) if k == c else None)
    part_b = jnp.where(grid.matched, part_b, crossed)
    return jnp.concatenate([jnp.concatenate([part_a[i], part_b[i]], axis=0) for i in range(grid.rows)], axis=axis)


def low(value):
    return value.astype(jnp.bfloat16)


def wide(value):
    return value.astype(jnp.float32)


def sum_rows(grid, blocks, matched):
    own = wide(lax.dynamic_index_in_dim(blocks, grid.row, 0, keepdims=False))
    for j in range(1, grid.rows):
        away = lax.dynamic_index_in_dim(blocks, (grid.row + j) % grid.rows, 0, keepdims=False)
        own = own + wide(grid.next_row(away, j, matched))
    return low(own)


def sum_planes(grid, block):
    count = grid.planes
    width = block.shape[1] // count
    piece = lambda at: lax.dynamic_slice_in_dim(block, at % count * width, width, 1)
    own = wide(piece(grid.z))
    for j in range(1, count):
        own = own + wide(grid.next_plane(piece(grid.z + j), j))
    own = low(own)
    parts = jnp.stack([own] + [grid.next_plane(own, j) for j in range(1, count)])
    return jnp.concatenate(
        [lax.dynamic_index_in_dim(parts, (grid.z - at) % count, 0, keepdims=False) for at in range(count)], axis=1
    )


def scatter_grad(grid, blocks):
    cut = cut_of(blocks.shape[1])
    over = lambda z, k, r, c: (z, k, r, 1 - c) if k != c else None
    part_a = sum_rows(grid, blocks[:, :cut], False)
    part_a = low(wide(part_a) + wide(grid.move(part_a, over)))
    part_b = blocks[:, cut:]
    part_b = low(wide(part_b) + wide(grid.move(part_b, over)))
    part_b = sum_rows(grid, part_b, True)
    block = sum_planes(grid, jnp.concatenate([part_a, part_b], axis=0))
    other = grid.move(block, lambda z, k, r, c: (z, 1 - k, r, c) if k == c else None)
    return wide(jnp.where(grid.matched, block, other))


def roll_rows(values, start):
    return lax.dynamic_slice_in_dim(jnp.concatenate([values, values], axis=0), start, values.shape[0], 0)


def large_start(lengths):
    starts = jnp.cumsum(lengths, axis=-1) - lengths
    return jnp.sum(jnp.where(lengths == MOST, starts, 0), axis=-1)


def doc_layout(lengths, places):
    ends = jnp.cumsum(lengths)
    segment = jnp.sum((places[:, None] >= ends[None, :]).astype(jnp.int32), axis=-1)
    chosen = (segment[:, None] == jnp.arange(DOCS, dtype=jnp.int32)[None, :]).astype(jnp.int32)
    position = places - jnp.sum(chosen * (ends - lengths)[None, :], axis=-1)
    return segment, position, segment < DOCS - 1


def to_chips(grid, values, seqs):
    got = []
    for t in range(seqs):
        piece = lax.dynamic_index_in_dim(values, (t + grid.row) % seqs, 0, keepdims=False) if seqs > 1 else values[0]
        got.append(grid.move(piece, lambda z, k, r, c: (z, r // seqs, k * seqs + (t + r) % seqs, c)))
    if seqs == 1:
        return got[0]
    stacked = jnp.stack(got)
    return jnp.concatenate(
        [lax.dynamic_index_in_dim(stacked, (grid.row - j) % seqs, 0, keepdims=False) for j in range(seqs)], axis=1
    )


def from_chips(grid, half, seqs):
    width = half.shape[1] // seqs
    got = []
    for t in range(seqs):
        at = (grid.row - t) % seqs
        piece = lax.dynamic_slice_in_dim(half, at * width, width, 1) if seqs > 1 else half
        back = {}
        for k in range(CORES):
            for r in range(grid.rows):
                back[(r // seqs, k * seqs + (t + r) % seqs)] = (k, r)

        def route(z, k, r, c, back=back):
            core, row = back[(k, r)]
            return (z, core, row, c)

        got.append(grid.move(piece, route))
    if seqs == 1:
        return got[0][None]
    stacked = jnp.stack(got)
    return jnp.stack(
        [lax.dynamic_index_in_dim(stacked, (s - grid.row) % seqs, 0, keepdims=False) for s in range(seqs)]
    )


def both_halves(grid, half):
    other = grid.swap_cores(half)
    return jnp.where(
        grid.core == 0, jnp.concatenate([half, other], axis=1), jnp.concatenate([other, half], axis=1)
    )


def own_half(grid, values):
    width = values.shape[1] // CORES
    return jnp.where(grid.core == 0, values[:, :width], values[:, width:])


def norm_forward(values, gain):
    center = jnp.mean(values, axis=-1, keepdims=True)
    spread = jnp.mean((values - center) ** 2, axis=-1, keepdims=True)
    inv_scale = lax.rsqrt(spread + norm_eps)
    normed = (values - center) * inv_scale
    return normed, inv_scale, low(normed * gain)


def norm_backward(grad_norm, normed, inv_scale, gain):
    scaled = grad_norm * gain
    mean_a = jnp.mean(scaled, axis=-1, keepdims=True)
    mean_b = jnp.mean(scaled * normed, axis=-1, keepdims=True)
    return inv_scale * (scaled - mean_a - normed * mean_b), jnp.sum(grad_norm * normed, axis=0)


def gelu_product(gate_part, up_part):
    return jax.nn.gelu(gate_part, approximate=False) * up_part


def shards(
    tokens_in, lengths, first_gain, joined_weight, mixer_weight, second_gain, expand_weight, shrink_weight, cotangent
):
    grid = Grid()
    rows = grid.rows
    width_here = tokens_in.shape[1]
    wide_here = joined_weight.shape[2]
    hidden_here = shrink_weight.shape[0]
    seqs = tokens_in.shape[0] // LEN
    assert rows == CORES * seqs and grid.cols == CORES
    chunks = ((512, 512), (512, 512), (hidden_here - 1024, 384))
    padded = sum(lanes for _, lanes in chunks)
    gains_here = jnp.pad(jnp.stack([first_gain, second_gain]), ((0, 6), (0, 0)))
    fit = lambda w: jnp.pad(w, ((0, 0), (0, padded - hidden_here)))
    (tokens, first, queries, keys, values, mixed, lse, middle, top, shrunk, second_back, gate_g, up_g, shrink_g, joined_full,
     mixer_half, small) = forward(
        tokens_in, cotangent, lengths, gains_here, joined_weight.reshape(width_here, 3 * wide_here), mixer_weight,
        fit(expand_weight[:, 0]), fit(expand_weight[:, 1]), shrink_weight, chunks)
    gain_a, gain_b = small[0, :D], small[1, :D]
    position, segment, valid = small[0, D:], small[1, D:], small[2, D:]
    freq = rope_base ** (-2.0 * jnp.arange(HD // 2, dtype=jnp.float32) / HD)
    angle = position[:, None] * freq
    cosine, sine = jnp.cos(angle), jnp.sin(angle)
    cosine = jnp.concatenate([cosine] * 4, axis=1)
    sine = jnp.concatenate([-sine, sine] * 2, axis=1)
    inputs = wide(jnp.concatenate([tokens[j] for j in range(rows)], axis=1))
    normed_a, inv_a, _ = norm_forward(inputs, gain_a)
    normed_b, inv_b, _ = norm_forward(middle, gain_b)

    sent = jnp.where(grid.core == 0, shrunk[:, D // 2 :], shrunk[:, : D // 2])
    block_half = own_half(grid, middle + shrunk) + wide(grid.swap_cores(low(sent)))
    leave = lambda half: from_chips(grid, half, seqs).reshape(seqs * LEN, width_here)
    block_output = leave(low(block_half))

    by_rows = lambda g: g.reshape(rows, g.shape[0] // rows, g.shape[1])
    by_cols = lambda g: jnp.stack(jnp.split(g, rows, axis=1))
    shrink_grad = scatter_grad(grid, by_cols(shrink_g[:hidden_here]))
    gate_weight_grad = scatter_grad(grid, by_rows(gate_g[:, :hidden_here]))
    up_weight_grad = scatter_grad(grid, by_rows(up_g[:, :hidden_here]))
    expand_grad = jnp.stack([gate_weight_grad, up_weight_grad], axis=1)
    second_back = second_back + wide(grid.swap_cores(low(second_back)))
    middle_part, second_gain_part = norm_backward(second_back, normed_b, inv_b, gain_b)
    middle_grad = wide(top) + middle_part
    middle_low = low(middle_grad)
    mixer_grad = scatter_grad(grid, by_cols(low(dot(mixed, middle_low, TN))))
    mixed_grad = low(dot(middle_low, mixer_half, NT))
    back = attend_back(queries, keys, values, mixed, mixed_grad, lse, cosine, sine, segment)
    joined_grad = scatter_grad(
        grid, by_rows(low(jnp.concatenate([dot(first, back[j], TN) for j in range(3)], axis=1)))
    ).reshape(width_here, 3, wide_here)
    joined_back = jnp.concatenate([back[0], back[1], back[2]], axis=1)
    first_back = dot(joined_back, joined_full, NT)
    first_back = first_back + wide(grid.swap_cores(low(first_back)))
    input_part, first_gain_part = norm_backward(first_back, normed_a, inv_a, gain_a)
    input_grad = wide(leave(low(own_half(grid, middle_grad + input_part))))

    sums = lax.psum(jnp.stack([first_gain_part, second_gain_part]) * (1.0 / CORES), MESH_AXES)
    sums = lax.dynamic_slice_in_dim(sums, grid.row * width_here, width_here, 1)
    return (block_output, input_grad, joined_grad, mixer_grad, expand_grad, shrink_grad, sums[0], sums[1])


def solution(mesh):
    placed = (
        P(("dp", "col"), "row"),
        P("dp", None),
        P("row"),
        P("row", None, "col"),
        P("col", "row"),
        P("row"),
        P("row", None, "col"),
        P("col", "row"),
        P(("dp", "col"), "row"),
    )
    return jax.shard_map(
        shards,
        mesh=mesh,
        in_specs=placed,
        out_specs=(
            P(("dp", "col"), "row"),
            P(("dp", "col"), "row"),
            P("row", None, "col"),
            P("col", "row"),
            P("row", None, "col"),
            P("col", "row"),
            P("row"),
            P("row"),
        ),
        check_vma=False,
    )
```

```python
import functools
import math

import jax
import jax.numpy as jnp
from jax import lax
from jax.experimental import pallas as pl
from jax.experimental.pallas import tpu as pltpu
from jax.sharding import PartitionSpec as P

D = 1024
HEADS = 16
HD = 64
FF = 2624
LEN = 1024
DOCS = 6
MOST = 800
CORES = 2

rope_base = 160000.0
norm_eps = 1e-05
masked_value = -1000000000.0

PAIR = 2 * HD
WIDE = 256
SOLID = MOST // WIDE * WIDE
REST = LEN - MOST
TO_EXP2 = math.log2(math.e) / math.sqrt(HD)

NT = (((1,), (1,)), ((), ()))
TN = (((0,), (0,)), ((), ()))
MESH_AXES = ("dp", "row", "col")


def lanes_of(shape):
    return lax.broadcasted_iota(jnp.int32, shape, len(shape) - 1)


def swap_halves(u):
    low_half = lanes_of(u.shape) % HD < HD // 2
    return jnp.where(low_half, pltpu.roll(u, PAIR - HD // 2, 1), pltpu.roll(u, HD // 2, 1))


def dot(left, right, dims=(((1,), (0,)), ((), ())), **more):
    return lax.dot_general(left, right, dims, preferred_element_type=jnp.float32, **more)


def only_head(values, head):
    return jnp.where(lanes_of(values.shape) // HD == head, values, jnp.zeros_like(values))


MESH_ID = pl.DeviceIdType.MESH
BLOCK = 256
HALF_ROWS = LEN // 2


class Place:
    def __init__(self):
        self.rows, self.cols = lax.axis_size("row"), lax.axis_size("col")
        self.planes = lax.axis_size("dp") // CORES
        dp = lax.axis_index("dp")
        self.z, self.core = dp // CORES, dp % CORES
        self.row, self.col = lax.axis_index("row"), lax.axis_index("col")
        self.matched = self.core == self.col
        self.parity = self.z % 2
        self.seqs = self.rows // CORES

    def at(self, z=None, core=None, row=None, col=None):
        z = self.z if z is None else z
        core = self.core if core is None else core
        return (z * CORES + core, self.row if row is None else row, self.col if col is None else col)

    def sibling(self):
        return self.at(core=1 - self.core)

    def across(self):
        return self.at(col=1 - self.col)

    def pair(self):
        return self.at(z=self.z + 1 - 2 * self.parity)

    def row_after(self, step):
        return lax.rem(self.row + step, self.rows)

    def row_before(self, step):
        return lax.rem(self.row + self.rows - step, self.rows)

    def barrier(self):
        sem = pltpu.get_barrier_semaphore()
        count = CORES * self.rows
        partners = [self.across(), self.pair()]
        for step in range(1, count):
            flat = lax.rem(self.core * self.rows + self.row + step, count)
            partners.append(self.at(core=flat // self.rows, row=lax.rem(flat, self.rows)))
        for partner in partners:
            pl.semaphore_signal(sem, inc=1, device_id=partner, device_id_type=MESH_ID)
        pl.semaphore_wait(sem, len(partners))


def remote(src, dst, send, recv, target):
    return pltpu.make_async_remote_copy(
        src_ref=src, dst_ref=dst, send_sem=send, recv_sem=recv, device_id=target, device_id_type=MESH_ID
    )


def shares(count):
    one = count * 2 // 5 // 16 * 16
    return count - 2 * one, one


class Weight:
    def __init__(self, place, source, slot, count, sems, index):
        self.place, self.source, self.slot = place, source, slot
        self.both, self.one = shares(count)
        self.sems = sems
        self.index = index
        self.local = sems[5].at[index]

    def sem(self, kind, row):
        return self.sems[kind].at[self.index, row]

    def plane_part(self):
        return self.place.parity * self.one, self.one + self.both

    def pair_part(self):
        return self.place.parity * (self.one + self.both), self.one

    def other_part(self):
        return (1 - self.place.parity) * (self.one + self.both), self.one

    def start_own(self):
        p = self.place
        start, size = self.plane_part()

        @pl.when(p.matched)
        def _():
            pltpu.make_async_copy(
                self.source(0, 2 * self.one + self.both), self.slot(p.row, 0, 2 * self.one + self.both), self.local
            ).start()
            for step in range(1, p.rows):
                remote(
                    self.source(start, size),
                    self.slot(p.row, start, size),
                    self.sem(0, step),
                    self.sem(3, p.row),
                    p.at(row=p.row_after(step)),
                ).start()
            remote(
                self.source(start, size), self.slot(p.row, start, size), self.sem(1, 0), self.sem(3, p.row), p.across()
            ).start()

    def wait_plane(self, row):
        p = self.place
        start, size = self.plane_part()
        piece = self.slot(row, start, size)
        remote(piece, piece, self.sem(0, 0), self.sem(3, row), p.across()).wait_recv()

    def send_pair(self, row, step):
        start, size = self.pair_part()
        piece = self.slot(row, start, size)
        return remote(piece, piece, self.sem(2, step), self.sem(4, row), self.place.pair())

    def send_across(self, row, step):
        start, size = self.plane_part()
        piece = self.slot(row, start, size)
        return remote(piece, piece, self.sem(1, step), self.sem(3, row), self.place.across())

    def forward_first(self):
        p = self.place

        @pl.when(p.matched)
        def _():
            for step in range(1, p.rows):
                row = p.row_before(step)
                self.wait_plane(row)
                self.send_across(row, step).start()
                self.send_pair(row, step).start()

        @pl.when(jnp.logical_not(p.matched))
        def _():
            self.wait_plane(p.row)
            self.send_pair(p.row, 0).start()

    def forward_second(self):
        p = self.place

        @pl.when(jnp.logical_not(p.matched))
        def _():
            for step in range(1, p.rows):
                row = p.row_before(step)
                self.wait_plane(row)
                self.send_pair(row, step).start()

    def finish(self):
        p = self.place
        start, size = self.other_part()

        def wait_other(row):
            piece = self.slot(row, start, size)
            remote(piece, piece, self.sem(2, 0), self.sem(4, row), p.pair()).wait_recv()

        for step in range(1, p.rows):
            wait_other(p.row_before(step))

        @pl.when(p.matched)
        def _():
            whole = self.slot(p.row, 0, 2 * self.one + self.both)
            pltpu.make_async_copy(whole, whole, self.local).wait()

        @pl.when(jnp.logical_not(p.matched))
        def _():
            wait_other(p.row)

    def drain(self):
        p = self.place
        start, size = self.plane_part()
        piece = self.slot(p.row, start, size)
        for step in range(1, p.rows):
            self.send_pair(p.row, step).wait_send()

        @pl.when(p.matched)
        def _():
            for step in range(1, p.rows):
                remote(piece, piece, self.sem(0, step), self.sem(3, p.row), p.across()).wait_send()
            for step in range(p.rows):
                self.send_across(p.row, step).wait_send()

        @pl.when(jnp.logical_not(p.matched))
        def _():
            self.send_pair(p.row, 0).wait_send()


def block_rows(i, size=BLOCK):
    return pl.ds(pl.multiple_of(i * size, size), size)


def gelu_parts(gate):
    phi = 0.5 * (1.0 + lax.erf(gate * (1.0 / math.sqrt(2.0))))
    return phi, jnp.exp(gate * gate * -0.5) * (1.0 / math.sqrt(2.0 * math.pi))


def forward_kernel(
    chunks,
    tokens_ref, cot_ref, lengths_ref, gains_ref, freq_ref, joined_ref, mixer_ref, gate_ref, up_ref, shrink_ref,
    *rest,
):
    n_chunks = len(chunks)
    outs, scratch = rest[:20], rest[20:]
    (o_tokens, o_first, o_q, o_k, o_v, o_mixed, o_lse, o_xhat, o_inv, o_top, o_own, o_other, o_back,
     o_gate, o_up, o_shrink, o_joined, o_mixer, o_small, o_table) = outs
    (tok, cot, meta_src, meta, gains, table, first, wj, wm, wg, wu, ws, q_s, k_s, v_s, v_t, out_t, lse, mixed, xhat, inv, second,
     top, shrunk, back, back_low, own_half, other_half, hid, dgate, dup, g_gate, g_up, g_shrink,
     tok_send, tok_recv, cot_send, cot_recv, swap_send, meta_send, meta_recv, gain_send, gain_recv,
     w_y, w_x, w_z, w_recv, w_recv_z, w_local, mix_send, mix_recv, mixed_send, mixed_recv, out_sem) = scratch
    p = Place()
    rows, seqs = p.rows, p.seqs
    width = tokens_ref.shape[1]
    wide = q_s.shape[1]
    pairs = wide // PAIR
    sems = (w_y, w_x, w_z, w_recv, w_recv_z, w_local)

    def down(ref, buf, count, col, size):
        source = lambda start, n: ref.at[pl.ds(start, n), pl.ds(col, size)]
        slot = lambda row, start, n: buf.at[pl.ds(row * count + start, n), :]
        return source, slot

    def along(ref, buf, at):
        source = lambda start, n: ref.at[pl.ds(at + start, n), :]
        slot = lambda row, start, n: buf.at[pl.ds(start, n), pl.ds(pl.multiple_of(row * width, width), width)]
        return source, slot

    joined = Weight(p, *down(joined_ref, wj, width, 0, 3 * wide), width, sems, 0)
    mixer = Weight(p, *along(mixer_ref, wm.at[p.core], 0), wide, sems, 1)
    gates, ups, shrinks = [], [], []
    at = 0
    for i, (count, lanes) in enumerate(chunks):
        gates.append(Weight(p, *down(gate_ref, wg[i], width, at, lanes), width, sems, 2 + 3 * i))
        ups.append(Weight(p, *down(up_ref, wu[i], width, at, lanes), width, sems, 3 + 3 * i))
        shrinks.append(Weight(p, *along(shrink_ref, ws[i], at), count, sems, 4 + 3 * i))
        at += count

    def group(i):
        return (gates[i], ups[i], shrinks[i])

    p.barrier()

    is_here = p.core == p.row // seqs

    def send_seq(ref, buf, send, recv):
        for t in range(seqs):
            seq = lax.rem(p.row + t, seqs)
            piece = ref.at[pl.ds(pl.multiple_of(seq * LEN, LEN), LEN), :]
            target = p.at(core=p.row // seqs, row=p.core * seqs + seq)

            def away():
                remote(piece, buf.at[p.row], send.at[t], recv.at[p.row], target).start()

            if t:
                away()
            else:
                pl.when(jnp.logical_not(is_here))(away)

                @pl.when(is_here)
                def _():
                    pltpu.make_async_copy(piece, buf.at[p.row], recv.at[p.row]).start()

    def take_seq(buf, send, recv, swap):
        for u in range(seqs):
            slot = p.core * seqs + u
            pltpu.make_async_copy(buf.at[slot], buf.at[slot], recv.at[slot]).wait()
            remote(buf.at[slot], buf.at[slot], swap.at[u], recv.at[slot], p.sibling()).start()

    def finish_seq(buf, send, recv, swap):
        for u in range(seqs):
            slot = (1 - p.core) * seqs + u
            remote(buf.at[slot], buf.at[slot], swap.at[u], recv.at[slot], p.sibling()).wait_recv()

    def drain_seq(ref, buf, send, recv, swap):
        for u in range(seqs):
            remote(buf.at[0], buf.at[0], swap.at[u], recv.at[0], p.sibling()).wait_send()
            if u:
                remote(buf.at[0], buf.at[0], send.at[u], recv.at[0], p.sibling()).wait_send()

        @pl.when(jnp.logical_not(is_here))
        def _():
            remote(buf.at[0], buf.at[0], send.at[0], recv.at[0], p.sibling()).wait_send()

    send_seq(tokens_ref, tok, tok_send, tok_recv)
    joined.start_own()
    for step in range(1, rows):
        remote(gains_ref, gains.at[p.row], gain_send.at[step], gain_recv.at[p.row], p.at(row=p.row_after(step))).start()
    pltpu.make_async_copy(gains_ref, gains.at[p.row], gain_recv.at[p.row]).start()

    place_row = lanes_of((1, LEN))
    for s in range(seqs):
        base = [lengths_ref[p.col * seqs + s, d] for d in range(DOCS)]
        segment = jnp.zeros((1, LEN), jnp.int32)
        start = jnp.zeros((1, LEN), jnp.int32)
        end = jnp.int32(0)
        for d in range(DOCS):
            end = end + base[d]
            past = place_row >= end
            segment = segment + past.astype(jnp.int32)
            start = jnp.where(past, end, start)
        meta_src[s, 0:1, :] = (place_row - start).astype(jnp.float32)
        meta_src[s, 1:2, :] = segment.astype(jnp.float32)
        meta_src[s, 2:3, :] = (segment < DOCS - 1).astype(jnp.float32)
        meta_src[s, 3:8, :] = jnp.zeros((5, LEN), jnp.float32)

    sends_meta = lax.rem(p.row, seqs) == 0

    @pl.when(sends_meta)
    def _():
        for t in range(seqs):
            target = p.at(core=p.row // seqs, row=p.core * seqs + t)

            def away():
                remote(meta_src.at[t], meta, meta_send.at[t], meta_recv, target).start()

            if t:
                away()
            else:
                pl.when(jnp.logical_not(is_here))(away)

                @pl.when(is_here)
                def _():
                    pltpu.make_async_copy(meta_src.at[t], meta, meta_recv).start()

    mixer.start_own()
    for weight in group(0):
        weight.start_own()
    send_seq(cot_ref, cot, cot_send, cot_recv)
    for i in range(1, n_chunks):
        for weight in group(i):
            weight.start_own()

    count, lanes = chunks[-1]
    if lanes != count:
        ws[-1][count:, :] = jnp.zeros((lanes - count, ws[-1].shape[1]), jnp.bfloat16)

    pltpu.make_async_copy(meta, meta, meta_recv).wait()
    columns = meta[...].T
    angle = columns[:, 0:1] * freq_ref[0:1, :]
    sign = jnp.where(lanes_of((1, PAIR)) % HD < HD // 2, -1.0, 1.0)
    table[0] = jnp.cos(angle)
    table[1] = jnp.sin(angle) * sign
    segment_col, valid_col = columns[:, 1:2], columns[:, 2:3]

    joined.forward_first()
    take_seq(tok, tok_send, tok_recv, swap_send.at[0])
    mixer.forward_first()
    for step in range(1, rows):
        row = p.row_before(step)
        remote(gains.at[row], gains.at[row], gain_send.at[step], gain_recv.at[row], p.sibling()).wait_recv()
    pltpu.make_async_copy(gains.at[p.row], gains.at[p.row], gain_recv.at[p.row]).wait()
    joined.forward_second()
    finish_seq(tok, tok_send, tok_recv, swap_send.at[0])

    def gain_of(kind):
        return jnp.concatenate([gains[j, kind : kind + 1, :] for j in range(rows)], axis=1)

    def norm(values):
        center = jnp.mean(values, axis=-1, keepdims=True)
        values = values - center
        spread = jnp.mean(values * values, axis=-1, keepdims=True)
        scale = lax.rsqrt(spread + norm_eps)
        return values * scale, scale

    def tokens_at(cut):
        return jnp.concatenate([tok[j, cut, :] for j in range(rows)], axis=1).astype(jnp.float32)

    gain_a, gain_b = gain_of(0), gain_of(1)

    @pl.loop(0, LEN // BLOCK)
    def _(i):
        cut = block_rows(i)
        first[cut, :] = (norm(tokens_at(cut))[0] * gain_a).astype(jnp.bfloat16)

    for weight in group(0):
        weight.forward_first()
    mixer.forward_second()
    joined.finish()

    def attention(pair):
        cols = slice(pair * PAIR, (pair + 1) * PAIR)

        @pl.loop(0, LEN // BLOCK)
        def _(i):
            cut = block_rows(i)
            part = first[cut, :]
            cosine, sine = table[0, cut, :], table[1, cut, :]
            for j, dst in ((0, q_s), (1, k_s)):
                raw = dot(part, wj[:, j * wide + pair * PAIR : j * wide + (pair + 1) * PAIR])
                dst[cut, cols] = (raw * cosine + swap_halves(raw) * sine).astype(jnp.bfloat16)
            v_s[cut, cols] = dot(part, wj[:, 2 * wide + pair * PAIR : 2 * wide + (pair + 1) * PAIR]).astype(jnp.bfloat16)

        v_t[...] = v_s[:, cols].astype(jnp.float32).T.astype(jnp.bfloat16)
        for head in range(2):
            lanes = slice(head * HD, (head + 1) * HD)

            @pl.loop(0, LEN // BLOCK)
            def _(i):
                cut = block_rows(i)
                scores = dot(k_s[:, cols], only_head(q_s[cut, cols], head), NT)
                scores = jnp.where(segment_col == meta[1:2, cut], scores, masked_value)
                peak = jnp.max(scores, axis=0, keepdims=True)
                weights = jnp.exp2((scores - peak) * TO_EXP2)
                total = jnp.sum(weights, axis=0, keepdims=True)
                out_t[lanes, cut] = dot(v_t[lanes, :], weights.astype(jnp.bfloat16)) / total
                lse[pair, head : head + 1, cut] = peak * TO_EXP2 + jnp.log2(total)

        mixed[p.core, :, cols] = out_t[...].T.astype(jnp.bfloat16)
        piece = mixed.at[p.core, :, cols]
        remote(piece, piece, mixed_send.at[pair], mixed_recv.at[pair], p.sibling()).start()

    steps = [[] for _ in range(pairs)]
    plan = [lambda i=i, half=half: [getattr(w, half)() for w in group(i)]
            for i in range(n_chunks) for half in (("forward_second",) if i == 0 else ("forward_first", "forward_second"))]
    plan.insert(1, lambda: take_seq(cot, cot_send, cot_recv, swap_send.at[1]))

    def share_mixer():
        mixer.finish()
        piece = wm.at[p.core]
        remote(piece, piece, mix_send, mix_recv, p.sibling()).start()

    plan.insert(1, share_mixer)
    for i, step in enumerate(plan):
        steps[i * pairs // len(plan)].append(step)
    for pair in range(pairs):
        attention(pair)
        for step in steps[pair]:
            step()

    for pair in range(pairs):
        piece = mixed.at[p.core, :, pair * PAIR : (pair + 1) * PAIR]
        remote(piece, piece, mixed_send.at[pair], mixed_recv.at[pair], p.sibling()).wait_recv()
    piece = wm.at[p.core]
    remote(piece, piece, mix_send, mix_recv, p.sibling()).wait_recv()
    finish_seq(cot, cot_send, cot_recv, swap_send.at[1])

    @pl.loop(0, LEN // BLOCK)
    def _(i):
        cut = block_rows(i)
        value = tokens_at(cut) + dot(mixed[0, cut, :], wm[0]) + dot(mixed[1, cut, :], wm[1])
        normed, scale = norm(value)
        xhat[cut, :] = normed.astype(jnp.bfloat16)
        inv[cut, :] = jnp.broadcast_to(scale, (BLOCK, PAIR))
        second[cut, :] = (normed * gain_b).astype(jnp.bfloat16)
        shrunk[cut, :] = jnp.where(lanes_of((1, D)) // (D // CORES) == p.core, value, 0.0)
        back[cut, :] = jnp.zeros((BLOCK, D), jnp.float32)

    valid_16 = valid_col > 0.5
    top[...] = jnp.where(valid_16, jnp.concatenate([cot[j] for j in range(rows)], axis=1), jnp.zeros((), jnp.bfloat16))

    keep = []

    def store(src, dst):
        copy = pltpu.make_async_copy(src, dst, out_sem.at[len(keep)])
        keep.append(copy)
        copy.start()

    for j in range(rows):
        store(tok.at[j], o_tokens.at[j])
    for src, dst in ((first, o_first), (q_s, o_q), (k_s, o_k), (v_s, o_v), (mixed.at[p.core], o_mixed), (lse, o_lse),
                     (xhat, o_xhat), (inv, o_inv), (table, o_table), (top, o_top), (wj, o_joined), (wm.at[p.core], o_mixer)):
        store(src, dst)
    for j in range(rows):
        store(gains.at[j], o_small.at[:, pl.ds(j * width, width)])
    store(meta, o_small.at[:, pl.ds(D, LEN)])

    at = 0
    for i, (count, lanes) in enumerate(chunks):
        for weight in group(i):
            weight.finish()

        @pl.loop(0, LEN // BLOCK)
        def _(t):
            cut = block_rows(t)
            part, grad = second[cut, :], top[cut, :]
            gate = dot(part, wg[i][...])
            up = dot(part, wu[i][...])
            hidden_grad = dot(grad, ws[i][...], NT).astype(jnp.bfloat16).astype(jnp.float32)
            phi, density = gelu_parts(gate)
            act = gate * phi
            hidden = (act * up).astype(jnp.bfloat16)
            d_gate = (hidden_grad * up * (phi + gate * density)).astype(jnp.bfloat16)
            d_up = (hidden_grad * act).astype(jnp.bfloat16)
            hid[cut, :lanes] = hidden
            dgate[cut, :lanes] = d_gate
            dup[cut, :lanes] = d_up
            shrunk[cut, :] += dot(hidden, ws[i][...])
            back[cut, :] += dot(d_gate, wg[i][...], NT) + dot(d_up, wu[i][...], NT)

        @pl.loop(0, D // BLOCK)
        def _(d):
            cut = block_rows(d)
            g_gate[i][cut, :] = dot(second[:, cut], dgate[:, :lanes], TN).astype(jnp.bfloat16)
            g_up[i][cut, :] = dot(second[:, cut], dup[:, :lanes], TN).astype(jnp.bfloat16)
            g_shrink[i][:, cut] = dot(hid[:, :lanes], top[:, cut], TN).astype(jnp.bfloat16)

        store(g_gate[i], o_gate.at[:, pl.ds(at, lanes)])
        store(g_up[i], o_up.at[:, pl.ds(at, lanes)])
        store(g_shrink[i], o_shrink.at[pl.ds(at, lanes), :])
        at += lanes

    @pl.loop(0, LEN // BLOCK)
    def _(i):
        cut = block_rows(i)
        back_low[cut, :] = back[cut, :].astype(jnp.bfloat16)
        value = shrunk[cut, :]
        left, right = value[:, : D // 2], value[:, D // 2 :]
        own_half[cut, :] = jnp.where(p.core == 0, left, right)
        other_half[cut, :] = jnp.where(p.core == 0, right, left).astype(jnp.bfloat16)

    store(back_low, o_back)
    store(own_half, o_own)
    store(other_half, o_other)

    drain_seq(tokens_ref, tok, tok_send, tok_recv, swap_send.at[0])
    drain_seq(cot_ref, cot, cot_send, cot_recv, swap_send.at[1])
    for step in range(1, rows):
        remote(gains_ref, gains.at[p.row], gain_send.at[step], gain_recv.at[p.row], p.sibling()).wait_send()

    @pl.when(sends_meta)
    def _():
        for t in range(1, seqs):
            remote(meta_src.at[t], meta, meta_send.at[t], meta_recv, p.sibling()).wait_send()

        @pl.when(jnp.logical_not(is_here))
        def _():
            remote(meta_src.at[0], meta, meta_send.at[0], meta_recv, p.sibling()).wait_send()

    for pair in range(pairs):
        piece = mixed.at[p.core, :, pair * PAIR : (pair + 1) * PAIR]
        remote(piece, piece, mixed_send.at[pair], mixed_recv.at[pair], p.sibling()).wait_send()
    piece = wm.at[p.core]
    remote(piece, piece, mix_send, mix_recv, p.sibling()).wait_send()
    for weight in [joined, mixer] + gates + ups + shrinks:
        weight.drain()
    for copy in keep:
        copy.wait()


def forward(tokens, cot, lengths, gains, joined, mixer, gate, up, shrink, chunks):
    rows = lax.axis_size("row")
    seqs = rows // CORES
    width = tokens.shape[1]
    wide = mixer.shape[0]
    pairs = wide // PAIR
    n_chunks = len(chunks)
    padded = sum(lanes for _, lanes in chunks)
    weights = 2 + 3 * n_chunks
    bf16, f32 = jnp.bfloat16, jnp.float32
    freq = rope_base ** (-2.0 * jnp.arange(HD // 2, dtype=f32) / HD)
    freq = jnp.broadcast_to(jnp.concatenate([freq] * 4)[None, :], (8, PAIR))
    outs = [
        ((rows, LEN, width), bf16), ((LEN, D), bf16), ((LEN, wide), bf16), ((LEN, wide), bf16), ((LEN, wide), bf16),
        ((LEN, wide), bf16), ((pairs, 2, LEN), f32), ((LEN, D), bf16), ((LEN, PAIR), f32), ((LEN, D), bf16),
        ((LEN, D // 2), f32), ((LEN, D // 2), bf16), ((LEN, D), bf16),
        ((D, padded), bf16), ((D, padded), bf16), ((padded, D), bf16), ((D, 3 * wide), bf16), ((wide, D), bf16),
        ((8, D + LEN), f32), ((2, LEN, PAIR), f32),
    ]
    V, dma = pltpu.VMEM, pltpu.SemaphoreType.DMA
    widest = max(lanes for _, lanes in chunks)
    scratch = [
        V((rows, LEN, width), bf16), V((rows, LEN, width), bf16), V((seqs, 8, LEN), f32), V((8, LEN), f32),
        V((rows, 8, width), f32), V((2, LEN, PAIR), f32), V((LEN, D), bf16), V((D, 3 * wide), bf16), V((CORES, wide, D), bf16),
        [V((D, lanes), bf16) for _, lanes in chunks], [V((D, lanes), bf16) for _, lanes in chunks],
        [V((lanes, D), bf16) for _, lanes in chunks],
        V((LEN, wide), bf16), V((LEN, wide), bf16), V((LEN, wide), bf16), V((PAIR, LEN), bf16), V((PAIR, LEN), f32),
        V((pairs, 2, LEN), f32), V((CORES, LEN, wide), bf16), V((LEN, D), bf16), V((LEN, PAIR), f32), V((LEN, D), bf16),
        V((LEN, D), bf16), V((LEN, D), f32), V((LEN, D), f32), V((LEN, D), bf16), V((LEN, D // 2), f32), V((LEN, D // 2), bf16), V((LEN, widest), bf16), V((LEN, widest), bf16), V((LEN, widest), bf16),
        [V((D, lanes), bf16) for _, lanes in chunks], [V((D, lanes), bf16) for _, lanes in chunks],
        [V((lanes, D), bf16) for _, lanes in chunks],
        dma((seqs,)), dma((rows,)), dma((seqs,)), dma((rows,)), dma((2, seqs)), dma((seqs,)), dma, dma((rows,)), dma((rows,)),
        dma((weights, rows)), dma((weights, rows)), dma((weights, rows)), dma((weights, rows)), dma((weights, rows)),
        dma((weights,)), dma, dma, dma((pairs,)), dma((pairs,)), dma((2 * rows + 16 + 3 * n_chunks,)),
    ]
    anywhere = pl.BlockSpec(memory_space=pl.ANY)
    in_specs = [anywhere] * 10
    in_specs[2] = pl.BlockSpec(memory_space=pltpu.SMEM)
    in_specs[4] = pl.BlockSpec(memory_space=pltpu.VMEM)
    return pl.pallas_call(
        functools.partial(forward_kernel, chunks),
        in_specs=in_specs,
        out_specs=[anywhere] * len(outs),
        out_shape=[jax.ShapeDtypeStruct(*o) for o in outs],
        scratch_shapes=scratch,
        compiler_params=pltpu.CompilerParams(
            collective_id=0, has_side_effects=True, vmem_limit_bytes=62 * 1024 * 1024
        ),
        name="layer_forward",
    )(tokens, cot, lengths, gains, freq, joined, mixer, gate, up, shrink)


def add_rows(count, target, *parts):
    step = 32 if count % 32 == 0 else 16

    @pl.loop(0, count // step)
    def _(i):
        cut = pl.ds(pl.multiple_of(i * step, step), step)
        total = parts[0][cut, :].astype(jnp.float32)
        for part in parts[1:]:
            total = total + part[cut, :].astype(jnp.float32)
        target[cut, :] = total.astype(target.dtype)


def first_share(count):
    return count * 5 // 16 // 16 * 16


class Grad:
    KINDS = 12

    def __init__(self, place, block, rows, bufs, sems, credits, index, stage=None):
        self.p, self.block, self.m, self.index, self.sems, self.stage = place, block, rows, index, sems, stage
        self.credits = credits
        self.a = first_share(rows)
        self.b = rows - self.a
        self.recv_a, self.recv_b, self.acc, self.more, self.zbuf = bufs
        self.levels = (place.planes - 1).bit_length()

    def sem(self, kind, at=0):
        return self.sems.at[self.index, kind, at]

    def low(self):
        return self.acc.at[pl.ds(0, self.a), :]

    def high(self):
        return self.acc.at[pl.ds(self.a, self.b), :]

    def send(self, src, dst, kind, at, target):
        return remote(src, dst, self.sem(kind, at), self.sem(kind + 1, at), target)

    def landed(self, buf, kind, at=0):
        self.send(buf, buf, kind, at, self.p.sibling()).wait_recv()

    def left(self, buf, kind, at=0):
        self.send(buf, buf, kind, at, self.p.sibling()).wait_send()

    def copies_y(self):
        p = self.p
        return [
            self.send(self.block(p.row_after(s), 0, self.a), self.recv_a.at[s - 1], 0, s, p.at(row=p.row_after(s)))
            for s in range(1, p.rows)
        ]

    def copies_x(self):
        return [
            self.send(self.block(j, self.a, self.b), self.recv_b.at[j], 2, j, self.p.across())
            for j in range(self.p.rows)
        ]

    def begin(self):
        for copy in self.copies_y():
            copy.start()

        @pl.when(jnp.logical_not(self.p.matched))
        def _():
            for copy in self.copies_x():
                copy.start()

    def own(self, row, start, size, slot):
        piece = self.block(row, start, size)
        if self.stage is None:
            return piece
        buf, sem = self.stage
        buf = buf.at[pl.ds(0, size), :]
        copy = pltpu.make_async_copy(piece, buf, sem)
        copy.start()
        copy.wait()
        return buf

    def sum_y(self):
        p = self.p
        own = self.own(p.row, 0, self.a, 0)
        for s in range(1, p.rows):
            self.landed(self.recv_a.at[s - 1], 0, s)
        add_rows(self.a, self.recv_a.at[0], own, *[self.recv_a.at[s - 1] for s in range(1, p.rows)])

        @pl.when(jnp.logical_not(p.matched))
        def _():
            self.send(self.recv_a.at[0], self.low(), 4, 0, p.across()).start()

    def sum_x(self):
        p = self.p

        @pl.when(p.matched)
        def _():
            for s in list(range(1, p.rows)) + [0]:
                row = p.row_after(s)
                own = self.own(row, self.a, self.b, 0)
                buf = self.recv_b.at[row]
                self.landed(buf, 2, row)
                add_rows(self.b, buf, own, buf)
                if s:
                    target = self.high() if s == 1 else self.more.at[s - 2]
                    self.send(buf, target, 6, s, p.at(row=row)).start()

    def span(self, level):
        start, size = 0, self.m
        for i in range(level):
            size //= 2
            start = start + self.bit(i) * size
        return start, size

    def bit(self, level):
        return lax.rem(self.p.z // (1 << level), 2)

    def plane(self, level):
        return self.p.at(z=self.p.z + (1 << level) * (1 - 2 * self.bit(level)))

    def rows_of(self, start, size):
        return self.acc.at[pl.ds(pl.multiple_of(start, 16), size), :]

    def z_copy(self, level):
        start, size = self.span(level)
        half = size // 2
        piece = self.rows_of(start + (1 - self.bit(level)) * half, half)
        return self.send(piece, self.zbuf[level], 8, level, self.plane(level))

    def z_back(self, level):
        piece = self.rows_of(*self.span(level + 1))
        return self.send(piece, piece, 10, level, self.plane(level))

    def z_return(self, level):
        pl.semaphore_wait(self.credits.at[self.index, level], 1)
        self.z_back(level).start()

    def sum_both(self):
        p = self.p

        @pl.when(p.matched)
        def _():
            self.landed(self.low(), 4)
            add_rows(self.a, self.low(), self.low(), self.recv_a.at[0])
            others = []
            for s in range(1, p.rows):
                buf = self.high() if s == 1 else self.more.at[s - 2]
                self.landed(buf, 6, s)
                others.append(buf)
            add_rows(self.b, self.high(), self.recv_b.at[p.row], *others)
            self.z_copy(0).start()

    def sum_z(self, level):
        @pl.when(self.p.matched)
        def _():
            start, size = self.span(level + 1)
            self.landed(self.zbuf[level], 8, level)
            piece = self.rows_of(start, size)
            add_rows(size, piece, piece, self.zbuf[level])
            self.z_copy(level).wait_send()
            pl.semaphore_signal(
                self.credits.at[self.index, level], inc=1, device_id=self.plane(level), device_id_type=MESH_ID
            )
            if level + 1 < self.levels:
                self.z_copy(level + 1).start()
            else:
                self.z_return(level)

    def give_z(self, level):
        @pl.when(self.p.matched)
        def _():
            start, size = self.span(level)
            half = size // 2
            self.landed(self.rows_of(start + (1 - self.bit(level)) * half, half), 10, level)
            if level:
                self.z_return(level - 1)
            else:
                self.final().start()

    def final(self):
        return remote(self.acc, self.acc, self.sem(12), self.sem(13), self.p.sibling())

    def store(self, out, sem):
        @pl.when(jnp.logical_not(self.p.matched))
        def _():
            self.final().wait_recv()

        copy = pltpu.make_async_copy(self.acc.at[pl.ds(0, out.shape[0]), pl.ds(0, out.shape[1])], out, sem)
        copy.start()
        return copy

    def drain(self):
        p = self.p
        for copy in self.copies_y():
            copy.wait_send()

        @pl.when(jnp.logical_not(p.matched))
        def _():
            for copy in self.copies_x():
                copy.wait_send()
            self.left(self.recv_a.at[0], 4)

        @pl.when(p.matched)
        def _():
            for s in range(1, p.rows):
                self.left(self.recv_b.at[0], 6, s)
            for level in range(self.levels):
                self.z_back(level).wait_send()
            self.final().wait_send()


def grad_bufs(rows, cols, blocks, planes):
    a = first_share(rows)
    V = lambda *shape: pltpu.VMEM(shape, jnp.bfloat16)
    levels = (planes - 1).bit_length()
    return [
        V(blocks - 1, a, cols), V(blocks, rows - a, cols), V(rows, cols), V(max(1, blocks - 2), rows - a, cols) if blocks > 2 else V(16, 128),
        [V(rows >> (i + 1), cols) for i in range(levels)],
    ]


def backward_kernel(
    tokens_ref, first_ref, q_ref, k_ref, v_ref, mixed_ref, lse_ref, xhat_ref, inv_ref, top_ref, own_ref, other_ref, back_ref,
    gate_ref, up_ref, shrink_ref, joined_ref, mixer_ref, small_ref, table_ref,
    o_block, o_input, o_joined, o_mixer, o_gate, o_up, o_shrink, o_gains,
    q_s, k_s, v_s, mixed, xa, xb, xc, wj, wm, lse, inv, small, table, back_other, keep_grad, middle_low, mixed_grad, g_mixer, g_joined, first_other,
    dk, dv, dq_t, k_t, own_half, other_half, block_half, gain_sum, gain_y, gain_x, gain_z, stage_row, stage_lane,
    shrink_bufs, gate_bufs, up_bufs, mixer_bufs, joined_bufs,
    load_sem, stage_sem, grad_sem, credit, back_send, back_recv, other_send, other_recv, first_send, first_recv, out_send, out_recv, in_send, in_recv,
    gain_send, gain_recv, out_sem,
):
    p = Place()
    rows, seqs, planes = p.rows, p.seqs, p.planes
    width = D // rows
    wide = q_s.shape[1]
    pairs = wide // PAIR
    levels = (planes - 1).bit_length()

    def by_row(ref):
        return lambda j, start, size: ref.at[pl.ds(pl.multiple_of(j * width + start, 16), size), :]

    def by_lane(ref):
        return lambda j, start, size: ref.at[pl.ds(start, size), pl.ds(pl.multiple_of(j * width, width), width)]

    shrink = Grad(p, by_lane(shrink_ref), shrink_ref.shape[0], shrink_bufs, grad_sem, credit, 0, (stage_lane, stage_sem.at[0]))
    gate = Grad(p, by_row(gate_ref), width, gate_bufs, grad_sem, credit, 1, (stage_row, stage_sem.at[1]))
    up = Grad(p, by_row(up_ref), width, up_bufs, grad_sem, credit, 2, (stage_row, stage_sem.at[2]))
    mixer = Grad(p, by_lane(g_mixer), wide, mixer_bufs, grad_sem, credit, 3)
    joined = Grad(p, by_row(g_joined), width, joined_bufs, grad_sem, credit, 4)

    sem = pltpu.get_barrier_semaphore()
    count = CORES * rows
    partners = [p.across()]
    for level in range(levels):
        bit = lax.rem(p.z // (1 << level), 2)
        partners.append(p.at(z=p.z + (1 << level) * (1 - 2 * bit)))
    for step in range(1, count):
        flat = lax.rem(p.core * rows + p.row + step, count)
        partners.append(p.at(core=flat // rows, row=lax.rem(flat, rows)))
    loads = {}

    def load(name, src, dst):
        copy = pltpu.make_async_copy(src, dst, load_sem.at[len(loads)])
        copy.start()
        loads[name] = copy

    load("small", small_ref, small)
    load("back", back_ref, xc)
    load("xhat", xhat_ref, xa)
    load("inv", inv_ref, inv)
    load("top", top_ref, xb)
    load("mixer", mixer_ref, wm)
    load("mixed", mixed_ref, mixed)
    load("q", q_ref, q_s)
    load("k", k_ref, k_s)
    load("v", v_ref, v_s)
    load("lse", lse_ref, lse)
    load("table", table_ref, table)
    load("joined", joined_ref, wj)
    load("own", own_ref, own_half)
    for partner in partners:
        pl.semaphore_signal(sem, inc=1, device_id=partner, device_id_type=MESH_ID)
    pl.semaphore_wait(sem, len(partners))

    def swap_block(i, src, dst, send, recv):
        cut = pl.ds(i * BLOCK, BLOCK)
        return remote(src.at[cut, :], dst.at[cut, :], send.at[i], recv.at[i], p.sibling())

    blocks_n = LEN // BLOCK
    for i in range(blocks_n):
        swap_block(i, back_ref, back_other, back_send, back_recv).start()
    for grad in (shrink, gate, up):
        grad.begin()
    other_copy = remote(other_ref, other_half, other_send, other_recv, p.sibling())
    other_copy.start()

    for name in ("small", "back", "xhat", "inv", "top", "mixer", "mixed"):
        loads[name].wait()
    gain_a, gain_b = small[0:1, :D], small[1:2, :D]
    gain_sum[...] = jnp.zeros_like(gain_sum)

    def norm_back(grad, normed, scale, gain):
        scaled = grad * gain
        mean_a = jnp.mean(scaled, axis=-1, keepdims=True)
        mean_b = jnp.mean(scaled * normed, axis=-1, keepdims=True)
        return scale * (scaled - mean_a - normed * mean_b)

    def own_of(value):
        return jnp.where(p.core == 0, value[:, : D // 2], value[:, D // 2 :])

    for i in range(blocks_n):
        cut = slice(i * BLOCK, (i + 1) * BLOCK)
        swap_block(i, back_ref, back_other, back_send, back_recv).wait_recv()
        grad = xc[cut, :].astype(jnp.float32) + back_other[cut, :].astype(jnp.float32)
        normed = xa[cut, :].astype(jnp.float32)
        gain_sum[1:2, :] += jnp.sum(grad * normed, axis=0, keepdims=True)
        value = xb[cut, :].astype(jnp.float32) + norm_back(grad, normed, inv[cut, 0:1], gain_b)
        keep_grad[cut, :] = own_of(value)
        value = value.astype(jnp.bfloat16)
        middle_low[cut, :] = value
        mixed_grad[cut, :] = dot(value, wm[...], NT).astype(jnp.bfloat16)

    @pl.loop(0, D // BLOCK)
    def _(d):
        cut = block_rows(d)
        g_mixer[:, cut] = dot(mixed[...], middle_low[:, cut], TN).astype(jnp.bfloat16)

    mixer.begin()
    load("first", first_ref, xa)
    for j in range(rows):
        load(f"tokens{j}", tokens_ref.at[j], xb.at[:, pl.ds(j * width, width)])

    def leave(src, dst, send, recv):
        core, seq = p.row // seqs, lax.rem(p.row, seqs)
        copies = []
        for u in range(seqs):
            row = p.core * seqs + u
            is_self = jnp.logical_and(core == p.core, row == p.row)
            piece = src.at[:, pl.ds(u * width, width)]
            copies.append((is_self, piece, dst(seq), send.at[u], recv.at[seq], p.at(core=core, row=row)))
        return copies

    def leave_start(copies):
        for is_self, piece, place, send, recv, target in copies:
            @pl.when(is_self)
            def _():
                pltpu.make_async_copy(piece, place, recv).start()

            @pl.when(jnp.logical_not(is_self))
            def _():
                remote(piece, place, send, recv, target).start()

    def leave_wait(copies, dst, recv):
        for s in range(seqs):
            pltpu.make_async_copy(dst(s), dst(s), recv.at[s]).wait()
        for is_self, piece, place, send, recv_sem, target in copies:
            @pl.when(jnp.logical_not(is_self))
            def _():
                remote(piece, place, send, recv_sem, target).wait_send()

    out_at = lambda s: o_block.at[pl.ds(pl.multiple_of(s * LEN, LEN), LEN), :]
    in_at = lambda s: o_input.at[pl.ds(pl.multiple_of(s * LEN, LEN), LEN), :]
    out_copies = leave(block_half, out_at, out_send, out_recv)
    in_copies = leave(mixed_grad, in_at, in_send, in_recv)

    def block_output():
        loads["own"].wait()
        other_copy.wait()
        add_rows(LEN, block_half, own_half, other_half)
        leave_start(out_copies)

    shrink.sum_y()
    gate.sum_y()
    for name in ("q", "k", "v", "lse", "table"):
        loads[name].wait()
    columns = small[:, D:].T
    segment_col = columns[:, 1:2]

    def attention(pair):
        cols = slice(pair * PAIR, (pair + 1) * PAIR)
        product = mixed[:, cols].astype(jnp.float32) * mixed_grad[:, cols].astype(jnp.float32)
        chooser = lax.broadcasted_iota(jnp.int32, (8, PAIR), 0) == lanes_of((8, PAIR)) // HD
        delta = dot(chooser.astype(jnp.float32), product, NT, precision=lax.Precision.HIGHEST)
        keys, values = k_s[:, cols], v_s[:, cols]
        k_t[...] = keys.astype(jnp.float32).T.astype(jnp.bfloat16)
        dk[...] = jnp.zeros_like(dk)
        dv[...] = jnp.zeros_like(dv)
        for head in range(2):
            lanes = slice(head * HD, (head + 1) * HD)
            for i in range(LEN // BLOCK):
                cut = slice(i * BLOCK, (i + 1) * BLOCK)
                q_part, g_part = only_head(q_s[cut, cols], head), only_head(mixed_grad[cut, cols], head)
                scores = dot(keys, q_part, NT)
                probs = jnp.exp2(scores * TO_EXP2 - lse[pair, head : head + 1, cut])
                probs = jnp.where(segment_col == small[1:2, D + i * BLOCK : D + (i + 1) * BLOCK], probs, 0.0)
                probs_grad = dot(values, g_part, NT)
                scores_grad = (probs * (probs_grad - delta[head : head + 1, cut])).astype(jnp.bfloat16)
                dv[...] += dot(probs.astype(jnp.bfloat16), g_part)
                dk[...] += dot(scores_grad, q_part)
                dq_t[lanes, cut] = dot(k_t[lanes, :], scores_grad)
        cosine, sine = table[0], table[1]
        scale = 1.0 / math.sqrt(HD)
        dqs = dq_t[...].T * scale
        q_s[:, cols] = (dqs * cosine - swap_halves(dqs) * sine).astype(jnp.bfloat16)
        dks = dk[...] * scale
        k_s[:, cols] = (dks * cosine - swap_halves(dks) * sine).astype(jnp.bfloat16)
        v_s[:, cols] = dv[...].astype(jnp.bfloat16)

    between = [
        [shrink.sum_x, up.sum_y],
        [shrink.sum_both, mixer.sum_y],
        [lambda: shrink.sum_z(0), gate.sum_x],
        [],
    ]
    for pair in range(pairs):
        attention(pair)
        for step in between[pair] if pair < len(between) else []:
            step()

    loads["first"].wait()

    @pl.loop(0, D // BLOCK)
    def _(d):
        cut = block_rows(d)
        part = xa[:, cut]
        for j, back in enumerate((q_s, k_s, v_s)):
            g_joined[cut, j * wide : (j + 1) * wide] = dot(part, back[...], TN).astype(jnp.bfloat16)

    joined.begin()
    loads["joined"].wait()
    for i in range(blocks_n):
        cut = slice(i * BLOCK, (i + 1) * BLOCK)
        value = dot(q_s[cut, :], wj[:, :wide], NT) + dot(k_s[cut, :], wj[:, wide : 2 * wide], NT)
        value = value + dot(v_s[cut, :], wj[:, 2 * wide :], NT)
        xc[cut, :] = value.astype(jnp.bfloat16)
        swap_block(i, xc, first_other, first_send, first_recv).start()

    def steps(*todo):
        for step in todo:
            step()

    each = range(levels)
    z_sum = lambda grad: [functools.partial(grad.sum_z, level) for level in each]
    z_give = lambda grad: [functools.partial(grad.give_z, level) for level in reversed(each)]
    steps(*z_sum(shrink)[1:], gate.sum_both)
    for j in range(rows):
        loads[f"tokens{j}"].wait()
    for i in range(blocks_n):
        cut = slice(i * BLOCK, (i + 1) * BLOCK)
        swap_block(i, xc, first_other, first_send, first_recv).wait_recv()
        grad = xc[cut, :].astype(jnp.float32) + first_other[cut, :].astype(jnp.float32)
        values = xb[cut, :].astype(jnp.float32)
        values = values - jnp.mean(values, axis=-1, keepdims=True)
        scale = lax.rsqrt(jnp.mean(values * values, axis=-1, keepdims=True) + norm_eps)
        normed = values * scale
        gain_sum[0:1, :] += jnp.sum(grad * normed, axis=0, keepdims=True)
        total = keep_grad[cut, :] + own_of(norm_back(grad, normed, scale, gain_a))
        mixed_grad[cut, :] = total.astype(jnp.bfloat16)
    leave_start(in_copies)

    def gain_copies():
        return [
            remote(gain_sum.at[:, pl.ds(pl.multiple_of(p.row_after(s) * width, width), width)], gain_y.at[s],
                   gain_send.at[s], gain_recv.at[s], p.at(row=p.row_after(s)))
            for s in range(1, rows)
        ]

    for copy in gain_copies():
        copy.start()
    steps(up.sum_x, *z_give(shrink)[:1], lambda: gate.sum_z(0), block_output, mixer.sum_x, joined.sum_y)
    for s in range(1, rows):
        remote(gain_y.at[s], gain_y.at[s], gain_send.at[s], gain_recv.at[s], p.sibling()).wait_recv()
    total = gain_sum[:, pl.ds(pl.multiple_of(p.row * width, width), width)]
    for s in range(1, rows):
        total = total + gain_y[s]
    gain_x[0] = total
    gain_across = remote(gain_x.at[0], gain_x.at[1], gain_send.at[rows], gain_recv.at[rows], p.across())
    gain_across.start()
    steps(*z_give(shrink)[1:], *z_sum(gate)[1:], up.sum_both, mixer.sum_both)
    gain_across.wait()
    gain_z[0] = gain_x[0] + gain_x[1]

    def gain_plane(level):
        bit = lax.rem(p.z // (1 << level), 2)
        return remote(gain_z.at[2 * level], gain_z.at[2 * level + 1], gain_send.at[rows + 1 + level],
                      gain_recv.at[rows + 1 + level], p.at(z=p.z + (1 << level) * (1 - 2 * bit)))

    stores = []

    def store(src_grad, out):
        stores.append(src_grad.store(out, out_sem.at[len(stores)]))

    gain_plane(0).start()
    steps(*z_give(gate)[:1], lambda: up.sum_z(0), lambda: mixer.sum_z(0), joined.sum_x)
    for level in each:
        gain_plane(level).wait()
        gain_z[2 * level + 2] = gain_z[2 * level] + gain_z[2 * level + 1]
        if level + 1 < levels:
            gain_plane(level + 1).start()
    store(shrink, o_shrink)
    steps(*z_give(gate)[1:], *z_sum(up)[1:], *z_sum(mixer)[1:], joined.sum_both)
    store(gate, o_gate)
    steps(lambda: joined.sum_z(0), *z_give(up)[:1], *z_give(mixer)[:1], *z_sum(joined)[1:])
    steps(*z_give(up)[1:], *z_give(mixer)[1:], *z_give(joined))
    store(up, o_up)
    store(mixer, o_mixer)
    store(joined, o_joined)
    gains_out = pltpu.make_async_copy(gain_z.at[2 * levels], o_gains, out_sem.at[len(stores)])
    gains_out.start()

    leave_wait(out_copies, out_at, out_recv)
    leave_wait(in_copies, in_at, in_recv)
    for i in range(blocks_n):
        swap_block(i, back_ref, back_other, back_send, back_recv).wait_send()
        swap_block(i, xc, first_other, first_send, first_recv).wait_send()
    for copy in gain_copies():
        copy.wait_send()
    for grad in (shrink, gate, up, mixer, joined):
        grad.drain()
    for copy in stores:
        copy.wait()
    gains_out.wait()


def backward(saved, hidden_here):
    (tokens, first, queries, keys, values, mixed, lse, xhat, inv, top, own, other, back, gate, up, shrink, joined, mixer,
     small, table) = saved
    rows = lax.axis_size("row")
    planes = lax.axis_size("dp") // CORES
    seqs = rows // CORES
    width = D // rows
    wide = queries.shape[1]
    pairs = wide // PAIR
    padded = gate.shape[1]
    levels = (planes - 1).bit_length()
    bf16, f32 = jnp.bfloat16, jnp.float32
    V, dma = pltpu.VMEM, pltpu.SemaphoreType.DMA
    outs = [
        ((seqs * LEN, width), bf16), ((seqs * LEN, width), bf16), ((width, 3 * wide), bf16), ((wide, width), bf16),
        ((width, padded), bf16), ((width, padded), bf16), ((hidden_here, width), bf16), ((8, width), f32),
    ]
    scratch = [
        V((LEN, wide), bf16), V((LEN, wide), bf16), V((LEN, wide), bf16), V((LEN, wide), bf16),
        V((LEN, D), bf16), V((LEN, D), bf16), V((LEN, D), bf16), V((D, 3 * wide), bf16), V((wide, D), bf16),
        V((pairs, 2, LEN), f32), V((LEN, PAIR), f32), V((8, D + LEN), f32), V((2, LEN, PAIR), f32), V((LEN, D), bf16),
        V((LEN, D // 2), f32), V((LEN, D), bf16), V((LEN, wide), bf16), V((wide, D), bf16), V((D, 3 * wide), bf16), V((LEN, D), bf16),
        V((LEN, PAIR), f32), V((LEN, PAIR), f32), V((PAIR, LEN), f32), V((PAIR, LEN), bf16),
        V((LEN, D // 2), f32), V((LEN, D // 2), bf16), V((LEN, D // 2), bf16),
        V((8, D), f32), V((rows, 8, width), f32), V((2, 8, width), f32), V((2 * levels + 1, 8, width), f32),
        V((width - first_share(width), padded), bf16), V((padded - first_share(padded), width), bf16),
        grad_bufs(padded, width, rows, planes), grad_bufs(width, padded, rows, planes), grad_bufs(width, padded, rows, planes),
        grad_bufs(wide, width, rows, planes), grad_bufs(width, 3 * wide, rows, planes),
        dma((15 + rows,)), dma((3,)), dma((5, 14, max(rows, levels))), pltpu.SemaphoreType.REGULAR((5, levels)),
        dma((4,)), dma((4,)), dma, dma, dma((4,)), dma((4,)),
        dma((seqs,)), dma((seqs,)), dma((seqs,)), dma((seqs,)), dma((rows + 1 + levels,)), dma((rows + 1 + levels,)), dma((6,)),
    ]
    anywhere = pl.BlockSpec(memory_space=pl.ANY)
    return pl.pallas_call(
        backward_kernel,
        in_specs=[anywhere] * len(saved),
        out_specs=[anywhere] * len(outs),
        out_shape=[jax.ShapeDtypeStruct(*o) for o in outs],
        scratch_shapes=scratch,
        compiler_params=pltpu.CompilerParams(
            collective_id=1, has_side_effects=True, vmem_limit_bytes=62 * 1024 * 1024
        ),
        name="layer_backward",
    )(*saved)


def shards(
    tokens_in, lengths, first_gain, joined_weight, mixer_weight, second_gain, expand_weight, shrink_weight, cotangent
):
    rows, cols = lax.axis_size("row"), lax.axis_size("col")
    width = tokens_in.shape[1]
    wide = joined_weight.shape[2]
    hidden_here = shrink_weight.shape[0]
    assert tokens_in.shape[0] * CORES == LEN * rows and cols == CORES
    chunks = ((512, 512), (512, 512), (hidden_here - 1024, 384))
    padded = sum(lanes for _, lanes in chunks)
    gains = jnp.pad(jnp.stack([first_gain, second_gain]), ((0, 6), (0, 0)))
    fit = lambda w: jnp.pad(w, ((0, 0), (0, padded - hidden_here)))
    saved = forward(
        tokens_in, cotangent, lengths, gains, joined_weight.reshape(width, 3 * wide), mixer_weight,
        fit(expand_weight[:, 0]), fit(expand_weight[:, 1]), shrink_weight, chunks,
    )
    block_output, input_grad, joined_grad, mixer_grad, gate_grad, up_grad, shrink_grad, gain_grads = backward(
        saved, hidden_here
    )
    f32 = jnp.float32
    expand_grad = jnp.stack([gate_grad[:, :hidden_here], up_grad[:, :hidden_here]], axis=1)
    return (
        block_output,
        input_grad.astype(f32),
        joined_grad.reshape(width, 3, wide).astype(f32),
        mixer_grad.astype(f32),
        expand_grad.astype(f32),
        shrink_grad.astype(f32),
        gain_grads[0],
        gain_grads[1],
    )


def solution(mesh):
    placed = (
        P(("dp", "col"), "row"),
        P("dp", None),
        P("row"),
        P("row", None, "col"),
        P("col", "row"),
        P("row"),
        P("row", None, "col"),
        P("col", "row"),
        P(("dp", "col"), "row"),
    )
    return jax.shard_map(
        shards,
        mesh=mesh,
        in_specs=placed,
        out_specs=(
            P(("dp", "col"), "row"),
            P(("dp", "col"), "row"),
            P("row", None, "col"),
            P("col", "row"),
            P("row", None, "col"),
            P("col", "row"),
            P("row"),
            P("row"),
        ),
        check_vma=False,
    )
```

```python
import functools
import math

import jax
import jax.numpy as jnp
from jax import lax
from jax.experimental import pallas as pl
from jax.experimental.pallas import tpu as pltpu
from jax.sharding import PartitionSpec as P

D = 1024
HEADS = 16
HD = 64
FF = 2624
LEN = 1024
DOCS = 6
MOST = 800
CORES = 2

rope_base = 160000.0
norm_eps = 1e-05
masked_value = -1000000000.0

PAIR = 2 * HD
WIDE = 256
SOLID = MOST // WIDE * WIDE
REST = LEN - MOST
TO_EXP2 = math.log2(math.e) / math.sqrt(HD)

NT = (((1,), (1,)), ((), ()))
TN = (((0,), (0,)), ((), ()))
MESH_AXES = ("dp", "row", "col")


def lanes_of(shape):
    return lax.broadcasted_iota(jnp.int32, shape, len(shape) - 1)


def swap_halves(u):
    low_half = lanes_of(u.shape) % HD < HD // 2
    return jnp.where(low_half, pltpu.roll(u, PAIR - HD // 2, 1), pltpu.roll(u, HD // 2, 1))


def dot(left, right, dims=(((1,), (0,)), ((), ())), **more):
    return lax.dot_general(left, right, dims, preferred_element_type=jnp.float32, **more)


def only_head(values, head):
    return jnp.where(lanes_of(values.shape) // HD == head, values, jnp.zeros_like(values))


MESH_ID = pl.DeviceIdType.MESH
BLOCK = 256
HALF_ROWS = LEN // 2


class Place:
    def __init__(self):
        self.rows, self.cols = lax.axis_size("row"), lax.axis_size("col")
        self.planes = lax.axis_size("dp") // CORES
        dp = lax.axis_index("dp")
        self.z, self.core = dp // CORES, dp % CORES
        self.row, self.col = lax.axis_index("row"), lax.axis_index("col")
        self.matched = self.core == self.col
        self.parity = self.z % 2
        self.inner = self.parity != (self.z // 2) % 2
        self.seqs = self.rows // CORES

    def at(self, z=None, core=None, row=None, col=None):
        z = self.z if z is None else z
        core = self.core if core is None else core
        return (z * CORES + core, self.row if row is None else row, self.col if col is None else col)

    def sibling(self):
        return self.at(core=1 - self.core)

    def across(self):
        return self.at(col=1 - self.col)

    def pair(self):
        return self.at(z=self.z + 1 - 2 * self.parity)

    def row_after(self, step):
        return lax.rem(self.row + step, self.rows)

    def row_before(self, step):
        return lax.rem(self.row + self.rows - step, self.rows)

    def group_bit(self, level):
        return lax.rem(self.z // (1 << level), 2)

    def mate(self, level):
        if level == 0:
            return self.pair()
        group = self.z // 2
        other = group + (1 << (level - 1)) * (1 - 2 * self.group_bit(level))
        shift = lax.rem(group, 2) + self.parity
        return self.at(z=2 * other + lax.rem(shift + lax.rem(other, 2), 2))

    def barrier(self, partners):
        sem = pltpu.get_barrier_semaphore()
        count = CORES * self.rows
        partners = list(partners)
        for step in range(1, count):
            flat = lax.rem(self.core * self.rows + self.row + step, count)
            partners.append(self.at(core=flat // self.rows, row=lax.rem(flat, self.rows)))
        for partner in partners:
            pl.semaphore_signal(sem, inc=1, device_id=partner, device_id_type=MESH_ID)
        pl.semaphore_wait(sem, len(partners))


def remote(src, dst, send, recv, target):
    return pltpu.make_async_remote_copy(
        src_ref=src, dst_ref=dst, send_sem=send, recv_sem=recv, device_id=target, device_id_type=MESH_ID
    )


def shares(count):
    one = count * 2 // 5 // 16 * 16
    return count - 2 * one, one


class Weight:
    def __init__(self, place, source, slot, count, sems, index):
        self.place, self.source, self.slot = place, source, slot
        self.both, self.one = shares(count)
        self.sems = sems
        self.index = index
        self.local = sems[5].at[index]

    def sem(self, kind, row):
        return self.sems[kind].at[self.index, row]

    def plane_part(self):
        return self.place.parity * self.one, self.one + self.both

    def pair_part(self):
        return self.place.parity * (self.one + self.both), self.one

    def other_part(self):
        return (1 - self.place.parity) * (self.one + self.both), self.one

    def own_y(self):
        p = self.place
        start, size = self.plane_part()
        for step in range(1, p.rows):
            remote(
                self.source(start, size),
                self.slot(p.row, start, size),
                self.sem(0, step),
                self.sem(3, p.row),
                p.at(row=p.row_after(step)),
            ).start()

    def own_x(self):
        p = self.place
        start, size = self.plane_part()
        remote(
            self.source(start, size), self.slot(p.row, start, size), self.sem(1, 0), self.sem(3, p.row), p.across()
        ).start()
        pltpu.make_async_copy(
            self.source(0, 2 * self.one + self.both), self.slot(p.row, 0, 2 * self.one + self.both), self.local
        ).start()

    def pass_on(self):
        p = self.place
        for step in range(1, p.rows):
            row = p.row_before(step)
            self.wait_plane(row)
            self.send_across(row, step).start()
            self.send_pair(row, step).start()

    def take_first(self):
        self.wait_plane(self.place.row)
        self.send_pair(self.place.row, 0).start()

    def take_others(self):
        p = self.place
        for step in range(1, p.rows):
            row = p.row_before(step)
            self.wait_plane(row)
            self.send_pair(row, step).start()

    def wait_plane(self, row):
        p = self.place
        start, size = self.plane_part()
        piece = self.slot(row, start, size)
        remote(piece, piece, self.sem(0, 0), self.sem(3, row), p.across()).wait_recv()

    def send_pair(self, row, step):
        start, size = self.pair_part()
        piece = self.slot(row, start, size)
        return remote(piece, piece, self.sem(2, step), self.sem(4, row), self.place.pair())

    def send_across(self, row, step):
        start, size = self.plane_part()
        piece = self.slot(row, start, size)
        return remote(piece, piece, self.sem(1, step), self.sem(3, row), self.place.across())

    def finish(self):
        p = self.place
        start, size = self.other_part()

        def wait_other(row):
            piece = self.slot(row, start, size)
            remote(piece, piece, self.sem(2, 0), self.sem(4, row), p.pair()).wait_recv()

        for step in range(1, p.rows):
            wait_other(p.row_before(step))

        @pl.when(p.matched)
        def _():
            whole = self.slot(p.row, 0, 2 * self.one + self.both)
            pltpu.make_async_copy(whole, whole, self.local).wait()

        @pl.when(jnp.logical_not(p.matched))
        def _():
            wait_other(p.row)

    def drain(self):
        p = self.place
        start, size = self.plane_part()
        piece = self.slot(p.row, start, size)
        for step in range(1, p.rows):
            self.send_pair(p.row, step).wait_send()

        @pl.when(p.matched)
        def _():
            for step in range(1, p.rows):
                remote(piece, piece, self.sem(0, step), self.sem(3, p.row), p.across()).wait_send()
            for step in range(p.rows):
                self.send_across(p.row, step).wait_send()

        @pl.when(jnp.logical_not(p.matched))
        def _():
            self.send_pair(p.row, 0).wait_send()


def block_rows(i, size=BLOCK):
    return pl.ds(pl.multiple_of(i * size, size), size)


def gelu_parts(gate):
    phi = 0.5 * (1.0 + lax.erf(gate * (1.0 / math.sqrt(2.0))))
    return phi, jnp.exp(gate * gate * -0.5) * (1.0 / math.sqrt(2.0 * math.pi))


def forward_kernel(
    chunks,
    tokens_ref, cot_ref, lengths_ref, gains_ref, freq_ref, joined_ref, mixer_ref, expand_ref, shrink_ref,
    *rest,
):
    n_chunks = len(chunks)
    outs, scratch = rest[:19], rest[19:]
    (o_tokens, o_first, o_q, o_k, o_v, o_mixed, o_lse, o_xhat, o_inv, o_top, o_own, o_other, o_back,
     o_expand, o_shrink, o_joined, o_mixer, o_small, o_table) = outs
    (tok, cot, meta_src, meta, gains, table, first, wj, wm, wg, wu, ws, q_s, k_s, v_s, v_t, out_t, lse, mixed, xhat, inv, second,
     top, shrunk, back, back_low, own_half, other_half, hid, dgate, dup, g_expand, g_shrink,
     tok_send, tok_recv, cot_send, cot_recv, swap_send, meta_send, meta_recv, gain_send, gain_recv,
     w_y, w_x, w_z, w_recv, w_recv_z, w_local, mix_send, mix_recv, mixed_send, mixed_recv, out_sem) = scratch
    p = Place()
    rows, seqs = p.rows, p.seqs
    width = tokens_ref.shape[1]
    wide = q_s.shape[1]
    pairs = wide // PAIR
    sems = (w_y, w_x, w_z, w_recv, w_recv_z, w_local)

    def down(ref, buf, col, size):
        source = lambda start, n: ref.at[:, pl.ds(start, n), pl.ds(col, size)]
        slot = lambda row, start, n: buf.at[:, pl.ds(row * width + start, n), :]
        return source, slot

    def along(ref, buf, at):
        source = lambda start, n: ref.at[pl.ds(at + start, n), :]
        slot = lambda row, start, n: buf.at[pl.ds(start, n), pl.ds(pl.multiple_of(row * width, width), width)]
        return source, slot

    half = wide // 2
    joined = [Weight(p, *down(joined_ref, wj.at[h], half * h, half), width, sems, h) for h in range(2)]
    mixer = Weight(p, *along(mixer_ref, wm.at[p.core], 0), wide, sems, 2)
    groups, at = [], 0
    for i, count in enumerate(chunks):
        groups.append([
            Weight(p, *along(ref, buf, at), count, sems, 3 + 3 * i + n)
            for n, (ref, buf) in enumerate(((expand_ref.at[0], wg[i]), (expand_ref.at[1], wu[i]), (shrink_ref, ws[i])))
        ])
        at += count

    place_row = lanes_of((1, LEN))
    for s in range(seqs):
        base = [lengths_ref[p.col * seqs + s, d] for d in range(DOCS)]
        segment = jnp.zeros((1, LEN), jnp.int32)
        start = jnp.zeros((1, LEN), jnp.int32)
        end = jnp.int32(0)
        for d in range(DOCS):
            end = end + base[d]
            past = place_row >= end
            segment = segment + past.astype(jnp.int32)
            start = jnp.where(past, end, start)
        meta_src[s, 0:1, :] = (place_row - start).astype(jnp.float32)
        meta_src[s, 1:2, :] = segment.astype(jnp.float32)
        meta_src[s, 2:3, :] = (segment < DOCS - 1).astype(jnp.float32)
        meta_src[s, 3:8, :] = jnp.zeros((5, LEN), jnp.float32)

    p.barrier([p.across(), p.pair()])

    is_here = p.core == p.row // seqs

    def send_seq(ref, buf, send, recv):
        for t in range(seqs):
            seq = lax.rem(p.row + t, seqs)
            piece = ref.at[pl.ds(pl.multiple_of(seq * LEN, LEN), LEN), :]
            target = p.at(core=p.row // seqs, row=p.core * seqs + seq)

            def away():
                remote(piece, buf.at[p.row], send.at[t], recv.at[p.row], target).start()

            if t:
                away()
            else:
                pl.when(jnp.logical_not(is_here))(away)

                @pl.when(is_here)
                def _():
                    pltpu.make_async_copy(piece, buf.at[p.row], recv.at[p.row]).start()

    def take_seq(buf, send, recv, swap):
        for u in range(seqs):
            slot = p.core * seqs + u
            pltpu.make_async_copy(buf.at[slot], buf.at[slot], recv.at[slot]).wait()
            remote(buf.at[slot], buf.at[slot], swap.at[u], recv.at[slot], p.sibling()).start()

    def finish_seq(buf, send, recv, swap):
        for u in range(seqs):
            slot = (1 - p.core) * seqs + u
            remote(buf.at[slot], buf.at[slot], swap.at[u], recv.at[slot], p.sibling()).wait_recv()

    def drain_seq(ref, buf, send, recv, swap):
        for u in range(seqs):
            remote(buf.at[0], buf.at[0], swap.at[u], recv.at[0], p.sibling()).wait_send()
            if u:
                remote(buf.at[0], buf.at[0], send.at[u], recv.at[0], p.sibling()).wait_send()

        @pl.when(jnp.logical_not(is_here))
        def _():
            remote(buf.at[0], buf.at[0], send.at[0], recv.at[0], p.sibling()).wait_send()

    sends_meta = lax.rem(p.row, seqs) == 0

    @pl.when(sends_meta)
    def _():
        for t in range(seqs):
            target = p.at(core=p.row // seqs, row=p.core * seqs + t)

            def away():
                remote(meta_src.at[t], meta, meta_send.at[t], meta_recv, target).start()

            if t:
                away()
            else:
                pl.when(jnp.logical_not(is_here))(away)

                @pl.when(is_here)
                def _():
                    pltpu.make_async_copy(meta_src.at[t], meta, meta_recv).start()

    for step in range(1, rows):
        remote(gains_ref, gains.at[p.row], gain_send.at[step], gain_recv.at[p.row], p.at(row=p.row_after(step))).start()
    pltpu.make_async_copy(gains_ref, gains.at[p.row], gain_recv.at[p.row]).start()
    def service(matched, unmatched):
        for here, actions in ((p.matched, matched), (jnp.logical_not(p.matched), unmatched)):
            if actions:

                @pl.when(here)
                def _():
                    for action in actions:
                        action()

    send_tokens = functools.partial(send_seq, tokens_ref, tok, tok_send, tok_recv)
    send_cot = functools.partial(send_seq, cot_ref, cot, cot_send, cot_recv)
    j0, j1 = joined
    (g0, u0, s0), (g1, u1, s1), (g2, u2, s2) = groups

    def each(action, *weights):
        return [functools.partial(getattr(weight, action)) for weight in weights]

    service(
        [j0.own_y, j0.own_x, send_tokens, j1.own_x, j1.own_y, mixer.own_y, j0.pass_on, mixer.own_x, g0.own_x, u0.own_x],
        [send_tokens, j0.take_first],
    )
    take_seq(tok, tok_send, tok_recv, swap_send.at[0])
    service(
        each("own_y", *groups[0], *groups[1]) + [send_cot] + each("own_y", *groups[2]), [j0.take_others, j1.take_first]
    )
    for step in range(1, rows):
        row = p.row_before(step)
        remote(gains.at[row], gains.at[row], gain_send.at[step], gain_recv.at[row], p.sibling()).wait_recv()
    pltpu.make_async_copy(gains.at[p.row], gains.at[p.row], gain_recv.at[p.row]).wait()
    pltpu.make_async_copy(meta, meta, meta_recv).wait()
    columns = meta[...].T
    angle = columns[:, 0:1] * freq_ref[0:1, :]
    sign = jnp.where(lanes_of((1, PAIR)) % HD < HD // 2, -1.0, 1.0)
    table[0] = jnp.cos(angle)
    table[1] = jnp.sin(angle) * sign
    segment_col, valid_col = columns[:, 1:2], columns[:, 2:3]
    finish_seq(tok, tok_send, tok_recv, swap_send.at[0])

    def gain_of(kind):
        return jnp.concatenate([gains[j, kind : kind + 1, :] for j in range(rows)], axis=1)

    def norm(values):
        center = jnp.mean(values, axis=-1, keepdims=True)
        values = values - center
        spread = jnp.mean(values * values, axis=-1, keepdims=True)
        scale = lax.rsqrt(spread + norm_eps)
        return values * scale, scale

    def tokens_at(cut):
        return jnp.concatenate([tok[j, cut, :] for j in range(rows)], axis=1).astype(jnp.float32)

    gain_a, gain_b = gain_of(0), gain_of(1)

    @pl.loop(0, LEN // BLOCK)
    def _(i):
        cut = block_rows(i)
        first[cut, :] = (norm(tokens_at(cut))[0] * gain_a).astype(jnp.bfloat16)

    service([j1.pass_on, s0.own_x], [mixer.take_first])
    j0.finish()

    def attention(pair, between):
        cols = slice(pair * PAIR, (pair + 1) * PAIR)
        per_half = pairs // 2

        def weight_of(j):
            at = pair % per_half * PAIR
            return wj[pair // per_half, j, :, at : at + PAIR]

        @pl.loop(0, LEN // BLOCK)
        def _(i):
            cut = block_rows(i)
            part = first[cut, :]
            cosine, sine = table[0, cut, :], table[1, cut, :]
            for j, dst in ((0, q_s), (1, k_s)):
                raw = dot(part, weight_of(j))
                dst[cut, cols] = (raw * cosine + swap_halves(raw) * sine).astype(jnp.bfloat16)
            v_s[cut, cols] = dot(part, weight_of(2)).astype(jnp.bfloat16)

        v_t[...] = v_s[:, cols].astype(jnp.float32).T.astype(jnp.bfloat16)
        for head in range(2):
            lanes = slice(head * HD, (head + 1) * HD)

            @pl.loop(0, LEN // BLOCK)
            def _(i):
                cut = block_rows(i)
                scores = dot(k_s[:, cols], only_head(q_s[cut, cols], head), NT)
                scores = jnp.where(segment_col == meta[1:2, cut], scores, masked_value)
                peak = jnp.max(scores, axis=0, keepdims=True)
                weights = jnp.exp2((scores - peak) * TO_EXP2)
                total = jnp.sum(weights, axis=0, keepdims=True)
                out_t[lanes, cut] = dot(v_t[lanes, :], weights.astype(jnp.bfloat16)) / total
                lse[pair, head : head + 1, cut] = peak * TO_EXP2 + jnp.log2(total)

            if head == 0:
                service(*between)

        mixed[p.core, :, cols] = out_t[...].T.astype(jnp.bfloat16)
        piece = mixed.at[p.core, :, cols]
        remote(piece, piece, mixed_send.at[pair], mixed_recv.at[pair], p.sibling()).start()

    def share_mixer():
        mixer.finish()
        piece = wm.at[p.core]
        remote(piece, piece, mix_send, mix_recv, p.sibling()).start()

    attention(0, ([mixer.pass_on, g1.own_x, u1.own_x], [g0.take_first, u0.take_first]))
    service([g0.pass_on, u0.pass_on], [])
    attention(1, ([s0.pass_on, s1.own_x], [j1.take_others]))
    service([g2.own_x, u2.own_x], [mixer.take_others, s0.take_first, send_cot])
    j1.finish()
    attention(2, ([g1.pass_on, u1.pass_on, s2.own_x], [g1.take_first, u1.take_first]))
    service([s1.pass_on], [g0.take_others])
    attention(3, ([], [u0.take_others]))
    share_mixer()
    service([], [s0.take_others, s1.take_first])
    take_seq(cot, cot_send, cot_recv, swap_send.at[1])

    for pair in range(pairs):
        piece = mixed.at[p.core, :, pair * PAIR : (pair + 1) * PAIR]
        remote(piece, piece, mixed_send.at[pair], mixed_recv.at[pair], p.sibling()).wait_recv()
    piece = wm.at[p.core]
    remote(piece, piece, mix_send, mix_recv, p.sibling()).wait_recv()
    finish_seq(cot, cot_send, cot_recv, swap_send.at[1])

    @pl.loop(0, LEN // BLOCK)
    def _(i):
        cut = block_rows(i)
        value = tokens_at(cut) + dot(mixed[0, cut, :], wm[0]) + dot(mixed[1, cut, :], wm[1])
        normed, scale = norm(value)
        xhat[cut, :] = normed.astype(jnp.bfloat16)
        inv[cut, :] = jnp.broadcast_to(scale, (BLOCK, PAIR))
        second[cut, :] = (normed * gain_b).astype(jnp.bfloat16)
        shrunk[cut, :] = jnp.where(lanes_of((1, D)) // (D // CORES) == p.core, value, 0.0)
        back[cut, :] = jnp.zeros((BLOCK, D), jnp.float32)

    valid_16 = valid_col > 0.5
    top[...] = jnp.where(valid_16, jnp.concatenate([cot[j] for j in range(rows)], axis=1), jnp.zeros((), jnp.bfloat16))

    keep = []

    def store(src, dst):
        copy = pltpu.make_async_copy(src, dst, out_sem.at[len(keep)])
        keep.append(copy)
        copy.start()

    for j in range(rows):
        store(tok.at[j], o_tokens.at[j])
    for src, dst in ((first, o_first), (q_s, o_q), (k_s, o_k), (v_s, o_v), (mixed.at[p.core], o_mixed), (lse, o_lse),
                     (xhat, o_xhat), (inv, o_inv), (table, o_table), (top, o_top), (wj.at[0], o_joined.at[0]), (wj.at[1], o_joined.at[1]), (wm.at[p.core], o_mixer)):
        store(src, dst)
    for j in range(rows):
        store(gains.at[j], o_small.at[:, pl.ds(j * width, width)])
    store(meta, o_small.at[:, pl.ds(D, LEN)])

    service([g2.pass_on, u2.pass_on, s2.pass_on], [g2.take_first, u2.take_first, g1.take_others])
    early = [([], [u1.take_others]), ([], [g2.take_others, u2.take_others]), ([], [])]
    middle = [([], [s1.take_others, s2.take_first]), ([], [s2.take_others]), ([], [])]
    at = 0
    for i, lanes in enumerate(chunks):
        for weight in groups[i]:
            weight.finish()

        @pl.loop(0, LEN // BLOCK)
        def _(t):
            cut = block_rows(t)
            part, grad = second[cut, :], top[cut, :]
            gate = dot(part, wg[i][...], NT)
            up = dot(part, wu[i][...], NT)
            hidden_grad = dot(grad, ws[i][...], NT).astype(jnp.bfloat16).astype(jnp.float32)
            phi, density = gelu_parts(gate)
            act = gate * phi
            hidden = (act * up).astype(jnp.bfloat16)
            d_gate = (hidden_grad * up * (phi + gate * density)).astype(jnp.bfloat16)
            d_up = (hidden_grad * act).astype(jnp.bfloat16)
            hid[cut, :lanes] = hidden
            dgate[cut, :lanes] = d_gate
            dup[cut, :lanes] = d_up
            shrunk[cut, :] += dot(hidden, ws[i][...])
            back[cut, :] += dot(d_gate, wg[i][...]) + dot(d_up, wu[i][...])

            @pl.when(t == LEN // BLOCK // 2 - 1)
            def _():
                service(*early[i])


        service(*middle[i])
        for n, (left, right) in enumerate(((dgate, second), (dup, second), (hid, top))):
            target = g_shrink[i] if n == 2 else g_expand[i]
            for start in range(0, lanes, BLOCK):
                size = min(BLOCK, lanes - start)
                spot = start if n == 2 else n * lanes + start
                target[spot : spot + size, :] = dot(left[:, start : start + size], right[...], TN).astype(jnp.bfloat16)

        store(g_expand[i], o_expand.at[pl.ds(2 * at, 2 * lanes), :])
        store(g_shrink[i], o_shrink.at[pl.ds(at, lanes), :])
        at += lanes

    @pl.loop(0, LEN // BLOCK)
    def _(i):
        cut = block_rows(i)
        back_low[cut, :] = back[cut, :].astype(jnp.bfloat16)
        value = shrunk[cut, :]
        left, right = value[:, : D // 2], value[:, D // 2 :]
        own_half[cut, :] = jnp.where(p.core == 0, left, right)
        other_half[cut, :] = jnp.where(p.core == 0, right, left).astype(jnp.bfloat16)

    store(back_low, o_back)
    store(own_half, o_own)
    store(other_half, o_other)

    drain_seq(tokens_ref, tok, tok_send, tok_recv, swap_send.at[0])
    drain_seq(cot_ref, cot, cot_send, cot_recv, swap_send.at[1])
    for step in range(1, rows):
        remote(gains_ref, gains.at[p.row], gain_send.at[step], gain_recv.at[p.row], p.sibling()).wait_send()

    @pl.when(sends_meta)
    def _():
        for t in range(1, seqs):
            remote(meta_src.at[t], meta, meta_send.at[t], meta_recv, p.sibling()).wait_send()

        @pl.when(jnp.logical_not(is_here))
        def _():
            remote(meta_src.at[0], meta, meta_send.at[0], meta_recv, p.sibling()).wait_send()

    for pair in range(pairs):
        piece = mixed.at[p.core, :, pair * PAIR : (pair + 1) * PAIR]
        remote(piece, piece, mixed_send.at[pair], mixed_recv.at[pair], p.sibling()).wait_send()
    piece = wm.at[p.core]
    remote(piece, piece, mix_send, mix_recv, p.sibling()).wait_send()
    for weight in joined + [mixer] + sum(groups, []):
        weight.drain()
    for copy in keep:
        copy.wait()


def forward(tokens, cot, lengths, gains, joined, mixer, expand, shrink, chunks):
    rows = lax.axis_size("row")
    seqs = rows // CORES
    width = tokens.shape[1]
    wide = mixer.shape[0]
    pairs = wide // PAIR
    n_chunks = len(chunks)
    hidden_here = sum(chunks)
    weights = 3 + 3 * n_chunks
    bf16, f32 = jnp.bfloat16, jnp.float32
    freq = rope_base ** (-2.0 * jnp.arange(HD // 2, dtype=f32) / HD)
    freq = jnp.broadcast_to(jnp.concatenate([freq] * 4)[None, :], (8, PAIR))
    outs = [
        ((rows, LEN, width), bf16), ((LEN, D), bf16), ((LEN, wide), bf16), ((LEN, wide), bf16), ((LEN, wide), bf16),
        ((LEN, wide), bf16), ((pairs, 2, LEN), f32), ((LEN, D), bf16), ((LEN, PAIR), f32), ((LEN, D), bf16),
        ((LEN, D // 2), f32), ((LEN, D // 2), bf16), ((LEN, D), bf16),
        ((2 * hidden_here, D), bf16), ((hidden_here, D), bf16), ((2, 3, D, wide // 2), bf16), ((wide, D), bf16),
        ((8, D + LEN), f32), ((2, LEN, PAIR), f32),
    ]
    V, dma = pltpu.VMEM, pltpu.SemaphoreType.DMA
    widest = max(chunks)
    scratch = [
        V((rows, LEN, width), bf16), V((rows, LEN, width), bf16), V((seqs, 8, LEN), f32), V((8, LEN), f32),
        V((rows, 8, width), f32), V((2, LEN, PAIR), f32), V((LEN, D), bf16), V((2, 3, D, wide // 2), bf16), V((CORES, wide, D), bf16),
        [V((lanes, D), bf16) for lanes in chunks], [V((lanes, D), bf16) for lanes in chunks], [V((lanes, D), bf16) for lanes in chunks],
        V((LEN, wide), bf16), V((LEN, wide), bf16), V((LEN, wide), bf16), V((PAIR, LEN), bf16), V((PAIR, LEN), f32),
        V((pairs, 2, LEN), f32), V((CORES, LEN, wide), bf16), V((LEN, D), bf16), V((LEN, PAIR), f32), V((LEN, D), bf16),
        V((LEN, D), bf16), V((LEN, D), f32), V((LEN, D), f32), V((LEN, D), bf16), V((LEN, D // 2), f32), V((LEN, D // 2), bf16), V((LEN, widest), bf16), V((LEN, widest), bf16), V((LEN, widest), bf16),
        [V((2 * lanes, D), bf16) for lanes in chunks],
        [V((lanes, D), bf16) for lanes in chunks],
        dma((seqs,)), dma((rows,)), dma((seqs,)), dma((rows,)), dma((2, seqs)), dma((seqs,)), dma, dma((rows,)), dma((rows,)),
        dma((weights, rows)), dma((weights, rows)), dma((weights, rows)), dma((weights, rows)), dma((weights, rows)),
        dma((weights,)), dma, dma, dma((pairs,)), dma((pairs,)), dma((2 * rows + 17 + 3 * n_chunks,)),
    ]
    anywhere = pl.BlockSpec(memory_space=pl.ANY)
    in_specs = [anywhere] * 9
    in_specs[2] = pl.BlockSpec(memory_space=pltpu.SMEM)
    in_specs[4] = pl.BlockSpec(memory_space=pltpu.VMEM)
    return pl.pallas_call(
        functools.partial(forward_kernel, chunks),
        in_specs=in_specs,
        out_specs=[anywhere] * len(outs),
        out_shape=[jax.ShapeDtypeStruct(*o) for o in outs],
        scratch_shapes=scratch,
        compiler_params=pltpu.CompilerParams(
            collective_id=0, has_side_effects=True, vmem_limit_bytes=62 * 1024 * 1024
        ),
        name="layer_forward",
    )(tokens, cot, lengths, gains, freq, joined, mixer, expand, shrink)


def add_rows(count, target, *parts):
    step = 32 if count % 32 == 0 else 16

    @pl.loop(0, count // step)
    def _(i):
        cut = pl.ds(pl.multiple_of(i * step, step), step)
        total = parts[0][cut, :].astype(jnp.float32)
        for part in parts[1:]:
            total = total + part[cut, :].astype(jnp.float32)
        target[cut, :] = total.astype(target.dtype)


def first_share(count):
    return count * 5 // 16 // 16 * 16


class Grad:
    def __init__(self, place, block, rows, bufs, sems, credits, index, stage=None):
        self.p, self.block, self.m, self.index, self.sems, self.stage = place, block, rows, index, sems, stage
        self.credits = credits
        self.a = first_share(rows)
        self.b = rows - self.a
        self.recv_a, self.recv_b, self.acc, self.more, self.zbuf = bufs
        self.levels = (place.planes - 1).bit_length()
        self.full = self.acc.shape[0]

    def sem(self, kind, at=0):
        return self.sems.at[self.index, kind, at]

    def low(self):
        return self.acc.at[pl.ds(0, self.a), :]

    def high(self):
        return self.acc.at[pl.ds(self.a, self.b), :]

    def send(self, src, dst, kind, at, target):
        return remote(src, dst, self.sem(kind, at), self.sem(kind + 1, at), target)

    def landed(self, buf, kind, at=0):
        self.send(buf, buf, kind, at, self.p.sibling()).wait_recv()

    def left(self, buf, kind, at=0):
        self.send(buf, buf, kind, at, self.p.sibling()).wait_send()

    def copies_y(self):
        p = self.p
        return [
            self.send(self.block(p.row_after(s), 0, self.a), self.recv_a.at[s - 1], 0, s, p.at(row=p.row_after(s)))
            for s in range(1, p.rows)
        ]

    def copies_x(self):
        return [
            self.send(self.block(j, self.a, self.b), self.recv_b.at[j], 2, j, self.p.across())
            for j in range(self.p.rows)
        ]

    def begin_y(self):
        for copy in self.copies_y():
            copy.start()

    def begin_x(self):
        @pl.when(jnp.logical_not(self.p.matched))
        def _():
            for copy in self.copies_x():
                copy.start()

    def own(self, row, start, size, slot):
        piece = self.block(row, start, size)
        if self.stage is None:
            return piece
        buf, sem = self.stage
        buf = buf.at[pl.ds(0, size), pl.ds(0, self.acc.shape[1])]
        copy = pltpu.make_async_copy(piece, buf, sem)
        copy.start()
        copy.wait()
        return buf

    def sum_y(self):
        p = self.p
        own = self.own(p.row, 0, self.a, 0)
        for s in range(1, p.rows):
            self.landed(self.recv_a.at[s - 1], 0, s)
        add_rows(self.a, self.recv_a.at[0], own, *[self.recv_a.at[s - 1] for s in range(1, p.rows)])

        @pl.when(jnp.logical_not(p.matched))
        def _():
            self.send(self.recv_a.at[0], self.low(), 4, 0, p.across()).start()

    def sum_x(self):
        p = self.p

        @pl.when(p.matched)
        def _():
            for s in list(range(1, p.rows)) + [0]:
                row = p.row_after(s)
                own = self.own(row, self.a, self.b, 0)
                buf = self.recv_b.at[row]
                self.landed(buf, 2, row)
                add_rows(self.b, buf, own, buf)
                if s:
                    target = self.high() if s == 1 else self.more.at[s - 2]
                    self.send(buf, target, 6, s, p.at(row=row)).start()

    def span(self, level):
        start, size = 0, self.full
        for i in range(1, level + 1):
            size //= 2
            start = start + self.p.group_bit(i) * size
        return start, size

    def rows_of(self, start, size):
        return self.acc.at[pl.ds(pl.multiple_of(start, 16), size), :]

    def z_copy(self, level):
        if level == 0:
            return self.send(self.acc, self.zbuf[0], 8, 0, self.p.mate(0))
        start, size = self.span(level - 1)
        half = size // 2
        piece = self.rows_of(start + (1 - self.p.group_bit(level)) * half, half)
        return self.send(piece, self.zbuf[level], 8, level, self.p.mate(level))

    def z_back(self, level):
        piece = self.acc if level == 0 else self.rows_of(*self.span(level))
        return self.send(piece, piece, 10, level, self.p.mate(level))

    def z_free(self, level):
        self.z_copy(level).wait_send()
        pl.semaphore_signal(
            self.credits.at[self.index, level], inc=1, device_id=self.p.mate(level), device_id_type=MESH_ID
        )

    def z_return(self, level):
        pl.semaphore_wait(self.credits.at[self.index, level], 1)
        self.z_back(level).start()

    def sum_both(self):
        p = self.p

        @pl.when(p.matched)
        def _():
            self.landed(self.low(), 4)
            add_rows(self.a, self.low(), self.low(), self.recv_a.at[0])
            others = []
            for s in range(1, p.rows):
                buf = self.high() if s == 1 else self.more.at[s - 2]
                self.landed(buf, 6, s)
                others.append(buf)
            add_rows(self.b, self.high(), self.recv_b.at[p.row], *others)

        @pl.when(jnp.logical_and(p.matched, jnp.logical_not(p.inner)))
        def _():
            self.z_copy(0).start()

    def z0(self):
        p = self.p

        @pl.when(jnp.logical_and(p.matched, p.inner))
        def _():
            self.landed(self.zbuf[0], 8, 0)
            add_rows(self.full, self.acc, self.acc, self.zbuf[0])
            if self.levels > 1:
                self.z_copy(1).start()
            else:
                self.z_return(0)
                self.final().start()

        @pl.when(jnp.logical_and(p.matched, jnp.logical_not(p.inner)))
        def _():
            self.z_free(0)

    def z1(self):
        @pl.when(jnp.logical_and(self.p.matched, self.p.inner))
        def _():
            for level in range(1, self.levels):
                start, size = self.span(level)
                self.landed(self.zbuf[level], 8, level)
                piece = self.rows_of(start, size)
                add_rows(size, piece, piece, self.zbuf[level])
                self.z_free(level)
                if level + 1 < self.levels:
                    self.z_copy(level + 1).start()
                else:
                    self.z_return(level)

    def g1(self):
        @pl.when(jnp.logical_and(self.p.matched, self.p.inner))
        def _():
            for level in range(self.levels - 1, 0, -1):
                start, size = self.span(level - 1)
                half = size // 2
                self.landed(self.rows_of(start + (1 - self.p.group_bit(level)) * half, half), 10, level)
                self.z_return(level - 1)
                if level == 1:
                    self.final().start()

    def g0(self):
        @pl.when(jnp.logical_and(self.p.matched, jnp.logical_not(self.p.inner)))
        def _():
            self.landed(self.acc, 10, 0)
            self.final().start()

    def final(self):
        return remote(self.acc, self.acc, self.sem(12), self.sem(13), self.p.sibling())

    def store(self, stores):
        @pl.when(jnp.logical_not(self.p.matched))
        def _():
            self.final().wait_recv()

        copies = [
            pltpu.make_async_copy(self.acc.at[pl.ds(row, rows), pl.ds(col, cols)], out, sem)
            for row, rows, col, cols, out, sem in stores
        ]
        for copy in copies:
            copy.start()
        return copies

    def drain(self):
        p = self.p
        for copy in self.copies_y():
            copy.wait_send()

        @pl.when(jnp.logical_not(p.matched))
        def _():
            for copy in self.copies_x():
                copy.wait_send()
            self.left(self.recv_a.at[0], 4)

        @pl.when(p.matched)
        def _():
            for s in range(1, p.rows):
                self.left(self.recv_b.at[0], 6, s)
            self.final().wait_send()

        @pl.when(jnp.logical_and(p.matched, p.inner))
        def _():
            for level in range(self.levels):
                self.z_back(level).wait_send()


def grad_bufs(rows, cols, blocks, planes):
    a = first_share(rows)
    V = lambda *shape: pltpu.VMEM(shape, jnp.bfloat16)
    levels = (planes - 1).bit_length()
    tile = 16 * max(1, planes // 2)
    full = -(-rows // tile) * tile
    return [
        V(blocks - 1, a, cols), V(blocks, rows - a, cols), V(full, cols), V(max(1, blocks - 2), rows - a, cols) if blocks > 2 else V(16, 128),
        [V(full >> i, cols) for i in range(levels)],
    ]


def backward_kernel(
    chunks,
    tokens_ref, first_ref, q_ref, k_ref, v_ref, mixed_ref, lse_ref, xhat_ref, inv_ref, top_ref, own_ref, other_ref, back_ref,
    expand_ref, shrink_ref, joined_ref, mixer_ref, small_ref, table_ref,
    o_block, o_input, o_joined, o_mixer, o_expand, o_shrink, o_gains,
    q_s, k_s, v_s, mixed, xa, xb, xc, wj, wm, lse, inv, small, table, other, keep_grad, middle_low, mixed_grad, g_mixer, g_joined,
    dk, dv, dq_t, k_t, own_half, block_half, gain_sum, gain_y, gain_x, gain_z, stage_lane, grad_scratch,
    load_sem, stage_sem, grad_sem, credit, swap_credit, back_send, back_recv, other_send, other_recv, first_send, first_recv,
    out_send, out_recv, in_send, in_recv, gain_send, gain_recv, out_sem,
):
    p = Place()
    rows, seqs, planes = p.rows, p.seqs, p.planes
    width = D // rows
    wide = q_s.shape[1]
    pairs = wide // PAIR
    levels = (planes - 1).bit_length()
    half = wide // 2

    def by_row(ref):
        return lambda j, start, size: ref.at[pl.ds(pl.multiple_of(j * width + start, 16), size), :]

    def by_lane(ref, at=0):
        return lambda j, start, size: ref.at[pl.ds(at + start, size), pl.ds(pl.multiple_of(j * width, width), width)]

    grads, places, at = {}, {}, 0
    stage = (stage_lane, stage_sem)

    def add_grad(name, block, count, stage, stores):
        i = len(grads)
        grads[name] = Grad(p, block, count, grad_scratch[i], grad_sem, credit, i, stage)
        places[name] = stores

    for i, count in enumerate(chunks):
        add_grad(("E", i), by_lane(expand_ref, 2 * at), 2 * count, stage,
                 [(j * count, count, 0, width, o_expand.at[j, pl.ds(at, count), :]) for j in range(2)])
        add_grad(("S", i), by_lane(shrink_ref, at), count, stage, [(0, count, 0, width, o_shrink.at[pl.ds(at, count), :])])
        at += count
    for h in range(2):
        add_grad(("J", h), by_row(g_joined.at[h]), width, None,
                 [(0, width, j * half, half, o_joined.at[j, :, pl.ds(h * half, half)]) for j in range(3)])
    add_grad(("M", 0), by_lane(g_mixer), wide, None, [(0, wide, 0, width, o_mixer)])

    loads = {}

    def load(name, src, dst):
        copy = pltpu.make_async_copy(src, dst, load_sem.at[len(loads)])
        copy.start()
        loads[name] = copy

    load("small", small_ref, small)
    load("back", back_ref, xc)
    load("xhat", xhat_ref, xa)
    load("inv", inv_ref, inv)
    load("top", top_ref, xb)
    load("mixer", mixer_ref, wm)
    load("mixed", mixed_ref, mixed)
    load("q", q_ref, q_s)
    load("k", k_ref, k_s)
    load("v", v_ref, v_s)
    load("lse", lse_ref, lse)
    load("table", table_ref, table)
    load("joined", joined_ref, wj)
    load("own", own_ref, own_half)
    p.barrier([p.across()] + [p.mate(level) for level in range(levels)])

    def swap_block(i, src, dst, send, recv):
        cut = pl.ds(i * BLOCK, BLOCK)
        return remote(src.at[cut, :], dst.at[cut, :], send.at[i], recv.at[i], p.sibling())

    blocks_n = LEN // BLOCK
    for i in range(blocks_n):
        swap_block(i, back_ref, other, back_send, back_recv).start()

    stores = []

    def run(*todo):
        for step in todo:
            if callable(step):
                step()
                continue
            action, kind, i = step
            grad = grads[kind, i]
            if action == "store":
                spots = [spot + (out_sem.at[len(stores) + n],) for n, spot in enumerate(places[kind, i])]
                stores.extend(grad.store(spots))
            elif action == "begin":
                grad.begin_y()
                grad.begin_x()
            else:
                getattr(grad, action)()

    run(("begin_y", "E", 0), ("begin_x", "E", 0), ("begin_x", "S", 0), ("begin_y", "S", 0))
    other_copy = remote(other_ref, block_half, other_send, other_recv, p.sibling())
    other_copy.start()

    for name in ("small", "back", "xhat", "inv", "top", "mixer", "mixed"):
        loads[name].wait()
    gain_a, gain_b = small[0:1, :D], small[1:2, :D]
    gain_sum[...] = jnp.zeros_like(gain_sum)
    for grad in grads.values():
        if grad.full != grad.m:
            grad.acc[grad.m :, :] = jnp.zeros((grad.full - grad.m, grad.acc.shape[1]), jnp.bfloat16)

    def norm_back(grad, normed, scale, gain):
        scaled = grad * gain
        mean_a = jnp.mean(scaled, axis=-1, keepdims=True)
        mean_b = jnp.mean(scaled * normed, axis=-1, keepdims=True)
        return scale * (scaled - mean_a - normed * mean_b)

    def own_of(value):
        return jnp.where(p.core == 0, value[:, : D // 2], value[:, D // 2 :])

    def second_norm(i):
        cut = slice(i * BLOCK, (i + 1) * BLOCK)
        swap_block(i, back_ref, other, back_send, back_recv).wait_recv()
        grad = xc[cut, :].astype(jnp.float32) + other[cut, :].astype(jnp.float32)
        normed = xa[cut, :].astype(jnp.float32)
        gain_sum[1:2, :] += jnp.sum(grad * normed, axis=0, keepdims=True)
        value = xb[cut, :].astype(jnp.float32) + norm_back(grad, normed, inv[cut, 0:1], gain_b)
        keep_grad[cut, :] = own_of(value)
        value = value.astype(jnp.bfloat16)
        middle_low[cut, :] = value
        mixed_grad[cut, :] = dot(value, wm[...], NT).astype(jnp.bfloat16)
    second_norm(0)
    second_norm(1)
    run(("begin_y", "E", 1))
    second_norm(2)
    second_norm(3)
    pl.semaphore_signal(swap_credit, inc=1, device_id=p.sibling(), device_id_type=MESH_ID)
    run(("begin_y", "S", 2))
    @pl.loop(0, D // BLOCK)
    def _(d):
        cut = block_rows(d)
        g_mixer[:, cut] = dot(mixed[...], middle_low[:, cut], TN).astype(jnp.bfloat16)

    load("first", first_ref, xa)
    for j in range(rows):
        load(f"tokens{j}", tokens_ref.at[j], xb.at[:, pl.ds(j * width, width)])

    def leave(src, dst, send, recv):
        core, seq = p.row // seqs, lax.rem(p.row, seqs)
        copies = []
        for u in range(seqs):
            row = p.core * seqs + u
            is_self = jnp.logical_and(core == p.core, row == p.row)
            piece = src.at[:, pl.ds(u * width, width)]
            copies.append((is_self, piece, dst(seq), send.at[u], recv.at[seq], p.at(core=core, row=row)))
        return copies

    def leave_start(copies):
        for is_self, piece, place, send, recv, target in copies:
            @pl.when(is_self)
            def _():
                pltpu.make_async_copy(piece, place, recv).start()

            @pl.when(jnp.logical_not(is_self))
            def _():
                remote(piece, place, send, recv, target).start()

    def leave_wait(copies, dst, recv):
        for s in range(seqs):
            pltpu.make_async_copy(dst(s), dst(s), recv.at[s]).wait()
        for is_self, piece, place, send, recv_sem, target in copies:
            @pl.when(jnp.logical_not(is_self))
            def _():
                remote(piece, place, send, recv_sem, target).wait_send()

    out_at = lambda s: o_block.at[pl.ds(pl.multiple_of(s * LEN, LEN), LEN), :]
    in_at = lambda s: o_input.at[pl.ds(pl.multiple_of(s * LEN, LEN), LEN), :]
    out_copies = leave(block_half, out_at, out_send, out_recv)
    in_copies = leave(mixed_grad, in_at, in_send, in_recv)

    def block_output():
        loads["own"].wait()
        other_copy.wait()
        add_rows(LEN, block_half, own_half, block_half)
        leave_start(out_copies)

    for name in ("q", "k", "v", "lse", "table"):
        loads[name].wait()
    columns = small[:, D:].T
    segment_col = columns[:, 1:2]

    def attention(pair):
        cols = slice(pair * PAIR, (pair + 1) * PAIR)
        product = mixed[:, cols].astype(jnp.float32) * mixed_grad[:, cols].astype(jnp.float32)
        chooser = lax.broadcasted_iota(jnp.int32, (8, PAIR), 0) == lanes_of((8, PAIR)) // HD
        delta = dot(chooser.astype(jnp.float32), product, NT, precision=lax.Precision.HIGHEST)
        keys, values = k_s[:, cols], v_s[:, cols]
        k_t[...] = keys.astype(jnp.float32).T.astype(jnp.bfloat16)
        dk[...] = jnp.zeros_like(dk)
        dv[...] = jnp.zeros_like(dv)
        for head in range(2):
            lanes = slice(head * HD, (head + 1) * HD)
            for i in range(LEN // BLOCK):
                cut = slice(i * BLOCK, (i + 1) * BLOCK)
                q_part, g_part = only_head(q_s[cut, cols], head), only_head(mixed_grad[cut, cols], head)
                scores = dot(keys, q_part, NT)
                probs = jnp.exp2(scores * TO_EXP2 - lse[pair, head : head + 1, cut])
                probs = jnp.where(segment_col == small[1:2, D + i * BLOCK : D + (i + 1) * BLOCK], probs, 0.0)
                probs_grad = dot(values, g_part, NT)
                scores_grad = (probs * (probs_grad - delta[head : head + 1, cut])).astype(jnp.bfloat16)
                dv[...] += dot(probs.astype(jnp.bfloat16), g_part)
                dk[...] += dot(scores_grad, q_part)
                dq_t[lanes, cut] = dot(k_t[lanes, :], scores_grad)
        cosine, sine = table[0], table[1]
        scale = 1.0 / math.sqrt(HD)
        dqs = dq_t[...].T * scale
        q_s[:, cols] = (dqs * cosine - swap_halves(dqs) * sine).astype(jnp.bfloat16)
        dks = dk[...] * scale
        k_s[:, cols] = (dks * cosine - swap_halves(dks) * sine).astype(jnp.bfloat16)
        v_s[:, cols] = dv[...].astype(jnp.bfloat16)

    def joined_weight_grad(h):
        @pl.loop(0, D // BLOCK)
        def _(d):
            cut = block_rows(d)
            part = xa[:, cut]
            for j, back in enumerate((q_s, k_s, v_s)):
                g_joined[h, cut, j * half : (j + 1) * half] = dot(
                    part, back[:, h * half : (h + 1) * half], TN
                ).astype(jnp.bfloat16)

    run(block_output, ("sum_y", "E", 0))
    attention(0)
    run(("sum_y", "S", 0), ("begin_x", "E", 1), ("sum_x", "E", 0), ("sum_x", "S", 0))
    attention(1)
    loads["first"].wait()
    joined_weight_grad(0)
    attention(2)
    run(
        ("begin_y", "S", 1), ("sum_y", "E", 1), ("sum_both", "E", 0), ("sum_x", "E", 1), ("sum_both", "S", 0),
        ("sum_y", "S", 2), ("begin_x", "S", 1),
    )
    attention(3)
    run(("begin_y", "M", 0))
    joined_weight_grad(1)
    run(
        ("z0", "E", 0), ("sum_both", "E", 1), ("begin_x", "J", 0), ("begin_y", "J", 0), ("begin_y", "J", 1),
        ("sum_y", "S", 1), ("begin_x", "S", 2),
    )
    loads["joined"].wait()
    pl.semaphore_wait(swap_credit, 1)
    for i in range(blocks_n):
        cut = slice(i * BLOCK, (i + 1) * BLOCK)
        value = jnp.zeros((BLOCK, D), jnp.float32)
        for h in range(2):
            for j, part in enumerate((q_s, k_s, v_s)):
                value = value + dot(part[cut, h * half : (h + 1) * half], wj[h, j], NT)
        xc[cut, :] = value.astype(jnp.bfloat16)
        swap_block(i, xc, other, first_send, first_recv).start()

    run(
        ("sum_x", "S", 1), ("z1", "E", 0), ("sum_y", "J", 0), ("sum_x", "J", 0), ("z0", "E", 1),
        ("sum_both", "S", 1), ("z0", "S", 0), ("sum_x", "S", 2), ("begin_x", "J", 1), ("g1", "E", 0),
    )
    for j in range(rows):
        loads[f"tokens{j}"].wait()
    for i in range(blocks_n):
        cut = slice(i * BLOCK, (i + 1) * BLOCK)
        swap_block(i, xc, other, first_send, first_recv).wait_recv()
        grad = xc[cut, :].astype(jnp.float32) + other[cut, :].astype(jnp.float32)
        values = xb[cut, :].astype(jnp.float32)
        values = values - jnp.mean(values, axis=-1, keepdims=True)
        scale = lax.rsqrt(jnp.mean(values * values, axis=-1, keepdims=True) + norm_eps)
        normed = values * scale
        gain_sum[0:1, :] += jnp.sum(grad * normed, axis=0, keepdims=True)
        total = keep_grad[cut, :] + own_of(norm_back(grad, normed, scale, gain_a))
        mixed_grad[cut, :] = total.astype(jnp.bfloat16)

    def gain_copies():
        return [
            remote(gain_sum.at[:, pl.ds(pl.multiple_of(p.row_after(s) * width, width), width)], gain_y.at[s],
                   gain_send.at[s], gain_recv.at[s], p.at(row=p.row_after(s)))
            for s in range(1, rows)
        ]

    gain_across = remote(gain_x.at[0], gain_x.at[1], gain_send.at[rows], gain_recv.at[rows], p.across())
    gain_total = gain_z.at[2 * levels]
    gain_back = remote(gain_total, gain_total, gain_send.at[rows + 1 + levels], gain_recv.at[rows + 1 + levels], p.sibling())

    def gain_plane(level):
        return remote(gain_z.at[2 * level], gain_z.at[2 * level + 1], gain_send.at[rows + 1 + level],
                      gain_recv.at[rows + 1 + level], p.mate(level))

    def gains_y():
        for s in range(1, rows):
            remote(gain_y.at[s], gain_y.at[s], gain_send.at[s], gain_recv.at[s], p.sibling()).wait_recv()
        total = gain_sum[:, pl.ds(pl.multiple_of(p.row * width, width), width)]
        for s in range(1, rows):
            total = total + gain_y[s]
        gain_x[0] = total
        pl.when(p.matched)(gain_across.start)

    def gains_x():
        @pl.when(jnp.logical_not(p.matched))
        def _():
            gain_across.wait_recv()
            gain_z[0] = gain_x[0] + gain_x[1]
            gain_plane(0).start()

    def gains_z():
        @pl.when(jnp.logical_not(p.matched))
        def _():
            for level in range(levels):
                gain_plane(level).wait()
                gain_z[2 * level + 2] = gain_z[2 * level] + gain_z[2 * level + 1]
                if level + 1 < levels:
                    gain_plane(level + 1).start()
            gain_back.start()
            gain_back.wait_send()

    def gains_end():
        @pl.when(p.matched)
        def _():
            gain_back.wait_recv()
            gain_across.wait_send()

    for copy in gain_copies():
        copy.start()
    leave_start(in_copies)

    run(
        ("z1", "E", 1), ("z1", "S", 0), ("sum_both", "J", 0), ("sum_y", "J", 1), ("sum_x", "J", 1),
        ("sum_both", "S", 2), ("g1", "E", 1), ("begin_x", "E", 2), gains_y, ("z0", "S", 1), ("begin_y", "E", 2),
        ("z0", "J", 0), ("z0", "S", 2), ("g1", "S", 0), ("z1", "S", 1), ("sum_both", "J", 1), ("sum_x", "E", 2),
        ("z1", "J", 0), ("sum_y", "E", 2), ("begin_x", "M", 0), ("z0", "J", 1), ("g0", "S", 0), ("g1", "S", 1),
        ("g1", "J", 0), ("sum_y", "M", 0), ("sum_both", "E", 2), gains_x, ("g0", "S", 1), ("z1", "S", 2),
        ("sum_x", "M", 0), ("z1", "J", 1), ("g1", "S", 2), ("z0", "E", 2), ("g1", "J", 1), ("z1", "E", 2),
        ("sum_both", "M", 0), ("g0", "E", 0), ("store", "E", 0), ("z0", "M", 0), ("g1", "E", 2), ("g0", "S", 2),
        gains_z, ("g0", "E", 2), ("g0", "J", 0), ("store", "S", 1), ("g0", "J", 1), ("store", "J", 0),
        ("z1", "M", 0), ("store", "S", 0), ("store", "S", 2), ("store", "J", 1), ("g0", "E", 1), ("store", "E", 1),
        ("store", "E", 2), ("g1", "M", 0), ("g0", "M", 0), ("store", "M", 0),
    )
    gains_end()
    gains_out = pltpu.make_async_copy(gain_z.at[2 * levels], o_gains, out_sem.at[len(stores)])
    gains_out.start()

    leave_wait(out_copies, out_at, out_recv)
    leave_wait(in_copies, in_at, in_recv)
    for i in range(blocks_n):
        swap_block(i, back_ref, other, back_send, back_recv).wait_send()
        swap_block(i, xc, other, first_send, first_recv).wait_send()
    for copy in gain_copies():
        copy.wait_send()
    for grad in grads.values():
        grad.drain()
    for copy in stores:
        copy.wait()
    gains_out.wait()


def backward(saved, chunks):
    (tokens, first, queries, keys, values, mixed, lse, xhat, inv, top, own, other, back, expand, shrink, joined, mixer,
     small, table) = saved
    rows = lax.axis_size("row")
    planes = lax.axis_size("dp") // CORES
    seqs = rows // CORES
    width = D // rows
    wide = queries.shape[1]
    pairs = wide // PAIR
    hidden_here = sum(chunks)
    widest = 2 * max(chunks)
    levels = (planes - 1).bit_length()
    bf16, f32 = jnp.bfloat16, jnp.float32
    V, dma = pltpu.VMEM, pltpu.SemaphoreType.DMA
    outs = [
        ((seqs * LEN, width), bf16), ((seqs * LEN, width), bf16), ((3, width, wide), bf16), ((wide, width), bf16),
        ((2, hidden_here, width), bf16), ((hidden_here, width), bf16), ((8, width), f32),
    ]
    grad_shapes = []
    for lanes in chunks:
        grad_shapes += [(2 * lanes, width), (lanes, width)]
    grad_shapes += [(width, 3 * wide // 2)] * 2 + [(wide, width)]
    count = len(grad_shapes)
    scratch = [
        V((LEN, wide), bf16), V((LEN, wide), bf16), V((LEN, wide), bf16), V((LEN, wide), bf16),
        V((LEN, D), bf16), V((LEN, D), bf16), V((LEN, D), bf16), V((2, 3, D, wide // 2), bf16), V((wide, D), bf16),
        V((pairs, 2, LEN), f32), V((LEN, PAIR), f32), V((8, D + LEN), f32), V((2, LEN, PAIR), f32), V((LEN, D), bf16),
        V((LEN, D // 2), f32), V((LEN, D), bf16), V((LEN, wide), bf16), V((wide, D), bf16), V((2, D, 3 * wide // 2), bf16),
        V((LEN, PAIR), f32), V((LEN, PAIR), f32), V((PAIR, LEN), f32), V((PAIR, LEN), bf16),
        V((LEN, D // 2), f32), V((LEN, D // 2), bf16),
        V((8, D), f32), V((rows, 8, width), f32), V((2, 8, width), f32), V((2 * levels + 1, 8, width), f32),
        V((widest - first_share(widest), width), bf16),
        [grad_bufs(*shape, rows, planes) for shape in grad_shapes],
        dma((15 + rows,)), dma, dma((count, 14, max(rows, levels))), pltpu.SemaphoreType.REGULAR((count, levels)),
        pltpu.SemaphoreType.REGULAR,
        dma((4,)), dma((4,)), dma, dma, dma((4,)), dma((4,)),
        dma((seqs,)), dma((seqs,)), dma((seqs,)), dma((seqs,)), dma((rows + 2 + levels,)), dma((rows + 2 + levels,)),
        dma((3 * len(chunks) + 8,)),
    ]
    anywhere = pl.BlockSpec(memory_space=pl.ANY)
    return pl.pallas_call(
        functools.partial(backward_kernel, chunks),
        in_specs=[anywhere] * len(saved),
        out_specs=[anywhere] * len(outs),
        out_shape=[jax.ShapeDtypeStruct(*o) for o in outs],
        scratch_shapes=scratch,
        compiler_params=pltpu.CompilerParams(
            collective_id=1, has_side_effects=True, vmem_limit_bytes=62 * 1024 * 1024
        ),
        name="layer_backward",
    )(*saved)


def shards(
    tokens_in, lengths, first_gain, joined_weight, mixer_weight, second_gain, expand_weight, shrink_weight, cotangent
):
    rows, cols = lax.axis_size("row"), lax.axis_size("col")
    hidden_here = shrink_weight.shape[0]
    assert tokens_in.shape[0] * CORES == LEN * rows and cols == CORES
    chunks = (512, 512, hidden_here - 1024)
    gains = jnp.pad(jnp.stack([first_gain, second_gain]), ((0, 6), (0, 0)))
    joined_here = joined_weight.transpose(1, 0, 2)
    expand_here = expand_weight.transpose(1, 2, 0)
    saved = forward(tokens_in, cotangent, lengths, gains, joined_here, mixer_weight, expand_here, shrink_weight, chunks)
    block_output, input_grad, joined_grad, mixer_grad, expand_grad, shrink_grad, gain_grads = backward(saved, chunks)
    f32 = jnp.float32
    return (
        block_output,
        input_grad.astype(f32),
        joined_grad.astype(f32).transpose(1, 0, 2),
        mixer_grad.astype(f32),
        expand_grad.astype(f32).transpose(2, 0, 1),
        shrink_grad.astype(f32),
        gain_grads[0],
        gain_grads[1],
    )


def solution(mesh):
    placed = (
        P(("dp", "col"), "row"),
        P("dp", None),
        P("row"),
        P("row", None, "col"),
        P("col", "row"),
        P("row"),
        P("row", None, "col"),
        P("col", "row"),
        P(("dp", "col"), "row"),
    )
    return jax.shard_map(
        shards,
        mesh=mesh,
        in_specs=placed,
        out_specs=(
            P(("dp", "col"), "row"),
            P(("dp", "col"), "row"),
            P("row", None, "col"),
            P("col", "row"),
            P("row", None, "col"),
            P("col", "row"),
            P("row"),
            P("row"),
        ),
        check_vma=False,
    )
```

```python
import functools
import math

import jax
import jax.numpy as jnp
from jax import lax
from jax.experimental import pallas as pl
from jax.experimental.pallas import tpu as pltpu
from jax.sharding import PartitionSpec as P

D = 1024
HEADS = 16
HD = 64
FF = 2624
LEN = 1024
DOCS = 6
MOST = 800
CORES = 2

rope_base = 160000.0
norm_eps = 1e-05
masked_value = -1000000000.0

PAIR = 2 * HD
WIDE = 256
SOLID = MOST // WIDE * WIDE
REST = LEN - MOST
TO_EXP2 = math.log2(math.e) / math.sqrt(HD)

NT = (((1,), (1,)), ((), ()))
TN = (((0,), (0,)), ((), ()))
MESH_AXES = ("dp", "row", "col")


def lanes_of(shape):
    return lax.broadcasted_iota(jnp.int32, shape, len(shape) - 1)


def swap_halves(u):
    low_half = lanes_of(u.shape) % HD < HD // 2
    return jnp.where(low_half, pltpu.roll(u, PAIR - HD // 2, 1), pltpu.roll(u, HD // 2, 1))


def dot(left, right, dims=(((1,), (0,)), ((), ())), **more):
    return lax.dot_general(left, right, dims, preferred_element_type=jnp.float32, **more)


def only_head(values, head):
    return jnp.where(lanes_of(values.shape) // HD == head, values, jnp.zeros_like(values))


MESH_ID = pl.DeviceIdType.MESH
BLOCK = 256
HALF_ROWS = LEN // 2


class Place:
    def __init__(self):
        self.rows, self.cols = lax.axis_size("row"), lax.axis_size("col")
        self.planes = lax.axis_size("dp") // CORES
        dp = lax.axis_index("dp")
        self.z, self.core = dp // CORES, dp % CORES
        self.row, self.col = lax.axis_index("row"), lax.axis_index("col")
        self.matched = self.core == self.col
        self.parity = self.z % 2
        self.inner = self.parity != (self.z // 2) % 2
        self.seqs = self.rows // CORES

    def at(self, z=None, core=None, row=None, col=None):
        z = self.z if z is None else z
        core = self.core if core is None else core
        return (z * CORES + core, self.row if row is None else row, self.col if col is None else col)

    def sibling(self):
        return self.at(core=1 - self.core)

    def across(self):
        return self.at(col=1 - self.col)

    def pair(self):
        return self.at(z=self.z + 1 - 2 * self.parity)

    def row_after(self, step):
        return lax.rem(self.row + step, self.rows)

    def row_before(self, step):
        return lax.rem(self.row + self.rows - step, self.rows)

    def group_bit(self, level):
        return lax.rem(self.z // (1 << level), 2)

    def mate(self, level):
        if level == 0:
            return self.pair()
        group = self.z // 2
        other = group + (1 << (level - 1)) * (1 - 2 * self.group_bit(level))
        shift = lax.rem(group, 2) + self.parity
        return self.at(z=2 * other + lax.rem(shift + lax.rem(other, 2), 2))

    def barrier(self, partners):
        sem = pltpu.get_barrier_semaphore()
        count = CORES * self.rows
        partners = list(partners)
        for step in range(1, count):
            flat = lax.rem(self.core * self.rows + self.row + step, count)
            partners.append(self.at(core=flat // self.rows, row=lax.rem(flat, self.rows)))
        for partner in partners:
            pl.semaphore_signal(sem, inc=1, device_id=partner, device_id_type=MESH_ID)
        pl.semaphore_wait(sem, len(partners))


def remote(src, dst, send, recv, target):
    return pltpu.make_async_remote_copy(
        src_ref=src, dst_ref=dst, send_sem=send, recv_sem=recv, device_id=target, device_id_type=MESH_ID
    )


def shares(count, part):
    one = int(count * part) // 16 * 16
    return count - 2 * one, one


class Weight:
    def __init__(self, place, source, slot, count, sems, index, part):
        self.place, self.source, self.slot = place, source, slot
        self.both, self.one = shares(count, part)
        self.sems = sems
        self.index = index
        self.local = sems[5].at[index]

    def sem(self, kind, row):
        return self.sems[kind].at[self.index, row]

    def plane_part(self):
        return self.place.parity * self.one, self.one + self.both

    def pair_part(self):
        return self.place.parity * (self.one + self.both), self.one

    def other_part(self):
        return (1 - self.place.parity) * (self.one + self.both), self.one

    def own_y(self):
        p = self.place
        start, size = self.plane_part()
        for step in range(1, p.rows):
            remote(
                self.source(start, size),
                self.slot(p.row, start, size),
                self.sem(0, step),
                self.sem(3, p.row),
                p.at(row=p.row_after(step)),
            ).start()

    def own_x(self):
        p = self.place
        start, size = self.plane_part()
        remote(
            self.source(start, size), self.slot(p.row, start, size), self.sem(1, 0), self.sem(3, p.row), p.across()
        ).start()
        pltpu.make_async_copy(
            self.source(0, 2 * self.one + self.both), self.slot(p.row, 0, 2 * self.one + self.both), self.local
        ).start()

    def pass_on(self):
        p = self.place
        for step in range(1, p.rows):
            row = p.row_before(step)
            self.wait_plane(row)
            self.send_across(row, step).start()
            self.send_pair(row, step).start()

    def take_first(self):
        self.wait_plane(self.place.row)
        self.send_pair(self.place.row, 0).start()

    def take_others(self):
        p = self.place
        for step in range(1, p.rows):
            row = p.row_before(step)
            self.wait_plane(row)
            self.send_pair(row, step).start()

    def wait_plane(self, row):
        p = self.place
        start, size = self.plane_part()
        piece = self.slot(row, start, size)
        remote(piece, piece, self.sem(0, 0), self.sem(3, row), p.across()).wait_recv()

    def send_pair(self, row, step):
        start, size = self.pair_part()
        piece = self.slot(row, start, size)
        return remote(piece, piece, self.sem(2, step), self.sem(4, row), self.place.pair())

    def send_across(self, row, step):
        start, size = self.plane_part()
        piece = self.slot(row, start, size)
        return remote(piece, piece, self.sem(1, step), self.sem(3, row), self.place.across())

    def finish(self):
        p = self.place
        start, size = self.other_part()

        def wait_other(row):
            piece = self.slot(row, start, size)
            remote(piece, piece, self.sem(2, 0), self.sem(4, row), p.pair()).wait_recv()

        for step in range(1, p.rows):
            wait_other(p.row_before(step))

        @pl.when(p.matched)
        def _():
            whole = self.slot(p.row, 0, 2 * self.one + self.both)
            pltpu.make_async_copy(whole, whole, self.local).wait()

        @pl.when(jnp.logical_not(p.matched))
        def _():
            wait_other(p.row)

    def drain(self):
        p = self.place
        start, size = self.plane_part()
        piece = self.slot(p.row, start, size)
        for step in range(1, p.rows):
            self.send_pair(p.row, step).wait_send()

        @pl.when(p.matched)
        def _():
            for step in range(1, p.rows):
                remote(piece, piece, self.sem(0, step), self.sem(3, p.row), p.across()).wait_send()
            for step in range(p.rows):
                self.send_across(p.row, step).wait_send()

        @pl.when(jnp.logical_not(p.matched))
        def _():
            self.send_pair(p.row, 0).wait_send()


def add_rows(count, target, *parts):
    step = next(s for s in (64, 32, 16) if count % s == 0)

    @pl.loop(0, count // step)
    def _(i):
        cut = pl.ds(pl.multiple_of(i * step, step), step)
        total = parts[0][cut, :].astype(jnp.float32)
        for part in parts[1:]:
            total = total + part[cut, :].astype(jnp.float32)
        target[cut, :] = total.astype(target.dtype)


def first_share(count):
    return count * 5 // 16 // 16 * 16


class Grad:
    def __init__(self, place, block, rows, bufs, sems, credits, index, stage=None, summed=None):
        self.p, self.block, self.m, self.index, self.sems, self.stage = place, block, rows, index, sems, stage
        self.credits, self.summed = credits, summed
        self.a = first_share(rows)
        self.b = rows - self.a
        self.recv_a, self.recv_b, self.acc, self.more, self.zbuf = bufs
        self.levels = (place.planes - 1).bit_length()
        self.full = self.acc.shape[0]

    def sem(self, kind, at=0):
        return self.sems.at[self.index, kind, at]

    def low(self):
        return self.acc.at[pl.ds(0, self.a), :]

    def high(self):
        return self.acc.at[pl.ds(self.a, self.b), :]

    def send(self, src, dst, kind, at, target):
        return remote(src, dst, self.sem(kind, at), self.sem(kind + 1, at), target)

    def landed(self, buf, kind, at=0):
        self.send(buf, buf, kind, at, self.p.sibling()).wait_recv()

    def left(self, buf, kind, at=0):
        self.send(buf, buf, kind, at, self.p.sibling()).wait_send()

    def copies_y(self):
        p = self.p
        return [
            self.send(self.block(p.row_after(s), 0, self.a), self.recv_a.at[s - 1], 0, s, p.at(row=p.row_after(s)))
            for s in range(1, p.rows)
        ]

    def copies_x(self):
        return [
            self.send(self.block(j, self.a, self.b), self.recv_b.at[j], 2, j, self.p.across())
            for j in range(self.p.rows)
        ]

    def begin_y(self):
        for copy in self.copies_y():
            copy.start()

    def begin_x(self):
        @pl.when(jnp.logical_not(self.p.matched))
        def _():
            for copy in self.copies_x():
                copy.start()

    def own(self, row, start, size, slot):
        piece = self.block(row, start, size)
        if self.stage is None:
            return piece, []
        buf, sem = self.stage
        buf = buf.at[slot, pl.ds(0, size), :]
        copy = pltpu.make_async_copy(piece, buf, sem.at[slot])
        copy.start()
        return buf, [copy]

    def sum_y(self):
        p = self.p
        own, copies = self.own(p.row, 0, self.a, 0)
        for s in range(1, p.rows):
            self.landed(self.recv_a.at[s - 1], 0, s)
        for copy in copies:
            copy.wait()
        add_rows(self.a, self.recv_a.at[0], own, *[self.recv_a.at[s - 1] for s in range(1, p.rows)])

        @pl.when(jnp.logical_not(p.matched))
        def _():
            self.send(self.recv_a.at[0], self.low(), 4, 0, p.across()).start()

    def sum_x(self):
        p = self.p

        @pl.when(p.matched)
        def _():
            steps = list(range(1, p.rows)) + [0]
            owns = [self.own(p.row_after(s), self.a, self.b, n) for n, s in enumerate(steps[:2])]
            for n, s in enumerate(steps):
                row = p.row_after(s)
                if n >= 2:
                    owns.append(self.own(row, self.a, self.b, n % 2))
                own, copies = owns[n]
                buf = self.recv_b.at[row]
                self.landed(buf, 2, row)
                for copy in copies:
                    copy.wait()
                add_rows(self.b, buf, own, buf)
                if s:
                    target = self.high() if s == 1 else self.more.at[s - 2]
                    self.send(buf, target, 6, s, p.at(row=row)).start()

    def span(self, level):
        start, size = 0, self.full
        for i in range(1, level + 1):
            size //= 2
            start = start + self.p.group_bit(i) * size
        return start, size

    def rows_of(self, start, size):
        return self.acc.at[pl.ds(pl.multiple_of(start, 16), size), :]

    def z_copy(self, level):
        if level == 0:
            return self.send(self.acc, self.zbuf[0], 8, 0, self.p.mate(0))
        start, size = self.span(level - 1)
        half = size // 2
        piece = self.rows_of(start + (1 - self.p.group_bit(level)) * half, half)
        return self.send(piece, self.zbuf[level], 8, level, self.p.mate(level))

    def z_back(self, level):
        piece = self.acc if level == 0 else self.rows_of(*self.span(level))
        return self.send(piece, piece, 10, level, self.p.mate(level))

    def z_free(self, level):
        self.z_copy(level).wait_send()
        pl.semaphore_signal(
            self.credits.at[self.index, level], inc=1, device_id=self.p.mate(level), device_id_type=MESH_ID
        )

    def z_return(self, level):
        pl.semaphore_wait(self.credits.at[self.index, level], 1)
        self.z_back(level).start()

    def plane_sum(self):
        p = self.p

        @pl.when(p.matched)
        def _():
            self.landed(self.low(), 4)
            add_rows(self.a, self.low(), self.low(), self.recv_a.at[0])
            others = []
            for s in range(1, p.rows):
                buf = self.high() if s == 1 else self.more.at[s - 2]
                self.landed(buf, 6, s)
                others.append(buf)
            add_rows(self.b, self.high(), self.recv_b.at[p.row], *others)

    def sum_both(self):
        p = self.p
        if self.summed is None:
            self.plane_sum()
        else:
            pl.when(p.matched)(self.summed.wait)

        @pl.when(jnp.logical_and(p.matched, jnp.logical_not(p.inner)))
        def _():
            self.z_copy(0).start()

    def z0(self):
        p = self.p

        @pl.when(jnp.logical_and(p.matched, p.inner))
        def _():
            self.landed(self.zbuf[0], 8, 0)
            add_rows(self.full, self.acc, self.acc, self.zbuf[0])
            if self.levels > 1:
                self.z_copy(1).start()
            else:
                self.z_return(0)
                self.final().start()

        @pl.when(jnp.logical_and(p.matched, jnp.logical_not(p.inner)))
        def _():
            self.z_free(0)

    def z1(self):
        @pl.when(jnp.logical_and(self.p.matched, self.p.inner))
        def _():
            for level in range(1, self.levels):
                start, size = self.span(level)
                self.landed(self.zbuf[level], 8, level)
                piece = self.rows_of(start, size)
                add_rows(size, piece, piece, self.zbuf[level])
                self.z_free(level)
                if level + 1 < self.levels:
                    self.z_copy(level + 1).start()
                else:
                    self.z_return(level)

    def g1(self):
        @pl.when(jnp.logical_and(self.p.matched, self.p.inner))
        def _():
            for level in range(self.levels - 1, 0, -1):
                start, size = self.span(level - 1)
                half = size // 2
                self.landed(self.rows_of(start + (1 - self.p.group_bit(level)) * half, half), 10, level)
                self.z_return(level - 1)
                if level == 1:
                    self.final().start()

    def g0(self):
        @pl.when(jnp.logical_and(self.p.matched, jnp.logical_not(self.p.inner)))
        def _():
            self.landed(self.acc, 10, 0)
            self.final().start()

    def final(self):
        return remote(self.acc, self.acc, self.sem(12), self.sem(13), self.p.sibling())

    def store(self, stores):
        @pl.when(jnp.logical_not(self.p.matched))
        def _():
            self.final().wait_recv()

        copies = [
            pltpu.make_async_copy(self.acc.at[pl.ds(row, rows), pl.ds(col, cols)], out, sem)
            for row, rows, col, cols, out, sem in stores
        ]
        for copy in copies:
            copy.start()
        return copies

    def drain_plane(self):
        p = self.p
        for copy in self.copies_y():
            copy.wait_send()

        @pl.when(jnp.logical_not(p.matched))
        def _():
            for copy in self.copies_x():
                copy.wait_send()
            self.left(self.recv_a.at[0], 4)

        @pl.when(p.matched)
        def _():
            for s in range(1, p.rows):
                self.left(self.recv_b.at[0], 6, s)

    def drain(self):
        p = self.p
        if self.summed is None:
            self.drain_plane()

        @pl.when(p.matched)
        def _():
            self.final().wait_send()

        @pl.when(jnp.logical_and(p.matched, p.inner))
        def _():
            for level in range(self.levels):
                self.z_back(level).wait_send()


def grad_rows(rows, planes):
    tile = 16 * max(1, planes // 2)
    return -(-rows // tile) * tile


def grad_bufs(rows, cols, blocks, planes, summed=False):
    a = first_share(rows)
    V = lambda *shape: pltpu.VMEM(shape, jnp.bfloat16)
    levels = (planes - 1).bit_length()
    full = grad_rows(rows, planes)
    none = V(16, 128)
    plane = [none, none] if summed else [V(blocks - 1, a, cols), V(blocks, rows - a, cols)]
    more = none if summed or blocks <= 2 else V(blocks - 2, rows - a, cols)
    return plane + [V(full, cols), more, [V(full >> i, cols) for i in range(levels)]]


def plane_bufs(rows, cols, blocks, planes):
    return grad_bufs(rows, cols, blocks, planes)[:4]


def block_rows(i, size=BLOCK):
    return pl.ds(pl.multiple_of(i * size, size), size)


def gelu_parts(gate):
    phi = 0.5 * (1.0 + lax.erf(gate * (1.0 / math.sqrt(2.0))))
    return phi, jnp.exp(gate * gate * -0.5) * (1.0 / math.sqrt(2.0 * math.pi))


def forward_kernel(
    chunks,
    tokens_ref, cot_ref, lengths_ref, gains_ref, freq_ref, joined_ref, mixer_ref, expand_ref, shrink_ref,
    *rest,
):
    n_chunks = len(chunks)
    outs, scratch = rest[:20], rest[20:]
    (o_tokens, o_first, o_q, o_k, o_v, o_mixed, o_lse, o_xhat, o_inv, o_top, o_own, o_other, o_back,
     o_expand, o_shrink, o_joined, o_mixer, o_small, o_table, o_sum) = outs
    (tok, cot, meta_src, meta, gains, table, first, wj, wm, wg, wu, ws, q_s, k_s, v_s, v_t, out_t, lse, mixed, xhat, inv, second,
     top, shrunk, back, back_low, other_half, hid, dgate, dup, g_expand, g_shrink, sum_bufs, sum_sem,
     tok_send, tok_recv, cot_send, cot_recv, swap_send, meta_send, meta_recv, gain_send, gain_recv,
     w_y, w_x, w_z, w_recv, w_recv_z, w_local, mix_send, mix_recv, mixed_send, mixed_recv, out_sem) = scratch
    p = Place()
    rows, seqs = p.rows, p.seqs
    width = tokens_ref.shape[1]
    wide = q_s.shape[1]
    pairs = wide // PAIR
    sems = (w_y, w_x, w_z, w_recv, w_recv_z, w_local)

    def down(ref, buf, col, size):
        source = lambda start, n: ref.at[:, pl.ds(start, n), pl.ds(col, size)]
        slot = lambda row, start, n: buf.at[:, pl.ds(row * width + start, n), :]
        return source, slot

    def along(ref, buf, at):
        source = lambda start, n: ref.at[pl.ds(at + start, n), :]
        slot = lambda row, start, n: buf.at[pl.ds(start, n), pl.ds(pl.multiple_of(row * width, width), width)]
        return source, slot

    half = wide // 2
    joined = [Weight(p, *down(joined_ref, wj.at[h], half * h, half), width, sems, h, 0.25) for h in range(2)]
    mixer = Weight(p, *along(mixer_ref, wm.at[p.core], 0), wide, sems, 2, 0.41)
    groups, at = [], 0
    for i, count in enumerate(chunks):
        groups.append([
            Weight(p, *along(ref, buf, at), count, sems, 3 + 3 * i + n, 0.41)
            for n, (ref, buf) in enumerate(((expand_ref.at[0], wg[i]), (expand_ref.at[1], wu[i]), (shrink_ref, ws[i])))
        ])
        at += count

    place_row = lanes_of((1, LEN))
    for s in range(seqs):
        base = [lengths_ref[p.col * seqs + s, d] for d in range(DOCS)]
        segment = jnp.zeros((1, LEN), jnp.int32)
        start = jnp.zeros((1, LEN), jnp.int32)
        end = jnp.int32(0)
        for d in range(DOCS):
            end = end + base[d]
            past = place_row >= end
            segment = segment + past.astype(jnp.int32)
            start = jnp.where(past, end, start)
        meta_src[s, 0:1, :] = (place_row - start).astype(jnp.float32)
        meta_src[s, 1:2, :] = segment.astype(jnp.float32)
        meta_src[s, 2:3, :] = (segment < DOCS - 1).astype(jnp.float32)
        meta_src[s, 3:8, :] = jnp.zeros((5, LEN), jnp.float32)

    p.barrier([p.across(), p.pair()])

    is_here = p.core == p.row // seqs

    blocks = range(LEN // BLOCK)

    def send_seq(ref, buf, send, recv, block):
        for t in range(seqs):
            seq = lax.rem(p.row + t, seqs)
            piece = ref.at[pl.ds(pl.multiple_of(seq * LEN + block * BLOCK, BLOCK), BLOCK), :]
            place = buf.at[p.row, pl.ds(block * BLOCK, BLOCK), :]
            target = p.at(core=p.row // seqs, row=p.core * seqs + seq)

            def away():
                remote(piece, place, send.at[t, block], recv.at[p.row, block], target).start()

            if t:
                away()
            else:
                pl.when(jnp.logical_not(is_here))(away)

                @pl.when(is_here)
                def _():
                    pltpu.make_async_copy(piece, place, recv.at[p.row, block]).start()

    def swap_seq(buf, slot, recv, swap, u, block):
        piece = buf.at[slot, pl.ds(block * BLOCK, BLOCK), :]
        return remote(piece, piece, swap.at[u, block], recv.at[slot, block], p.sibling())

    def take_seq(buf, recv, swap, block):
        for u in range(seqs):
            slot = p.core * seqs + u
            piece = buf.at[slot, pl.ds(block * BLOCK, BLOCK), :]
            pltpu.make_async_copy(piece, piece, recv.at[slot, block]).wait()
            swap_seq(buf, slot, recv, swap, u, block).start()

    def finish_seq(buf, recv, swap, block):
        for u in range(seqs):
            swap_seq(buf, (1 - p.core) * seqs + u, recv, swap, u, block).wait_recv()

    def drain_seq(buf, send, recv, swap):
        for block in blocks:
            piece = buf.at[0, pl.ds(0, BLOCK), :]
            for u in range(seqs):
                swap_seq(buf, 0, recv, swap, u, block).wait_send()
                if u:
                    remote(piece, piece, send.at[u, block], recv.at[0, block], p.sibling()).wait_send()

            @pl.when(jnp.logical_not(is_here))
            def _():
                remote(piece, piece, send.at[0, block], recv.at[0, block], p.sibling()).wait_send()

    sends_meta = lax.rem(p.row, seqs) == 0

    @pl.when(sends_meta)
    def _():
        for t in range(seqs):
            target = p.at(core=p.row // seqs, row=p.core * seqs + t)

            def away():
                remote(meta_src.at[t], meta, meta_send.at[t], meta_recv, target).start()

            if t:
                away()
            else:
                pl.when(jnp.logical_not(is_here))(away)

                @pl.when(is_here)
                def _():
                    pltpu.make_async_copy(meta_src.at[t], meta, meta_recv).start()

    for step in range(1, rows):
        remote(gains_ref, gains.at[p.row], gain_send.at[step], gain_recv.at[p.row], p.at(row=p.row_after(step))).start()
    pltpu.make_async_copy(gains_ref, gains.at[p.row], gain_recv.at[p.row]).start()
    def service(matched, unmatched):
        for here, actions in ((p.matched, matched), (jnp.logical_not(p.matched), unmatched)):
            if actions:

                @pl.when(here)
                def _():
                    for action in actions:
                        action()

    tokens_of = [functools.partial(send_seq, tokens_ref, tok, tok_send, tok_recv, block) for block in blocks]
    cot_of = [functools.partial(send_seq, cot_ref, cot, cot_send, cot_recv, block) for block in blocks]
    j0, j1 = joined
    (g0, u0, s0), (g1, u1, s1), (g2, u2, s2) = groups

    def each(action, *weights):
        return [functools.partial(getattr(weight, action)) for weight in weights]

    few = len(blocks) // 2
    service(
        tokens_of[:few] + [j0.own_y, j0.own_x] + tokens_of[few:] + [j1.own_x, j1.own_y, mixer.own_y],
        tokens_of,
    )
    pltpu.make_async_copy(meta, meta, meta_recv).wait()
    columns = meta[...].T
    angle = columns[:, 0:1] * freq_ref[0:1, :]
    sign = jnp.where(lanes_of((1, PAIR)) % HD < HD // 2, -1.0, 1.0)
    table[0] = jnp.cos(angle)
    table[1] = jnp.sin(angle) * sign
    segment_col, valid_col = columns[:, 1:2], columns[:, 2:3]

    def gain_of(kind):
        return jnp.concatenate([gains[j, kind : kind + 1, :] for j in range(rows)], axis=1)

    def norm(values):
        center = jnp.mean(values, axis=-1, keepdims=True)
        values = values - center
        spread = jnp.mean(values * values, axis=-1, keepdims=True)
        scale = lax.rsqrt(spread + norm_eps)
        return values * scale, scale

    def tokens_at(cut):
        return jnp.concatenate([tok[j, cut, :] for j in range(rows)], axis=1).astype(jnp.float32)

    def first_norm(block):
        cut = slice(block * BLOCK, (block + 1) * BLOCK)
        finish_seq(tok, tok_recv, swap_send.at[0], block)
        first[cut, :] = (norm(tokens_at(cut))[0] * gain_a).astype(jnp.bfloat16)

    for block in blocks[:few]:
        take_seq(tok, tok_recv, swap_send.at[0], block)
    service([j0.pass_on, mixer.own_x, g0.own_x, u0.own_x], [j0.take_first])
    for step in range(1, rows):
        row = p.row_before(step)
        remote(gains.at[row], gains.at[row], gain_send.at[step], gain_recv.at[row], p.sibling()).wait_recv()
    pltpu.make_async_copy(gains.at[p.row], gains.at[p.row], gain_recv.at[p.row]).wait()
    gain_a, gain_b = gain_of(0), gain_of(1)
    for block in blocks[few:]:
        take_seq(tok, tok_recv, swap_send.at[0], block)
        first_norm(block - few)
    service(each("own_y", *groups[0], *groups[1]) + cot_of + each("own_y", *groups[2]), [j0.take_others, j1.take_first])
    for block in blocks[few:]:
        first_norm(block)
    service([j1.pass_on, s0.own_x], [mixer.take_first])
    j0.finish()

    def attention(pair, between):
        cols = slice(pair * PAIR, (pair + 1) * PAIR)
        per_half = pairs // 2

        def weight_of(j):
            at = pair % per_half * PAIR
            return wj[pair // per_half, j, :, at : at + PAIR]

        @pl.loop(0, LEN // BLOCK)
        def _(i):
            cut = block_rows(i)
            part = first[cut, :]
            cosine, sine = table[0, cut, :], table[1, cut, :]
            for j, dst in ((0, q_s), (1, k_s)):
                raw = dot(part, weight_of(j))
                dst[cut, cols] = (raw * cosine + swap_halves(raw) * sine).astype(jnp.bfloat16)
            v_s[cut, cols] = dot(part, weight_of(2)).astype(jnp.bfloat16)

        v_t[...] = v_s[:, cols].astype(jnp.float32).T.astype(jnp.bfloat16)
        for head in range(2):
            lanes = slice(head * HD, (head + 1) * HD)

            @pl.loop(0, LEN // BLOCK)
            def _(i):
                cut = block_rows(i)
                scores = dot(k_s[:, cols], only_head(q_s[cut, cols], head), NT)
                scores = jnp.where(segment_col == meta[1:2, cut], scores, masked_value)
                peak = jnp.max(scores, axis=0, keepdims=True)
                weights = jnp.exp2((scores - peak) * TO_EXP2)
                total = jnp.sum(weights, axis=0, keepdims=True)
                out_t[lanes, cut] = dot(v_t[lanes, :], weights.astype(jnp.bfloat16)) / total
                lse[pair, head : head + 1, cut] = peak * TO_EXP2 + jnp.log2(total)

            if head == 0:
                service(*between)

        mixed[p.core, :, cols] = out_t[...].T.astype(jnp.bfloat16)
        piece = mixed.at[p.core, :, cols]
        remote(piece, piece, mixed_send.at[pair], mixed_recv.at[pair], p.sibling()).start()

    def share_mixer():
        mixer.finish()
        piece = wm.at[p.core]
        remote(piece, piece, mix_send, mix_recv, p.sibling()).start()

    attention(0, ([mixer.pass_on, g1.own_x, u1.own_x], [g0.take_first]))
    service([g0.pass_on, u0.pass_on], [j1.take_others, u0.take_first])
    attention(1, ([s0.pass_on, s1.own_x], [s0.take_first]))
    service([g2.own_x, u2.own_x], [mixer.take_others] + cot_of)
    j1.finish()
    attention(2, ([g1.pass_on, u1.pass_on, s2.own_x], [g1.take_first, u1.take_first]))
    service([s1.pass_on], [g0.take_others])
    attention(3, ([], [u0.take_others]))
    share_mixer()
    service([], [s0.take_others, s1.take_first])
    for block in blocks:
        take_seq(cot, cot_recv, swap_send.at[1], block)

    for pair in range(pairs):
        piece = mixed.at[p.core, :, pair * PAIR : (pair + 1) * PAIR]
        remote(piece, piece, mixed_send.at[pair], mixed_recv.at[pair], p.sibling()).wait_recv()
    piece = wm.at[p.core]
    remote(piece, piece, mix_send, mix_recv, p.sibling()).wait_recv()
    for block in blocks:
        finish_seq(cot, cot_recv, swap_send.at[1], block)

    @pl.loop(0, LEN // BLOCK)
    def _(i):
        cut = block_rows(i)
        value = tokens_at(cut) + dot(mixed[0, cut, :], wm[0]) + dot(mixed[1, cut, :], wm[1])
        normed, scale = norm(value)
        xhat[cut, :] = normed.astype(jnp.bfloat16)
        inv[cut, :] = jnp.broadcast_to(scale, (BLOCK, PAIR))
        second[cut, :] = (normed * gain_b).astype(jnp.bfloat16)
        shrunk[cut, :] = jnp.where(lanes_of((1, D)) // (D // CORES) == p.core, value, 0.0)
        back[cut, :] = jnp.zeros((BLOCK, D), jnp.float32)

    valid_16 = valid_col > 0.5
    top[...] = jnp.where(valid_16, jnp.concatenate([cot[j] for j in range(rows)], axis=1), jnp.zeros((), jnp.bfloat16))

    keep = []

    def store(src, dst):
        copy = pltpu.make_async_copy(src, dst, out_sem.at[len(keep)])
        keep.append(copy)
        copy.start()

    for j in range(rows):
        store(tok.at[j], o_tokens.at[j])
    for src, dst in ((first, o_first), (q_s, o_q), (k_s, o_k), (v_s, o_v), (mixed.at[p.core], o_mixed), (lse, o_lse),
                     (xhat, o_xhat), (inv, o_inv), (table, o_table), (top, o_top), (wj.at[0], o_joined.at[0]), (wj.at[1], o_joined.at[1]), (wm.at[p.core], o_mixer)):
        store(src, dst)
    for j in range(rows):
        store(gains.at[j], o_small.at[:, pl.ds(j * width, width)])
    store(meta, o_small.at[:, pl.ds(D, LEN)])

    service([g2.pass_on, u2.pass_on, s2.pass_on], [g2.take_first, u2.take_first, g1.take_others])
    early = [([], [u1.take_others]), ([], [g2.take_others, u2.take_others]), ([], [])]
    middle = [([], [s1.take_others, s2.take_first]), ([], [s2.take_others]), ([], [])]

    def first_block(row, start, size):
        return g_expand[0].at[pl.ds(start, size), pl.ds(pl.multiple_of(row * width, width), width)]

    plane = Grad(p, first_block, 2 * chunks[0], (*sum_bufs, []), sum_sem, None, 0)
    then_early = [[], [], [plane.sum_x]]
    at = 0
    for i, lanes in enumerate(chunks):
        for weight in groups[i]:
            weight.finish()

        @pl.loop(0, LEN // BLOCK)
        def _(t):
            cut = block_rows(t)
            part, grad = second[cut, :], top[cut, :]
            gate = dot(part, wg[i][...], NT)
            up = dot(part, wu[i][...], NT)
            hidden_grad = dot(grad, ws[i][...], NT).astype(jnp.bfloat16).astype(jnp.float32)
            phi, density = gelu_parts(gate)
            act = gate * phi
            hidden = (act * up).astype(jnp.bfloat16)
            d_gate = (hidden_grad * up * (phi + gate * density)).astype(jnp.bfloat16)
            d_up = (hidden_grad * act).astype(jnp.bfloat16)
            hid[cut, :lanes] = hidden
            dgate[cut, :lanes] = d_gate
            dup[cut, :lanes] = d_up
            value = shrunk[cut, :] + dot(hidden, ws[i][...])
            grad_sum = back[cut, :] + dot(d_gate, wg[i][...]) + dot(d_up, wu[i][...])
            if i + 1 < n_chunks:
                shrunk[cut, :] = value
                back[cut, :] = grad_sum
            else:
                back_low[cut, :] = grad_sum.astype(jnp.bfloat16)
                left, right = value[:, : D // 2], value[:, D // 2 :]
                shrunk[cut, : D // 2] = jnp.where(p.core == 0, left, right)
                other_half[cut, :] = jnp.where(p.core == 0, right, left).astype(jnp.bfloat16)

            @pl.when(t == LEN // BLOCK // 2 - 1)
            def _():
                service(*early[i])
                for action in then_early[i]:
                    action()


        service(*middle[i])
        if i == 1:
            plane.sum_y()
        if i + 1 == n_chunks:
            store(back_low, o_back)
            store(shrunk.at[:, pl.ds(0, D // 2)], o_own)
            store(other_half, o_other)
        for n, (left, right) in enumerate(((dgate, second), (dup, second), (hid, top))):
            target = g_shrink[i] if n == 2 else g_expand[i]
            for start in range(0, lanes, BLOCK):
                size = min(BLOCK, lanes - start)
                spot = start if n == 2 else n * lanes + start
                target[spot : spot + size, :] = dot(left[:, start : start + size], right[...], TN).astype(jnp.bfloat16)
            if n == 1 and i == 0:
                plane.begin_y()
                plane.begin_x()

        if i:
            store(g_expand[i], o_expand.at[pl.ds(2 * at, 2 * lanes), :])
        store(g_shrink[i], o_shrink.at[pl.ds(at, lanes), :])
        at += lanes

    plane.plane_sum()
    store(plane.acc, o_sum)

    plane.drain_plane()
    drain_seq(tok, tok_send, tok_recv, swap_send.at[0])
    drain_seq(cot, cot_send, cot_recv, swap_send.at[1])
    for step in range(1, rows):
        remote(gains_ref, gains.at[p.row], gain_send.at[step], gain_recv.at[p.row], p.sibling()).wait_send()

    @pl.when(sends_meta)
    def _():
        for t in range(1, seqs):
            remote(meta_src.at[t], meta, meta_send.at[t], meta_recv, p.sibling()).wait_send()

        @pl.when(jnp.logical_not(is_here))
        def _():
            remote(meta_src.at[0], meta, meta_send.at[0], meta_recv, p.sibling()).wait_send()

    for pair in range(pairs):
        piece = mixed.at[p.core, :, pair * PAIR : (pair + 1) * PAIR]
        remote(piece, piece, mixed_send.at[pair], mixed_recv.at[pair], p.sibling()).wait_send()
    piece = wm.at[p.core]
    remote(piece, piece, mix_send, mix_recv, p.sibling()).wait_send()
    for weight in joined + [mixer] + sum(groups, []):
        weight.drain()
    for copy in keep:
        copy.wait()


def forward(tokens, cot, lengths, gains, joined, mixer, expand, shrink, chunks):
    rows = lax.axis_size("row")
    seqs = rows // CORES
    width = tokens.shape[1]
    wide = mixer.shape[0]
    pairs = wide // PAIR
    blocks = LEN // BLOCK
    n_chunks = len(chunks)
    hidden_here = sum(chunks)
    planes = lax.axis_size("dp") // CORES
    weights = 3 + 3 * n_chunks
    bf16, f32 = jnp.bfloat16, jnp.float32
    freq = rope_base ** (-2.0 * jnp.arange(HD // 2, dtype=f32) / HD)
    freq = jnp.broadcast_to(jnp.concatenate([freq] * 4)[None, :], (8, PAIR))
    outs = [
        ((rows, LEN, width), bf16), ((LEN, D), bf16), ((LEN, wide), bf16), ((LEN, wide), bf16), ((LEN, wide), bf16),
        ((LEN, wide), bf16), ((pairs, 2, LEN), f32), ((LEN, D), bf16), ((LEN, PAIR), f32), ((LEN, D), bf16),
        ((LEN, D // 2), f32), ((LEN, D // 2), bf16), ((LEN, D), bf16),
        ((2 * hidden_here, D), bf16), ((hidden_here, D), bf16), ((2, 3, D, wide // 2), bf16), ((wide, D), bf16),
        ((8, D + LEN), f32), ((2, LEN, PAIR), f32), ((grad_rows(2 * chunks[0], planes), width), bf16),
    ]
    V, dma = pltpu.VMEM, pltpu.SemaphoreType.DMA
    widest = max(chunks)
    scratch = [
        V((rows, LEN, width), bf16), V((rows, LEN, width), bf16), V((seqs, 8, LEN), f32), V((8, LEN), f32),
        V((rows, 8, width), f32), V((2, LEN, PAIR), f32), V((LEN, D), bf16), V((2, 3, D, wide // 2), bf16), V((CORES, wide, D), bf16),
        [V((lanes, D), bf16) for lanes in chunks], [V((lanes, D), bf16) for lanes in chunks], [V((lanes, D), bf16) for lanes in chunks],
        V((LEN, wide), bf16), V((LEN, wide), bf16), V((LEN, wide), bf16), V((PAIR, LEN), bf16), V((PAIR, LEN), f32),
        V((pairs, 2, LEN), f32), V((CORES, LEN, wide), bf16), V((LEN, D), bf16), V((LEN, PAIR), f32), V((LEN, D), bf16),
        V((LEN, D), bf16), V((LEN, D), f32), V((LEN, D), f32), V((LEN, D), bf16), V((LEN, D // 2), bf16), V((LEN, widest), bf16), V((LEN, widest), bf16), V((LEN, widest), bf16),
        [V((2 * lanes, D), bf16) for lanes in chunks],
        [V((lanes, D), bf16) for lanes in chunks],
        plane_bufs(2 * chunks[0], width, rows, planes), dma((1, 14, rows)),
        dma((seqs, blocks)), dma((rows, blocks)), dma((seqs, blocks)), dma((rows, blocks)), dma((2, seqs, blocks)), dma((seqs,)), dma,
        dma((rows,)), dma((rows,)),
        dma((weights, rows)), dma((weights, rows)), dma((weights, rows)), dma((weights, rows)), dma((weights, rows)),
        dma((weights,)), dma, dma, dma((pairs,)), dma((pairs,)), dma((2 * rows + 17 + 3 * n_chunks,)),
    ]
    anywhere = pl.BlockSpec(memory_space=pl.ANY)
    in_specs = [anywhere] * 9
    in_specs[2] = pl.BlockSpec(memory_space=pltpu.SMEM)
    in_specs[4] = pl.BlockSpec(memory_space=pltpu.VMEM)
    return pl.pallas_call(
        functools.partial(forward_kernel, chunks),
        in_specs=in_specs,
        out_specs=[anywhere] * len(outs),
        out_shape=[jax.ShapeDtypeStruct(*o) for o in outs],
        scratch_shapes=scratch,
        compiler_params=pltpu.CompilerParams(
            collective_id=0, has_side_effects=True, vmem_limit_bytes=62 * 1024 * 1024
        ),
        name="layer_forward",
    )(tokens, cot, lengths, gains, freq, joined, mixer, expand, shrink)


def backward_kernel(
    chunks,
    tokens_ref, first_ref, q_ref, k_ref, v_ref, mixed_ref, lse_ref, xhat_ref, inv_ref, top_ref, own_ref, other_ref, back_ref,
    expand_ref, shrink_ref, joined_ref, mixer_ref, small_ref, table_ref, sum_ref,
    o_block, o_input, o_joined, o_mixer, o_expand, o_shrink, o_gains,
    q_s, k_s, v_s, mixed, xa, xb, xc, wj, wm, lse, inv, small, table, other, keep_grad, middle_low, mixed_grad, g_mixer, g_joined,
    dk, dv, dq_t, k_t, delta, own_half, block_half, gain_sum, gain_y, gain_x, gain_z, stage_lane, grad_scratch,
    load_sem, stage_sem, sum_sem, grad_sem, credit, swap_credit, back_send, back_recv, other_send, other_recv, first_send, first_recv,
    out_send, out_recv, in_send, in_recv, gain_send, gain_recv, out_sem,
):
    p = Place()
    rows, seqs, planes = p.rows, p.seqs, p.planes
    width = D // rows
    wide = q_s.shape[1]
    pairs = wide // PAIR
    levels = (planes - 1).bit_length()
    half = wide // 2

    def by_row(ref):
        return lambda j, start, size: ref.at[pl.ds(pl.multiple_of(j * width + start, 16), size), :]

    def by_lane(ref, at=0):
        return lambda j, start, size: ref.at[pl.ds(at + start, size), pl.ds(pl.multiple_of(j * width, width), width)]

    grads, places, at = {}, {}, 0
    stage = (stage_lane, stage_sem)

    def add_grad(name, block, count, stage, stores, summed=None):
        i = len(grads)
        grads[name] = Grad(p, block, count, grad_scratch[i], grad_sem, credit, i, stage, summed)
        places[name] = stores

    for i, count in enumerate(chunks):
        add_grad(("E", i), by_lane(expand_ref, 2 * at), 2 * count, stage,
                 [(j * count, count, 0, width, o_expand.at[j, pl.ds(at, count), :]) for j in range(2)],
                 None if i else pltpu.make_async_copy(sum_ref, grad_scratch[0][2], sum_sem))
        add_grad(("S", i), by_lane(shrink_ref, at), count, stage, [(0, count, 0, width, o_shrink.at[pl.ds(at, count), :])])
        at += count
    for h in range(2):
        add_grad(("J", h), by_row(g_joined.at[h]), width, None,
                 [(0, width, j * half, half, o_joined.at[j, :, pl.ds(h * half, half)]) for j in range(3)])
    add_grad(("M", 0), by_lane(g_mixer), wide, None, [(0, wide, 0, width, o_mixer)])

    loads = {}

    def load(name, src, dst):
        copy = pltpu.make_async_copy(src, dst, load_sem.at[len(loads)])
        copy.start()
        loads[name] = copy

    load("small", small_ref, small)
    load("back", back_ref, xc)
    load("xhat", xhat_ref, xa)
    load("inv", inv_ref, inv)
    load("top", top_ref, xb)
    load("mixer", mixer_ref, wm)
    load("mixed", mixed_ref, mixed)
    load("q", q_ref, q_s)
    load("k", k_ref, k_s)
    load("v", v_ref, v_s)
    load("lse", lse_ref, lse)
    load("table", table_ref, table)
    load("joined", joined_ref, wj)
    load("own", own_ref, own_half)
    pl.when(p.matched)(grads["E", 0].summed.start)
    p.barrier([p.across()] + [p.mate(level) for level in range(levels)])

    def swap_block(i, src, dst, send, recv):
        cut = pl.ds(i * BLOCK, BLOCK)
        return remote(src.at[cut, :], dst.at[cut, :], send.at[i], recv.at[i], p.sibling())

    blocks_n = LEN // BLOCK
    for i in range(blocks_n):
        swap_block(i, back_ref, other, back_send, back_recv).start()

    stores = []

    def run(*todo):
        for step in todo:
            if callable(step):
                step()
                continue
            action, kind, i = step
            grad = grads[kind, i]
            if action == "store":
                spots = [spot + (out_sem.at[len(stores) + n],) for n, spot in enumerate(places[kind, i])]
                stores.extend(grad.store(spots))
            elif action == "begin":
                grad.begin_y()
                grad.begin_x()
            else:
                getattr(grad, action)()

    run(("begin_x", "E", 1), ("begin_y", "E", 2), ("begin_x", "S", 0), ("begin_y", "S", 2), ("begin_y", "E", 1))
    other_copy = remote(other_ref, block_half, other_send, other_recv, p.sibling())
    other_copy.start()

    for name in ("small", "back", "xhat", "inv", "top", "mixer", "mixed"):
        loads[name].wait()
    gain_a, gain_b = small[0:1, :D], small[1:2, :D]
    gain_sum[...] = jnp.zeros_like(gain_sum)
    for grad in grads.values():
        if grad.full != grad.m and grad.summed is None:
            grad.acc[grad.m :, :] = jnp.zeros((grad.full - grad.m, grad.acc.shape[1]), jnp.bfloat16)

    def norm_back(grad, normed, scale, gain):
        scaled = grad * gain
        mean_a = jnp.mean(scaled, axis=-1, keepdims=True)
        mean_b = jnp.mean(scaled * normed, axis=-1, keepdims=True)
        return scale * (scaled - mean_a - normed * mean_b)

    def own_of(value):
        return jnp.where(p.core == 0, value[:, : D // 2], value[:, D // 2 :])

    def second_norm(i):
        cut = slice(i * BLOCK, (i + 1) * BLOCK)
        swap_block(i, back_ref, other, back_send, back_recv).wait_recv()
        grad = xc[cut, :].astype(jnp.float32) + other[cut, :].astype(jnp.float32)
        normed = xa[cut, :].astype(jnp.float32)
        gain_sum[1:2, :] += jnp.sum(grad * normed, axis=0, keepdims=True)
        value = xb[cut, :].astype(jnp.float32) + norm_back(grad, normed, inv[cut, 0:1], gain_b)
        keep_grad[cut, :] = own_of(value)
        value = value.astype(jnp.bfloat16)
        middle_low[cut, :] = value
        mixed_grad[cut, :] = dot(value, wm[...], NT).astype(jnp.bfloat16)
    second_norm(0)
    second_norm(1)
    run(("begin_y", "S", 0))
    second_norm(2)
    second_norm(3)
    pl.semaphore_signal(swap_credit, inc=1, device_id=p.sibling(), device_id_type=MESH_ID)
    run(("begin_x", "S", 2))
    @pl.loop(0, D // BLOCK)
    def _(d):
        cut = block_rows(d)
        g_mixer[:, cut] = dot(mixed[...], middle_low[:, cut], TN).astype(jnp.bfloat16)

    load("first", first_ref, xa)
    for j in range(rows):
        load(f"tokens{j}", tokens_ref.at[j], xb.at[:, pl.ds(j * width, width)])

    def leave(src, dst, send, recv):
        core, seq = p.row // seqs, lax.rem(p.row, seqs)
        copies = []
        for u in range(seqs):
            row = p.core * seqs + u
            is_self = jnp.logical_and(core == p.core, row == p.row)
            piece = src.at[:, pl.ds(u * width, width)]
            copies.append((is_self, piece, dst(seq), send.at[u], recv.at[seq], p.at(core=core, row=row)))
        return copies

    def leave_start(copies):
        for is_self, piece, place, send, recv, target in copies:
            @pl.when(is_self)
            def _():
                pltpu.make_async_copy(piece, place, recv).start()

            @pl.when(jnp.logical_not(is_self))
            def _():
                remote(piece, place, send, recv, target).start()

    def leave_wait(copies, dst, recv):
        for s in range(seqs):
            pltpu.make_async_copy(dst(s), dst(s), recv.at[s]).wait()
        for is_self, piece, place, send, recv_sem, target in copies:
            @pl.when(jnp.logical_not(is_self))
            def _():
                remote(piece, place, send, recv_sem, target).wait_send()

    out_at = lambda s: o_block.at[pl.ds(pl.multiple_of(s * LEN, LEN), LEN), :]
    in_at = lambda s: o_input.at[pl.ds(pl.multiple_of(s * LEN, LEN), LEN), :]
    out_copies = leave(block_half, out_at, out_send, out_recv)
    in_copies = leave(mixed_grad, in_at, in_send, in_recv)

    def block_output():
        loads["own"].wait()
        other_copy.wait()
        add_rows(LEN, block_half, own_half, block_half)
        leave_start(out_copies)

    for name in ("q", "k", "v", "lse", "table"):
        loads[name].wait()
    columns = small[:, D:].T
    segment_col = columns[:, 1:2]

    def attention_start(pair):
        cols = slice(pair * PAIR, (pair + 1) * PAIR)
        product = mixed[:, cols].astype(jnp.float32) * mixed_grad[:, cols].astype(jnp.float32)
        chooser = lax.broadcasted_iota(jnp.int32, (8, PAIR), 0) == lanes_of((8, PAIR)) // HD
        delta[...] = dot(chooser.astype(jnp.float32), product, NT, precision=lax.Precision.HIGHEST)
        k_t[...] = k_s[:, cols].astype(jnp.float32).T.astype(jnp.bfloat16)
        dk[...] = jnp.zeros_like(dk)
        dv[...] = jnp.zeros_like(dv)

    def attention_head(pair, head):
        cols = slice(pair * PAIR, (pair + 1) * PAIR)
        keys, values = k_s[:, cols], v_s[:, cols]
        lanes = slice(head * HD, (head + 1) * HD)
        for i in range(LEN // BLOCK):
            cut = slice(i * BLOCK, (i + 1) * BLOCK)
            q_part, g_part = only_head(q_s[cut, cols], head), only_head(mixed_grad[cut, cols], head)
            scores = dot(keys, q_part, NT)
            probs = jnp.exp2(scores * TO_EXP2 - lse[pair, head : head + 1, cut])
            probs = jnp.where(segment_col == small[1:2, D + i * BLOCK : D + (i + 1) * BLOCK], probs, 0.0)
            probs_grad = dot(values, g_part, NT)
            scores_grad = (probs * (probs_grad - delta[head : head + 1, cut])).astype(jnp.bfloat16)
            dv[...] += dot(probs.astype(jnp.bfloat16), g_part)
            dk[...] += dot(scores_grad, q_part)
            dq_t[lanes, cut] = dot(k_t[lanes, :], scores_grad)

    def attention_end(pair):
        cols = slice(pair * PAIR, (pair + 1) * PAIR)
        cosine, sine = table[0], table[1]
        scale = 1.0 / math.sqrt(HD)
        dqs = dq_t[...].T * scale
        q_s[:, cols] = (dqs * cosine - swap_halves(dqs) * sine).astype(jnp.bfloat16)
        dks = dk[...] * scale
        k_s[:, cols] = (dks * cosine - swap_halves(dks) * sine).astype(jnp.bfloat16)
        v_s[:, cols] = dv[...].astype(jnp.bfloat16)

    def joined_weight_grad(h):
        @pl.loop(0, D // BLOCK)
        def _(d):
            cut = block_rows(d)
            part = xa[:, cut]
            for j, back in enumerate((q_s, k_s, v_s)):
                g_joined[h, cut, j * half : (j + 1) * half] = dot(
                    part, back[:, h * half : (h + 1) * half], TN
                ).astype(jnp.bfloat16)

    run(("sum_both", "E", 0))
    attention_start(0)
    attention_head(0, 0)
    attention_head(0, 1)
    attention_end(0)
    attention_start(1)
    attention_head(1, 0)
    attention_head(1, 1)
    attention_end(1)
    run(("z0", "E", 0), ("sum_x", "E", 1), ("sum_y", "E", 1))
    loads["first"].wait()
    joined_weight_grad(0)
    attention_start(2)
    attention_head(2, 0)
    run(
        ("begin_y", "M", 0), ("begin_x", "J", 0), ("sum_y", "S", 2), ("sum_x", "S", 2), ("begin_y", "J", 0),
        ("z1", "E", 0), ("sum_x", "S", 0), ("sum_both", "E", 1),
    )
    attention_head(2, 1)
    attention_end(2)
    attention_start(3)
    attention_head(3, 0)
    attention_head(3, 1)
    attention_end(3)
    run(
        ("sum_both", "S", 2), ("sum_x", "J", 0), ("z0", "E", 1), ("sum_y", "S", 0), ("z0", "S", 2),
        ("sum_both", "S", 0), ("g1", "E", 0), ("begin_x", "E", 2), ("sum_x", "E", 2), ("sum_y", "J", 0),
        ("sum_y", "E", 2), ("z1", "E", 1), ("sum_both", "J", 0), ("sum_both", "E", 2),
    )
    joined_weight_grad(1)
    run(
        ("begin_x", "J", 1), ("begin_y", "J", 1), ("z1", "S", 2), ("z0", "S", 0), ("begin_y", "S", 1),
        ("z0", "J", 0), ("g1", "E", 1), ("sum_x", "J", 1), ("sum_y", "J", 1), ("z1", "S", 0), ("begin_x", "M", 0),
    )
    loads["joined"].wait()
    pl.semaphore_wait(swap_credit, 1)

    def first_back(i):
        cut = slice(i * BLOCK, (i + 1) * BLOCK)
        value = jnp.zeros((BLOCK, D), jnp.float32)
        for h in range(2):
            for j, part in enumerate((q_s, k_s, v_s)):
                value = value + dot(part[cut, h * half : (h + 1) * half], wj[h, j], NT)
        xc[cut, :] = value.astype(jnp.bfloat16)
        swap_block(i, xc, other, first_send, first_recv).start()

    first_back(0)
    first_back(1)

    run(
        ("g0", "E", 0), ("g1", "S", 2), ("z0", "E", 2), ("sum_both", "J", 1), ("z1", "J", 0), ("g1", "S", 0),
        ("begin_x", "S", 1), ("sum_x", "M", 0), ("sum_y", "M", 0), ("sum_y", "S", 1), ("z1", "E", 2), ("g1", "J", 0),
        ("g0", "S", 2), ("sum_x", "S", 1), ("z0", "J", 1), ("sum_both", "M", 0),
    )
    first_back(2)
    first_back(3)
    run(("store", "E", 0), ("sum_both", "S", 1), ("g0", "E", 1), ("g1", "E", 2), ("z1", "J", 1))
    for j in range(rows):
        loads[f"tokens{j}"].wait()
    for i in range(blocks_n):
        cut = slice(i * BLOCK, (i + 1) * BLOCK)
        swap_block(i, xc, other, first_send, first_recv).wait_recv()
        grad = xc[cut, :].astype(jnp.float32) + other[cut, :].astype(jnp.float32)
        values = xb[cut, :].astype(jnp.float32)
        values = values - jnp.mean(values, axis=-1, keepdims=True)
        scale = lax.rsqrt(jnp.mean(values * values, axis=-1, keepdims=True) + norm_eps)
        normed = values * scale
        gain_sum[0:1, :] += jnp.sum(grad * normed, axis=0, keepdims=True)
        total = keep_grad[cut, :] + own_of(norm_back(grad, normed, scale, gain_a))
        mixed_grad[cut, :] = total.astype(jnp.bfloat16)

    def gain_copies():
        return [
            remote(gain_sum.at[:, pl.ds(pl.multiple_of(p.row_after(s) * width, width), width)], gain_y.at[s],
                   gain_send.at[s], gain_recv.at[s], p.at(row=p.row_after(s)))
            for s in range(1, rows)
        ]

    gain_across = remote(gain_x.at[0], gain_x.at[1], gain_send.at[rows], gain_recv.at[rows], p.across())
    gain_total = gain_z.at[2 * levels]
    gain_back = remote(gain_total, gain_total, gain_send.at[rows + 1 + levels], gain_recv.at[rows + 1 + levels], p.sibling())

    def gain_plane(level):
        return remote(gain_z.at[2 * level], gain_z.at[2 * level + 1], gain_send.at[rows + 1 + level],
                      gain_recv.at[rows + 1 + level], p.mate(level))

    def gains_y():
        for s in range(1, rows):
            remote(gain_y.at[s], gain_y.at[s], gain_send.at[s], gain_recv.at[s], p.sibling()).wait_recv()
        total = gain_sum[:, pl.ds(pl.multiple_of(p.row * width, width), width)]
        for s in range(1, rows):
            total = total + gain_y[s]
        gain_x[0] = total
        pl.when(p.matched)(gain_across.start)

    def gains_x():
        @pl.when(jnp.logical_not(p.matched))
        def _():
            gain_across.wait_recv()
            gain_z[0] = gain_x[0] + gain_x[1]
            gain_plane(0).start()

    def gains_z():
        @pl.when(jnp.logical_not(p.matched))
        def _():
            for level in range(levels):
                gain_plane(level).wait()
                gain_z[2 * level + 2] = gain_z[2 * level] + gain_z[2 * level + 1]
                if level + 1 < levels:
                    gain_plane(level + 1).start()
            gain_back.start()
            gain_back.wait_send()

    def gains_end():
        @pl.when(p.matched)
        def _():
            gain_back.wait_recv()
            gain_across.wait_send()

    for copy in gain_copies():
        copy.start()
    leave_start(in_copies)

    run(
        ("z0", "S", 1), ("g1", "J", 1), ("z0", "M", 0), ("g0", "J", 1), gains_y, ("store", "S", 2), ("z1", "S", 1),
        ("store", "E", 1), ("z1", "M", 0), ("g1", "S", 1), gains_x, ("g0", "E", 2), block_output, ("g0", "S", 1),
        ("g0", "S", 0), ("store", "J", 1), ("g0", "J", 0), gains_z, ("store", "S", 0), ("store", "J", 0),
        ("g1", "M", 0), ("store", "E", 2), ("store", "S", 1), ("g0", "M", 0), ("store", "M", 0),
    )
    gains_end()
    gains_out = pltpu.make_async_copy(gain_z.at[2 * levels], o_gains, out_sem.at[len(stores)])
    gains_out.start()

    leave_wait(out_copies, out_at, out_recv)
    leave_wait(in_copies, in_at, in_recv)
    for i in range(blocks_n):
        swap_block(i, back_ref, other, back_send, back_recv).wait_send()
        swap_block(i, xc, other, first_send, first_recv).wait_send()
    for copy in gain_copies():
        copy.wait_send()
    for grad in grads.values():
        grad.drain()
    for copy in stores:
        copy.wait()
    gains_out.wait()


def backward(saved, chunks):
    (tokens, first, queries, keys, values, mixed, lse, xhat, inv, top, own, other, back, expand, shrink, joined, mixer,
     small, table, plane_sum) = saved
    rows = lax.axis_size("row")
    planes = lax.axis_size("dp") // CORES
    seqs = rows // CORES
    width = D // rows
    wide = queries.shape[1]
    pairs = wide // PAIR
    hidden_here = sum(chunks)
    widest = 2 * max(chunks)
    levels = (planes - 1).bit_length()
    bf16, f32 = jnp.bfloat16, jnp.float32
    V, dma = pltpu.VMEM, pltpu.SemaphoreType.DMA
    outs = [
        ((seqs * LEN, width), bf16), ((seqs * LEN, width), bf16), ((3, width, wide), bf16), ((wide, width), bf16),
        ((2, hidden_here, width), bf16), ((hidden_here, width), bf16), ((8, width), f32),
    ]
    grad_shapes = []
    for lanes in chunks:
        grad_shapes += [(2 * lanes, width), (lanes, width)]
    grad_shapes += [(width, 3 * wide // 2)] * 2 + [(wide, width)]
    count = len(grad_shapes)
    scratch = [
        V((LEN, wide), bf16), V((LEN, wide), bf16), V((LEN, wide), bf16), V((LEN, wide), bf16),
        V((LEN, D), bf16), V((LEN, D), bf16), V((LEN, D), bf16), V((2, 3, D, wide // 2), bf16), V((wide, D), bf16),
        V((pairs, 2, LEN), f32), V((LEN, PAIR), f32), V((8, D + LEN), f32), V((2, LEN, PAIR), f32), V((LEN, D), bf16),
        V((LEN, D // 2), f32), V((LEN, D), bf16), V((LEN, wide), bf16), V((wide, D), bf16), V((2, D, 3 * wide // 2), bf16),
        V((LEN, PAIR), f32), V((LEN, PAIR), f32), V((PAIR, LEN), f32), V((PAIR, LEN), bf16), V((8, LEN), f32),
        V((LEN, D // 2), f32), V((LEN, D // 2), bf16),
        V((8, D), f32), V((rows, 8, width), f32), V((2, 8, width), f32), V((2 * levels + 1, 8, width), f32),
        V((2, widest - first_share(widest), width), bf16),
        [grad_bufs(*shape, rows, planes, i == 0) for i, shape in enumerate(grad_shapes)],
        dma((15 + rows,)), dma((2,)), dma, dma((count, 14, max(rows, levels))), pltpu.SemaphoreType.REGULAR((count, levels)),
        pltpu.SemaphoreType.REGULAR,
        dma((4,)), dma((4,)), dma, dma, dma((4,)), dma((4,)),
        dma((seqs,)), dma((seqs,)), dma((seqs,)), dma((seqs,)), dma((rows + 2 + levels,)), dma((rows + 2 + levels,)),
        dma((3 * len(chunks) + 8,)),
    ]
    anywhere = pl.BlockSpec(memory_space=pl.ANY)
    return pl.pallas_call(
        functools.partial(backward_kernel, chunks),
        in_specs=[anywhere] * len(saved),
        out_specs=[anywhere] * len(outs),
        out_shape=[jax.ShapeDtypeStruct(*o) for o in outs],
        scratch_shapes=scratch,
        compiler_params=pltpu.CompilerParams(
            collective_id=1, has_side_effects=True, vmem_limit_bytes=62 * 1024 * 1024
        ),
        name="layer_backward",
    )(*saved)


def shards(
    tokens_in, lengths, first_gain, joined_weight, mixer_weight, second_gain, expand_weight, shrink_weight, cotangent
):
    rows, cols = lax.axis_size("row"), lax.axis_size("col")
    hidden_here = shrink_weight.shape[0]
    assert tokens_in.shape[0] * CORES == LEN * rows and cols == CORES
    chunks = (512, 512, hidden_here - 1024)
    gains = jnp.pad(jnp.stack([first_gain, second_gain]), ((0, 6), (0, 0)))
    joined_here = joined_weight.transpose(1, 0, 2)
    expand_here = expand_weight.transpose(1, 2, 0)
    saved = forward(tokens_in, cotangent, lengths, gains, joined_here, mixer_weight, expand_here, shrink_weight, chunks)
    block_output, input_grad, joined_grad, mixer_grad, expand_grad, shrink_grad, gain_grads = backward(saved, chunks)
    f32 = jnp.float32
    return (
        block_output,
        input_grad.astype(f32),
        joined_grad.astype(f32).transpose(1, 0, 2),
        mixer_grad.astype(f32),
        expand_grad.astype(f32).transpose(2, 0, 1),
        shrink_grad.astype(f32),
        gain_grads[0],
        gain_grads[1],
    )


def solution(mesh):
    placed = (
        P(("dp", "col"), "row"),
        P("dp", None),
        P("row"),
        P("row", None, "col"),
        P("col", "row"),
        P("row"),
        P("row", None, "col"),
        P("col", "row"),
        P(("dp", "col"), "row"),
    )
    return jax.shard_map(
        shards,
        mesh=mesh,
        in_specs=placed,
        out_specs=(
            P(("dp", "col"), "row"),
            P(("dp", "col"), "row"),
            P("row", None, "col"),
            P("col", "row"),
            P("row", None, "col"),
            P("col", "row"),
            P("row"),
            P("row"),
        ),
        check_vma=False,
    )
```

```python
import functools
import math

import jax
import jax.numpy as jnp
import numpy as np
from jax import lax
from jax.experimental import pallas as pl
from jax.experimental.pallas import tpu as pltpu
from jax.sharding import PartitionSpec as P

D = 1024
HEADS = 16
HD = 64
FF = 2624
LEN = 1024
DOCS = 6
MOST = 800
CORES = 2

rope_base = 160000.0
norm_eps = 1e-05
masked_value = -1000000000.0

PAIR = 2 * HD
WIDE = 256
SOLID = MOST // WIDE * WIDE
REST = LEN - MOST
TO_EXP2 = math.log2(math.e) / math.sqrt(HD)

NT = (((1,), (1,)), ((), ()))
TN = (((0,), (0,)), ((), ()))
MESH_AXES = ("dp", "row", "col")


def lanes_of(shape):
    return lax.broadcasted_iota(jnp.int32, shape, len(shape) - 1)


def swap_halves(u):
    low_half = lanes_of(u.shape) % HD < HD // 2
    return jnp.where(low_half, pltpu.roll(u, u.shape[1] - HD // 2, 1), pltpu.roll(u, HD // 2, 1))


def dot(left, right, dims=(((1,), (0,)), ((), ())), **more):
    return lax.dot_general(left, right, dims, preferred_element_type=jnp.float32, **more)


def only_head(values, head):
    return jnp.where(lanes_of(values.shape) // HD == head, values, jnp.zeros_like(values))


MESH_ID = pl.DeviceIdType.MESH
BLOCK = 256
HALF_ROWS = LEN // 2


class Place:
    def __init__(self):
        self.rows, self.cols = lax.axis_size("row"), lax.axis_size("col")
        self.planes = lax.axis_size("dp") // CORES
        dp = lax.axis_index("dp")
        self.z, self.core = dp // CORES, dp % CORES
        self.row, self.col = lax.axis_index("row"), lax.axis_index("col")
        self.matched = self.core == self.col
        self.parity = self.z % 2
        self.inner = self.parity != (self.z // 2) % 2
        self.seqs = self.rows // CORES

    def at(self, z=None, core=None, row=None, col=None):
        z = self.z if z is None else z
        core = self.core if core is None else core
        return (z * CORES + core, self.row if row is None else row, self.col if col is None else col)

    def sibling(self):
        return self.at(core=1 - self.core)

    def across(self):
        return self.at(col=1 - self.col)

    def pair(self):
        return self.at(z=self.z + 1 - 2 * self.parity)

    def row_after(self, step):
        return lax.rem(self.row + step, self.rows)

    def row_before(self, step):
        return lax.rem(self.row + self.rows - step, self.rows)

    def group_bit(self, level):
        return lax.rem(self.z // (1 << level), 2)

    def mate(self, level):
        if level == 0:
            return self.pair()
        group = self.z // 2
        other = group + (1 << (level - 1)) * (1 - 2 * self.group_bit(level))
        shift = lax.rem(group, 2) + self.parity
        return self.at(z=2 * other + lax.rem(shift + lax.rem(other, 2), 2))

    def barrier(self, partners):
        sem = pltpu.get_barrier_semaphore()
        count = CORES * self.rows
        partners = list(partners)
        for step in range(1, count):
            flat = lax.rem(self.core * self.rows + self.row + step, count)
            partners.append(self.at(core=flat // self.rows, row=lax.rem(flat, self.rows)))
        for partner in partners:
            pl.semaphore_signal(sem, inc=1, device_id=partner, device_id_type=MESH_ID)
        pl.semaphore_wait(sem, len(partners))


def remote(src, dst, send, recv, target):
    return pltpu.make_async_remote_copy(
        src_ref=src, dst_ref=dst, send_sem=send, recv_sem=recv, device_id=target, device_id_type=MESH_ID
    )


def shares(count, part):
    one = int(count * part) // 16 * 16
    return count - 2 * one, one


class Weight:
    def __init__(self, place, source, slot, count, sems, index, part):
        self.place, self.source, self.slot = place, source, slot
        self.both, self.one = shares(count, part)
        self.sems = sems
        self.index = index
        self.local = sems[5].at[index]

    def sem(self, kind, row):
        return self.sems[kind].at[self.index, row]

    def plane_part(self):
        return self.place.parity * self.one, self.one + self.both

    def pair_part(self):
        return self.place.parity * (self.one + self.both), self.one

    def other_part(self):
        return (1 - self.place.parity) * (self.one + self.both), self.one

    def own_y(self):
        p = self.place
        start, size = self.plane_part()
        for step in range(1, p.rows):
            remote(
                self.source(start, size),
                self.slot(p.row, start, size),
                self.sem(0, step),
                self.sem(3, p.row),
                p.at(row=p.row_after(step)),
            ).start()

    def own_x(self):
        p = self.place
        start, size = self.plane_part()
        remote(
            self.source(start, size), self.slot(p.row, start, size), self.sem(1, 0), self.sem(3, p.row), p.across()
        ).start()
        pltpu.make_async_copy(
            self.source(0, 2 * self.one + self.both), self.slot(p.row, 0, 2 * self.one + self.both), self.local
        ).start()

    def pass_on(self):
        p = self.place
        for step in range(1, p.rows):
            row = p.row_before(step)
            self.wait_plane(row)
            self.send_across(row, step).start()
            self.send_pair(row, step).start()

    def take_first(self):
        self.wait_plane(self.place.row)
        self.send_pair(self.place.row, 0).start()

    def take_others(self):
        p = self.place
        for step in range(1, p.rows):
            row = p.row_before(step)
            self.wait_plane(row)
            self.send_pair(row, step).start()

    def wait_plane(self, row):
        p = self.place
        start, size = self.plane_part()
        piece = self.slot(row, start, size)
        remote(piece, piece, self.sem(0, 0), self.sem(3, row), p.across()).wait_recv()

    def send_pair(self, row, step):
        start, size = self.pair_part()
        piece = self.slot(row, start, size)
        return remote(piece, piece, self.sem(2, step), self.sem(4, row), self.place.pair())

    def send_across(self, row, step):
        start, size = self.plane_part()
        piece = self.slot(row, start, size)
        return remote(piece, piece, self.sem(1, step), self.sem(3, row), self.place.across())

    def finish(self):
        p = self.place
        start, size = self.other_part()

        def wait_other(row):
            piece = self.slot(row, start, size)
            remote(piece, piece, self.sem(2, 0), self.sem(4, row), p.pair()).wait_recv()

        for step in range(1, p.rows):
            wait_other(p.row_before(step))

        @pl.when(p.matched)
        def _():
            whole = self.slot(p.row, 0, 2 * self.one + self.both)
            pltpu.make_async_copy(whole, whole, self.local).wait()

        @pl.when(jnp.logical_not(p.matched))
        def _():
            wait_other(p.row)

    def drain(self):
        p = self.place
        start, size = self.plane_part()
        piece = self.slot(p.row, start, size)
        for step in range(1, p.rows):
            self.send_pair(p.row, step).wait_send()

        @pl.when(p.matched)
        def _():
            for step in range(1, p.rows):
                remote(piece, piece, self.sem(0, step), self.sem(3, p.row), p.across()).wait_send()
            for step in range(p.rows):
                self.send_across(p.row, step).wait_send()

        @pl.when(jnp.logical_not(p.matched))
        def _():
            self.send_pair(p.row, 0).wait_send()


def add_rows(count, target, *parts):
    step = next(s for s in (64, 32, 16) if count % s == 0)

    @pl.loop(0, count // step)
    def _(i):
        cut = pl.ds(pl.multiple_of(i * step, step), step)
        total = parts[0][cut, :].astype(jnp.float32)
        for part in parts[1:]:
            total = total + part[cut, :].astype(jnp.float32)
        target[cut, :] = total.astype(target.dtype)


def first_share(count, share=5 / 16):
    return int(count * share) // 16 * 16


class Grad:
    def __init__(self, place, block, rows, bufs, sems, credits, index, stage=None, summed=None, share=5 / 16):
        self.p, self.block, self.m, self.index, self.sems, self.stage = place, block, rows, index, sems, stage
        self.credits, self.summed = credits, summed
        self.a = first_share(rows, share)
        self.b = rows - self.a
        self.recv_a, self.recv_b, self.acc, self.more, self.zbuf = bufs
        self.levels = (place.planes - 1).bit_length()
        self.full = self.acc.shape[0]

    def sem(self, kind, at=0):
        return self.sems.at[self.index, kind, at]

    def low(self):
        return self.acc.at[pl.ds(0, self.a), :]

    def high(self):
        return self.acc.at[pl.ds(self.a, self.b), :]

    def send(self, src, dst, kind, at, target):
        return remote(src, dst, self.sem(kind, at), self.sem(kind + 1, at), target)

    def landed(self, buf, kind, at=0):
        self.send(buf, buf, kind, at, self.p.sibling()).wait_recv()

    def left(self, buf, kind, at=0):
        self.send(buf, buf, kind, at, self.p.sibling()).wait_send()

    def copies_y(self):
        p = self.p
        return [
            self.send(self.block(p.row_after(s), 0, self.a), self.recv_a.at[s - 1], 0, s, p.at(row=p.row_after(s)))
            for s in range(1, p.rows)
        ]

    def copies_x(self):
        return [
            self.send(self.block(j, self.a, self.b), self.recv_b.at[j], 2, j, self.p.across())
            for j in range(self.p.rows)
        ]

    def begin_y(self):
        for copy in self.copies_y():
            copy.start()

    def begin_x(self):
        @pl.when(jnp.logical_not(self.p.matched))
        def _():
            for copy in self.copies_x():
                copy.start()

    def own(self, row, start, size, slot):
        piece = self.block(row, start, size)
        if self.stage is None:
            return piece, []
        buf, sem = self.stage
        buf = buf.at[slot, pl.ds(0, size), :]
        copy = pltpu.make_async_copy(piece, buf, sem.at[slot])
        copy.start()
        return buf, [copy]

    def sum_y(self):
        p = self.p
        own, copies = self.own(p.row, 0, self.a, 0)
        for s in range(1, p.rows):
            self.landed(self.recv_a.at[s - 1], 0, s)
        for copy in copies:
            copy.wait()
        add_rows(self.a, self.recv_a.at[0], own, *[self.recv_a.at[s - 1] for s in range(1, p.rows)])

        @pl.when(jnp.logical_not(p.matched))
        def _():
            self.send(self.recv_a.at[0], self.low(), 4, 0, p.across()).start()

    def sum_x(self):
        p = self.p

        @pl.when(p.matched)
        def _():
            steps = list(range(1, p.rows)) + [0]
            owns = [self.own(p.row_after(s), self.a, self.b, n) for n, s in enumerate(steps[:2])]
            for n, s in enumerate(steps):
                row = p.row_after(s)
                if n >= 2:
                    owns.append(self.own(row, self.a, self.b, n % 2))
                own, copies = owns[n]
                buf = self.recv_b.at[row]
                self.landed(buf, 2, row)
                for copy in copies:
                    copy.wait()
                add_rows(self.b, buf, own, buf)
                if s:
                    target = self.high() if s == 1 else self.more.at[s - 2]
                    self.send(buf, target, 6, s, p.at(row=row)).start()

    def span(self, level):
        start, size = 0, self.full
        for i in range(1, level + 1):
            size //= 2
            start = start + self.p.group_bit(i) * size
        return start, size

    def rows_of(self, start, size):
        return self.acc.at[pl.ds(pl.multiple_of(start, 16), size), :]

    def z_copy(self, level):
        if level == 0:
            return self.send(self.acc, self.zbuf[0], 8, 0, self.p.mate(0))
        start, size = self.span(level - 1)
        half = size // 2
        piece = self.rows_of(start + (1 - self.p.group_bit(level)) * half, half)
        return self.send(piece, self.zbuf[level], 8, level, self.p.mate(level))

    def z_back(self, level):
        piece = self.acc if level == 0 else self.rows_of(*self.span(level))
        return self.send(piece, piece, 10, level, self.p.mate(level))

    def z_free(self, level):
        self.z_copy(level).wait_send()
        pl.semaphore_signal(
            self.credits.at[self.index, level], inc=1, device_id=self.p.mate(level), device_id_type=MESH_ID
        )

    def z_return(self, level):
        pl.semaphore_wait(self.credits.at[self.index, level], 1)
        self.z_back(level).start()

    def plane_sum(self):
        p = self.p

        @pl.when(p.matched)
        def _():
            self.landed(self.low(), 4)
            add_rows(self.a, self.low(), self.low(), self.recv_a.at[0])
            others = []
            for s in range(1, p.rows):
                buf = self.high() if s == 1 else self.more.at[s - 2]
                self.landed(buf, 6, s)
                others.append(buf)
            add_rows(self.b, self.high(), self.recv_b.at[p.row], *others)

    def sum_both(self):
        p = self.p
        if self.summed is None:
            self.plane_sum()
        else:
            pl.when(p.matched)(self.summed.wait)

        @pl.when(jnp.logical_and(p.matched, jnp.logical_not(p.inner)))
        def _():
            self.z_copy(0).start()

    def z0(self):
        p = self.p

        @pl.when(jnp.logical_and(p.matched, p.inner))
        def _():
            self.landed(self.zbuf[0], 8, 0)
            add_rows(self.full, self.acc, self.acc, self.zbuf[0])
            if self.levels > 1:
                self.z_copy(1).start()
            else:
                self.z_return(0)
                self.final().start()

        @pl.when(jnp.logical_and(p.matched, jnp.logical_not(p.inner)))
        def _():
            self.z_free(0)

    def z1(self):
        @pl.when(jnp.logical_and(self.p.matched, self.p.inner))
        def _():
            for level in range(1, self.levels):
                start, size = self.span(level)
                self.landed(self.zbuf[level], 8, level)
                piece = self.rows_of(start, size)
                add_rows(size, piece, piece, self.zbuf[level])
                self.z_free(level)
                if level + 1 < self.levels:
                    self.z_copy(level + 1).start()
                else:
                    self.z_return(level)

    def g1(self):
        @pl.when(jnp.logical_and(self.p.matched, self.p.inner))
        def _():
            for level in range(self.levels - 1, 0, -1):
                start, size = self.span(level - 1)
                half = size // 2
                self.landed(self.rows_of(start + (1 - self.p.group_bit(level)) * half, half), 10, level)
                self.z_return(level - 1)
                if level == 1:
                    self.final().start()

    def g0(self):
        @pl.when(jnp.logical_and(self.p.matched, jnp.logical_not(self.p.inner)))
        def _():
            self.landed(self.acc, 10, 0)
            self.final().start()

    def final(self):
        return remote(self.acc, self.acc, self.sem(12), self.sem(13), self.p.sibling())

    def store(self, stores):
        @pl.when(jnp.logical_not(self.p.matched))
        def _():
            self.final().wait_recv()

        copies = [
            pltpu.make_async_copy(self.acc.at[pl.ds(row, rows), pl.ds(col, cols)], out, sem)
            for row, rows, col, cols, out, sem in stores
        ]
        for copy in copies:
            copy.start()
        return copies

    def drain_plane(self):
        p = self.p
        for copy in self.copies_y():
            copy.wait_send()

        @pl.when(jnp.logical_not(p.matched))
        def _():
            for copy in self.copies_x():
                copy.wait_send()
            self.left(self.recv_a.at[0], 4)

        @pl.when(p.matched)
        def _():
            for s in range(1, p.rows):
                self.left(self.recv_b.at[0], 6, s)

    def drain(self):
        p = self.p
        if self.summed is None:
            self.drain_plane()

        @pl.when(p.matched)
        def _():
            self.final().wait_send()

        @pl.when(jnp.logical_and(p.matched, p.inner))
        def _():
            for level in range(self.levels):
                self.z_back(level).wait_send()


def grad_rows(rows, planes):
    tile = 16 * max(1, planes // 2)
    return -(-rows // tile) * tile


def grad_bufs(rows, cols, blocks, planes, summed=False, share=5 / 16):
    a = first_share(rows, share)
    V = lambda *shape: pltpu.VMEM(shape, jnp.bfloat16)
    levels = (planes - 1).bit_length()
    full = grad_rows(rows, planes)
    none = V(16, 128)
    plane = [none, none] if summed else [V(blocks - 1, a, cols), V(blocks, rows - a, cols)]
    more = none if summed or blocks <= 2 else V(blocks - 2, rows - a, cols)
    return plane + [V(full, cols), more, [V(full >> i, cols) for i in range(levels)]]


def plane_bufs(rows, cols, blocks, planes):
    return grad_bufs(rows, cols, blocks, planes, False, 1 / 2)[:4]


def block_rows(i, size=BLOCK):
    return pl.ds(pl.multiple_of(i * size, size), size)


def gelu_parts(gate):
    phi = 0.5 * (1.0 + lax.erf(gate * (1.0 / math.sqrt(2.0))))
    return phi, jnp.exp(gate * gate * -0.5) * (1.0 / math.sqrt(2.0 * math.pi))


def forward_kernel(
    chunks,
    tokens_ref, cot_ref, lengths_ref, first_gain_ref, second_gain_ref, freq_ref, joined_ref, mixer_ref, expand_ref, shrink_ref,
    *rest,
):
    n_chunks = len(chunks)
    outs, scratch = rest[:20], rest[20:]
    (o_tokens, o_first, o_q, o_k, o_v, o_mixed, o_lse, o_xhat, o_inv, o_top, o_own, o_other, o_back,
     o_expand, o_shrink, o_joined, o_mixer, o_small, o_table, o_sum) = outs
    (tok, cot, meta_src, meta, gains_ref, gains, table, first, wj, wm, wg, wu, ws, q_s, k_s, v_s, v_t, out_t, lse, mixed, xhat, inv, second,
     top, shrunk, back, back_low, other_half, hid, dgate, dup, g_expand, g_shrink, sum_bufs, sum_sem,
     tok_send, tok_recv, cot_send, cot_recv, swap_send, meta_send, meta_recv, gain_send, gain_recv,
     w_y, w_x, w_z, w_recv, w_recv_z, w_local, mix_send, mix_recv, mixed_send, mixed_recv, out_sem) = scratch
    p = Place()
    rows, seqs = p.rows, p.seqs
    width = tokens_ref.shape[1]
    wide = q_s.shape[1]
    pairs = wide // PAIR
    sems = (w_y, w_x, w_z, w_recv, w_recv_z, w_local)

    def down(ref, buf, col, size):
        source = lambda start, n: ref.at[:, pl.ds(start, n), pl.ds(col, size)]
        slot = lambda row, start, n: buf.at[:, pl.ds(row * width + start, n), :]
        return source, slot

    def along(ref, buf, at):
        source = lambda start, n: ref.at[pl.ds(at + start, n), :]
        slot = lambda row, start, n: buf.at[pl.ds(start, n), pl.ds(pl.multiple_of(row * width, width), width)]
        return source, slot

    half = wide // 2
    joined = [Weight(p, *down(joined_ref, wj.at[h], half * h, half), width, sems, h, 0.25) for h in range(2)]
    mixer = Weight(p, *along(mixer_ref, wm.at[p.core], 0), wide, sems, 2, 0.41)
    groups, at = [], 0
    for i, count in enumerate(chunks):
        groups.append([
            Weight(p, *along(ref, buf, at), count, sems, 3 + 3 * i + n, 0.41)
            for n, (ref, buf) in enumerate(((expand_ref.at[0], wg[i]), (expand_ref.at[1], wu[i]), (shrink_ref, ws[i])))
        ])
        at += count

    place_row = lanes_of((1, LEN))
    for s in range(seqs):
        base = [lengths_ref[p.col * seqs + s, d] for d in range(DOCS)]
        segment = jnp.zeros((1, LEN), jnp.int32)
        start = jnp.zeros((1, LEN), jnp.int32)
        end = jnp.int32(0)
        for d in range(DOCS):
            end = end + base[d]
            past = place_row >= end
            segment = segment + past.astype(jnp.int32)
            start = jnp.where(past, end, start)
        meta_src[s, 0:1, :] = (place_row - start).astype(jnp.float32)
        meta_src[s, 1:2, :] = segment.astype(jnp.float32)
        meta_src[s, 2:3, :] = (segment < DOCS - 1).astype(jnp.float32)
        meta_src[s, 3:8, :] = jnp.zeros((5, LEN), jnp.float32)

    gains_ref[0:1, :] = first_gain_ref[...]
    gains_ref[1:2, :] = second_gain_ref[...]
    gains_ref[2:8, :] = jnp.zeros((6, width), jnp.float32)
    p.barrier([p.across(), p.pair()])

    is_here = p.core == p.row // seqs

    blocks = range(LEN // BLOCK)

    def send_seq(ref, buf, send, recv, block):
        for t in range(seqs):
            seq = lax.rem(p.row + t, seqs)
            piece = ref.at[pl.ds(pl.multiple_of(seq * LEN + block * BLOCK, BLOCK), BLOCK), :]
            place = buf.at[p.row, pl.ds(block * BLOCK, BLOCK), :]
            target = p.at(core=p.row // seqs, row=p.core * seqs + seq)

            def away():
                remote(piece, place, send.at[t, block], recv.at[p.row, block], target).start()

            if t:
                away()
            else:
                pl.when(jnp.logical_not(is_here))(away)

                @pl.when(is_here)
                def _():
                    pltpu.make_async_copy(piece, place, recv.at[p.row, block]).start()

    def swap_seq(buf, slot, recv, swap, u, block):
        piece = buf.at[slot, pl.ds(block * BLOCK, BLOCK), :]
        return remote(piece, piece, swap.at[u, block], recv.at[slot, block], p.sibling())

    def take_seq(buf, recv, swap, block):
        for u in range(seqs):
            slot = p.core * seqs + u
            piece = buf.at[slot, pl.ds(block * BLOCK, BLOCK), :]
            pltpu.make_async_copy(piece, piece, recv.at[slot, block]).wait()
            swap_seq(buf, slot, recv, swap, u, block).start()

    def finish_seq(buf, recv, swap, block):
        for u in range(seqs):
            swap_seq(buf, (1 - p.core) * seqs + u, recv, swap, u, block).wait_recv()

    def drain_seq(buf, send, recv, swap):
        for block in blocks:
            piece = buf.at[0, pl.ds(0, BLOCK), :]
            for u in range(seqs):
                swap_seq(buf, 0, recv, swap, u, block).wait_send()
                if u:
                    remote(piece, piece, send.at[u, block], recv.at[0, block], p.sibling()).wait_send()

            @pl.when(jnp.logical_not(is_here))
            def _():
                remote(piece, piece, send.at[0, block], recv.at[0, block], p.sibling()).wait_send()

    sends_meta = lax.rem(p.row, seqs) == 0

    @pl.when(sends_meta)
    def _():
        for t in range(seqs):
            target = p.at(core=p.row // seqs, row=p.core * seqs + t)

            def away():
                remote(meta_src.at[t], meta, meta_send.at[t], meta_recv, target).start()

            if t:
                away()
            else:
                pl.when(jnp.logical_not(is_here))(away)

                @pl.when(is_here)
                def _():
                    pltpu.make_async_copy(meta_src.at[t], meta, meta_recv).start()

    for step in range(1, rows):
        remote(gains_ref, gains.at[p.row], gain_send.at[step], gain_recv.at[p.row], p.at(row=p.row_after(step))).start()
    pltpu.make_async_copy(gains_ref, gains.at[p.row], gain_recv.at[p.row]).start()
    def service(matched, unmatched):
        for here, actions in ((p.matched, matched), (jnp.logical_not(p.matched), unmatched)):
            if actions:

                @pl.when(here)
                def _():
                    for action in actions:
                        action()

    tokens_of = [functools.partial(send_seq, tokens_ref, tok, tok_send, tok_recv, block) for block in blocks]
    cot_of = [functools.partial(send_seq, cot_ref, cot, cot_send, cot_recv, block) for block in blocks]
    j0, j1 = joined
    (g0, u0, s0), (g1, u1, s1), (g2, u2, s2) = groups

    def each(action, *weights):
        return [functools.partial(getattr(weight, action)) for weight in weights]

    few = len(blocks) // 2
    service(
        tokens_of[:few] + [j0.own_y, j0.own_x] + tokens_of[few:] + [j1.own_x, j1.own_y, mixer.own_y],
        tokens_of,
    )
    pltpu.make_async_copy(meta, meta, meta_recv).wait()
    columns = meta[...].T
    angle = columns[:, 0:1] * freq_ref[0:1, :]
    sign = jnp.where(lanes_of((1, PAIR)) % HD < HD // 2, -1.0, 1.0)
    table[0] = jnp.cos(angle)
    table[1] = jnp.sin(angle) * sign
    segment_col, valid_col = columns[:, 1:2], columns[:, 2:3]

    def gain_of(kind):
        return jnp.concatenate([gains[j, kind : kind + 1, :] for j in range(rows)], axis=1)

    def norm(values):
        center = jnp.mean(values, axis=-1, keepdims=True)
        values = values - center
        spread = jnp.mean(values * values, axis=-1, keepdims=True)
        scale = lax.rsqrt(spread + norm_eps)
        return values * scale, scale

    def tokens_at(cut):
        return jnp.concatenate([tok[j, cut, :] for j in range(rows)], axis=1).astype(jnp.float32)

    def first_norm(block):
        cut = slice(block * BLOCK, (block + 1) * BLOCK)
        finish_seq(tok, tok_recv, swap_send.at[0], block)
        first[cut, :] = (norm(tokens_at(cut))[0] * gain_a).astype(jnp.bfloat16)

    for block in blocks[:few]:
        take_seq(tok, tok_recv, swap_send.at[0], block)
    service([j0.pass_on, mixer.own_x, g0.own_x, u0.own_x], [j0.take_first])
    for step in range(1, rows):
        row = p.row_before(step)
        remote(gains.at[row], gains.at[row], gain_send.at[step], gain_recv.at[row], p.sibling()).wait_recv()
    pltpu.make_async_copy(gains.at[p.row], gains.at[p.row], gain_recv.at[p.row]).wait()
    gain_a, gain_b = gain_of(0), gain_of(1)
    for block in blocks[few:]:
        take_seq(tok, tok_recv, swap_send.at[0], block)
        first_norm(block - few)
    service(each("own_y", *groups[0], *groups[1]) + cot_of + each("own_y", *groups[2]), [j0.take_others, j1.take_first])
    for block in blocks[few:]:
        first_norm(block)
    service([j1.pass_on, s0.own_x], [mixer.take_first])
    j0.finish()

    def project(h):
        cols = slice(h * half, (h + 1) * half)

        @pl.loop(0, LEN // BLOCK)
        def _(i):
            cut = block_rows(i)
            part = first[cut, :]
            cosine, sine = (jnp.concatenate([table[n, cut, :]] * (half // PAIR), axis=1) for n in range(2))
            for j, dst in ((0, q_s), (1, k_s)):
                raw = dot(part, wj[h, j])
                dst[cut, cols] = (raw * cosine + swap_halves(raw) * sine).astype(jnp.bfloat16)
            v_s[cut, cols] = dot(part, wj[h, 2]).astype(jnp.bfloat16)

    def attention(pair, between):
        cols = slice(pair * PAIR, (pair + 1) * PAIR)
        v_t[...] = v_s[:, cols].astype(jnp.float32).T.astype(jnp.bfloat16)
        for head in range(2):
            lanes = slice(head * HD, (head + 1) * HD)

            @pl.loop(0, LEN // BLOCK)
            def _(i):
                cut = block_rows(i)
                scores = dot(k_s[:, cols], only_head(q_s[cut, cols], head), NT)
                scores = jnp.where(segment_col == meta[1:2, cut], scores, masked_value)
                peak = jnp.max(scores, axis=0, keepdims=True)
                weights = jnp.exp2((scores - peak) * TO_EXP2)
                total = jnp.sum(weights, axis=0, keepdims=True)
                out_t[lanes, cut] = dot(v_t[lanes, :], weights.astype(jnp.bfloat16)) / total
                lse[pair, head : head + 1, cut] = peak * TO_EXP2 + jnp.log2(total)

            if head == 0:
                service(*between)

        mixed[p.core, :, cols] = out_t[...].T.astype(jnp.bfloat16)
        piece = mixed.at[p.core, :, cols]
        remote(piece, piece, mixed_send.at[pair], mixed_recv.at[pair], p.sibling()).start()

    def share_mixer():
        mixer.finish()
        piece = wm.at[p.core]
        remote(piece, piece, mix_send, mix_recv, p.sibling()).start()

    project(0)
    attention(0, ([mixer.pass_on, g1.own_x, u1.own_x], [g0.take_first]))
    service([g0.pass_on, u0.pass_on], [j1.take_others, u0.take_first])
    attention(1, ([s0.pass_on, s1.own_x], [s0.take_first]))
    service([g2.own_x, u2.own_x], [mixer.take_others] + cot_of)
    j1.finish()
    project(1)
    attention(2, ([g1.pass_on, u1.pass_on, s2.own_x], [g1.take_first, u1.take_first]))
    service([s1.pass_on], [g0.take_others])
    attention(3, ([], [u0.take_others]))
    share_mixer()
    service([], [s0.take_others, s1.take_first])
    for block in blocks:
        take_seq(cot, cot_recv, swap_send.at[1], block)

    for pair in range(pairs):
        piece = mixed.at[p.core, :, pair * PAIR : (pair + 1) * PAIR]
        remote(piece, piece, mixed_send.at[pair], mixed_recv.at[pair], p.sibling()).wait_recv()
    piece = wm.at[p.core]
    remote(piece, piece, mix_send, mix_recv, p.sibling()).wait_recv()
    for block in blocks:
        finish_seq(cot, cot_recv, swap_send.at[1], block)

    @pl.loop(0, LEN // BLOCK)
    def _(i):
        cut = block_rows(i)
        value = tokens_at(cut) + dot(mixed[0, cut, :], wm[0]) + dot(mixed[1, cut, :], wm[1])
        normed, scale = norm(value)
        xhat[cut, :] = normed.astype(jnp.bfloat16)
        inv[cut, :] = jnp.broadcast_to(scale, (BLOCK, PAIR))
        second[cut, :] = (normed * gain_b).astype(jnp.bfloat16)
        shrunk[cut, :] = jnp.where(lanes_of((1, D)) // (D // CORES) == p.core, value, 0.0)
        back[cut, :] = jnp.zeros((BLOCK, D), jnp.float32)

    valid_16 = valid_col > 0.5
    top[...] = jnp.where(valid_16, jnp.concatenate([cot[j] for j in range(rows)], axis=1), jnp.zeros((), jnp.bfloat16))

    keep = []

    def store(src, dst):
        copy = pltpu.make_async_copy(src, dst, out_sem.at[len(keep)])
        keep.append(copy)
        copy.start()

    for j in range(rows):
        store(tok.at[j], o_tokens.at[j])
    for src, dst in ((first, o_first), (q_s, o_q), (k_s, o_k), (v_s, o_v), (mixed.at[p.core], o_mixed), (lse, o_lse),
                     (xhat, o_xhat), (inv, o_inv), (table, o_table), (top, o_top), (wj.at[0], o_joined.at[0]), (wj.at[1], o_joined.at[1]), (wm.at[p.core], o_mixer)):
        store(src, dst)
    for j in range(rows):
        store(gains.at[j], o_small.at[:, pl.ds(j * width, width)])
    store(meta, o_small.at[:, pl.ds(D, LEN)])

    service([g2.pass_on, u2.pass_on, s2.pass_on], [g2.take_first, u2.take_first, g1.take_others])
    early = [([], [u1.take_others]), ([], [g2.take_others, u2.take_others]), ([], [])]
    middle = [([], [s1.take_others, s2.take_first]), ([], [s2.take_others]), ([], [])]

    def first_block(row, start, size):
        return g_expand[0].at[pl.ds(start, size), pl.ds(pl.multiple_of(row * width, width), width)]

    plane = Grad(p, first_block, 2 * chunks[0], (*sum_bufs, []), sum_sem, None, 0, share=1 / 2)
    then_early = [[], [], [plane.sum_x]]
    at = 0
    for i, lanes in enumerate(chunks):
        for weight in groups[i]:
            weight.finish()

        @pl.loop(0, LEN // BLOCK)
        def _(t):
            cut = block_rows(t)
            part, grad = second[cut, :], top[cut, :]
            gate = dot(part, wg[i][...], NT)
            up = dot(part, wu[i][...], NT)
            hidden_grad = dot(grad, ws[i][...], NT).astype(jnp.bfloat16).astype(jnp.float32)
            phi, density = gelu_parts(gate)
            act = gate * phi
            hidden = (act * up).astype(jnp.bfloat16)
            d_gate = (hidden_grad * up * (phi + gate * density)).astype(jnp.bfloat16)
            d_up = (hidden_grad * act).astype(jnp.bfloat16)
            hid[cut, :lanes] = hidden
            dgate[cut, :lanes] = d_gate
            dup[cut, :lanes] = d_up
            value = shrunk[cut, :] + dot(hidden, ws[i][...])
            grad_sum = back[cut, :] + dot(d_gate, wg[i][...]) + dot(d_up, wu[i][...])
            if i + 1 < n_chunks:
                shrunk[cut, :] = value
                back[cut, :] = grad_sum
            else:
                back_low[cut, :] = grad_sum.astype(jnp.bfloat16)
                left, right = value[:, : D // 2], value[:, D // 2 :]
                shrunk[cut, : D // 2] = jnp.where(p.core == 0, left, right)
                other_half[cut, :] = jnp.where(p.core == 0, right, left).astype(jnp.bfloat16)

            @pl.when(t == LEN // BLOCK // 2 - 1)
            def _():
                service(*early[i])
                for action in then_early[i]:
                    action()


        service(*middle[i])
        if i == 1:
            plane.sum_y()
        if i + 1 == n_chunks:
            store(back_low, o_back)
            store(shrunk.at[:, pl.ds(0, D // 2)], o_own)
            store(other_half, o_other)
        for n, (left, right) in enumerate(((dgate, second), (dup, second), (hid, top))):
            target = g_shrink[i] if n == 2 else g_expand[i]
            for start in range(0, lanes, BLOCK):
                size = min(BLOCK, lanes - start)
                spot = start if n == 2 else n * lanes + start
                target[spot : spot + size, :] = dot(left[:, start : start + size], right[...], TN).astype(jnp.bfloat16)
            if n == 1 and i == 0:
                plane.begin_y()
                plane.begin_x()

        if i:
            store(g_expand[i], o_expand.at[pl.ds(2 * at, 2 * lanes), :])
        store(g_shrink[i], o_shrink.at[pl.ds(at, lanes), :])
        at += lanes

    plane.plane_sum()
    store(plane.acc, o_sum)

    plane.drain_plane()
    drain_seq(tok, tok_send, tok_recv, swap_send.at[0])
    drain_seq(cot, cot_send, cot_recv, swap_send.at[1])
    for step in range(1, rows):
        remote(gains_ref, gains.at[p.row], gain_send.at[step], gain_recv.at[p.row], p.sibling()).wait_send()

    @pl.when(sends_meta)
    def _():
        for t in range(1, seqs):
            remote(meta_src.at[t], meta, meta_send.at[t], meta_recv, p.sibling()).wait_send()

        @pl.when(jnp.logical_not(is_here))
        def _():
            remote(meta_src.at[0], meta, meta_send.at[0], meta_recv, p.sibling()).wait_send()

    for pair in range(pairs):
        piece = mixed.at[p.core, :, pair * PAIR : (pair + 1) * PAIR]
        remote(piece, piece, mixed_send.at[pair], mixed_recv.at[pair], p.sibling()).wait_send()
    piece = wm.at[p.core]
    remote(piece, piece, mix_send, mix_recv, p.sibling()).wait_send()
    for weight in joined + [mixer] + sum(groups, []):
        weight.drain()
    for copy in keep:
        copy.wait()


def forward(tokens, cot, lengths, first_gain, second_gain, joined, mixer, expand, shrink, chunks):
    rows = lax.axis_size("row")
    seqs = rows // CORES
    width = tokens.shape[1]
    wide = mixer.shape[0]
    pairs = wide // PAIR
    blocks = LEN // BLOCK
    n_chunks = len(chunks)
    hidden_here = sum(chunks)
    planes = lax.axis_size("dp") // CORES
    weights = 3 + 3 * n_chunks
    bf16, f32 = jnp.bfloat16, jnp.float32
    freq = np.tile((rope_base ** (-2.0 * np.arange(HD // 2) / HD)).astype(np.float32), (8, 4))
    outs = [
        ((rows, LEN, width), bf16), ((LEN, D), bf16), ((LEN, wide), bf16), ((LEN, wide), bf16), ((LEN, wide), bf16),
        ((LEN, wide), bf16), ((pairs, 2, LEN), f32), ((LEN, D), bf16), ((LEN, PAIR), f32), ((LEN, D), bf16),
        ((LEN, D // 2), f32), ((LEN, D // 2), bf16), ((LEN, D), bf16),
        ((2 * hidden_here, D), bf16), ((hidden_here, D), bf16), ((2, 3, D, wide // 2), bf16), ((wide, D), bf16),
        ((8, D + LEN), f32), ((2, LEN, PAIR), f32), ((grad_rows(2 * chunks[0], planes), width), bf16),
    ]
    V, dma = pltpu.VMEM, pltpu.SemaphoreType.DMA
    widest = max(chunks)
    scratch = [
        V((rows, LEN, width), bf16), V((rows, LEN, width), bf16), V((seqs, 8, LEN), f32), V((8, LEN), f32),
        V((8, width), f32), V((rows, 8, width), f32), V((2, LEN, PAIR), f32), V((LEN, D), bf16), V((2, 3, D, wide // 2), bf16), V((CORES, wide, D), bf16),
        [V((lanes, D), bf16) for lanes in chunks], [V((lanes, D), bf16) for lanes in chunks], [V((lanes, D), bf16) for lanes in chunks],
        V((LEN, wide), bf16), V((LEN, wide), bf16), V((LEN, wide), bf16), V((PAIR, LEN), bf16), V((PAIR, LEN), f32),
        V((pairs, 2, LEN), f32), V((CORES, LEN, wide), bf16), V((LEN, D), bf16), V((LEN, PAIR), f32), V((LEN, D), bf16),
        V((LEN, D), bf16), V((LEN, D), f32), V((LEN, D), f32), V((LEN, D), bf16), V((LEN, D // 2), bf16), V((LEN, widest), bf16), V((LEN, widest), bf16), V((LEN, widest), bf16),
        [V((2 * lanes, D), bf16) for lanes in chunks],
        [V((lanes, D), bf16) for lanes in chunks],
        plane_bufs(2 * chunks[0], width, rows, planes), dma((1, 14, rows)),
        dma((seqs, blocks)), dma((rows, blocks)), dma((seqs, blocks)), dma((rows, blocks)), dma((2, seqs, blocks)), dma((seqs,)), dma,
        dma((rows,)), dma((rows,)),
        dma((weights, rows)), dma((weights, rows)), dma((weights, rows)), dma((weights, rows)), dma((weights, rows)),
        dma((weights,)), dma, dma, dma((pairs,)), dma((pairs,)), dma((2 * rows + 17 + 3 * n_chunks,)),
    ]
    anywhere = pl.BlockSpec(memory_space=pl.ANY)
    in_specs = [anywhere] * 10
    in_specs[2] = pl.BlockSpec(memory_space=pltpu.SMEM)
    in_specs[3:6] = [pl.BlockSpec(memory_space=pltpu.VMEM)] * 3
    return pl.pallas_call(
        functools.partial(forward_kernel, chunks),
        in_specs=in_specs,
        out_specs=[anywhere] * len(outs),
        out_shape=[jax.ShapeDtypeStruct(*o) for o in outs],
        scratch_shapes=scratch,
        compiler_params=pltpu.CompilerParams(
            collective_id=0, has_side_effects=True, vmem_limit_bytes=62 * 1024 * 1024
        ),
        name="layer_forward",
    )(tokens, cot, lengths, first_gain[None, :], second_gain[None, :], freq, joined, mixer, expand, shrink)


def backward_kernel(
    chunks,
    tokens_ref, first_ref, q_ref, k_ref, v_ref, mixed_ref, lse_ref, xhat_ref, inv_ref, top_ref, own_ref, other_ref, back_ref,
    expand_ref, shrink_ref, joined_ref, mixer_ref, small_ref, table_ref, sum_ref,
    o_block, o_input, o_joined, o_mixer, o_expand, o_shrink, o_gains,
    q_s, k_s, v_s, mixed, xa, xb, xc, wj, wm, lse, inv, small, table, other, keep_grad, middle_low, mixed_grad, g_mixer, g_joined,
    dk, dv, dq_t, k_t, delta, own_half, block_half, gain_sum, gain_y, gain_x, gain_z, stage_lane, grad_scratch,
    load_sem, stage_sem, sum_sem, grad_sem, credit, swap_credit, back_send, back_recv, other_send, other_recv, first_send, first_recv,
    out_send, out_recv, in_send, in_recv, gain_send, gain_recv, out_sem,
):
    p = Place()
    rows, seqs, planes = p.rows, p.seqs, p.planes
    width = D // rows
    wide = q_s.shape[1]
    pairs = wide // PAIR
    levels = (planes - 1).bit_length()
    half = wide // 2

    def by_row(ref):
        return lambda j, start, size: ref.at[pl.ds(pl.multiple_of(j * width + start, 16), size), :]

    def by_lane(ref, at=0):
        return lambda j, start, size: ref.at[pl.ds(at + start, size), pl.ds(pl.multiple_of(j * width, width), width)]

    grads, places, at = {}, {}, 0
    stage = (stage_lane, stage_sem)

    def add_grad(name, block, count, stage, stores, summed=None):
        i = len(grads)
        grads[name] = Grad(p, block, count, grad_scratch[i], grad_sem, credit, i, stage, summed)
        places[name] = stores

    for i, count in enumerate(chunks):
        add_grad(("E", i), by_lane(expand_ref, 2 * at), 2 * count, stage,
                 [(j * count, count, 0, width, o_expand.at[j, pl.ds(at, count), :]) for j in range(2)],
                 None if i else pltpu.make_async_copy(sum_ref, grad_scratch[0][2], sum_sem))
        add_grad(("S", i), by_lane(shrink_ref, at), count, stage, [(0, count, 0, width, o_shrink.at[pl.ds(at, count), :])])
        at += count
    for h in range(2):
        add_grad(("J", h), by_row(g_joined.at[h]), width, None,
                 [(0, width, j * half, half, o_joined.at[j, :, pl.ds(h * half, half)]) for j in range(3)])
    add_grad(("M", 0), by_lane(g_mixer), wide, None, [(0, wide, 0, width, o_mixer)])

    loads = {}

    def load(name, src, dst):
        copy = pltpu.make_async_copy(src, dst, load_sem.at[len(loads)])
        copy.start()
        loads[name] = copy

    load("small", small_ref, small)
    load("back", back_ref, xc)
    load("xhat", xhat_ref, xa)
    load("inv", inv_ref, inv)
    load("top", top_ref, xb)
    load("mixer", mixer_ref, wm)
    load("mixed", mixed_ref, mixed)
    load("q", q_ref, q_s)
    load("k", k_ref, k_s)
    load("v", v_ref, v_s)
    load("lse", lse_ref, lse)
    load("table", table_ref, table)
    load("joined", joined_ref, wj)
    load("own", own_ref, own_half)
    pl.when(p.matched)(grads["E", 0].summed.start)
    p.barrier([p.across()] + [p.mate(level) for level in range(levels)])

    def swap_block(i, src, dst, send, recv):
        cut = pl.ds(i * BLOCK, BLOCK)
        return remote(src.at[cut, :], dst.at[cut, :], send.at[i], recv.at[i], p.sibling())

    blocks_n = LEN // BLOCK
    for i in range(blocks_n):
        swap_block(i, back_ref, other, back_send, back_recv).start()

    stores = []

    def run(*todo):
        for step in todo:
            if callable(step):
                step()
                continue
            action, kind, i = step
            grad = grads[kind, i]
            if action == "store":
                spots = [spot + (out_sem.at[len(stores) + n],) for n, spot in enumerate(places[kind, i])]
                stores.extend(grad.store(spots))
            elif action == "begin":
                grad.begin_y()
                grad.begin_x()
            else:
                getattr(grad, action)()

    run(("begin_x", "E", 1), ("begin_y", "E", 2), ("begin_x", "S", 0), ("begin_y", "S", 2), ("begin_y", "E", 1))
    other_copy = remote(other_ref, block_half, other_send, other_recv, p.sibling())
    other_copy.start()

    for name in ("small", "back", "xhat", "inv", "top", "mixer", "mixed"):
        loads[name].wait()
    gain_a, gain_b = small[0:1, :D], small[1:2, :D]
    gain_sum[...] = jnp.zeros_like(gain_sum)
    for grad in grads.values():
        if grad.full != grad.m and grad.summed is None:
            grad.acc[grad.m :, :] = jnp.zeros((grad.full - grad.m, grad.acc.shape[1]), jnp.bfloat16)

    def norm_back(grad, normed, scale, gain):
        scaled = grad * gain
        mean_a = jnp.mean(scaled, axis=-1, keepdims=True)
        mean_b = jnp.mean(scaled * normed, axis=-1, keepdims=True)
        return scale * (scaled - mean_a - normed * mean_b)

    def own_of(value):
        return jnp.where(p.core == 0, value[:, : D // 2], value[:, D // 2 :])

    def second_norm(i):
        cut = slice(i * BLOCK, (i + 1) * BLOCK)
        swap_block(i, back_ref, other, back_send, back_recv).wait_recv()
        grad = xc[cut, :].astype(jnp.float32) + other[cut, :].astype(jnp.float32)
        normed = xa[cut, :].astype(jnp.float32)
        gain_sum[1:2, :] += jnp.sum(grad * normed, axis=0, keepdims=True)
        value = xb[cut, :].astype(jnp.float32) + norm_back(grad, normed, inv[cut, 0:1], gain_b)
        keep_grad[cut, :] = own_of(value)
        value = value.astype(jnp.bfloat16)
        middle_low[cut, :] = value
        mixed_grad[cut, :] = dot(value, wm[...], NT).astype(jnp.bfloat16)
    second_norm(0)
    second_norm(1)
    run(("begin_y", "S", 0))
    second_norm(2)
    second_norm(3)
    pl.semaphore_signal(swap_credit, inc=1, device_id=p.sibling(), device_id_type=MESH_ID)
    run(("begin_x", "S", 2))
    @pl.loop(0, D // BLOCK)
    def _(d):
        cut = block_rows(d)
        g_mixer[:, cut] = dot(mixed[...], middle_low[:, cut], TN).astype(jnp.bfloat16)

    load("first", first_ref, xa)
    for j in range(rows):
        load(f"tokens{j}", tokens_ref.at[j], xb.at[:, pl.ds(j * width, width)])

    def leave(src, dst, send, recv):
        core, seq = p.row // seqs, lax.rem(p.row, seqs)
        copies = []
        for u in range(seqs):
            row = p.core * seqs + u
            is_self = jnp.logical_and(core == p.core, row == p.row)
            piece = src.at[:, pl.ds(u * width, width)]
            copies.append((is_self, piece, dst(seq), send.at[u], recv.at[seq], p.at(core=core, row=row)))
        return copies

    def leave_start(copies):
        for is_self, piece, place, send, recv, target in copies:
            @pl.when(is_self)
            def _():
                pltpu.make_async_copy(piece, place, recv).start()

            @pl.when(jnp.logical_not(is_self))
            def _():
                remote(piece, place, send, recv, target).start()

    def leave_wait(copies, dst, recv):
        for s in range(seqs):
            pltpu.make_async_copy(dst(s), dst(s), recv.at[s]).wait()
        for is_self, piece, place, send, recv_sem, target in copies:
            @pl.when(jnp.logical_not(is_self))
            def _():
                remote(piece, place, send, recv_sem, target).wait_send()

    out_at = lambda s: o_block.at[pl.ds(pl.multiple_of(s * LEN, LEN), LEN), :]
    in_at = lambda s: o_input.at[pl.ds(pl.multiple_of(s * LEN, LEN), LEN), :]
    out_copies = leave(block_half, out_at, out_send, out_recv)
    in_copies = leave(mixed_grad, in_at, in_send, in_recv)

    def block_output():
        loads["own"].wait()
        other_copy.wait()
        add_rows(LEN, block_half, own_half, block_half)
        leave_start(out_copies)

    for name in ("q", "k", "v", "lse", "table"):
        loads[name].wait()
    columns = small[:, D:].T
    segment_col = columns[:, 1:2]

    def attention_start(pair):
        cols = slice(pair * PAIR, (pair + 1) * PAIR)
        product = mixed[:, cols].astype(jnp.float32) * mixed_grad[:, cols].astype(jnp.float32)
        chooser = lax.broadcasted_iota(jnp.int32, (8, PAIR), 0) == lanes_of((8, PAIR)) // HD
        delta[...] = dot(chooser.astype(jnp.float32), product, NT, precision=lax.Precision.HIGHEST)
        k_t[...] = k_s[:, cols].astype(jnp.float32).T.astype(jnp.bfloat16)
        dk[...] = jnp.zeros_like(dk)
        dv[...] = jnp.zeros_like(dv)

    def attention_head(pair, head):
        cols = slice(pair * PAIR, (pair + 1) * PAIR)
        keys, values = k_s[:, cols], v_s[:, cols]
        lanes = slice(head * HD, (head + 1) * HD)
        for i in range(LEN // BLOCK):
            cut = slice(i * BLOCK, (i + 1) * BLOCK)
            q_part, g_part = only_head(q_s[cut, cols], head), only_head(mixed_grad[cut, cols], head)
            scores = dot(keys, q_part, NT)
            probs = jnp.exp2(scores * TO_EXP2 - lse[pair, head : head + 1, cut])
            probs = jnp.where(segment_col == small[1:2, D + i * BLOCK : D + (i + 1) * BLOCK], probs, 0.0)
            probs_grad = dot(values, g_part, NT)
            scores_grad = (probs * (probs_grad - delta[head : head + 1, cut])).astype(jnp.bfloat16)
            dv[...] += dot(probs.astype(jnp.bfloat16), g_part)
            dk[...] += dot(scores_grad, q_part)
            dq_t[lanes, cut] = dot(k_t[lanes, :], scores_grad)

    def attention_end(pair):
        cols = slice(pair * PAIR, (pair + 1) * PAIR)
        cosine, sine = table[0], table[1]
        scale = 1.0 / math.sqrt(HD)
        dqs = dq_t[...].T * scale
        q_s[:, cols] = (dqs * cosine - swap_halves(dqs) * sine).astype(jnp.bfloat16)
        dks = dk[...] * scale
        k_s[:, cols] = (dks * cosine - swap_halves(dks) * sine).astype(jnp.bfloat16)
        v_s[:, cols] = dv[...].astype(jnp.bfloat16)

    def joined_weight_grad(h):
        @pl.loop(0, D // BLOCK)
        def _(d):
            cut = block_rows(d)
            part = xa[:, cut]
            for j, back in enumerate((q_s, k_s, v_s)):
                g_joined[h, cut, j * half : (j + 1) * half] = dot(
                    part, back[:, h * half : (h + 1) * half], TN
                ).astype(jnp.bfloat16)

    run(("sum_both", "E", 0))
    attention_start(0)
    attention_head(0, 0)
    attention_head(0, 1)
    attention_end(0)
    attention_start(1)
    attention_head(1, 0)
    attention_head(1, 1)
    attention_end(1)
    run(("z0", "E", 0), ("sum_x", "E", 1), ("sum_y", "E", 1))
    loads["first"].wait()
    joined_weight_grad(0)
    attention_start(2)
    attention_head(2, 0)
    run(
        ("begin_y", "M", 0), ("begin_x", "J", 0), ("sum_y", "S", 2), ("sum_x", "S", 2), ("begin_y", "J", 0),
        ("z1", "E", 0), ("sum_x", "S", 0), ("sum_both", "E", 1),
    )
    attention_head(2, 1)
    attention_end(2)
    attention_start(3)
    attention_head(3, 0)
    attention_head(3, 1)
    attention_end(3)
    run(
        ("sum_both", "S", 2), ("sum_x", "J", 0), ("z0", "E", 1), ("sum_y", "S", 0), ("z0", "S", 2),
        ("sum_both", "S", 0), ("g1", "E", 0), ("begin_x", "E", 2), ("sum_x", "E", 2), ("sum_y", "J", 0),
        ("sum_y", "E", 2), ("z1", "E", 1), ("sum_both", "J", 0), ("sum_both", "E", 2),
    )
    joined_weight_grad(1)
    run(
        ("begin_x", "J", 1), ("begin_y", "J", 1), ("z1", "S", 2), ("z0", "S", 0), ("begin_y", "S", 1),
        ("z0", "J", 0), ("g1", "E", 1), ("sum_x", "J", 1), ("sum_y", "J", 1), ("z1", "S", 0), ("begin_x", "M", 0),
    )
    loads["joined"].wait()
    pl.semaphore_wait(swap_credit, 1)

    def first_back(i):
        cut = slice(i * BLOCK, (i + 1) * BLOCK)
        value = jnp.zeros((BLOCK, D), jnp.float32)
        for h in range(2):
            for j, part in enumerate((q_s, k_s, v_s)):
                value = value + dot(part[cut, h * half : (h + 1) * half], wj[h, j], NT)
        xc[cut, :] = value.astype(jnp.bfloat16)
        swap_block(i, xc, other, first_send, first_recv).start()

    first_back(0)
    first_back(1)

    run(
        ("g0", "E", 0), ("g1", "S", 2), ("z0", "E", 2), ("sum_both", "J", 1), ("z1", "J", 0), ("g1", "S", 0),
        ("begin_x", "S", 1), ("sum_x", "M", 0), ("sum_y", "M", 0), ("sum_y", "S", 1), ("z1", "E", 2), ("g1", "J", 0),
        ("g0", "S", 2), ("sum_x", "S", 1), ("z0", "J", 1), ("sum_both", "M", 0),
    )
    first_back(2)
    first_back(3)
    run(("store", "E", 0), ("sum_both", "S", 1), ("g0", "E", 1), ("g1", "E", 2), ("z1", "J", 1))
    for j in range(rows):
        loads[f"tokens{j}"].wait()
    for i in range(blocks_n):
        cut = slice(i * BLOCK, (i + 1) * BLOCK)
        swap_block(i, xc, other, first_send, first_recv).wait_recv()
        grad = xc[cut, :].astype(jnp.float32) + other[cut, :].astype(jnp.float32)
        values = xb[cut, :].astype(jnp.float32)
        values = values - jnp.mean(values, axis=-1, keepdims=True)
        scale = lax.rsqrt(jnp.mean(values * values, axis=-1, keepdims=True) + norm_eps)
        normed = values * scale
        gain_sum[0:1, :] += jnp.sum(grad * normed, axis=0, keepdims=True)
        total = keep_grad[cut, :] + own_of(norm_back(grad, normed, scale, gain_a))
        mixed_grad[cut, :] = total.astype(jnp.bfloat16)

    def gain_copies():
        return [
            remote(gain_sum.at[:, pl.ds(pl.multiple_of(p.row_after(s) * width, width), width)], gain_y.at[s],
                   gain_send.at[s], gain_recv.at[s], p.at(row=p.row_after(s)))
            for s in range(1, rows)
        ]

    gain_across = remote(gain_x.at[0], gain_x.at[1], gain_send.at[rows], gain_recv.at[rows], p.across())
    gain_total = gain_z.at[2 * levels]
    gain_back = remote(gain_total, gain_total, gain_send.at[rows + 1 + levels], gain_recv.at[rows + 1 + levels], p.sibling())

    def gain_plane(level):
        return remote(gain_z.at[2 * level], gain_z.at[2 * level + 1], gain_send.at[rows + 1 + level],
                      gain_recv.at[rows + 1 + level], p.mate(level))

    def gains_y():
        for s in range(1, rows):
            remote(gain_y.at[s], gain_y.at[s], gain_send.at[s], gain_recv.at[s], p.sibling()).wait_recv()
        total = gain_sum[:, pl.ds(pl.multiple_of(p.row * width, width), width)]
        for s in range(1, rows):
            total = total + gain_y[s]
        gain_x[0] = total
        pl.when(p.matched)(gain_across.start)

    def gains_x():
        @pl.when(jnp.logical_not(p.matched))
        def _():
            gain_across.wait_recv()
            gain_z[0] = gain_x[0] + gain_x[1]
            gain_plane(0).start()

    def gains_z():
        @pl.when(jnp.logical_not(p.matched))
        def _():
            for level in range(levels):
                gain_plane(level).wait()
                gain_z[2 * level + 2] = gain_z[2 * level] + gain_z[2 * level + 1]
                if level + 1 < levels:
                    gain_plane(level + 1).start()
            gain_back.start()
            gain_back.wait_send()

    def gains_end():
        @pl.when(p.matched)
        def _():
            gain_back.wait_recv()
            gain_across.wait_send()

    for copy in gain_copies():
        copy.start()
    leave_start(in_copies)

    run(
        ("z0", "S", 1), ("g1", "J", 1), ("z0", "M", 0), ("g0", "J", 1), gains_y, ("store", "S", 2), ("z1", "S", 1),
        ("store", "E", 1), ("z1", "M", 0), ("g1", "S", 1), gains_x, ("g0", "E", 2), block_output, ("g0", "S", 1),
        ("g0", "S", 0), ("store", "J", 1), ("g0", "J", 0), gains_z, ("store", "S", 0), ("store", "J", 0),
        ("g1", "M", 0), ("store", "E", 2), ("store", "S", 1), ("g0", "M", 0), ("store", "M", 0),
    )
    gains_end()
    gains_out = pltpu.make_async_copy(gain_z.at[2 * levels], o_gains, out_sem.at[len(stores)])
    gains_out.start()

    leave_wait(out_copies, out_at, out_recv)
    leave_wait(in_copies, in_at, in_recv)
    for i in range(blocks_n):
        swap_block(i, back_ref, other, back_send, back_recv).wait_send()
        swap_block(i, xc, other, first_send, first_recv).wait_send()
    for copy in gain_copies():
        copy.wait_send()
    for grad in grads.values():
        grad.drain()
    for copy in stores:
        copy.wait()
    gains_out.wait()


def backward(saved, chunks):
    (tokens, first, queries, keys, values, mixed, lse, xhat, inv, top, own, other, back, expand, shrink, joined, mixer,
     small, table, plane_sum) = saved
    rows = lax.axis_size("row")
    planes = lax.axis_size("dp") // CORES
    seqs = rows // CORES
    width = D // rows
    wide = queries.shape[1]
    pairs = wide // PAIR
    hidden_here = sum(chunks)
    widest = 2 * max(chunks)
    levels = (planes - 1).bit_length()
    bf16, f32 = jnp.bfloat16, jnp.float32
    V, dma = pltpu.VMEM, pltpu.SemaphoreType.DMA
    outs = [
        ((seqs * LEN, width), bf16), ((seqs * LEN, width), bf16), ((3, width, wide), bf16), ((wide, width), bf16),
        ((2, hidden_here, width), bf16), ((hidden_here, width), bf16), ((8, width), f32),
    ]
    grad_shapes = []
    for lanes in chunks:
        grad_shapes += [(2 * lanes, width), (lanes, width)]
    grad_shapes += [(width, 3 * wide // 2)] * 2 + [(wide, width)]
    count = len(grad_shapes)
    scratch = [
        V((LEN, wide), bf16), V((LEN, wide), bf16), V((LEN, wide), bf16), V((LEN, wide), bf16),
        V((LEN, D), bf16), V((LEN, D), bf16), V((LEN, D), bf16), V((2, 3, D, wide // 2), bf16), V((wide, D), bf16),
        V((pairs, 2, LEN), f32), V((LEN, PAIR), f32), V((8, D + LEN), f32), V((2, LEN, PAIR), f32), V((LEN, D), bf16),
        V((LEN, D // 2), f32), V((LEN, D), bf16), V((LEN, wide), bf16), V((wide, D), bf16), V((2, D, 3 * wide // 2), bf16),
        V((LEN, PAIR), f32), V((LEN, PAIR), f32), V((PAIR, LEN), f32), V((PAIR, LEN), bf16), V((8, LEN), f32),
        V((LEN, D // 2), f32), V((LEN, D // 2), bf16),
        V((8, D), f32), V((rows, 8, width), f32), V((2, 8, width), f32), V((2 * levels + 1, 8, width), f32),
        V((2, widest - first_share(widest), width), bf16),
        [grad_bufs(*shape, rows, planes, i == 0) for i, shape in enumerate(grad_shapes)],
        dma((15 + rows,)), dma((2,)), dma, dma((count, 14, max(rows, levels))), pltpu.SemaphoreType.REGULAR((count, levels)),
        pltpu.SemaphoreType.REGULAR,
        dma((4,)), dma((4,)), dma, dma, dma((4,)), dma((4,)),
        dma((seqs,)), dma((seqs,)), dma((seqs,)), dma((seqs,)), dma((rows + 2 + levels,)), dma((rows + 2 + levels,)),
        dma((3 * len(chunks) + 8,)),
    ]
    anywhere = pl.BlockSpec(memory_space=pl.ANY)
    return pl.pallas_call(
        functools.partial(backward_kernel, chunks),
        in_specs=[anywhere] * len(saved),
        out_specs=[anywhere] * len(outs),
        out_shape=[jax.ShapeDtypeStruct(*o) for o in outs],
        scratch_shapes=scratch,
        compiler_params=pltpu.CompilerParams(
            collective_id=1, has_side_effects=True, vmem_limit_bytes=62 * 1024 * 1024
        ),
        name="layer_backward",
    )(*saved)


def finish_kernel(*refs):
    count = len(refs) // 2
    gains_ref, firsts, seconds = refs[count - 1], *refs[-2:]
    for src, dst in zip(refs[: count - 1], refs[count:]):
        dst[...] = src[...].astype(dst.dtype)
    firsts[...] = gains_ref[0:1, :]
    seconds[...] = gains_ref[1:2, :]


def finish(block, *rest):
    steps = 4
    *grads, gains = rest
    arrays = [x.reshape(-1, x.shape[-1]) for x in (block, *grads)]

    def spec(x):
        parts = next(n for n in (steps, steps // 2, 1) if x.shape[0] % (16 * n) == 0)
        return pl.BlockSpec((x.shape[0] // parts, x.shape[1]), lambda i: (i * parts // steps, 0))

    whole = lambda rows: pl.BlockSpec((rows, gains.shape[1]), lambda i: (0, 0))
    shape = jax.ShapeDtypeStruct
    outs = pl.pallas_call(
        finish_kernel,
        grid=(steps,),
        in_specs=[spec(x) for x in arrays] + [whole(8)],
        out_specs=[spec(x) for x in arrays] + [whole(1)] * 2,
        out_shape=[shape(arrays[0].shape, block.dtype)]
        + [shape(x.shape, jnp.float32) for x in arrays[1:]]
        + [shape((1, gains.shape[1]), jnp.float32)] * 2,
        compiler_params=pltpu.CompilerParams(vmem_limit_bytes=60 * 1024 * 1024),
        name="layer_finish",
    )(*arrays, gains)
    return [out.reshape(x.shape) for out, x in zip(outs, (block, *grads))] + [outs[-2][0], outs[-1][0]]


def shards(
    tokens_in, lengths, first_gain, joined_weight, mixer_weight, second_gain, expand_weight, shrink_weight, cotangent
):
    rows, cols = lax.axis_size("row"), lax.axis_size("col")
    hidden_here = shrink_weight.shape[0]
    assert tokens_in.shape[0] * CORES == LEN * rows and cols == CORES
    chunks = (512, 512, hidden_here - 1024)
    joined_here = joined_weight.transpose(1, 0, 2)
    expand_here = expand_weight.transpose(1, 2, 0)
    saved = forward(
        tokens_in, cotangent, lengths, first_gain, second_gain, joined_here, mixer_weight, expand_here, shrink_weight, chunks
    )
    block_output, input_grad, joined_grad, mixer_grad, expand_grad, shrink_grad, *gains = finish(*backward(saved, chunks))
    return (
        block_output,
        input_grad,
        joined_grad.transpose(1, 0, 2),
        mixer_grad,
        expand_grad.transpose(2, 0, 1),
        shrink_grad,
        gains[0],
        gains[1],
    )


def solution(mesh):
    placed = (
        P(("dp", "col"), "row"),
        P("dp", None),
        P("row"),
        P("row", None, "col"),
        P("col", "row"),
        P("row"),
        P("row", None, "col"),
        P("col", "row"),
        P(("dp", "col"), "row"),
    )
    return jax.shard_map(
        shards,
        mesh=mesh,
        in_specs=placed,
        out_specs=(
            P(("dp", "col"), "row"),
            P(("dp", "col"), "row"),
            P("row", None, "col"),
            P("col", "row"),
            P("row", None, "col"),
            P("col", "row"),
            P("row"),
            P("row"),
        ),
        check_vma=False,
    )
```

```python
import functools
import math

import jax
import jax.numpy as jnp
import numpy as np
from jax import lax
from jax.experimental import pallas as pl
from jax.experimental.pallas import tpu as pltpu
from jax.sharding import PartitionSpec as P

D = 1024
HEADS = 16
HD = 64
FF = 2624
LEN = 1024
DOCS = 6
MOST = 800
CORES = 2

rope_base = 160000.0
norm_eps = 1e-05
masked_value = -1000000000.0

PAIR = 2 * HD
WIDE = 256
SOLID = MOST // WIDE * WIDE
REST = LEN - MOST
TO_EXP2 = math.log2(math.e) / math.sqrt(HD)

NT = (((1,), (1,)), ((), ()))
TN = (((0,), (0,)), ((), ()))
MESH_AXES = ("dp", "row", "col")


def lanes_of(shape):
    return lax.broadcasted_iota(jnp.int32, shape, len(shape) - 1)


def swap_halves(u):
    low_half = lanes_of(u.shape) % HD < HD // 2
    return jnp.where(low_half, pltpu.roll(u, u.shape[1] - HD // 2, 1), pltpu.roll(u, HD // 2, 1))


def dot(left, right, dims=(((1,), (0,)), ((), ())), **more):
    return lax.dot_general(left, right, dims, preferred_element_type=jnp.float32, **more)


def only_head(values, head):
    return jnp.where(lanes_of(values.shape) // HD == head, values, jnp.zeros_like(values))


MESH_ID = pl.DeviceIdType.MESH
BLOCK = 256
HALF_ROWS = LEN // 2


class Place:
    def __init__(self):
        self.rows, self.cols = lax.axis_size("row"), lax.axis_size("col")
        self.planes = lax.axis_size("dp") // CORES
        dp = lax.axis_index("dp")
        self.z, self.core = dp // CORES, dp % CORES
        self.row, self.col = lax.axis_index("row"), lax.axis_index("col")
        self.matched = self.core == self.col
        self.parity = self.z % 2
        self.inner = self.parity != (self.z // 2) % 2
        self.seqs = self.rows // CORES

    def at(self, z=None, core=None, row=None, col=None):
        z = self.z if z is None else z
        core = self.core if core is None else core
        return (z * CORES + core, self.row if row is None else row, self.col if col is None else col)

    def sibling(self):
        return self.at(core=1 - self.core)

    def across(self):
        return self.at(col=1 - self.col)

    def pair(self):
        return self.at(z=self.z + 1 - 2 * self.parity)

    def row_after(self, step):
        return lax.rem(self.row + step, self.rows)

    def row_before(self, step):
        return lax.rem(self.row + self.rows - step, self.rows)

    def group_bit(self, level):
        return lax.rem(self.z // (1 << level), 2)

    def mate(self, level):
        if level == 0:
            return self.pair()
        group = self.z // 2
        other = group + (1 << (level - 1)) * (1 - 2 * self.group_bit(level))
        shift = lax.rem(group, 2) + self.parity
        return self.at(z=2 * other + lax.rem(shift + lax.rem(other, 2), 2))

    def barrier(self, partners):
        sem = pltpu.get_barrier_semaphore()
        count = CORES * self.rows
        partners = list(partners)
        for step in range(1, count):
            flat = lax.rem(self.core * self.rows + self.row + step, count)
            partners.append(self.at(core=flat // self.rows, row=lax.rem(flat, self.rows)))
        for partner in partners:
            pl.semaphore_signal(sem, inc=1, device_id=partner, device_id_type=MESH_ID)
        pl.semaphore_wait(sem, len(partners))


def remote(src, dst, send, recv, target):
    return pltpu.make_async_remote_copy(
        src_ref=src, dst_ref=dst, send_sem=send, recv_sem=recv, device_id=target, device_id_type=MESH_ID
    )


def shares(count, part):
    one = int(count * part) // 16 * 16
    return count - 2 * one, one


class Weight:
    def __init__(self, place, source, slot, count, sems, index, part):
        self.place, self.source, self.slot = place, source, slot
        self.both, self.one = shares(count, part)
        self.sems = sems
        self.index = index
        self.local = sems[5].at[index]

    def sem(self, kind, row):
        return self.sems[kind].at[self.index, row]

    def plane_part(self):
        return self.place.parity * self.one, self.one + self.both

    def pair_part(self):
        return self.place.parity * (self.one + self.both), self.one

    def other_part(self):
        return (1 - self.place.parity) * (self.one + self.both), self.one

    def own_y(self):
        p = self.place
        start, size = self.plane_part()
        for step in range(1, p.rows):
            remote(
                self.source(start, size),
                self.slot(p.row, start, size),
                self.sem(0, step),
                self.sem(3, p.row),
                p.at(row=p.row_after(step)),
            ).start()

    def own_x(self):
        p = self.place
        start, size = self.plane_part()
        remote(
            self.source(start, size), self.slot(p.row, start, size), self.sem(1, 0), self.sem(3, p.row), p.across()
        ).start()
        pltpu.make_async_copy(
            self.source(0, 2 * self.one + self.both), self.slot(p.row, 0, 2 * self.one + self.both), self.local
        ).start()

    def pass_on(self):
        p = self.place
        for step in range(1, p.rows):
            row = p.row_before(step)
            self.wait_plane(row)
            self.send_across(row, step).start()
            self.send_pair(row, step).start()

    def take_first(self):
        self.wait_plane(self.place.row)
        self.send_pair(self.place.row, 0).start()

    def take_others(self):
        p = self.place
        for step in range(1, p.rows):
            row = p.row_before(step)
            self.wait_plane(row)
            self.send_pair(row, step).start()

    def wait_plane(self, row):
        p = self.place
        start, size = self.plane_part()
        piece = self.slot(row, start, size)
        remote(piece, piece, self.sem(0, 0), self.sem(3, row), p.across()).wait_recv()

    def send_pair(self, row, step):
        start, size = self.pair_part()
        piece = self.slot(row, start, size)
        return remote(piece, piece, self.sem(2, step), self.sem(4, row), self.place.pair())

    def send_across(self, row, step):
        start, size = self.plane_part()
        piece = self.slot(row, start, size)
        return remote(piece, piece, self.sem(1, step), self.sem(3, row), self.place.across())

    def finish(self):
        p = self.place
        start, size = self.other_part()

        def wait_other(row):
            piece = self.slot(row, start, size)
            remote(piece, piece, self.sem(2, 0), self.sem(4, row), p.pair()).wait_recv()

        for step in range(1, p.rows):
            wait_other(p.row_before(step))

        @pl.when(p.matched)
        def _():
            whole = self.slot(p.row, 0, 2 * self.one + self.both)
            pltpu.make_async_copy(whole, whole, self.local).wait()

        @pl.when(jnp.logical_not(p.matched))
        def _():
            wait_other(p.row)

    def drain(self):
        p = self.place
        start, size = self.plane_part()
        piece = self.slot(p.row, start, size)
        for step in range(1, p.rows):
            self.send_pair(p.row, step).wait_send()

        @pl.when(p.matched)
        def _():
            for step in range(1, p.rows):
                remote(piece, piece, self.sem(0, step), self.sem(3, p.row), p.across()).wait_send()
            for step in range(p.rows):
                self.send_across(p.row, step).wait_send()

        @pl.when(jnp.logical_not(p.matched))
        def _():
            self.send_pair(p.row, 0).wait_send()


def add_rows(count, target, *parts):
    step = next(s for s in (64, 32, 16) if count % s == 0)

    @pl.loop(0, count // step)
    def _(i):
        cut = pl.ds(pl.multiple_of(i * step, step), step)
        total = parts[0][cut, :].astype(jnp.float32)
        for part in parts[1:]:
            total = total + part[cut, :].astype(jnp.float32)
        target[cut, :] = total.astype(target.dtype)


def first_share(count, share=5 / 16):
    return int(count * share) // 16 * 16


class Grad:
    def __init__(self, place, block, rows, bufs, sems, credits, index, stage=None, summed=None, share=5 / 16):
        self.p, self.block, self.m, self.index, self.sems, self.stage = place, block, rows, index, sems, stage
        self.credits, self.summed = credits, summed
        self.a = first_share(rows, share)
        self.b = rows - self.a
        self.recv_a, self.recv_b, self.acc, self.more, self.zbuf = bufs
        self.levels = (place.planes - 1).bit_length()
        self.full = self.acc.shape[0]

    def sem(self, kind, at=0):
        return self.sems.at[self.index, kind, at]

    def low(self):
        return self.acc.at[pl.ds(0, self.a), :]

    def high(self):
        return self.acc.at[pl.ds(self.a, self.b), :]

    def send(self, src, dst, kind, at, target):
        return remote(src, dst, self.sem(kind, at), self.sem(kind + 1, at), target)

    def landed(self, buf, kind, at=0):
        self.send(buf, buf, kind, at, self.p.sibling()).wait_recv()

    def left(self, buf, kind, at=0):
        self.send(buf, buf, kind, at, self.p.sibling()).wait_send()

    def copies_y(self):
        p = self.p
        return [
            self.send(self.block(p.row_after(s), 0, self.a), self.recv_a.at[s - 1], 0, s, p.at(row=p.row_after(s)))
            for s in range(1, p.rows)
        ]

    def copies_x(self):
        return [
            self.send(self.block(j, self.a, self.b), self.recv_b.at[j], 2, j, self.p.across())
            for j in range(self.p.rows)
        ]

    def begin_y(self):
        for copy in self.copies_y():
            copy.start()

    def begin_x(self):
        @pl.when(jnp.logical_not(self.p.matched))
        def _():
            for copy in self.copies_x():
                copy.start()

    def own(self, row, start, size, slot):
        piece = self.block(row, start, size)
        if self.stage is None:
            return piece, []
        buf, sem = self.stage
        buf = buf.at[slot, pl.ds(0, size), :]
        copy = pltpu.make_async_copy(piece, buf, sem.at[slot])
        copy.start()
        return buf, [copy]

    def sum_y(self):
        p = self.p
        own, copies = self.own(p.row, 0, self.a, 0)
        for s in range(1, p.rows):
            self.landed(self.recv_a.at[s - 1], 0, s)
        for copy in copies:
            copy.wait()
        add_rows(self.a, self.recv_a.at[0], own, *[self.recv_a.at[s - 1] for s in range(1, p.rows)])

        @pl.when(jnp.logical_not(p.matched))
        def _():
            self.send(self.recv_a.at[0], self.low(), 4, 0, p.across()).start()

    def sum_x(self):
        p = self.p

        @pl.when(p.matched)
        def _():
            steps = list(range(1, p.rows)) + [0]
            owns = [self.own(p.row_after(s), self.a, self.b, n) for n, s in enumerate(steps[:2])]
            for n, s in enumerate(steps):
                row = p.row_after(s)
                if n >= 2:
                    owns.append(self.own(row, self.a, self.b, n % 2))
                own, copies = owns[n]
                buf = self.recv_b.at[row]
                self.landed(buf, 2, row)
                for copy in copies:
                    copy.wait()
                add_rows(self.b, buf, own, buf)
                if s:
                    target = self.high() if s == 1 else self.more.at[s - 2]
                    self.send(buf, target, 6, s, p.at(row=row)).start()

    def span(self, level):
        start, size = 0, self.full
        for i in range(1, level + 1):
            size //= 2
            start = start + self.p.group_bit(i) * size
        return start, size

    def rows_of(self, start, size):
        return self.acc.at[pl.ds(pl.multiple_of(start, 16), size), :]

    def z_copy(self, level):
        if level == 0:
            return self.send(self.acc, self.zbuf[0], 8, 0, self.p.mate(0))
        start, size = self.span(level - 1)
        half = size // 2
        piece = self.rows_of(start + (1 - self.p.group_bit(level)) * half, half)
        return self.send(piece, self.zbuf[level], 8, level, self.p.mate(level))

    def z_back(self, level):
        piece = self.acc if level == 0 else self.rows_of(*self.span(level))
        return self.send(piece, piece, 10, level, self.p.mate(level))

    def z_free(self, level):
        self.z_copy(level).wait_send()
        pl.semaphore_signal(
            self.credits.at[self.index, level], inc=1, device_id=self.p.mate(level), device_id_type=MESH_ID
        )

    def z_return(self, level):
        pl.semaphore_wait(self.credits.at[self.index, level], 1)
        self.z_back(level).start()

    def plane_sum(self):
        p = self.p

        @pl.when(p.matched)
        def _():
            self.landed(self.low(), 4)
            add_rows(self.a, self.low(), self.low(), self.recv_a.at[0])
            others = []
            for s in range(1, p.rows):
                buf = self.high() if s == 1 else self.more.at[s - 2]
                self.landed(buf, 6, s)
                others.append(buf)
            add_rows(self.b, self.high(), self.recv_b.at[p.row], *others)

    def sum_both(self):
        p = self.p
        if self.summed is None:
            self.plane_sum()
        else:
            pl.when(p.matched)(self.summed.wait)

        @pl.when(jnp.logical_and(p.matched, jnp.logical_not(p.inner)))
        def _():
            self.z_copy(0).start()

    def z0(self):
        p = self.p

        @pl.when(jnp.logical_and(p.matched, p.inner))
        def _():
            self.landed(self.zbuf[0], 8, 0)
            add_rows(self.full, self.acc, self.acc, self.zbuf[0])
            if self.levels > 1:
                self.z_copy(1).start()
            else:
                self.z_return(0)
                self.final().start()

        @pl.when(jnp.logical_and(p.matched, jnp.logical_not(p.inner)))
        def _():
            self.z_free(0)

    def z1(self):
        @pl.when(jnp.logical_and(self.p.matched, self.p.inner))
        def _():
            for level in range(1, self.levels):
                start, size = self.span(level)
                self.landed(self.zbuf[level], 8, level)
                piece = self.rows_of(start, size)
                add_rows(size, piece, piece, self.zbuf[level])
                self.z_free(level)
                if level + 1 < self.levels:
                    self.z_copy(level + 1).start()
                else:
                    self.z_return(level)

    def g1(self):
        @pl.when(jnp.logical_and(self.p.matched, self.p.inner))
        def _():
            for level in range(self.levels - 1, 0, -1):
                start, size = self.span(level - 1)
                half = size // 2
                self.landed(self.rows_of(start + (1 - self.p.group_bit(level)) * half, half), 10, level)
                self.z_return(level - 1)
                if level == 1:
                    self.final().start()

    def g0(self):
        @pl.when(jnp.logical_and(self.p.matched, jnp.logical_not(self.p.inner)))
        def _():
            self.landed(self.acc, 10, 0)
            self.final().start()

    def final(self):
        return remote(self.acc, self.acc, self.sem(12), self.sem(13), self.p.sibling())

    def store(self, stores):
        @pl.when(jnp.logical_not(self.p.matched))
        def _():
            self.final().wait_recv()

        copies = [
            pltpu.make_async_copy(self.acc.at[pl.ds(row, rows), pl.ds(col, cols)], out, sem)
            for row, rows, col, cols, out, sem in stores
        ]
        for copy in copies:
            copy.start()
        return copies

    def drain_plane(self):
        p = self.p
        for copy in self.copies_y():
            copy.wait_send()

        @pl.when(jnp.logical_not(p.matched))
        def _():
            for copy in self.copies_x():
                copy.wait_send()
            self.left(self.recv_a.at[0], 4)

        @pl.when(p.matched)
        def _():
            for s in range(1, p.rows):
                self.left(self.recv_b.at[0], 6, s)

    def drain(self):
        p = self.p
        if self.summed is None:
            self.drain_plane()

        @pl.when(p.matched)
        def _():
            self.final().wait_send()

        @pl.when(jnp.logical_and(p.matched, p.inner))
        def _():
            for level in range(self.levels):
                self.z_back(level).wait_send()


def grad_rows(rows, planes):
    tile = 16 * max(1, planes // 2)
    return -(-rows // tile) * tile


def grad_bufs(rows, cols, blocks, planes, summed=False, share=5 / 16):
    a = first_share(rows, share)
    V = lambda *shape: pltpu.VMEM(shape, jnp.bfloat16)
    levels = (planes - 1).bit_length()
    full = grad_rows(rows, planes)
    none = V(16, 128)
    plane = [none, none] if summed else [V(blocks - 1, a, cols), V(blocks, rows - a, cols)]
    more = none if summed or blocks <= 2 else V(blocks - 2, rows - a, cols)
    return plane + [V(full, cols), more, [V(full >> i, cols) for i in range(levels)]]


def plane_bufs(rows, cols, blocks, planes):
    return grad_bufs(rows, cols, blocks, planes, False, 1 / 2)[:4]


def block_rows(i, size=BLOCK):
    return pl.ds(pl.multiple_of(i * size, size), size)


def gelu_parts(gate):
    phi = 0.5 * (1.0 + lax.erf(gate * (1.0 / math.sqrt(2.0))))
    return phi, jnp.exp(gate * gate * -0.5) * (1.0 / math.sqrt(2.0 * math.pi))


def forward_kernel(
    chunks,
    tokens_ref, cot_ref, lengths_ref, first_gain_ref, second_gain_ref, freq_ref, joined_ref, mixer_ref, expand_ref, shrink_ref,
    *rest,
):
    n_chunks = len(chunks)
    outs, scratch = rest[:20], rest[20:]
    (o_tokens, o_first, o_q, o_k, o_v, o_mixed, o_lse, o_xhat, o_inv, o_top, o_own, o_other, o_back,
     o_expand, o_shrink, o_joined, o_mixer, o_small, o_table, o_sum) = outs
    (tok, cot, meta_src, meta, gains_ref, gains, table, first, wj, wm, wg, wu, ws, q_s, k_s, v_s, v_t, out_t, lse, mixed, xhat, inv, second,
     top, shrunk, back, back_low, other_half, hid, dgate, dup, g_expand, g_shrink, sum_bufs, sum_sem,
     tok_send, tok_recv, cot_send, cot_recv, swap_send, meta_send, meta_recv, gain_send, gain_recv,
     w_y, w_x, w_z, w_recv, w_recv_z, w_local, mix_send, mix_recv, mixed_send, mixed_recv, out_sem) = scratch
    p = Place()
    rows, seqs = p.rows, p.seqs
    width = tokens_ref.shape[1]
    wide = q_s.shape[1]
    pairs = wide // PAIR
    sems = (w_y, w_x, w_z, w_recv, w_recv_z, w_local)

    def down(ref, buf, col, size):
        source = lambda start, n: ref.at[:, pl.ds(start, n), pl.ds(col, size)]
        slot = lambda row, start, n: buf.at[:, pl.ds(row * width + start, n), :]
        return source, slot

    def along(ref, buf, at):
        source = lambda start, n: ref.at[pl.ds(at + start, n), :]
        slot = lambda row, start, n: buf.at[pl.ds(start, n), pl.ds(pl.multiple_of(row * width, width), width)]
        return source, slot

    half = wide // 2
    joined = [Weight(p, *down(joined_ref, wj.at[h], half * h, half), width, sems, h, 0.25) for h in range(2)]
    mixer = Weight(p, *along(mixer_ref, wm.at[p.core], 0), wide, sems, 2, 0.41)
    groups, at = [], 0
    for i, count in enumerate(chunks):
        groups.append([
            Weight(p, *along(ref, buf, at), count, sems, 3 + 3 * i + n, 0.41)
            for n, (ref, buf) in enumerate(((expand_ref.at[0], wg[i]), (expand_ref.at[1], wu[i]), (shrink_ref, ws[i])))
        ])
        at += count

    place_row = lanes_of((1, LEN))
    for s in range(seqs):
        base = [lengths_ref[p.col * seqs + s, d] for d in range(DOCS)]
        segment = jnp.zeros((1, LEN), jnp.int32)
        start = jnp.zeros((1, LEN), jnp.int32)
        end = jnp.int32(0)
        for d in range(DOCS):
            end = end + base[d]
            past = place_row >= end
            segment = segment + past.astype(jnp.int32)
            start = jnp.where(past, end, start)
        meta_src[s, 0:1, :] = (place_row - start).astype(jnp.float32)
        meta_src[s, 1:2, :] = segment.astype(jnp.float32)
        meta_src[s, 2:3, :] = (segment < DOCS - 1).astype(jnp.float32)
        meta_src[s, 3:8, :] = jnp.zeros((5, LEN), jnp.float32)

    gains_ref[0:1, :] = first_gain_ref[...]
    gains_ref[1:2, :] = second_gain_ref[...]
    gains_ref[2:8, :] = jnp.zeros((6, width), jnp.float32)
    p.barrier([p.across(), p.pair()])

    is_here = p.core == p.row // seqs

    blocks = range(LEN // BLOCK)

    def send_seq(ref, buf, send, recv, block):
        for t in range(seqs):
            seq = lax.rem(p.row + t, seqs)
            piece = ref.at[pl.ds(pl.multiple_of(seq * LEN + block * BLOCK, BLOCK), BLOCK), :]
            place = buf.at[p.row, pl.ds(block * BLOCK, BLOCK), :]
            target = p.at(core=p.row // seqs, row=p.core * seqs + seq)

            def away():
                remote(piece, place, send.at[t, block], recv.at[p.row, block], target).start()

            if t:
                away()
            else:
                pl.when(jnp.logical_not(is_here))(away)

                @pl.when(is_here)
                def _():
                    pltpu.make_async_copy(piece, place, recv.at[p.row, block]).start()

    def swap_seq(buf, slot, recv, swap, u, block):
        piece = buf.at[slot, pl.ds(block * BLOCK, BLOCK), :]
        return remote(piece, piece, swap.at[u, block], recv.at[slot, block], p.sibling())

    def take_seq(buf, recv, swap, block):
        for u in range(seqs):
            slot = p.core * seqs + u
            piece = buf.at[slot, pl.ds(block * BLOCK, BLOCK), :]
            pltpu.make_async_copy(piece, piece, recv.at[slot, block]).wait()
            swap_seq(buf, slot, recv, swap, u, block).start()

    def finish_seq(buf, recv, swap, block):
        for u in range(seqs):
            swap_seq(buf, (1 - p.core) * seqs + u, recv, swap, u, block).wait_recv()

    def drain_seq(buf, send, recv, swap):
        for block in blocks:
            piece = buf.at[0, pl.ds(0, BLOCK), :]
            for u in range(seqs):
                swap_seq(buf, 0, recv, swap, u, block).wait_send()
                if u:
                    remote(piece, piece, send.at[u, block], recv.at[0, block], p.sibling()).wait_send()

            @pl.when(jnp.logical_not(is_here))
            def _():
                remote(piece, piece, send.at[0, block], recv.at[0, block], p.sibling()).wait_send()

    sends_meta = lax.rem(p.row, seqs) == 0

    @pl.when(sends_meta)
    def _():
        for t in range(seqs):
            target = p.at(core=p.row // seqs, row=p.core * seqs + t)

            def away():
                remote(meta_src.at[t], meta, meta_send.at[t], meta_recv, target).start()

            if t:
                away()
            else:
                pl.when(jnp.logical_not(is_here))(away)

                @pl.when(is_here)
                def _():
                    pltpu.make_async_copy(meta_src.at[t], meta, meta_recv).start()

    for step in range(1, rows):
        remote(gains_ref, gains.at[p.row], gain_send.at[step], gain_recv.at[p.row], p.at(row=p.row_after(step))).start()
    pltpu.make_async_copy(gains_ref, gains.at[p.row], gain_recv.at[p.row]).start()
    def service(matched, unmatched):
        for here, actions in ((p.matched, matched), (jnp.logical_not(p.matched), unmatched)):
            if actions:

                @pl.when(here)
                def _():
                    for action in actions:
                        action()

    tokens_of = [functools.partial(send_seq, tokens_ref, tok, tok_send, tok_recv, block) for block in blocks]
    cot_of = [functools.partial(send_seq, cot_ref, cot, cot_send, cot_recv, block) for block in blocks]
    j0, j1 = joined
    (g0, u0, s0), (g1, u1, s1), (g2, u2, s2) = groups

    def each(action, *weights):
        return [functools.partial(getattr(weight, action)) for weight in weights]

    service(
        [g0.own_x, tokens_of[3], j1.own_x, j0.own_x, j0.own_y, tokens_of[1], j0.pass_on, tokens_of[2], tokens_of[0], g0.own_y, j1.own_y],
        [g0.take_first, tokens_of[2], tokens_of[0], tokens_of[1], j0.take_first],
    )

    def gain_of(kind):
        return jnp.concatenate([gains[j, kind : kind + 1, :] for j in range(rows)], axis=1)

    def norm(values):
        center = jnp.mean(values, axis=-1, keepdims=True)
        values = values - center
        spread = jnp.mean(values * values, axis=-1, keepdims=True)
        scale = lax.rsqrt(spread + norm_eps)
        return values * scale, scale

    def tokens_at(cut):
        return jnp.concatenate([tok[j, cut, :] for j in range(rows)], axis=1).astype(jnp.float32)

    def first_norm(block):
        cut = slice(block * BLOCK, (block + 1) * BLOCK)
        finish_seq(tok, tok_recv, swap_send.at[0], block)
        first[cut, :] = (norm(tokens_at(cut))[0] * gain_a).astype(jnp.bfloat16)

    for step in range(1, rows):
        row = p.row_before(step)
        remote(gains.at[row], gains.at[row], gain_send.at[step], gain_recv.at[row], p.sibling()).wait_recv()
    pltpu.make_async_copy(gains.at[p.row], gains.at[p.row], gain_recv.at[p.row]).wait()
    gain_a, gain_b = gain_of(0), gain_of(1)
    pltpu.make_async_copy(meta, meta, meta_recv).wait()
    columns = meta[...].T
    angle = columns[:, 0:1] * freq_ref[0:1, :]
    sign = jnp.where(lanes_of((1, PAIR)) % HD < HD // 2, -1.0, 1.0)
    table[0] = jnp.cos(angle)
    table[1] = jnp.sin(angle) * sign
    segment_col, valid_col = columns[:, 1:2], columns[:, 2:3]
    take_seq(tok, tok_recv, swap_send.at[0], 0)
    service([], [tokens_of[3]])
    take_seq(tok, tok_recv, swap_send.at[0], 1)
    service(
        [mixer.own_y, u1.own_x, u0.own_x, u0.own_y, j1.pass_on, s0.own_x, s1.own_x, s0.own_y, g0.pass_on],
        [j1.take_first, j0.take_others],
    )
    take_seq(tok, tok_recv, swap_send.at[0], 2)
    service([s1.own_y], [])
    first_norm(0)
    service([g2.own_y], [])
    take_seq(tok, tok_recv, swap_send.at[0], 3)
    first_norm(1)
    service([mixer.own_x], [u1.take_first])
    first_norm(2)
    first_norm(3)
    service([mixer.pass_on], [u0.take_first])

    def project(h):
        cols = slice(h * half, (h + 1) * half)

        @pl.loop(0, LEN // BLOCK)
        def _(i):
            cut = block_rows(i)
            part = first[cut, :]
            cosine, sine = (jnp.concatenate([table[n, cut, :]] * (half // PAIR), axis=1) for n in range(2))
            for j, dst in ((0, q_s), (1, k_s)):
                raw = dot(part, wj[h, j])
                dst[cut, cols] = (raw * cosine + swap_halves(raw) * sine).astype(jnp.bfloat16)
            v_s[cut, cols] = dot(part, wj[h, 2]).astype(jnp.bfloat16)

    def attention(pair, between):
        cols = slice(pair * PAIR, (pair + 1) * PAIR)
        v_t[...] = v_s[:, cols].astype(jnp.float32).T.astype(jnp.bfloat16)
        for head in range(2):
            lanes = slice(head * HD, (head + 1) * HD)

            @pl.loop(0, LEN // BLOCK)
            def _(i):
                cut = block_rows(i)
                scores = dot(k_s[:, cols], only_head(q_s[cut, cols], head), NT)
                scores = jnp.where(segment_col == meta[1:2, cut], scores, masked_value)
                peak = jnp.max(scores, axis=0, keepdims=True)
                weights = jnp.exp2((scores - peak) * TO_EXP2)
                total = jnp.sum(weights, axis=0, keepdims=True)
                out_t[lanes, cut] = dot(v_t[lanes, :], weights.astype(jnp.bfloat16)) / total
                lse[pair, head : head + 1, cut] = peak * TO_EXP2 + jnp.log2(total)

            if head == 0:
                service(*between)

        mixed[p.core, :, cols] = out_t[...].T.astype(jnp.bfloat16)
        piece = mixed.at[p.core, :, cols]
        remote(piece, piece, mixed_send.at[pair], mixed_recv.at[pair], p.sibling()).start()

    def share_mixer():
        mixer.finish()
        piece = wm.at[p.core]
        remote(piece, piece, mix_send, mix_recv, p.sibling()).start()

    j0.finish()
    project(0)
    service([u1.own_y], [])
    attention(0, ([*cot_of], []))
    service([s0.pass_on, g1.own_y, s2.own_y, u0.pass_on], [j1.take_others])
    attention(1, ([], []))
    service([u2.own_x, g1.own_x], [s1.take_first, *cot_of, s0.take_first])
    j1.finish()
    project(1)
    service([], [g0.take_others])
    attention(2, ([], [mixer.take_first]))
    service([u1.pass_on, s1.pass_on], [mixer.take_others])
    attention(3, ([], []))
    service([s2.own_x], [])
    service([g2.own_x, g1.pass_on, g2.pass_on], [])
    share_mixer()
    service([], [s0.take_others, u0.take_others])
    for block in blocks:
        take_seq(cot, cot_recv, swap_send.at[1], block)

    for pair in range(pairs):
        piece = mixed.at[p.core, :, pair * PAIR : (pair + 1) * PAIR]
        remote(piece, piece, mixed_send.at[pair], mixed_recv.at[pair], p.sibling()).wait_recv()
    piece = wm.at[p.core]
    remote(piece, piece, mix_send, mix_recv, p.sibling()).wait_recv()
    for block in blocks:
        finish_seq(cot, cot_recv, swap_send.at[1], block)

    @pl.loop(0, LEN // BLOCK)
    def _(i):
        cut = block_rows(i)
        value = tokens_at(cut) + dot(mixed[0, cut, :], wm[0]) + dot(mixed[1, cut, :], wm[1])
        normed, scale = norm(value)
        xhat[cut, :] = normed.astype(jnp.bfloat16)
        inv[cut, :] = jnp.broadcast_to(scale, (BLOCK, PAIR))
        second[cut, :] = (normed * gain_b).astype(jnp.bfloat16)
        shrunk[cut, :] = jnp.where(lanes_of((1, D)) // (D // CORES) == p.core, value, 0.0)
        back[cut, :] = jnp.zeros((BLOCK, D), jnp.float32)

    valid_16 = valid_col > 0.5
    top[...] = jnp.where(valid_16, jnp.concatenate([cot[j] for j in range(rows)], axis=1), jnp.zeros((), jnp.bfloat16))

    keep = []

    def store(src, dst):
        copy = pltpu.make_async_copy(src, dst, out_sem.at[len(keep)])
        keep.append(copy)
        copy.start()

    for j in range(rows):
        store(tok.at[j], o_tokens.at[j])
    for src, dst in ((first, o_first), (q_s, o_q), (k_s, o_k), (v_s, o_v), (mixed.at[p.core], o_mixed), (lse, o_lse),
                     (xhat, o_xhat), (inv, o_inv), (table, o_table), (top, o_top), (wj.at[0], o_joined.at[0]), (wj.at[1], o_joined.at[1]), (wm.at[p.core], o_mixer)):
        store(src, dst)
    for j in range(rows):
        store(gains.at[j], o_small.at[:, pl.ds(j * width, width)])
    store(meta, o_small.at[:, pl.ds(D, LEN)])

    service([], [u1.take_others, g1.take_first])
    early = [
        ([], []),
        ([], [g2.take_others]),
        ([], []),
    ]
    middle = [
        ([u2.own_y, s2.pass_on], [g1.take_others, g2.take_first, s2.take_first]),
        ([], [u2.take_others]),
        ([], []),
    ]
    ready = [
        ([], [s1.take_others]),
        ([], []),
        ([], []),
    ]
    late = [
        ([u2.pass_on], [s2.take_others, u2.take_first]),
        ([], []),
        ([], []),
    ]

    def first_block(row, start, size):
        return g_expand[0].at[pl.ds(start, size), pl.ds(pl.multiple_of(row * width, width), width)]

    plane = Grad(p, first_block, 2 * chunks[0], (*sum_bufs, []), sum_sem, None, 0, share=1 / 2)
    then_early = [[], [], [plane.sum_x]]
    at = 0
    for i, lanes in enumerate(chunks):
        for weight in groups[i]:
            weight.finish()
        service(*ready[i])

        @pl.loop(0, LEN // BLOCK)
        def _(t):
            cut = block_rows(t)
            part, grad = second[cut, :], top[cut, :]
            gate = dot(part, wg[i][...], NT)
            up = dot(part, wu[i][...], NT)
            hidden_grad = dot(grad, ws[i][...], NT).astype(jnp.bfloat16).astype(jnp.float32)
            phi, density = gelu_parts(gate)
            act = gate * phi
            hidden = (act * up).astype(jnp.bfloat16)
            d_gate = (hidden_grad * up * (phi + gate * density)).astype(jnp.bfloat16)
            d_up = (hidden_grad * act).astype(jnp.bfloat16)
            hid[cut, :lanes] = hidden
            dgate[cut, :lanes] = d_gate
            dup[cut, :lanes] = d_up
            value = shrunk[cut, :] + dot(hidden, ws[i][...])
            grad_sum = back[cut, :] + dot(d_gate, wg[i][...]) + dot(d_up, wu[i][...])
            if i + 1 < n_chunks:
                shrunk[cut, :] = value
                back[cut, :] = grad_sum
            else:
                back_low[cut, :] = grad_sum.astype(jnp.bfloat16)
                left, right = value[:, : D // 2], value[:, D // 2 :]
                shrunk[cut, : D // 2] = jnp.where(p.core == 0, left, right)
                other_half[cut, :] = jnp.where(p.core == 0, right, left).astype(jnp.bfloat16)

            @pl.when(t == LEN // BLOCK // 2 - 1)
            def _():
                service(*early[i])
                for action in then_early[i]:
                    action()


        service(*middle[i])
        if i == 1:
            plane.sum_y()
        if i + 1 == n_chunks:
            store(back_low, o_back)
            store(shrunk.at[:, pl.ds(0, D // 2)], o_own)
            store(other_half, o_other)
        for n, (left, right) in enumerate(((dgate, second), (dup, second), (hid, top))):
            target = g_shrink[i] if n == 2 else g_expand[i]
            for start in range(0, lanes, BLOCK):
                size = min(BLOCK, lanes - start)
                spot = start if n == 2 else n * lanes + start
                target[spot : spot + size, :] = dot(left[:, start : start + size], right[...], TN).astype(jnp.bfloat16)
            if n == 1 and i == 0:
                plane.begin_y()
                plane.begin_x()

        if i:
            store(g_expand[i], o_expand.at[pl.ds(2 * at, 2 * lanes), :])
        store(g_shrink[i], o_shrink.at[pl.ds(at, lanes), :])
        service(*late[i])
        at += lanes

    plane.plane_sum()
    store(plane.acc, o_sum)

    plane.drain_plane()
    drain_seq(tok, tok_send, tok_recv, swap_send.at[0])
    drain_seq(cot, cot_send, cot_recv, swap_send.at[1])
    for step in range(1, rows):
        remote(gains_ref, gains.at[p.row], gain_send.at[step], gain_recv.at[p.row], p.sibling()).wait_send()

    @pl.when(sends_meta)
    def _():
        for t in range(1, seqs):
            remote(meta_src.at[t], meta, meta_send.at[t], meta_recv, p.sibling()).wait_send()

        @pl.when(jnp.logical_not(is_here))
        def _():
            remote(meta_src.at[0], meta, meta_send.at[0], meta_recv, p.sibling()).wait_send()

    for pair in range(pairs):
        piece = mixed.at[p.core, :, pair * PAIR : (pair + 1) * PAIR]
        remote(piece, piece, mixed_send.at[pair], mixed_recv.at[pair], p.sibling()).wait_send()
    piece = wm.at[p.core]
    remote(piece, piece, mix_send, mix_recv, p.sibling()).wait_send()
    for weight in joined + [mixer] + sum(groups, []):
        weight.drain()
    for copy in keep:
        copy.wait()


def forward(tokens, cot, lengths, first_gain, second_gain, joined, mixer, expand, shrink, chunks):
    rows = lax.axis_size("row")
    seqs = rows // CORES
    width = tokens.shape[1]
    wide = mixer.shape[0]
    pairs = wide // PAIR
    blocks = LEN // BLOCK
    n_chunks = len(chunks)
    hidden_here = sum(chunks)
    planes = lax.axis_size("dp") // CORES
    weights = 3 + 3 * n_chunks
    bf16, f32 = jnp.bfloat16, jnp.float32
    freq = np.tile((rope_base ** (-2.0 * np.arange(HD // 2) / HD)).astype(np.float32), (8, 4))
    outs = [
        ((rows, LEN, width), bf16), ((LEN, D), bf16), ((LEN, wide), bf16), ((LEN, wide), bf16), ((LEN, wide), bf16),
        ((LEN, wide), bf16), ((pairs, 2, LEN), f32), ((LEN, D), bf16), ((LEN, PAIR), f32), ((LEN, D), bf16),
        ((LEN, D // 2), f32), ((LEN, D // 2), bf16), ((LEN, D), bf16),
        ((2 * hidden_here, D), bf16), ((hidden_here, D), bf16), ((2, 3, D, wide // 2), bf16), ((wide, D), bf16),
        ((8, D + LEN), f32), ((2, LEN, PAIR), f32), ((grad_rows(2 * chunks[0], planes), width), bf16),
    ]
    V, dma = pltpu.VMEM, pltpu.SemaphoreType.DMA
    widest = max(chunks)
    scratch = [
        V((rows, LEN, width), bf16), V((rows, LEN, width), bf16), V((seqs, 8, LEN), f32), V((8, LEN), f32),
        V((8, width), f32), V((rows, 8, width), f32), V((2, LEN, PAIR), f32), V((LEN, D), bf16), V((2, 3, D, wide // 2), bf16), V((CORES, wide, D), bf16),
        [V((lanes, D), bf16) for lanes in chunks], [V((lanes, D), bf16) for lanes in chunks], [V((lanes, D), bf16) for lanes in chunks],
        V((LEN, wide), bf16), V((LEN, wide), bf16), V((LEN, wide), bf16), V((PAIR, LEN), bf16), V((PAIR, LEN), f32),
        V((pairs, 2, LEN), f32), V((CORES, LEN, wide), bf16), V((LEN, D), bf16), V((LEN, PAIR), f32), V((LEN, D), bf16),
        V((LEN, D), bf16), V((LEN, D), f32), V((LEN, D), f32), V((LEN, D), bf16), V((LEN, D // 2), bf16), V((LEN, widest), bf16), V((LEN, widest), bf16), V((LEN, widest), bf16),
        [V((2 * lanes, D), bf16) for lanes in chunks],
        [V((lanes, D), bf16) for lanes in chunks],
        plane_bufs(2 * chunks[0], width, rows, planes), dma((1, 14, rows)),
        dma((seqs, blocks)), dma((rows, blocks)), dma((seqs, blocks)), dma((rows, blocks)), dma((2, seqs, blocks)), dma((seqs,)), dma,
        dma((rows,)), dma((rows,)),
        dma((weights, rows)), dma((weights, rows)), dma((weights, rows)), dma((weights, rows)), dma((weights, rows)),
        dma((weights,)), dma, dma, dma((pairs,)), dma((pairs,)), dma((2 * rows + 17 + 3 * n_chunks,)),
    ]
    anywhere = pl.BlockSpec(memory_space=pl.ANY)
    in_specs = [anywhere] * 10
    in_specs[2] = pl.BlockSpec(memory_space=pltpu.SMEM)
    in_specs[3:6] = [pl.BlockSpec(memory_space=pltpu.VMEM)] * 3
    return pl.pallas_call(
        functools.partial(forward_kernel, chunks),
        in_specs=in_specs,
        out_specs=[anywhere] * len(outs),
        out_shape=[jax.ShapeDtypeStruct(*o) for o in outs],
        scratch_shapes=scratch,
        compiler_params=pltpu.CompilerParams(
            collective_id=0, has_side_effects=True, vmem_limit_bytes=62 * 1024 * 1024
        ),
        name="layer_forward",
    )(tokens, cot, lengths, first_gain[None, :], second_gain[None, :], freq, joined, mixer, expand, shrink)


def backward_kernel(
    chunks,
    tokens_ref, first_ref, q_ref, k_ref, v_ref, mixed_ref, lse_ref, xhat_ref, inv_ref, top_ref, own_ref, other_ref, back_ref,
    expand_ref, shrink_ref, joined_ref, mixer_ref, small_ref, table_ref, sum_ref,
    o_block, o_input, o_joined, o_mixer, o_expand, o_shrink, o_gains,
    q_s, k_s, v_s, mixed, xa, xb, xc, wj, wm, lse, inv, small, table, other, keep_grad, middle_low, mixed_grad, g_mixer, g_joined,
    dk, dv, dq_t, k_t, delta, own_half, block_half, gain_sum, gain_y, gain_x, gain_z, stage_lane, grad_scratch,
    load_sem, stage_sem, sum_sem, grad_sem, credit, swap_credit, back_send, back_recv, other_send, other_recv, first_send, first_recv,
    out_send, out_recv, in_send, in_recv, gain_send, gain_recv, out_sem,
):
    p = Place()
    rows, seqs, planes = p.rows, p.seqs, p.planes
    width = D // rows
    wide = q_s.shape[1]
    pairs = wide // PAIR
    levels = (planes - 1).bit_length()
    half = wide // 2

    def by_row(ref):
        return lambda j, start, size: ref.at[pl.ds(pl.multiple_of(j * width + start, 16), size), :]

    def by_lane(ref, at=0):
        return lambda j, start, size: ref.at[pl.ds(at + start, size), pl.ds(pl.multiple_of(j * width, width), width)]

    grads, places, at = {}, {}, 0
    stage = (stage_lane, stage_sem)

    def add_grad(name, block, count, stage, stores, summed=None):
        i = len(grads)
        grads[name] = Grad(p, block, count, grad_scratch[i], grad_sem, credit, i, stage, summed)
        places[name] = stores

    for i, count in enumerate(chunks):
        add_grad(("E", i), by_lane(expand_ref, 2 * at), 2 * count, stage,
                 [(j * count, count, 0, width, o_expand.at[j, pl.ds(at, count), :]) for j in range(2)],
                 None if i else pltpu.make_async_copy(sum_ref, grad_scratch[0][2], sum_sem))
        add_grad(("S", i), by_lane(shrink_ref, at), count, stage, [(0, count, 0, width, o_shrink.at[pl.ds(at, count), :])])
        at += count
    for h in range(2):
        add_grad(("J", h), by_row(g_joined.at[h]), width, None,
                 [(0, width, j * half, half, o_joined.at[j, :, pl.ds(h * half, half)]) for j in range(3)])
    add_grad(("M", 0), by_lane(g_mixer), wide, None, [(0, wide, 0, width, o_mixer)])

    loads = {}

    def load(name, src, dst):
        copy = pltpu.make_async_copy(src, dst, load_sem.at[len(loads)])
        copy.start()
        loads[name] = copy

    load("small", small_ref, small)
    load("back", back_ref, xc)
    load("xhat", xhat_ref, xa)
    load("inv", inv_ref, inv)
    load("top", top_ref, xb)
    load("mixer", mixer_ref, wm)
    load("mixed", mixed_ref, mixed)
    load("q", q_ref, q_s)
    load("k", k_ref, k_s)
    load("v", v_ref, v_s)
    load("lse", lse_ref, lse)
    load("table", table_ref, table)
    load("joined", joined_ref, wj)
    load("own", own_ref, own_half)
    pl.when(p.matched)(grads["E", 0].summed.start)
    p.barrier([p.across()] + [p.mate(level) for level in range(levels)])

    def swap_block(i, src, dst, send, recv):
        cut = pl.ds(i * BLOCK, BLOCK)
        return remote(src.at[cut, :], dst.at[cut, :], send.at[i], recv.at[i], p.sibling())

    blocks_n = LEN // BLOCK
    for i in range(blocks_n):
        swap_block(i, back_ref, other, back_send, back_recv).start()

    stores = []

    def run(*todo):
        for step in todo:
            if callable(step):
                step()
                continue
            action, kind, i = step
            grad = grads[kind, i]
            if action == "store":
                spots = [spot + (out_sem.at[len(stores) + n],) for n, spot in enumerate(places[kind, i])]
                stores.extend(grad.store(spots))
            elif action == "begin":
                grad.begin_y()
                grad.begin_x()
            else:
                getattr(grad, action)()

    run(("begin_x", "E", 1), ("begin_y", "E", 2), ("begin_x", "S", 0), ("begin_y", "S", 2), ("begin_y", "E", 1))
    other_copy = remote(other_ref, block_half, other_send, other_recv, p.sibling())
    other_copy.start()

    for name in ("small", "back", "xhat", "inv", "top", "mixer", "mixed"):
        loads[name].wait()
    gain_a, gain_b = small[0:1, :D], small[1:2, :D]
    gain_sum[...] = jnp.zeros_like(gain_sum)
    for grad in grads.values():
        if grad.full != grad.m and grad.summed is None:
            grad.acc[grad.m :, :] = jnp.zeros((grad.full - grad.m, grad.acc.shape[1]), jnp.bfloat16)

    def norm_back(grad, normed, scale, gain):
        scaled = grad * gain
        mean_a = jnp.mean(scaled, axis=-1, keepdims=True)
        mean_b = jnp.mean(scaled * normed, axis=-1, keepdims=True)
        return scale * (scaled - mean_a - normed * mean_b)

    def own_of(value):
        return jnp.where(p.core == 0, value[:, : D // 2], value[:, D // 2 :])

    def second_norm(i):
        cut = slice(i * BLOCK, (i + 1) * BLOCK)
        swap_block(i, back_ref, other, back_send, back_recv).wait_recv()
        grad = xc[cut, :].astype(jnp.float32) + other[cut, :].astype(jnp.float32)
        normed = xa[cut, :].astype(jnp.float32)
        gain_sum[1:2, :] += jnp.sum(grad * normed, axis=0, keepdims=True)
        value = xb[cut, :].astype(jnp.float32) + norm_back(grad, normed, inv[cut, 0:1], gain_b)
        keep_grad[cut, :] = own_of(value)
        value = value.astype(jnp.bfloat16)
        middle_low[cut, :] = value
        mixed_grad[cut, :] = dot(value, wm[...], NT).astype(jnp.bfloat16)
    second_norm(0)
    second_norm(1)
    run(("begin_y", "S", 0))
    second_norm(2)
    second_norm(3)
    pl.semaphore_signal(swap_credit, inc=1, device_id=p.sibling(), device_id_type=MESH_ID)
    run(("begin_x", "S", 2))
    @pl.loop(0, D // BLOCK)
    def _(d):
        cut = block_rows(d)
        g_mixer[:, cut] = dot(mixed[...], middle_low[:, cut], TN).astype(jnp.bfloat16)

    load("first", first_ref, xa)
    for j in range(rows):
        load(f"tokens{j}", tokens_ref.at[j], xb.at[:, pl.ds(j * width, width)])

    def leave(src, dst, send, recv):
        core, seq = p.row // seqs, lax.rem(p.row, seqs)
        copies = []
        for u in range(seqs):
            row = p.core * seqs + u
            is_self = jnp.logical_and(core == p.core, row == p.row)
            piece = src.at[:, pl.ds(u * width, width)]
            copies.append((is_self, piece, dst(seq), send.at[u], recv.at[seq], p.at(core=core, row=row)))
        return copies

    def leave_start(copies):
        for is_self, piece, place, send, recv, target in copies:
            @pl.when(is_self)
            def _():
                pltpu.make_async_copy(piece, place, recv).start()

            @pl.when(jnp.logical_not(is_self))
            def _():
                remote(piece, place, send, recv, target).start()

    def leave_wait(copies, dst, recv):
        for s in range(seqs):
            pltpu.make_async_copy(dst(s), dst(s), recv.at[s]).wait()
        for is_self, piece, place, send, recv_sem, target in copies:
            @pl.when(jnp.logical_not(is_self))
            def _():
                remote(piece, place, send, recv_sem, target).wait_send()

    out_at = lambda s: o_block.at[pl.ds(pl.multiple_of(s * LEN, LEN), LEN), :]
    in_at = lambda s: o_input.at[pl.ds(pl.multiple_of(s * LEN, LEN), LEN), :]
    out_copies = leave(block_half, out_at, out_send, out_recv)
    in_copies = leave(mixed_grad, in_at, in_send, in_recv)

    def block_output():
        loads["own"].wait()
        other_copy.wait()
        add_rows(LEN, block_half, own_half, block_half)
        leave_start(out_copies)

    for name in ("q", "k", "v", "lse", "table"):
        loads[name].wait()
    columns = small[:, D:].T
    segment_col = columns[:, 1:2]

    def attention_start(pair):
        cols = slice(pair * PAIR, (pair + 1) * PAIR)
        product = mixed[:, cols].astype(jnp.float32) * mixed_grad[:, cols].astype(jnp.float32)
        chooser = lax.broadcasted_iota(jnp.int32, (8, PAIR), 0) == lanes_of((8, PAIR)) // HD
        delta[...] = dot(chooser.astype(jnp.float32), product, NT, precision=lax.Precision.HIGHEST)
        k_t[...] = k_s[:, cols].astype(jnp.float32).T.astype(jnp.bfloat16)
        dk[...] = jnp.zeros_like(dk)
        dv[...] = jnp.zeros_like(dv)

    def attention_head(pair, head):
        cols = slice(pair * PAIR, (pair + 1) * PAIR)
        keys, values = k_s[:, cols], v_s[:, cols]
        lanes = slice(head * HD, (head + 1) * HD)
        for i in range(LEN // BLOCK):
            cut = slice(i * BLOCK, (i + 1) * BLOCK)
            q_part, g_part = only_head(q_s[cut, cols], head), only_head(mixed_grad[cut, cols], head)
            scores = dot(keys, q_part, NT)
            probs = jnp.exp2(scores * TO_EXP2 - lse[pair, head : head + 1, cut])
            probs = jnp.where(segment_col == small[1:2, D + i * BLOCK : D + (i + 1) * BLOCK], probs, 0.0)
            probs_grad = dot(values, g_part, NT)
            scores_grad = (probs * (probs_grad - delta[head : head + 1, cut])).astype(jnp.bfloat16)
            dv[...] += dot(probs.astype(jnp.bfloat16), g_part)
            dk[...] += dot(scores_grad, q_part)
            dq_t[lanes, cut] = dot(k_t[lanes, :], scores_grad)

    def attention_end(pair):
        cols = slice(pair * PAIR, (pair + 1) * PAIR)
        cosine, sine = table[0], table[1]
        scale = 1.0 / math.sqrt(HD)
        dqs = dq_t[...].T * scale
        q_s[:, cols] = (dqs * cosine - swap_halves(dqs) * sine).astype(jnp.bfloat16)
        dks = dk[...] * scale
        k_s[:, cols] = (dks * cosine - swap_halves(dks) * sine).astype(jnp.bfloat16)
        v_s[:, cols] = dv[...].astype(jnp.bfloat16)

    def joined_weight_grad(h):
        @pl.loop(0, D // BLOCK)
        def _(d):
            cut = block_rows(d)
            part = xa[:, cut]
            for j, back in enumerate((q_s, k_s, v_s)):
                g_joined[h, cut, j * half : (j + 1) * half] = dot(
                    part, back[:, h * half : (h + 1) * half], TN
                ).astype(jnp.bfloat16)

    run(("sum_both", "E", 0))
    attention_start(0)
    attention_head(0, 0)
    attention_head(0, 1)
    attention_end(0)
    attention_start(1)
    attention_head(1, 0)
    attention_head(1, 1)
    attention_end(1)
    run(("z0", "E", 0), ("sum_x", "E", 1), ("sum_y", "E", 1))
    loads["first"].wait()
    joined_weight_grad(0)
    attention_start(2)
    attention_head(2, 0)
    run(
        ("begin_y", "M", 0), ("begin_x", "J", 0), ("sum_y", "S", 2), ("sum_x", "S", 2), ("begin_y", "J", 0),
        ("z1", "E", 0), ("sum_x", "S", 0), ("sum_both", "E", 1),
    )
    attention_head(2, 1)
    attention_end(2)
    attention_start(3)
    attention_head(3, 0)
    attention_head(3, 1)
    attention_end(3)
    run(
        ("sum_both", "S", 2), ("sum_x", "J", 0), ("z0", "E", 1), ("sum_y", "S", 0), ("z0", "S", 2),
        ("sum_both", "S", 0), ("g1", "E", 0), ("begin_x", "E", 2), ("sum_x", "E", 2), ("sum_y", "J", 0),
        ("sum_y", "E", 2), ("z1", "E", 1), ("sum_both", "J", 0), ("sum_both", "E", 2),
    )
    joined_weight_grad(1)
    run(
        ("begin_x", "J", 1), ("begin_y", "J", 1), ("z1", "S", 2), ("z0", "S", 0), ("begin_y", "S", 1),
        ("z0", "J", 0), ("g1", "E", 1), ("sum_x", "J", 1), ("sum_y", "J", 1), ("z1", "S", 0), ("begin_x", "M", 0),
    )
    loads["joined"].wait()
    pl.semaphore_wait(swap_credit, 1)

    def first_back(i):
        cut = slice(i * BLOCK, (i + 1) * BLOCK)
        value = jnp.zeros((BLOCK, D), jnp.float32)
        for h in range(2):
            for j, part in enumerate((q_s, k_s, v_s)):
                value = value + dot(part[cut, h * half : (h + 1) * half], wj[h, j], NT)
        xc[cut, :] = value.astype(jnp.bfloat16)
        swap_block(i, xc, other, first_send, first_recv).start()

    first_back(0)
    first_back(1)

    run(
        ("g0", "E", 0), ("g1", "S", 2), ("z0", "E", 2), ("sum_both", "J", 1), ("z1", "J", 0), ("g1", "S", 0),
        ("begin_x", "S", 1), ("sum_x", "M", 0), ("sum_y", "M", 0), ("sum_y", "S", 1), ("z1", "E", 2), ("g1", "J", 0),
        ("g0", "S", 2), ("sum_x", "S", 1), ("z0", "J", 1), ("sum_both", "M", 0),
    )
    first_back(2)
    first_back(3)
    run(("store", "E", 0), ("sum_both", "S", 1), ("g0", "E", 1), ("g1", "E", 2), ("z1", "J", 1))
    for j in range(rows):
        loads[f"tokens{j}"].wait()
    for i in range(blocks_n):
        cut = slice(i * BLOCK, (i + 1) * BLOCK)
        swap_block(i, xc, other, first_send, first_recv).wait_recv()
        grad = xc[cut, :].astype(jnp.float32) + other[cut, :].astype(jnp.float32)
        values = xb[cut, :].astype(jnp.float32)
        values = values - jnp.mean(values, axis=-1, keepdims=True)
        scale = lax.rsqrt(jnp.mean(values * values, axis=-1, keepdims=True) + norm_eps)
        normed = values * scale
        gain_sum[0:1, :] += jnp.sum(grad * normed, axis=0, keepdims=True)
        total = keep_grad[cut, :] + own_of(norm_back(grad, normed, scale, gain_a))
        mixed_grad[cut, :] = total.astype(jnp.bfloat16)

    def gain_copies():
        return [
            remote(gain_sum.at[:, pl.ds(pl.multiple_of(p.row_after(s) * width, width), width)], gain_y.at[s],
                   gain_send.at[s], gain_recv.at[s], p.at(row=p.row_after(s)))
            for s in range(1, rows)
        ]

    gain_across = remote(gain_x.at[0], gain_x.at[1], gain_send.at[rows], gain_recv.at[rows], p.across())
    gain_total = gain_z.at[2 * levels]
    gain_back = remote(gain_total, gain_total, gain_send.at[rows + 1 + levels], gain_recv.at[rows + 1 + levels], p.sibling())

    def gain_plane(level):
        return remote(gain_z.at[2 * level], gain_z.at[2 * level + 1], gain_send.at[rows + 1 + level],
                      gain_recv.at[rows + 1 + level], p.mate(level))

    def gains_y():
        for s in range(1, rows):
            remote(gain_y.at[s], gain_y.at[s], gain_send.at[s], gain_recv.at[s], p.sibling()).wait_recv()
        total = gain_sum[:, pl.ds(pl.multiple_of(p.row * width, width), width)]
        for s in range(1, rows):
            total = total + gain_y[s]
        gain_x[0] = total
        pl.when(p.matched)(gain_across.start)

    def gains_x():
        @pl.when(jnp.logical_not(p.matched))
        def _():
            gain_across.wait_recv()
            gain_z[0] = gain_x[0] + gain_x[1]
            gain_plane(0).start()

    def gains_z():
        @pl.when(jnp.logical_not(p.matched))
        def _():
            for level in range(levels):
                gain_plane(level).wait()
                gain_z[2 * level + 2] = gain_z[2 * level] + gain_z[2 * level + 1]
                if level + 1 < levels:
                    gain_plane(level + 1).start()
            gain_back.start()
            gain_back.wait_send()

    def gains_end():
        @pl.when(p.matched)
        def _():
            gain_back.wait_recv()
            gain_across.wait_send()

    for copy in gain_copies():
        copy.start()
    leave_start(in_copies)

    run(
        ("z0", "S", 1), ("g1", "J", 1), ("z0", "M", 0), ("g0", "J", 1), gains_y, ("store", "S", 2), ("z1", "S", 1),
        ("store", "E", 1), ("z1", "M", 0), ("g1", "S", 1), gains_x, ("g0", "E", 2), block_output, ("g0", "S", 1),
        ("g0", "S", 0), ("store", "J", 1), ("g0", "J", 0), gains_z, ("store", "S", 0), ("store", "J", 0),
        ("g1", "M", 0), ("store", "E", 2), ("store", "S", 1), ("g0", "M", 0), ("store", "M", 0),
    )
    gains_end()
    gains_out = pltpu.make_async_copy(gain_z.at[2 * levels], o_gains, out_sem.at[len(stores)])
    gains_out.start()

    leave_wait(out_copies, out_at, out_recv)
    leave_wait(in_copies, in_at, in_recv)
    for i in range(blocks_n):
        swap_block(i, back_ref, other, back_send, back_recv).wait_send()
        swap_block(i, xc, other, first_send, first_recv).wait_send()
    for copy in gain_copies():
        copy.wait_send()
    for grad in grads.values():
        grad.drain()
    for copy in stores:
        copy.wait()
    gains_out.wait()


def backward(saved, chunks):
    (tokens, first, queries, keys, values, mixed, lse, xhat, inv, top, own, other, back, expand, shrink, joined, mixer,
     small, table, plane_sum) = saved
    rows = lax.axis_size("row")
    planes = lax.axis_size("dp") // CORES
    seqs = rows // CORES
    width = D // rows
    wide = queries.shape[1]
    pairs = wide // PAIR
    hidden_here = sum(chunks)
    widest = 2 * max(chunks)
    levels = (planes - 1).bit_length()
    bf16, f32 = jnp.bfloat16, jnp.float32
    V, dma = pltpu.VMEM, pltpu.SemaphoreType.DMA
    outs = [
        ((seqs * LEN, width), bf16), ((seqs * LEN, width), bf16), ((3, width, wide), bf16), ((wide, width), bf16),
        ((2, hidden_here, width), bf16), ((hidden_here, width), bf16), ((8, width), f32),
    ]
    grad_shapes = []
    for lanes in chunks:
        grad_shapes += [(2 * lanes, width), (lanes, width)]
    grad_shapes += [(width, 3 * wide // 2)] * 2 + [(wide, width)]
    count = len(grad_shapes)
    scratch = [
        V((LEN, wide), bf16), V((LEN, wide), bf16), V((LEN, wide), bf16), V((LEN, wide), bf16),
        V((LEN, D), bf16), V((LEN, D), bf16), V((LEN, D), bf16), V((2, 3, D, wide // 2), bf16), V((wide, D), bf16),
        V((pairs, 2, LEN), f32), V((LEN, PAIR), f32), V((8, D + LEN), f32), V((2, LEN, PAIR), f32), V((LEN, D), bf16),
        V((LEN, D // 2), f32), V((LEN, D), bf16), V((LEN, wide), bf16), V((wide, D), bf16), V((2, D, 3 * wide // 2), bf16),
        V((LEN, PAIR), f32), V((LEN, PAIR), f32), V((PAIR, LEN), f32), V((PAIR, LEN), bf16), V((8, LEN), f32),
        V((LEN, D // 2), f32), V((LEN, D // 2), bf16),
        V((8, D), f32), V((rows, 8, width), f32), V((2, 8, width), f32), V((2 * levels + 1, 8, width), f32),
        V((2, widest - first_share(widest), width), bf16),
        [grad_bufs(*shape, rows, planes, i == 0) for i, shape in enumerate(grad_shapes)],
        dma((15 + rows,)), dma((2,)), dma, dma((count, 14, max(rows, levels))), pltpu.SemaphoreType.REGULAR((count, levels)),
        pltpu.SemaphoreType.REGULAR,
        dma((4,)), dma((4,)), dma, dma, dma((4,)), dma((4,)),
        dma((seqs,)), dma((seqs,)), dma((seqs,)), dma((seqs,)), dma((rows + 2 + levels,)), dma((rows + 2 + levels,)),
        dma((3 * len(chunks) + 8,)),
    ]
    anywhere = pl.BlockSpec(memory_space=pl.ANY)
    return pl.pallas_call(
        functools.partial(backward_kernel, chunks),
        in_specs=[anywhere] * len(saved),
        out_specs=[anywhere] * len(outs),
        out_shape=[jax.ShapeDtypeStruct(*o) for o in outs],
        scratch_shapes=scratch,
        compiler_params=pltpu.CompilerParams(
            collective_id=1, has_side_effects=True, vmem_limit_bytes=62 * 1024 * 1024
        ),
        name="layer_backward",
    )(*saved)


def finish_kernel(*refs):
    count = len(refs) // 2
    gains_ref, firsts, seconds = refs[count - 1], *refs[-2:]
    for src, dst in zip(refs[: count - 1], refs[count:]):
        dst[...] = src[...].astype(dst.dtype)
    firsts[...] = gains_ref[0:1, :]
    seconds[...] = gains_ref[1:2, :]


def finish(block, *rest):
    steps = 4
    *grads, gains = rest
    arrays = [x.reshape(-1, x.shape[-1]) for x in (block, *grads)]

    def spec(x):
        parts = next(n for n in (steps, steps // 2, 1) if x.shape[0] % (16 * n) == 0)
        return pl.BlockSpec((x.shape[0] // parts, x.shape[1]), lambda i: (i * parts // steps, 0))

    whole = lambda rows: pl.BlockSpec((rows, gains.shape[1]), lambda i: (0, 0))
    shape = jax.ShapeDtypeStruct
    outs = pl.pallas_call(
        finish_kernel,
        grid=(steps,),
        in_specs=[spec(x) for x in arrays] + [whole(8)],
        out_specs=[spec(x) for x in arrays] + [whole(1)] * 2,
        out_shape=[shape(arrays[0].shape, block.dtype)]
        + [shape(x.shape, jnp.float32) for x in arrays[1:]]
        + [shape((1, gains.shape[1]), jnp.float32)] * 2,
        compiler_params=pltpu.CompilerParams(vmem_limit_bytes=60 * 1024 * 1024),
        name="layer_finish",
    )(*arrays, gains)
    return [out.reshape(x.shape) for out, x in zip(outs, (block, *grads))] + [outs[-2][0], outs[-1][0]]


def shards(
    tokens_in, lengths, first_gain, joined_weight, mixer_weight, second_gain, expand_weight, shrink_weight, cotangent
):
    rows, cols = lax.axis_size("row"), lax.axis_size("col")
    hidden_here = shrink_weight.shape[0]
    assert tokens_in.shape[0] * CORES == LEN * rows and cols == CORES
    chunks = (512, 512, hidden_here - 1024)
    joined_here = joined_weight.transpose(1, 0, 2)
    expand_here = expand_weight.transpose(1, 2, 0)
    saved = forward(
        tokens_in, cotangent, lengths, first_gain, second_gain, joined_here, mixer_weight, expand_here, shrink_weight, chunks
    )
    block_output, input_grad, joined_grad, mixer_grad, expand_grad, shrink_grad, *gains = finish(*backward(saved, chunks))
    return (
        block_output,
        input_grad,
        joined_grad.transpose(1, 0, 2),
        mixer_grad,
        expand_grad.transpose(2, 0, 1),
        shrink_grad,
        gains[0],
        gains[1],
    )


def solution(mesh):
    placed = (
        P(("dp", "col"), "row"),
        P("dp", None),
        P("row"),
        P("row", None, "col"),
        P("col", "row"),
        P("row"),
        P("row", None, "col"),
        P("col", "row"),
        P(("dp", "col"), "row"),
    )
    return jax.shard_map(
        shards,
        mesh=mesh,
        in_specs=placed,
        out_specs=(
            P(("dp", "col"), "row"),
            P(("dp", "col"), "row"),
            P("row", None, "col"),
            P("col", "row"),
            P("row", None, "col"),
            P("col", "row"),
            P("row"),
            P("row"),
        ),
        check_vma=False,
    )
```

```python
import functools
import math

import jax
import jax.numpy as jnp
import numpy as np
from jax import lax
from jax.experimental import pallas as pl
from jax.experimental.pallas import tpu as pltpu
from jax.sharding import PartitionSpec as P

D = 1024
HEADS = 16
HD = 64
FF = 2624
LEN = 1024
DOCS = 6
MOST = 800
CORES = 2

rope_base = 160000.0
norm_eps = 1e-05
masked_value = -1000000000.0

PAIR = 2 * HD
WIDE = 256
SOLID = MOST // WIDE * WIDE
REST = LEN - MOST
TO_EXP2 = math.log2(math.e) / math.sqrt(HD)

NT = (((1,), (1,)), ((), ()))
TN = (((0,), (0,)), ((), ()))
MESH_AXES = ("dp", "row", "col")


def lanes_of(shape):
    return lax.broadcasted_iota(jnp.int32, shape, len(shape) - 1)


def swap_halves(u):
    low_half = lanes_of(u.shape) % HD < HD // 2
    return jnp.where(low_half, pltpu.roll(u, u.shape[1] - HD // 2, 1), pltpu.roll(u, HD // 2, 1))


def dot(left, right, dims=(((1,), (0,)), ((), ())), **more):
    return lax.dot_general(left, right, dims, preferred_element_type=jnp.float32, **more)


def only_head(values, head):
    return jnp.where(lanes_of(values.shape) // HD == head, values, jnp.zeros_like(values))


MESH_ID = pl.DeviceIdType.MESH
BLOCK = 256
WIDE_BLOCK = 512


class Place:
    def __init__(self):
        self.rows, self.cols = lax.axis_size("row"), lax.axis_size("col")
        self.planes = lax.axis_size("dp") // CORES
        dp = lax.axis_index("dp")
        self.z, self.core = dp // CORES, dp % CORES
        self.row, self.col = lax.axis_index("row"), lax.axis_index("col")
        self.matched = self.core == self.col
        self.parity = self.z % 2
        self.inner = self.parity != (self.z // 2) % 2
        self.seqs = self.rows // CORES

    def at(self, z=None, core=None, row=None, col=None):
        z = self.z if z is None else z
        core = self.core if core is None else core
        return (z * CORES + core, self.row if row is None else row, self.col if col is None else col)

    def sibling(self):
        return self.at(core=1 - self.core)

    def across(self):
        return self.at(col=1 - self.col)

    def pair(self):
        return self.at(z=self.z + 1 - 2 * self.parity)

    def row_after(self, step):
        return lax.rem(self.row + step, self.rows)

    def row_before(self, step):
        return lax.rem(self.row + self.rows - step, self.rows)

    def group_bit(self, level):
        return lax.rem(self.z // (1 << level), 2)

    def mate(self, level):
        if level == 0:
            return self.pair()
        group = self.z // 2
        other = group + (1 << (level - 1)) * (1 - 2 * self.group_bit(level))
        shift = lax.rem(group, 2) + self.parity
        return self.at(z=2 * other + lax.rem(shift + lax.rem(other, 2), 2))

    def barrier(self, partners):
        sem = pltpu.get_barrier_semaphore()
        count = CORES * self.rows
        partners = list(partners)
        for step in range(1, count):
            flat = lax.rem(self.core * self.rows + self.row + step, count)
            partners.append(self.at(core=flat // self.rows, row=lax.rem(flat, self.rows)))
        for partner in partners:
            pl.semaphore_signal(sem, inc=1, device_id=partner, device_id_type=MESH_ID)
        pl.semaphore_wait(sem, len(partners))


def remote(src, dst, send, recv, target):
    return pltpu.make_async_remote_copy(
        src_ref=src, dst_ref=dst, send_sem=send, recv_sem=recv, device_id=target, device_id_type=MESH_ID
    )


def shares(count, part):
    one = int(count * part) // 16 * 16
    return count - 2 * one, one


class Weight:
    def __init__(self, place, source, slot, count, sems, index, part):
        self.place, self.source, self.slot = place, source, slot
        self.both, self.one = shares(count, part)
        self.sems = sems
        self.index = index
        self.local = sems[5].at[index]

    def sem(self, kind, row):
        return self.sems[kind].at[self.index, row]

    def plane_part(self):
        return self.place.parity * self.one, self.one + self.both

    def pair_part(self):
        return self.place.parity * (self.one + self.both), self.one

    def other_part(self):
        return (1 - self.place.parity) * (self.one + self.both), self.one

    def own_y(self):
        p = self.place
        start, size = self.plane_part()
        for step in range(1, p.rows):
            remote(
                self.source(start, size),
                self.slot(p.row, start, size),
                self.sem(0, step),
                self.sem(3, p.row),
                p.at(row=p.row_after(step)),
            ).start()

    def own_x(self):
        p = self.place
        start, size = self.plane_part()
        remote(
            self.source(start, size), self.slot(p.row, start, size), self.sem(1, 0), self.sem(3, p.row), p.across()
        ).start()
        pltpu.make_async_copy(
            self.source(0, 2 * self.one + self.both), self.slot(p.row, 0, 2 * self.one + self.both), self.local
        ).start()

    def pass_on(self):
        p = self.place
        for step in range(1, p.rows):
            row = p.row_before(step)
            self.wait_plane(row)
            self.send_across(row, step).start()
            self.send_pair(row, step).start()

    def take_first(self):
        self.wait_plane(self.place.row)
        self.send_pair(self.place.row, 0).start()

    def take_others(self):
        p = self.place
        for step in range(1, p.rows):
            row = p.row_before(step)
            self.wait_plane(row)
            self.send_pair(row, step).start()

    def wait_plane(self, row):
        p = self.place
        start, size = self.plane_part()
        piece = self.slot(row, start, size)
        remote(piece, piece, self.sem(0, 0), self.sem(3, row), p.across()).wait_recv()

    def send_pair(self, row, step):
        start, size = self.pair_part()
        piece = self.slot(row, start, size)
        return remote(piece, piece, self.sem(2, step), self.sem(4, row), self.place.pair())

    def send_across(self, row, step):
        start, size = self.plane_part()
        piece = self.slot(row, start, size)
        return remote(piece, piece, self.sem(1, step), self.sem(3, row), self.place.across())

    def finish(self):
        p = self.place
        start, size = self.other_part()

        def wait_other(row):
            piece = self.slot(row, start, size)
            remote(piece, piece, self.sem(2, 0), self.sem(4, row), p.pair()).wait_recv()

        for step in range(1, p.rows):
            wait_other(p.row_before(step))

        @pl.when(p.matched)
        def _():
            whole = self.slot(p.row, 0, 2 * self.one + self.both)
            pltpu.make_async_copy(whole, whole, self.local).wait()

        @pl.when(jnp.logical_not(p.matched))
        def _():
            wait_other(p.row)

    def drain(self):
        p = self.place
        start, size = self.plane_part()
        piece = self.slot(p.row, start, size)
        for step in range(1, p.rows):
            self.send_pair(p.row, step).wait_send()

        @pl.when(p.matched)
        def _():
            for step in range(1, p.rows):
                remote(piece, piece, self.sem(0, step), self.sem(3, p.row), p.across()).wait_send()
            for step in range(p.rows):
                self.send_across(p.row, step).wait_send()

        @pl.when(jnp.logical_not(p.matched))
        def _():
            self.send_pair(p.row, 0).wait_send()


def add_rows(count, target, *parts):
    step = next(s for s in (64, 32, 16) if count % s == 0)

    @pl.loop(0, count // step)
    def _(i):
        cut = pl.ds(pl.multiple_of(i * step, step), step)
        total = parts[0][cut, :].astype(jnp.float32)
        for part in parts[1:]:
            total = total + part[cut, :].astype(jnp.float32)
        target[cut, :] = total.astype(target.dtype)


def first_share(count, share=5 / 16):
    return int(count * share) // 16 * 16


class Grad:
    def __init__(self, place, block, rows, bufs, sems, credits, index, stage=None, summed=None, share=5 / 16):
        self.p, self.block, self.m, self.index, self.sems, self.stage = place, block, rows, index, sems, stage
        self.credits, self.summed = credits, summed
        self.a = first_share(rows, share)
        self.b = rows - self.a
        self.recv_a, self.recv_b, self.acc, self.more, self.zbuf = bufs
        self.levels = (place.planes - 1).bit_length()
        self.full = self.acc.shape[0]

    def sem(self, kind, at=0):
        return self.sems.at[self.index, kind, at]

    def low(self):
        return self.acc.at[pl.ds(0, self.a), :]

    def high(self):
        return self.acc.at[pl.ds(self.a, self.b), :]

    def send(self, src, dst, kind, at, target):
        return remote(src, dst, self.sem(kind, at), self.sem(kind + 1, at), target)

    def landed(self, buf, kind, at=0):
        self.send(buf, buf, kind, at, self.p.sibling()).wait_recv()

    def left(self, buf, kind, at=0):
        self.send(buf, buf, kind, at, self.p.sibling()).wait_send()

    def copies_y(self):
        p = self.p
        return [
            self.send(self.block(p.row_after(s), 0, self.a), self.recv_a.at[s - 1], 0, s, p.at(row=p.row_after(s)))
            for s in range(1, p.rows)
        ]

    def copies_x(self):
        return [
            self.send(self.block(j, self.a, self.b), self.recv_b.at[j], 2, j, self.p.across())
            for j in range(self.p.rows)
        ]

    def begin_y(self):
        for copy in self.copies_y():
            copy.start()

    def begin_x(self):
        @pl.when(jnp.logical_not(self.p.matched))
        def _():
            for copy in self.copies_x():
                copy.start()

    def own(self, row, start, size, slot):
        piece = self.block(row, start, size)
        if self.stage is None:
            return piece, []
        buf, sem = self.stage
        buf = buf.at[slot, pl.ds(0, size), :]
        copy = pltpu.make_async_copy(piece, buf, sem.at[slot])
        copy.start()
        return buf, [copy]

    def sum_y(self):
        p = self.p
        own, copies = self.own(p.row, 0, self.a, 0)
        for s in range(1, p.rows):
            self.landed(self.recv_a.at[s - 1], 0, s)
        for copy in copies:
            copy.wait()
        add_rows(self.a, self.recv_a.at[0], own, *[self.recv_a.at[s - 1] for s in range(1, p.rows)])

        @pl.when(jnp.logical_not(p.matched))
        def _():
            self.send(self.recv_a.at[0], self.low(), 4, 0, p.across()).start()

    def sum_x(self):
        p = self.p

        @pl.when(p.matched)
        def _():
            steps = list(range(1, p.rows)) + [0]
            owns = [self.own(p.row_after(s), self.a, self.b, n) for n, s in enumerate(steps[:2])]
            for n, s in enumerate(steps):
                row = p.row_after(s)
                if n >= 2:
                    owns.append(self.own(row, self.a, self.b, n % 2))
                own, copies = owns[n]
                buf = self.recv_b.at[row]
                self.landed(buf, 2, row)
                for copy in copies:
                    copy.wait()
                add_rows(self.b, buf, own, buf)
                if s:
                    target = self.high() if s == 1 else self.more.at[s - 2]
                    self.send(buf, target, 6, s, p.at(row=row)).start()

    def span(self, level):
        start, size = 0, self.full
        for i in range(1, level + 1):
            size //= 2
            start = start + self.p.group_bit(i) * size
        return start, size

    def rows_of(self, start, size):
        return self.acc.at[pl.ds(pl.multiple_of(start, 16), size), :]

    def z_copy(self, level):
        if level == 0:
            return self.send(self.acc, self.zbuf[0], 8, 0, self.p.mate(0))
        start, size = self.span(level - 1)
        half = size // 2
        piece = self.rows_of(start + (1 - self.p.group_bit(level)) * half, half)
        return self.send(piece, self.zbuf[level], 8, level, self.p.mate(level))

    def z_back(self, level):
        piece = self.acc if level == 0 else self.rows_of(*self.span(level))
        return self.send(piece, piece, 10, level, self.p.mate(level))

    def z_free(self, level):
        self.z_copy(level).wait_send()
        pl.semaphore_signal(
            self.credits.at[self.index, level], inc=1, device_id=self.p.mate(level), device_id_type=MESH_ID
        )

    def z_return(self, level):
        pl.semaphore_wait(self.credits.at[self.index, level], 1)
        self.z_back(level).start()

    def plane_sum(self):
        p = self.p

        @pl.when(p.matched)
        def _():
            self.landed(self.low(), 4)
            add_rows(self.a, self.low(), self.low(), self.recv_a.at[0])
            others = []
            for s in range(1, p.rows):
                buf = self.high() if s == 1 else self.more.at[s - 2]
                self.landed(buf, 6, s)
                others.append(buf)
            add_rows(self.b, self.high(), self.recv_b.at[p.row], *others)

    def sum_both(self):
        p = self.p
        if self.summed is None:
            self.plane_sum()
        else:
            pl.when(p.matched)(self.summed.wait)

        @pl.when(jnp.logical_and(p.matched, jnp.logical_not(p.inner)))
        def _():
            self.z_copy(0).start()

    def z0(self):
        p = self.p

        @pl.when(jnp.logical_and(p.matched, p.inner))
        def _():
            self.landed(self.zbuf[0], 8, 0)
            add_rows(self.full, self.acc, self.acc, self.zbuf[0])
            if self.levels > 1:
                self.z_copy(1).start()
            else:
                self.z_return(0)
                self.final().start()

        @pl.when(jnp.logical_and(p.matched, jnp.logical_not(p.inner)))
        def _():
            self.z_free(0)

    def z1(self):
        @pl.when(jnp.logical_and(self.p.matched, self.p.inner))
        def _():
            for level in range(1, self.levels):
                start, size = self.span(level)
                self.landed(self.zbuf[level], 8, level)
                piece = self.rows_of(start, size)
                add_rows(size, piece, piece, self.zbuf[level])
                self.z_free(level)
                if level + 1 < self.levels:
                    self.z_copy(level + 1).start()
                else:
                    self.z_return(level)

    def g1(self):
        @pl.when(jnp.logical_and(self.p.matched, self.p.inner))
        def _():
            for level in range(self.levels - 1, 0, -1):
                start, size = self.span(level - 1)
                half = size // 2
                self.landed(self.rows_of(start + (1 - self.p.group_bit(level)) * half, half), 10, level)
                self.z_return(level - 1)
                if level == 1:
                    self.final().start()

    def g0(self):
        @pl.when(jnp.logical_and(self.p.matched, jnp.logical_not(self.p.inner)))
        def _():
            self.landed(self.acc, 10, 0)
            self.final().start()

    def final(self):
        return remote(self.acc, self.acc, self.sem(12), self.sem(13), self.p.sibling())

    def store(self, stores):
        @pl.when(jnp.logical_not(self.p.matched))
        def _():
            self.final().wait_recv()

        copies = [
            pltpu.make_async_copy(self.acc.at[pl.ds(row, rows), pl.ds(col, cols)], out, sem)
            for row, rows, col, cols, out, sem in stores
        ]
        for copy in copies:
            copy.start()
        return copies

    def drain_plane(self):
        p = self.p
        for copy in self.copies_y():
            copy.wait_send()

        @pl.when(jnp.logical_not(p.matched))
        def _():
            for copy in self.copies_x():
                copy.wait_send()
            self.left(self.recv_a.at[0], 4)

        @pl.when(p.matched)
        def _():
            for s in range(1, p.rows):
                self.left(self.recv_b.at[0], 6, s)

    def drain(self):
        p = self.p
        if self.summed is None:
            self.drain_plane()

        @pl.when(p.matched)
        def _():
            self.final().wait_send()

        @pl.when(jnp.logical_and(p.matched, p.inner))
        def _():
            for level in range(self.levels):
                self.z_back(level).wait_send()


def grad_rows(rows, planes):
    tile = 16 * max(1, planes // 2)
    return -(-rows // tile) * tile


def grad_bufs(rows, cols, blocks, planes, summed=False, share=5 / 16):
    a = first_share(rows, share)
    V = lambda *shape: pltpu.VMEM(shape, jnp.bfloat16)
    levels = (planes - 1).bit_length()
    full = grad_rows(rows, planes)
    none = V(16, 128)
    plane = [none, none] if summed else [V(blocks - 1, a, cols), V(blocks, rows - a, cols)]
    more = none if summed or blocks <= 2 else V(blocks - 2, rows - a, cols)
    return plane + [V(full, cols), more, [V(full >> i, cols) for i in range(levels)]]


def plane_bufs(rows, cols, blocks, planes):
    return grad_bufs(rows, cols, blocks, planes, False, 1 / 2)[:4]


def block_rows(i, size=BLOCK):
    return pl.ds(pl.multiple_of(i * size, size), size)


def gelu_parts(gate):
    phi = 0.5 * (1.0 + lax.erf(gate * (1.0 / math.sqrt(2.0))))
    return phi, jnp.exp(gate * gate * -0.5) * (1.0 / math.sqrt(2.0 * math.pi))


def forward_kernel(
    chunks,
    tokens_ref, cot_ref, lengths_ref, first_gain_ref, second_gain_ref, freq_ref, joined_ref, mixer_ref, expand_ref, shrink_ref,
    *rest,
):
    n_chunks = len(chunks)
    outs, scratch = rest[:20], rest[20:]
    (o_tokens, o_first, o_q, o_k, o_v, o_mixed, o_lse, o_xhat, o_inv, o_top, o_own, o_other, o_back,
     o_expand, o_shrink, o_joined, o_mixer, o_small, o_table, o_sum) = outs
    (tok, cot, meta_src, meta, gains_ref, gains, table, first, wj, wm, wg, wu, ws, q_s, k_s, v_s, v_t, out_t, lse, mixed, xhat, inv, second,
     top, shrunk, back, other_half, hid, dgate, dup, g_expand, g_shrink, sum_bufs, sum_sem,
     tok_send, tok_recv, cot_send, cot_recv, swap_send, meta_send, meta_recv, gain_send, gain_recv,
     w_y, w_x, w_z, w_recv, w_recv_z, w_local, mix_send, mix_recv, mixed_send, mixed_recv, out_sem) = scratch
    p = Place()
    rows, seqs = p.rows, p.seqs
    width = tokens_ref.shape[1]
    wide = q_s.shape[1]
    pairs = wide // PAIR
    sems = (w_y, w_x, w_z, w_recv, w_recv_z, w_local)

    def down(ref, buf, col, size):
        source = lambda start, n: ref.at[:, pl.ds(start, n), pl.ds(col, size)]
        slot = lambda row, start, n: buf.at[:, pl.ds(row * width + start, n), :]
        return source, slot

    def along(ref, buf, at):
        source = lambda start, n: ref.at[pl.ds(at + start, n), :]
        slot = lambda row, start, n: buf.at[pl.ds(start, n), pl.ds(pl.multiple_of(row * width, width), width)]
        return source, slot

    half = wide // 2
    joined = [Weight(p, *down(joined_ref, wj.at[h], half * h, half), width, sems, h, 0.25) for h in range(2)]
    mixer = Weight(p, *along(mixer_ref, wm.at[p.core], 0), wide, sems, 2, 0.41)
    groups, at = [], 0
    for i, count in enumerate(chunks):
        groups.append([
            Weight(p, *along(ref, buf, at), count, sems, 3 + 3 * i + n, 0.41)
            for n, (ref, buf) in enumerate(((expand_ref.at[0], wg[i]), (expand_ref.at[1], wu[i]), (shrink_ref, ws[i])))
        ])
        at += count

    place_row = lanes_of((1, LEN))
    for s in range(seqs):
        base = [lengths_ref[p.col * seqs + s, d] for d in range(DOCS)]
        segment = jnp.zeros((1, LEN), jnp.int32)
        start = jnp.zeros((1, LEN), jnp.int32)
        end = jnp.int32(0)
        for d in range(DOCS):
            end = end + base[d]
            past = place_row >= end
            segment = segment + past.astype(jnp.int32)
            start = jnp.where(past, end, start)
        meta_src[s, 0:1, :] = (place_row - start).astype(jnp.float32)
        meta_src[s, 1:2, :] = segment.astype(jnp.float32)
        meta_src[s, 2:3, :] = (segment < DOCS - 1).astype(jnp.float32)
        meta_src[s, 3:8, :] = jnp.zeros((5, LEN), jnp.float32)

    gains_ref[0:1, :] = first_gain_ref[...]
    gains_ref[1:2, :] = second_gain_ref[...]
    gains_ref[2:8, :] = jnp.zeros((6, width), jnp.float32)
    p.barrier([p.across(), p.pair()])

    is_here = p.core == p.row // seqs

    blocks = range(LEN // BLOCK)

    def send_seq(ref, buf, send, recv, block):
        for t in range(seqs):
            seq = lax.rem(p.row + t, seqs)
            piece = ref.at[pl.ds(pl.multiple_of(seq * LEN + block * BLOCK, BLOCK), BLOCK), :]
            place = buf.at[p.row, pl.ds(block * BLOCK, BLOCK), :]
            target = p.at(core=p.row // seqs, row=p.core * seqs + seq)

            def away():
                remote(piece, place, send.at[t, block], recv.at[p.row, block], target).start()

            if t:
                away()
            else:
                pl.when(jnp.logical_not(is_here))(away)

                @pl.when(is_here)
                def _():
                    pltpu.make_async_copy(piece, place, recv.at[p.row, block]).start()

    def swap_seq(buf, slot, recv, swap, u, block):
        piece = buf.at[slot, pl.ds(block * BLOCK, BLOCK), :]
        return remote(piece, piece, swap.at[u, block], recv.at[slot, block], p.sibling())

    def take_seq(buf, recv, swap, block):
        for u in range(seqs):
            slot = p.core * seqs + u
            piece = buf.at[slot, pl.ds(block * BLOCK, BLOCK), :]
            pltpu.make_async_copy(piece, piece, recv.at[slot, block]).wait()
            swap_seq(buf, slot, recv, swap, u, block).start()

    def finish_seq(buf, recv, swap, block):
        for u in range(seqs):
            swap_seq(buf, (1 - p.core) * seqs + u, recv, swap, u, block).wait_recv()

    def drain_seq(buf, send, recv, swap):
        for block in blocks:
            piece = buf.at[0, pl.ds(0, BLOCK), :]
            for u in range(seqs):
                swap_seq(buf, 0, recv, swap, u, block).wait_send()
                if u:
                    remote(piece, piece, send.at[u, block], recv.at[0, block], p.sibling()).wait_send()

            @pl.when(jnp.logical_not(is_here))
            def _():
                remote(piece, piece, send.at[0, block], recv.at[0, block], p.sibling()).wait_send()

    sends_meta = lax.rem(p.row, seqs) == 0

    @pl.when(sends_meta)
    def _():
        for t in range(seqs):
            target = p.at(core=p.row // seqs, row=p.core * seqs + t)

            def away():
                remote(meta_src.at[t], meta, meta_send.at[t], meta_recv, target).start()

            if t:
                away()
            else:
                pl.when(jnp.logical_not(is_here))(away)

                @pl.when(is_here)
                def _():
                    pltpu.make_async_copy(meta_src.at[t], meta, meta_recv).start()

    for step in range(1, rows):
        remote(gains_ref, gains.at[p.row], gain_send.at[step], gain_recv.at[p.row], p.at(row=p.row_after(step))).start()
    pltpu.make_async_copy(gains_ref, gains.at[p.row], gain_recv.at[p.row]).start()
    def service(matched, unmatched):
        for here, actions in ((p.matched, matched), (jnp.logical_not(p.matched), unmatched)):
            if actions:

                @pl.when(here)
                def _():
                    for action in actions:
                        action()

    tokens_of = [functools.partial(send_seq, tokens_ref, tok, tok_send, tok_recv, block) for block in blocks]
    cot_of = [functools.partial(send_seq, cot_ref, cot, cot_send, cot_recv, block) for block in blocks]
    j0, j1 = joined
    (g0, u0, s0), (g1, u1, s1), (g2, u2, s2) = groups

    def each(action, *weights):
        return [functools.partial(getattr(weight, action)) for weight in weights]

    service(
        [g0.own_x, tokens_of[3], j1.own_x, j0.own_x, j0.own_y, tokens_of[1], j0.pass_on, tokens_of[2], tokens_of[0], g0.own_y, j1.own_y],
        [g0.take_first, tokens_of[2], tokens_of[0], tokens_of[1], j0.take_first],
    )

    def gain_of(kind):
        return jnp.concatenate([gains[j, kind : kind + 1, :] for j in range(rows)], axis=1)

    def norm(values):
        center = jnp.mean(values, axis=-1, keepdims=True)
        values = values - center
        spread = jnp.mean(values * values, axis=-1, keepdims=True)
        scale = lax.rsqrt(spread + norm_eps)
        return values * scale, scale

    def tokens_at(cut):
        return jnp.concatenate([tok[j, cut, :] for j in range(rows)], axis=1).astype(jnp.float32)

    def first_norm(block):
        cut = slice(block * BLOCK, (block + 1) * BLOCK)
        finish_seq(tok, tok_recv, swap_send.at[0], block)
        first[cut, :] = (norm(tokens_at(cut))[0] * gain_a).astype(jnp.bfloat16)

    for step in range(1, rows):
        row = p.row_before(step)
        remote(gains.at[row], gains.at[row], gain_send.at[step], gain_recv.at[row], p.sibling()).wait_recv()
    pltpu.make_async_copy(gains.at[p.row], gains.at[p.row], gain_recv.at[p.row]).wait()
    gain_a, gain_b = gain_of(0), gain_of(1)
    pltpu.make_async_copy(meta, meta, meta_recv).wait()
    columns = meta[...].T
    angle = columns[:, 0:1] * freq_ref[0:1, :]
    sign = jnp.where(lanes_of((1, PAIR)) % HD < HD // 2, -1.0, 1.0)
    table[0] = jnp.cos(angle)
    table[1] = jnp.sin(angle) * sign
    segment_col, valid_col = columns[:, 1:2], columns[:, 2:3]
    take_seq(tok, tok_recv, swap_send.at[0], 0)
    service([], [tokens_of[3]])
    take_seq(tok, tok_recv, swap_send.at[0], 1)
    service(
        [mixer.own_y, u1.own_x, u0.own_x, u0.own_y, j1.pass_on, s0.own_x, s1.own_x, s0.own_y, g0.pass_on],
        [j1.take_first, j0.take_others],
    )
    take_seq(tok, tok_recv, swap_send.at[0], 2)
    service([s1.own_y], [])
    first_norm(0)
    service([g2.own_y], [])
    take_seq(tok, tok_recv, swap_send.at[0], 3)
    first_norm(1)
    service([mixer.own_x], [u1.take_first])
    first_norm(2)
    first_norm(3)
    service([mixer.pass_on], [u0.take_first])

    def project(h):
        cols = slice(h * half, (h + 1) * half)

        @pl.loop(0, LEN // BLOCK)
        def _(i):
            cut = block_rows(i)
            part = first[cut, :]
            cosine, sine = (jnp.concatenate([table[n, cut, :]] * (half // PAIR), axis=1) for n in range(2))
            for j, dst in ((0, q_s), (1, k_s)):
                raw = dot(part, wj[h, j])
                dst[cut, cols] = (raw * cosine + swap_halves(raw) * sine).astype(jnp.bfloat16)
            v_s[cut, cols] = dot(part, wj[h, 2]).astype(jnp.bfloat16)

    def attention(pair, between):
        cols = slice(pair * PAIR, (pair + 1) * PAIR)
        v_t[...] = v_s[:, cols].astype(jnp.float32).T.astype(jnp.bfloat16)
        for head in range(2):
            lanes = slice(head * HD, (head + 1) * HD)

            @pl.loop(0, LEN // BLOCK)
            def _(i):
                cut = block_rows(i)
                scores = dot(k_s[:, cols], only_head(q_s[cut, cols], head), NT)
                scores = jnp.where(segment_col == meta[1:2, cut], scores, masked_value)
                peak = jnp.max(scores, axis=0, keepdims=True)
                weights = jnp.exp2((scores - peak) * TO_EXP2)
                total = jnp.sum(weights, axis=0, keepdims=True)
                out_t[lanes, cut] = dot(v_t[lanes, :], weights.astype(jnp.bfloat16)) / total
                lse[pair, head : head + 1, cut] = peak * TO_EXP2 + jnp.log2(total)

            if head == 0:
                service(*between)

        mixed[p.core, :, cols] = out_t[...].T.astype(jnp.bfloat16)
        piece = mixed.at[p.core, :, cols]
        remote(piece, piece, mixed_send.at[pair], mixed_recv.at[pair], p.sibling()).start()

    def share_mixer():
        mixer.finish()
        piece = wm.at[p.core]
        remote(piece, piece, mix_send, mix_recv, p.sibling()).start()

    j0.finish()
    project(0)
    service([u1.own_y], [])
    attention(0, ([*cot_of], []))
    service([s0.pass_on, g1.own_y, s2.own_y, u0.pass_on], [j1.take_others])
    attention(1, ([], []))
    service([u2.own_x, g1.own_x], [s1.take_first, *cot_of, s0.take_first])
    j1.finish()
    project(1)
    service([], [g0.take_others])
    attention(2, ([], [mixer.take_first]))
    service([u1.pass_on, s1.pass_on], [mixer.take_others])
    attention(3, ([], []))
    service([s2.own_x], [])
    service([g2.own_x, g1.pass_on, g2.pass_on], [])
    share_mixer()
    service([], [s0.take_others, u0.take_others])
    for block in blocks:
        take_seq(cot, cot_recv, swap_send.at[1], block)

    for pair in range(pairs):
        piece = mixed.at[p.core, :, pair * PAIR : (pair + 1) * PAIR]
        remote(piece, piece, mixed_send.at[pair], mixed_recv.at[pair], p.sibling()).wait_recv()
    piece = wm.at[p.core]
    remote(piece, piece, mix_send, mix_recv, p.sibling()).wait_recv()
    for block in blocks:
        finish_seq(cot, cot_recv, swap_send.at[1], block)

    @pl.loop(0, LEN // BLOCK)
    def _(i):
        cut = block_rows(i)
        value = tokens_at(cut) + dot(mixed[0, cut, :], wm[0]) + dot(mixed[1, cut, :], wm[1])
        normed, scale = norm(value)
        xhat[cut, :] = normed.astype(jnp.bfloat16)
        inv[cut, :] = jnp.broadcast_to(scale, (BLOCK, PAIR))
        second[cut, :] = (normed * gain_b).astype(jnp.bfloat16)
        shrunk[cut, :] = jnp.where(lanes_of((1, D)) // (D // CORES) == p.core, value, 0.0)
        back[cut, :] = jnp.zeros((BLOCK, D), jnp.float32)

    valid_16 = valid_col > 0.5
    top[...] = jnp.where(valid_16, jnp.concatenate([cot[j] for j in range(rows)], axis=1), jnp.zeros((), jnp.bfloat16))

    keep = []

    def store(src, dst):
        copy = pltpu.make_async_copy(src, dst, out_sem.at[len(keep)])
        keep.append(copy)
        copy.start()
        return copy

    for j in range(rows):
        store(tok.at[j], o_tokens.at[j])
    for src, dst in ((first, o_first), (q_s, o_q), (k_s, o_k), (v_s, o_v), (mixed.at[p.core], o_mixed), (lse, o_lse),
                     (inv, o_inv), (table, o_table), (top, o_top), (wj.at[0], o_joined.at[0]), (wj.at[1], o_joined.at[1]), (wm.at[p.core], o_mixer)):
        store(src, dst)
    xhat_copy = store(xhat, o_xhat)
    for j in range(rows):
        store(gains.at[j], o_small.at[:, pl.ds(j * width, width)])
    store(meta, o_small.at[:, pl.ds(D, LEN)])

    service([], [u1.take_others, g1.take_first])
    early = [
        ([], []),
        ([], [g2.take_others]),
        ([], []),
    ]
    middle = [
        ([u2.own_y, s2.pass_on], [g1.take_others, g2.take_first, s2.take_first]),
        ([], [u2.take_others]),
        ([], []),
    ]
    ready = [
        ([], [s1.take_others]),
        ([], []),
        ([], []),
    ]
    late = [
        ([u2.pass_on], [s2.take_others, u2.take_first]),
        ([], []),
        ([], []),
    ]

    def first_block(row, start, size):
        return g_expand[0].at[pl.ds(start, size), pl.ds(pl.multiple_of(row * width, width), width)]

    plane = Grad(p, first_block, 2 * chunks[0], (*sum_bufs, []), sum_sem, None, 0, share=1 / 2)
    then_early = [[], [], [plane.sum_x]]
    at = 0
    for i, lanes in enumerate(chunks):
        if i + 1 == n_chunks:
            xhat_copy.wait()
        for weight in groups[i]:
            weight.finish()
        service(*ready[i])

        @pl.loop(0, LEN // WIDE_BLOCK)
        def _(t):
            cut = block_rows(t, WIDE_BLOCK)
            part, grad = second[cut, :], top[cut, :]
            gate = dot(part, wg[i][...], NT)
            up = dot(part, wu[i][...], NT)
            hidden_grad = dot(grad, ws[i][...], NT).astype(jnp.bfloat16).astype(jnp.float32)
            phi, density = gelu_parts(gate)
            act = gate * phi
            hidden = (act * up).astype(jnp.bfloat16)
            d_gate = (hidden_grad * up * (phi + gate * density)).astype(jnp.bfloat16)
            d_up = (hidden_grad * act).astype(jnp.bfloat16)
            hid[cut, :lanes] = hidden
            dgate[cut, :lanes] = d_gate
            dup[cut, :lanes] = d_up
            value = shrunk[cut, :] + dot(hidden, ws[i][...])
            grad_sum = back[cut, :] + dot(d_gate, wg[i][...]) + dot(d_up, wu[i][...])
            if i + 1 < n_chunks:
                shrunk[cut, :] = value
                back[cut, :] = grad_sum
            else:
                xhat[cut, :] = grad_sum.astype(jnp.bfloat16)
                left, right = value[:, : D // 2], value[:, D // 2 :]
                shrunk[cut, : D // 2] = jnp.where(p.core == 0, left, right)
                other_half[cut, :] = jnp.where(p.core == 0, right, left).astype(jnp.bfloat16)

            @pl.when(t == LEN // WIDE_BLOCK // 2 - 1)
            def _():
                service(*early[i])
                for action in then_early[i]:
                    action()


        service(*middle[i])
        if i == 1:
            plane.sum_y()
        if i + 1 == n_chunks:
            store(xhat, o_back)
            store(shrunk.at[:, pl.ds(0, D // 2)], o_own)
            store(other_half, o_other)
        for n, (left, right) in enumerate(((dgate, second), (dup, second), (hid, top))):
            target = g_shrink[i] if n == 2 else g_expand[i]
            for start in range(0, lanes, BLOCK):
                size = min(BLOCK, lanes - start)
                spot = start if n == 2 else n * lanes + start
                target[spot : spot + size, :] = dot(left[:, start : start + size], right[...], TN).astype(jnp.bfloat16)
            if n == 1 and i == 0:
                plane.begin_y()
                plane.begin_x()

        if i:
            store(g_expand[i], o_expand.at[pl.ds(2 * at, 2 * lanes), :])
        store(g_shrink[i], o_shrink.at[pl.ds(at, lanes), :])
        service(*late[i])
        at += lanes

    plane.plane_sum()
    store(plane.acc, o_sum)

    plane.drain_plane()
    drain_seq(tok, tok_send, tok_recv, swap_send.at[0])
    drain_seq(cot, cot_send, cot_recv, swap_send.at[1])
    for step in range(1, rows):
        remote(gains_ref, gains.at[p.row], gain_send.at[step], gain_recv.at[p.row], p.sibling()).wait_send()

    @pl.when(sends_meta)
    def _():
        for t in range(1, seqs):
            remote(meta_src.at[t], meta, meta_send.at[t], meta_recv, p.sibling()).wait_send()

        @pl.when(jnp.logical_not(is_here))
        def _():
            remote(meta_src.at[0], meta, meta_send.at[0], meta_recv, p.sibling()).wait_send()

    for pair in range(pairs):
        piece = mixed.at[p.core, :, pair * PAIR : (pair + 1) * PAIR]
        remote(piece, piece, mixed_send.at[pair], mixed_recv.at[pair], p.sibling()).wait_send()
    piece = wm.at[p.core]
    remote(piece, piece, mix_send, mix_recv, p.sibling()).wait_send()
    for weight in joined + [mixer] + sum(groups, []):
        weight.drain()
    for copy in keep:
        if copy is not xhat_copy:
            copy.wait()


def forward(tokens, cot, lengths, first_gain, second_gain, joined, mixer, expand, shrink, chunks):
    rows = lax.axis_size("row")
    seqs = rows // CORES
    width = tokens.shape[1]
    wide = mixer.shape[0]
    pairs = wide // PAIR
    blocks = LEN // BLOCK
    n_chunks = len(chunks)
    hidden_here = sum(chunks)
    planes = lax.axis_size("dp") // CORES
    weights = 3 + 3 * n_chunks
    bf16, f32 = jnp.bfloat16, jnp.float32
    freq = np.tile((rope_base ** (-2.0 * np.arange(HD // 2) / HD)).astype(np.float32), (8, 4))
    outs = [
        ((rows, LEN, width), bf16), ((LEN, D), bf16), ((LEN, wide), bf16), ((LEN, wide), bf16), ((LEN, wide), bf16),
        ((LEN, wide), bf16), ((pairs, 2, LEN), f32), ((LEN, D), bf16), ((LEN, PAIR), f32), ((LEN, D), bf16),
        ((LEN, D // 2), f32), ((LEN, D // 2), bf16), ((LEN, D), bf16),
        ((2 * hidden_here, D), bf16), ((hidden_here, D), bf16), ((2, 3, D, wide // 2), bf16), ((wide, D), bf16),
        ((8, D + LEN), f32), ((2, LEN, PAIR), f32), ((grad_rows(2 * chunks[0], planes), width), bf16),
    ]
    V, dma = pltpu.VMEM, pltpu.SemaphoreType.DMA
    widest = max(chunks)
    scratch = [
        V((rows, LEN, width), bf16), V((rows, LEN, width), bf16), V((seqs, 8, LEN), f32), V((8, LEN), f32),
        V((8, width), f32), V((rows, 8, width), f32), V((2, LEN, PAIR), f32), V((LEN, D), bf16), V((2, 3, D, wide // 2), bf16), V((CORES, wide, D), bf16),
        [V((lanes, D), bf16) for lanes in chunks], [V((lanes, D), bf16) for lanes in chunks], [V((lanes, D), bf16) for lanes in chunks],
        V((LEN, wide), bf16), V((LEN, wide), bf16), V((LEN, wide), bf16), V((PAIR, LEN), bf16), V((PAIR, LEN), f32),
        V((pairs, 2, LEN), f32), V((CORES, LEN, wide), bf16), V((LEN, D), bf16), V((LEN, PAIR), f32), V((LEN, D), bf16),
        V((LEN, D), bf16), V((LEN, D), f32), V((LEN, D), f32), V((LEN, D // 2), bf16), V((LEN, widest), bf16), V((LEN, widest), bf16), V((LEN, widest), bf16),
        [V((2 * lanes, D), bf16) for lanes in chunks],
        [V((lanes, D), bf16) for lanes in chunks],
        plane_bufs(2 * chunks[0], width, rows, planes), dma((1, 14, rows)),
        dma((seqs, blocks)), dma((rows, blocks)), dma((seqs, blocks)), dma((rows, blocks)), dma((2, seqs, blocks)), dma((seqs,)), dma,
        dma((rows,)), dma((rows,)),
        dma((weights, rows)), dma((weights, rows)), dma((weights, rows)), dma((weights, rows)), dma((weights, rows)),
        dma((weights,)), dma, dma, dma((pairs,)), dma((pairs,)), dma((2 * rows + 17 + 3 * n_chunks,)),
    ]
    anywhere = pl.BlockSpec(memory_space=pl.ANY)
    in_specs = [anywhere] * 10
    in_specs[2] = pl.BlockSpec(memory_space=pltpu.SMEM)
    in_specs[3:6] = [pl.BlockSpec(memory_space=pltpu.VMEM)] * 3
    return pl.pallas_call(
        functools.partial(forward_kernel, chunks),
        in_specs=in_specs,
        out_specs=[anywhere] * len(outs),
        out_shape=[jax.ShapeDtypeStruct(*o) for o in outs],
        scratch_shapes=scratch,
        compiler_params=pltpu.CompilerParams(
            collective_id=0, has_side_effects=True, vmem_limit_bytes=62 * 1024 * 1024
        ),
        name="layer_forward",
    )(tokens, cot, lengths, first_gain[None, :], second_gain[None, :], freq, joined, mixer, expand, shrink)


def backward_kernel(
    chunks,
    tokens_ref, first_ref, q_ref, k_ref, v_ref, mixed_ref, lse_ref, xhat_ref, inv_ref, top_ref, own_ref, other_ref, back_ref,
    expand_ref, shrink_ref, joined_ref, mixer_ref, small_ref, table_ref, sum_ref,
    o_block, o_input, o_joined, o_mixer, o_expand, o_shrink, o_gains,
    q_s, k_s, v_s, mixed, xa, xb, xc, wj, wm, lse, inv, small, table, other, keep_grad, middle_low, mixed_grad, g_mixer, g_joined,
    dk, dv, dq_t, k_t, delta, own_half, block_half, gain_sum, gain_y, gain_x, gain_z, stage_lane, grad_scratch,
    load_sem, stage_sem, sum_sem, grad_sem, credit, swap_credit, back_send, back_recv, other_send, other_recv, first_send, first_recv,
    out_send, out_recv, in_send, in_recv, gain_send, gain_recv, out_sem,
):
    p = Place()
    rows, seqs, planes = p.rows, p.seqs, p.planes
    width = D // rows
    wide = q_s.shape[1]
    pairs = wide // PAIR
    levels = (planes - 1).bit_length()
    half = wide // 2

    def by_row(ref):
        return lambda j, start, size: ref.at[pl.ds(pl.multiple_of(j * width + start, 16), size), :]

    def by_lane(ref, at=0):
        return lambda j, start, size: ref.at[pl.ds(at + start, size), pl.ds(pl.multiple_of(j * width, width), width)]

    grads, places, at = {}, {}, 0
    stage = (stage_lane, stage_sem)

    def add_grad(name, block, count, stage, stores, summed=None):
        i = len(grads)
        grads[name] = Grad(p, block, count, grad_scratch[i], grad_sem, credit, i, stage, summed)
        places[name] = stores

    for i, count in enumerate(chunks):
        add_grad(("E", i), by_lane(expand_ref, 2 * at), 2 * count, stage,
                 [(j * count, count, 0, width, o_expand.at[j, pl.ds(at, count), :]) for j in range(2)],
                 None if i else pltpu.make_async_copy(sum_ref, grad_scratch[0][2], sum_sem))
        add_grad(("S", i), by_lane(shrink_ref, at), count, stage, [(0, count, 0, width, o_shrink.at[pl.ds(at, count), :])])
        at += count
    for h in range(2):
        add_grad(("J", h), by_row(g_joined.at[h]), width, None,
                 [(0, width, j * half, half, o_joined.at[j, :, pl.ds(h * half, half)]) for j in range(3)])
    add_grad(("M", 0), by_lane(g_mixer), wide, None, [(0, wide, 0, width, o_mixer)])

    loads = {}

    def load(name, src, dst):
        copy = pltpu.make_async_copy(src, dst, load_sem.at[len(loads)])
        copy.start()
        loads[name] = copy

    load("small", small_ref, small)
    load("back", back_ref, xc)
    load("xhat", xhat_ref, xa)
    load("inv", inv_ref, inv)
    load("top", top_ref, xb)
    load("mixer", mixer_ref, wm)
    load("mixed", mixed_ref, mixed)
    load("q", q_ref, q_s)
    load("k", k_ref, k_s)
    load("v", v_ref, v_s)
    load("lse", lse_ref, lse)
    load("table", table_ref, table)
    load("joined", joined_ref, wj)
    load("own", own_ref, own_half)
    pl.when(p.matched)(grads["E", 0].summed.start)
    p.barrier([p.across()] + [p.mate(level) for level in range(levels)])

    def swap_block(i, src, dst, send, recv):
        cut = pl.ds(i * BLOCK, BLOCK)
        return remote(src.at[cut, :], dst.at[cut, :], send.at[i], recv.at[i], p.sibling())

    blocks_n = LEN // BLOCK
    for i in range(blocks_n):
        swap_block(i, back_ref, other, back_send, back_recv).start()

    stores = []

    def run(*todo):
        for step in todo:
            if callable(step):
                step()
                continue
            action, kind, i = step
            grad = grads[kind, i]
            if action == "store":
                spots = [spot + (out_sem.at[len(stores) + n],) for n, spot in enumerate(places[kind, i])]
                stores.extend(grad.store(spots))
            elif action == "begin":
                grad.begin_y()
                grad.begin_x()
            else:
                getattr(grad, action)()

    run(("begin_x", "E", 1), ("begin_y", "E", 2), ("begin_x", "S", 0), ("begin_y", "S", 2), ("begin_y", "E", 1))
    other_copy = remote(other_ref, block_half, other_send, other_recv, p.sibling())
    other_copy.start()

    for name in ("small", "back", "xhat", "inv", "top", "mixer", "mixed"):
        loads[name].wait()
    gain_a, gain_b = small[0:1, :D], small[1:2, :D]
    gain_sum[...] = jnp.zeros_like(gain_sum)
    for grad in grads.values():
        if grad.full != grad.m and grad.summed is None:
            grad.acc[grad.m :, :] = jnp.zeros((grad.full - grad.m, grad.acc.shape[1]), jnp.bfloat16)

    def norm_back(grad, normed, scale, gain):
        scaled = grad * gain
        mean_a = jnp.mean(scaled, axis=-1, keepdims=True)
        mean_b = jnp.mean(scaled * normed, axis=-1, keepdims=True)
        return scale * (scaled - mean_a - normed * mean_b)

    def own_of(value):
        return jnp.where(p.core == 0, value[:, : D // 2], value[:, D // 2 :])

    def second_norm(i):
        cut = slice(i * BLOCK, (i + 1) * BLOCK)
        swap_block(i, back_ref, other, back_send, back_recv).wait_recv()
        grad = xc[cut, :].astype(jnp.float32) + other[cut, :].astype(jnp.float32)
        normed = xa[cut, :].astype(jnp.float32)
        gain_sum[1:2, :] += jnp.sum(grad * normed, axis=0, keepdims=True)
        value = xb[cut, :].astype(jnp.float32) + norm_back(grad, normed, inv[cut, 0:1], gain_b)
        keep_grad[cut, :] = own_of(value)
        value = value.astype(jnp.bfloat16)
        middle_low[cut, :] = value
        mixed_grad[cut, :] = dot(value, wm[...], NT).astype(jnp.bfloat16)
    second_norm(0)
    second_norm(1)
    run(("begin_y", "S", 0))
    second_norm(2)
    second_norm(3)
    pl.semaphore_signal(swap_credit, inc=1, device_id=p.sibling(), device_id_type=MESH_ID)
    run(("begin_x", "S", 2))
    @pl.loop(0, D // BLOCK)
    def _(d):
        cut = block_rows(d)
        g_mixer[:, cut] = dot(mixed[...], middle_low[:, cut], TN).astype(jnp.bfloat16)

    load("first", first_ref, xa)
    for j in range(rows):
        load(f"tokens{j}", tokens_ref.at[j], xb.at[:, pl.ds(j * width, width)])

    def leave(src, dst, send, recv):
        core, seq = p.row // seqs, lax.rem(p.row, seqs)
        copies = []
        for u in range(seqs):
            row = p.core * seqs + u
            is_self = jnp.logical_and(core == p.core, row == p.row)
            piece = src.at[:, pl.ds(u * width, width)]
            copies.append((is_self, piece, dst(seq), send.at[u], recv.at[seq], p.at(core=core, row=row)))
        return copies

    def leave_start(copies):
        for is_self, piece, place, send, recv, target in copies:
            @pl.when(is_self)
            def _():
                pltpu.make_async_copy(piece, place, recv).start()

            @pl.when(jnp.logical_not(is_self))
            def _():
                remote(piece, place, send, recv, target).start()

    def leave_wait(copies, dst, recv):
        for s in range(seqs):
            pltpu.make_async_copy(dst(s), dst(s), recv.at[s]).wait()
        for is_self, piece, place, send, recv_sem, target in copies:
            @pl.when(jnp.logical_not(is_self))
            def _():
                remote(piece, place, send, recv_sem, target).wait_send()

    out_at = lambda s: o_block.at[pl.ds(pl.multiple_of(s * LEN, LEN), LEN), :]
    in_at = lambda s: o_input.at[pl.ds(pl.multiple_of(s * LEN, LEN), LEN), :]
    out_copies = leave(block_half, out_at, out_send, out_recv)
    in_copies = leave(mixed_grad, in_at, in_send, in_recv)

    def block_output():
        loads["own"].wait()
        other_copy.wait()
        add_rows(LEN, block_half, own_half, block_half)
        leave_start(out_copies)

    for name in ("q", "k", "v", "lse", "table"):
        loads[name].wait()
    columns = small[:, D:].T
    segment_col = columns[:, 1:2]

    def attention_start(pair):
        cols = slice(pair * PAIR, (pair + 1) * PAIR)
        product = mixed[:, cols].astype(jnp.float32) * mixed_grad[:, cols].astype(jnp.float32)
        chooser = lax.broadcasted_iota(jnp.int32, (8, PAIR), 0) == lanes_of((8, PAIR)) // HD
        delta[...] = dot(chooser.astype(jnp.float32), product, NT, precision=lax.Precision.HIGHEST)
        k_t[...] = k_s[:, cols].astype(jnp.float32).T.astype(jnp.bfloat16)
        dk[...] = jnp.zeros_like(dk)
        dv[...] = jnp.zeros_like(dv)

    def attention_head(pair, head):
        cols = slice(pair * PAIR, (pair + 1) * PAIR)
        keys, values = k_s[:, cols], v_s[:, cols]
        lanes = slice(head * HD, (head + 1) * HD)
        for i in range(LEN // BLOCK):
            cut = slice(i * BLOCK, (i + 1) * BLOCK)
            q_part, g_part = only_head(q_s[cut, cols], head), only_head(mixed_grad[cut, cols], head)
            scores = dot(keys, q_part, NT)
            probs = jnp.exp2(scores * TO_EXP2 - lse[pair, head : head + 1, cut])
            probs = jnp.where(segment_col == small[1:2, D + i * BLOCK : D + (i + 1) * BLOCK], probs, 0.0)
            probs_grad = dot(values, g_part, NT)
            scores_grad = (probs * (probs_grad - delta[head : head + 1, cut])).astype(jnp.bfloat16)
            dv[...] += dot(probs.astype(jnp.bfloat16), g_part)
            dk[...] += dot(scores_grad, q_part)
            dq_t[lanes, cut] = dot(k_t[lanes, :], scores_grad)

    def attention_end(pair):
        cols = slice(pair * PAIR, (pair + 1) * PAIR)
        cosine, sine = table[0], table[1]
        scale = 1.0 / math.sqrt(HD)
        dqs = dq_t[...].T * scale
        q_s[:, cols] = (dqs * cosine - swap_halves(dqs) * sine).astype(jnp.bfloat16)
        dks = dk[...] * scale
        k_s[:, cols] = (dks * cosine - swap_halves(dks) * sine).astype(jnp.bfloat16)
        v_s[:, cols] = dv[...].astype(jnp.bfloat16)

    def joined_weight_grad(h):
        @pl.loop(0, D // BLOCK)
        def _(d):
            cut = block_rows(d)
            part = xa[:, cut]
            for j, back in enumerate((q_s, k_s, v_s)):
                g_joined[h, cut, j * half : (j + 1) * half] = dot(
                    part, back[:, h * half : (h + 1) * half], TN
                ).astype(jnp.bfloat16)

    run(("sum_both", "E", 0))
    attention_start(0)
    attention_head(0, 0)
    attention_head(0, 1)
    attention_end(0)
    attention_start(1)
    attention_head(1, 0)
    attention_head(1, 1)
    attention_end(1)
    run(("z0", "E", 0), ("sum_x", "E", 1), ("sum_y", "E", 1))
    loads["first"].wait()
    joined_weight_grad(0)
    attention_start(2)
    attention_head(2, 0)
    run(
        ("begin_y", "M", 0), ("begin_x", "J", 0), ("sum_y", "S", 2), ("sum_x", "S", 2), ("begin_y", "J", 0),
        ("z1", "E", 0), ("sum_x", "S", 0), ("sum_both", "E", 1),
    )
    attention_head(2, 1)
    attention_end(2)
    attention_start(3)
    attention_head(3, 0)
    attention_head(3, 1)
    attention_end(3)
    run(
        ("sum_both", "S", 2), ("sum_x", "J", 0), ("z0", "E", 1), ("sum_y", "S", 0), ("z0", "S", 2),
        ("sum_both", "S", 0), ("g1", "E", 0), ("begin_x", "E", 2), ("sum_x", "E", 2), ("sum_y", "J", 0),
        ("sum_y", "E", 2), ("z1", "E", 1), ("sum_both", "J", 0), ("sum_both", "E", 2),
    )
    joined_weight_grad(1)
    run(
        ("begin_x", "J", 1), ("begin_y", "J", 1), ("z1", "S", 2), ("z0", "S", 0), ("begin_y", "S", 1),
        ("z0", "J", 0), ("g1", "E", 1), ("sum_x", "J", 1), ("sum_y", "J", 1), ("z1", "S", 0), ("begin_x", "M", 0),
    )
    loads["joined"].wait()
    pl.semaphore_wait(swap_credit, 1)

    def first_back(i):
        cut = slice(i * BLOCK, (i + 1) * BLOCK)
        value = jnp.zeros((BLOCK, D), jnp.float32)
        for h in range(2):
            for j, part in enumerate((q_s, k_s, v_s)):
                value = value + dot(part[cut, h * half : (h + 1) * half], wj[h, j], NT)
        xc[cut, :] = value.astype(jnp.bfloat16)
        swap_block(i, xc, other, first_send, first_recv).start()

    first_back(0)
    first_back(1)

    run(
        ("g0", "E", 0), ("g1", "S", 2), ("z0", "E", 2), ("sum_both", "J", 1), ("z1", "J", 0), ("g1", "S", 0),
        ("begin_x", "S", 1), ("sum_x", "M", 0), ("sum_y", "M", 0), ("sum_y", "S", 1), ("z1", "E", 2), ("g1", "J", 0),
        ("g0", "S", 2), ("sum_x", "S", 1), ("z0", "J", 1), ("sum_both", "M", 0),
    )
    first_back(2)
    first_back(3)
    run(("store", "E", 0), ("sum_both", "S", 1), ("g0", "E", 1), ("g1", "E", 2), ("z1", "J", 1))
    for j in range(rows):
        loads[f"tokens{j}"].wait()
    for i in range(blocks_n):
        cut = slice(i * BLOCK, (i + 1) * BLOCK)
        swap_block(i, xc, other, first_send, first_recv).wait_recv()
        grad = xc[cut, :].astype(jnp.float32) + other[cut, :].astype(jnp.float32)
        values = xb[cut, :].astype(jnp.float32)
        values = values - jnp.mean(values, axis=-1, keepdims=True)
        scale = lax.rsqrt(jnp.mean(values * values, axis=-1, keepdims=True) + norm_eps)
        normed = values * scale
        gain_sum[0:1, :] += jnp.sum(grad * normed, axis=0, keepdims=True)
        total = keep_grad[cut, :] + own_of(norm_back(grad, normed, scale, gain_a))
        mixed_grad[cut, :] = total.astype(jnp.bfloat16)

    def gain_copies():
        return [
            remote(gain_sum.at[:, pl.ds(pl.multiple_of(p.row_after(s) * width, width), width)], gain_y.at[s],
                   gain_send.at[s], gain_recv.at[s], p.at(row=p.row_after(s)))
            for s in range(1, rows)
        ]

    gain_across = remote(gain_x.at[0], gain_x.at[1], gain_send.at[rows], gain_recv.at[rows], p.across())
    gain_total = gain_z.at[2 * levels]
    gain_back = remote(gain_total, gain_total, gain_send.at[rows + 1 + levels], gain_recv.at[rows + 1 + levels], p.sibling())

    def gain_plane(level):
        return remote(gain_z.at[2 * level], gain_z.at[2 * level + 1], gain_send.at[rows + 1 + level],
                      gain_recv.at[rows + 1 + level], p.mate(level))

    def gains_y():
        for s in range(1, rows):
            remote(gain_y.at[s], gain_y.at[s], gain_send.at[s], gain_recv.at[s], p.sibling()).wait_recv()
        total = gain_sum[:, pl.ds(pl.multiple_of(p.row * width, width), width)]
        for s in range(1, rows):
            total = total + gain_y[s]
        gain_x[0] = total
        pl.when(p.matched)(gain_across.start)

    def gains_x():
        @pl.when(jnp.logical_not(p.matched))
        def _():
            gain_across.wait_recv()
            gain_z[0] = gain_x[0] + gain_x[1]
            gain_plane(0).start()

    def gains_z():
        @pl.when(jnp.logical_not(p.matched))
        def _():
            for level in range(levels):
                gain_plane(level).wait()
                gain_z[2 * level + 2] = gain_z[2 * level] + gain_z[2 * level + 1]
                if level + 1 < levels:
                    gain_plane(level + 1).start()
            gain_back.start()
            gain_back.wait_send()

    def gains_end():
        @pl.when(p.matched)
        def _():
            gain_back.wait_recv()
            gain_across.wait_send()

    for copy in gain_copies():
        copy.start()
    leave_start(in_copies)

    run(
        ("z0", "S", 1), ("g1", "J", 1), ("z0", "M", 0), ("g0", "J", 1), gains_y, ("store", "S", 2), ("z1", "S", 1),
        ("store", "E", 1), ("z1", "M", 0), ("g1", "S", 1), gains_x, ("g0", "E", 2), block_output, ("g0", "S", 1),
        ("g0", "S", 0), ("store", "J", 1), ("g0", "J", 0), gains_z, ("store", "S", 0), ("store", "J", 0),
        ("g1", "M", 0), ("store", "E", 2), ("store", "S", 1), ("g0", "M", 0), ("store", "M", 0),
    )
    gains_end()
    gains_out = pltpu.make_async_copy(gain_z.at[2 * levels], o_gains, out_sem.at[len(stores)])
    gains_out.start()

    leave_wait(out_copies, out_at, out_recv)
    leave_wait(in_copies, in_at, in_recv)
    for i in range(blocks_n):
        swap_block(i, back_ref, other, back_send, back_recv).wait_send()
        swap_block(i, xc, other, first_send, first_recv).wait_send()
    for copy in gain_copies():
        copy.wait_send()
    for grad in grads.values():
        grad.drain()
    for copy in stores:
        copy.wait()
    gains_out.wait()


def backward(saved, chunks):
    (tokens, first, queries, keys, values, mixed, lse, xhat, inv, top, own, other, back, expand, shrink, joined, mixer,
     small, table, plane_sum) = saved
    rows = lax.axis_size("row")
    planes = lax.axis_size("dp") // CORES
    seqs = rows // CORES
    width = D // rows
    wide = queries.shape[1]
    pairs = wide // PAIR
    hidden_here = sum(chunks)
    widest = 2 * max(chunks)
    levels = (planes - 1).bit_length()
    bf16, f32 = jnp.bfloat16, jnp.float32
    V, dma = pltpu.VMEM, pltpu.SemaphoreType.DMA
    outs = [
        ((seqs * LEN, width), bf16), ((seqs * LEN, width), bf16), ((3, width, wide), bf16), ((wide, width), bf16),
        ((2, hidden_here, width), bf16), ((hidden_here, width), bf16), ((8, width), f32),
    ]
    grad_shapes = []
    for lanes in chunks:
        grad_shapes += [(2 * lanes, width), (lanes, width)]
    grad_shapes += [(width, 3 * wide // 2)] * 2 + [(wide, width)]
    count = len(grad_shapes)
    scratch = [
        V((LEN, wide), bf16), V((LEN, wide), bf16), V((LEN, wide), bf16), V((LEN, wide), bf16),
        V((LEN, D), bf16), V((LEN, D), bf16), V((LEN, D), bf16), V((2, 3, D, wide // 2), bf16), V((wide, D), bf16),
        V((pairs, 2, LEN), f32), V((LEN, PAIR), f32), V((8, D + LEN), f32), V((2, LEN, PAIR), f32), V((LEN, D), bf16),
        V((LEN, D // 2), f32), V((LEN, D), bf16), V((LEN, wide), bf16), V((wide, D), bf16), V((2, D, 3 * wide // 2), bf16),
        V((LEN, PAIR), f32), V((LEN, PAIR), f32), V((PAIR, LEN), f32), V((PAIR, LEN), bf16), V((8, LEN), f32),
        V((LEN, D // 2), f32), V((LEN, D // 2), bf16),
        V((8, D), f32), V((rows, 8, width), f32), V((2, 8, width), f32), V((2 * levels + 1, 8, width), f32),
        V((2, widest - first_share(widest), width), bf16),
        [grad_bufs(*shape, rows, planes, i == 0) for i, shape in enumerate(grad_shapes)],
        dma((15 + rows,)), dma((2,)), dma, dma((count, 14, max(rows, levels))), pltpu.SemaphoreType.REGULAR((count, levels)),
        pltpu.SemaphoreType.REGULAR,
        dma((4,)), dma((4,)), dma, dma, dma((4,)), dma((4,)),
        dma((seqs,)), dma((seqs,)), dma((seqs,)), dma((seqs,)), dma((rows + 2 + levels,)), dma((rows + 2 + levels,)),
        dma((3 * len(chunks) + 8,)),
    ]
    anywhere = pl.BlockSpec(memory_space=pl.ANY)
    return pl.pallas_call(
        functools.partial(backward_kernel, chunks),
        in_specs=[anywhere] * len(saved),
        out_specs=[anywhere] * len(outs),
        out_shape=[jax.ShapeDtypeStruct(*o) for o in outs],
        scratch_shapes=scratch,
        compiler_params=pltpu.CompilerParams(
            collective_id=1, has_side_effects=True, vmem_limit_bytes=62 * 1024 * 1024
        ),
        name="layer_backward",
    )(*saved)


def finish_kernel(*refs):
    count = len(refs) // 2
    gains_ref, firsts, seconds = refs[count - 1], *refs[-2:]
    for src, dst in zip(refs[: count - 1], refs[count:]):
        dst[...] = src[...].astype(dst.dtype)
    firsts[...] = gains_ref[0:1, :]
    seconds[...] = gains_ref[1:2, :]


def finish(block, *rest):
    steps = 4
    *grads, gains = rest
    arrays = [x.reshape(-1, x.shape[-1]) for x in (block, *grads)]

    def spec(x):
        parts = next(n for n in (steps, steps // 2, 1) if x.shape[0] % (16 * n) == 0)
        return pl.BlockSpec((x.shape[0] // parts, x.shape[1]), lambda i: (i * parts // steps, 0))

    whole = lambda rows: pl.BlockSpec((rows, gains.shape[1]), lambda i: (0, 0))
    shape = jax.ShapeDtypeStruct
    outs = pl.pallas_call(
        finish_kernel,
        grid=(steps,),
        in_specs=[spec(x) for x in arrays] + [whole(8)],
        out_specs=[spec(x) for x in arrays] + [whole(1)] * 2,
        out_shape=[shape(arrays[0].shape, block.dtype)]
        + [shape(x.shape, jnp.float32) for x in arrays[1:]]
        + [shape((1, gains.shape[1]), jnp.float32)] * 2,
        compiler_params=pltpu.CompilerParams(vmem_limit_bytes=60 * 1024 * 1024),
        name="layer_finish",
    )(*arrays, gains)
    return [out.reshape(x.shape) for out, x in zip(outs, (block, *grads))] + [outs[-2][0], outs[-1][0]]


def shards(
    tokens_in, lengths, first_gain, joined_weight, mixer_weight, second_gain, expand_weight, shrink_weight, cotangent
):
    rows, cols = lax.axis_size("row"), lax.axis_size("col")
    hidden_here = shrink_weight.shape[0]
    assert tokens_in.shape[0] * CORES == LEN * rows and cols == CORES
    chunks = (512, 512, hidden_here - 1024)
    joined_here = joined_weight.transpose(1, 0, 2)
    expand_here = expand_weight.transpose(1, 2, 0)
    saved = forward(
        tokens_in, cotangent, lengths, first_gain, second_gain, joined_here, mixer_weight, expand_here, shrink_weight, chunks
    )
    block_output, input_grad, joined_grad, mixer_grad, expand_grad, shrink_grad, *gains = finish(*backward(saved, chunks))
    return (
        block_output,
        input_grad,
        joined_grad.transpose(1, 0, 2),
        mixer_grad,
        expand_grad.transpose(2, 0, 1),
        shrink_grad,
        gains[0],
        gains[1],
    )


def solution(mesh):
    placed = (
        P(("dp", "col"), "row"),
        P("dp", None),
        P("row"),
        P("row", None, "col"),
        P("col", "row"),
        P("row"),
        P("row", None, "col"),
        P("col", "row"),
        P(("dp", "col"), "row"),
    )
    return jax.shard_map(
        shards,
        mesh=mesh,
        in_specs=placed,
        out_specs=(
            P(("dp", "col"), "row"),
            P(("dp", "col"), "row"),
            P("row", None, "col"),
            P("col", "row"),
            P("row", None, "col"),
            P("col", "row"),
            P("row"),
            P("row"),
        ),
        check_vma=False,
    )
```

```python
import functools
import math

import jax
import jax.numpy as jnp
import numpy as np
from jax import lax
from jax.experimental import pallas as pl
from jax.experimental.pallas import tpu as pltpu
from jax.sharding import PartitionSpec as P

D = 1024
HEADS = 16
HD = 64
FF = 2624
LEN = 1024
DOCS = 6
MOST = 800
CORES = 2

rope_base = 160000.0
norm_eps = 1e-05
masked_value = -1000000000.0

PAIR = 2 * HD
WIDE = 256
SOLID = MOST // WIDE * WIDE
REST = LEN - MOST
TO_EXP2 = math.log2(math.e) / math.sqrt(HD)

NT = (((1,), (1,)), ((), ()))
TN = (((0,), (0,)), ((), ()))
MESH_AXES = ("dp", "row", "col")


def lanes_of(shape):
    return lax.broadcasted_iota(jnp.int32, shape, len(shape) - 1)


def swap_halves(u):
    low_half = lanes_of(u.shape) % HD < HD // 2
    return jnp.where(low_half, pltpu.roll(u, u.shape[1] - HD // 2, 1), pltpu.roll(u, HD // 2, 1))


def dot(left, right, dims=(((1,), (0,)), ((), ())), **more):
    return lax.dot_general(left, right, dims, preferred_element_type=jnp.float32, **more)


def only_head(values, head):
    return jnp.where(lanes_of(values.shape) // HD == head, values, jnp.zeros_like(values))


MESH_ID = pl.DeviceIdType.MESH
BLOCK = 256
WIDE_BLOCK = 512


class Place:
    def __init__(self):
        self.rows, self.cols = lax.axis_size("row"), lax.axis_size("col")
        self.planes = lax.axis_size("dp") // CORES
        dp = lax.axis_index("dp")
        self.z, self.core = dp // CORES, dp % CORES
        self.row, self.col = lax.axis_index("row"), lax.axis_index("col")
        self.matched = self.core == self.col
        self.parity = self.z % 2
        self.inner = self.parity != (self.z // 2) % 2
        self.seqs = self.rows // CORES

    def at(self, z=None, core=None, row=None, col=None):
        z = self.z if z is None else z
        core = self.core if core is None else core
        return (z * CORES + core, self.row if row is None else row, self.col if col is None else col)

    def sibling(self):
        return self.at(core=1 - self.core)

    def across(self):
        return self.at(col=1 - self.col)

    def pair(self):
        return self.at(z=self.z + 1 - 2 * self.parity)

    def row_after(self, step):
        return lax.rem(self.row + step, self.rows)

    def row_before(self, step):
        return lax.rem(self.row + self.rows - step, self.rows)

    def group_bit(self, level):
        return lax.rem(self.z // (1 << level), 2)

    def mate(self, level):
        if level == 0:
            return self.pair()
        group = self.z // 2
        other = group + (1 << (level - 1)) * (1 - 2 * self.group_bit(level))
        shift = lax.rem(group, 2) + self.parity
        return self.at(z=2 * other + lax.rem(shift + lax.rem(other, 2), 2))

    def barrier(self, partners):
        sem = pltpu.get_barrier_semaphore()
        count = CORES * self.rows
        partners = list(partners)
        for step in range(1, count):
            flat = lax.rem(self.core * self.rows + self.row + step, count)
            partners.append(self.at(core=flat // self.rows, row=lax.rem(flat, self.rows)))
        for partner in partners:
            pl.semaphore_signal(sem, inc=1, device_id=partner, device_id_type=MESH_ID)
        pl.semaphore_wait(sem, len(partners))


def remote(src, dst, send, recv, target):
    return pltpu.make_async_remote_copy(
        src_ref=src, dst_ref=dst, send_sem=send, recv_sem=recv, device_id=target, device_id_type=MESH_ID
    )


def shares(count, part):
    one = int(count * part) // 16 * 16
    return count - 2 * one, one


class Weight:
    def __init__(self, place, source, slot, count, sems, index, part):
        self.place, self.source, self.slot = place, source, slot
        self.both, self.one = shares(count, part)
        self.sems = sems
        self.index = index
        self.local = sems[5].at[index]

    def sem(self, kind, row):
        return self.sems[kind].at[self.index, row]

    def plane_part(self):
        return self.place.parity * self.one, self.one + self.both

    def pair_part(self):
        return self.place.parity * (self.one + self.both), self.one

    def other_part(self):
        return (1 - self.place.parity) * (self.one + self.both), self.one

    def own_y(self):
        p = self.place
        start, size = self.plane_part()
        for step in range(1, p.rows):
            remote(
                self.source(start, size),
                self.slot(p.row, start, size),
                self.sem(0, step),
                self.sem(3, p.row),
                p.at(row=p.row_after(step)),
            ).start()

    def own_x(self):
        p = self.place
        start, size = self.plane_part()
        remote(
            self.source(start, size), self.slot(p.row, start, size), self.sem(1, 0), self.sem(3, p.row), p.across()
        ).start()
        pltpu.make_async_copy(
            self.source(0, 2 * self.one + self.both), self.slot(p.row, 0, 2 * self.one + self.both), self.local
        ).start()

    def pass_on(self):
        p = self.place
        for step in range(1, p.rows):
            row = p.row_before(step)
            self.wait_plane(row)
            self.send_across(row, step).start()
            self.send_pair(row, step).start()

    def take_first(self):
        self.wait_plane(self.place.row)
        self.send_pair(self.place.row, 0).start()

    def take_others(self):
        p = self.place
        for step in range(1, p.rows):
            row = p.row_before(step)
            self.wait_plane(row)
            self.send_pair(row, step).start()

    def wait_plane(self, row):
        p = self.place
        start, size = self.plane_part()
        piece = self.slot(row, start, size)
        remote(piece, piece, self.sem(0, 0), self.sem(3, row), p.across()).wait_recv()

    def send_pair(self, row, step):
        start, size = self.pair_part()
        piece = self.slot(row, start, size)
        return remote(piece, piece, self.sem(2, step), self.sem(4, row), self.place.pair())

    def send_across(self, row, step):
        start, size = self.plane_part()
        piece = self.slot(row, start, size)
        return remote(piece, piece, self.sem(1, step), self.sem(3, row), self.place.across())

    def finish(self):
        p = self.place
        start, size = self.other_part()

        def wait_other(row):
            piece = self.slot(row, start, size)
            remote(piece, piece, self.sem(2, 0), self.sem(4, row), p.pair()).wait_recv()

        for step in range(1, p.rows):
            wait_other(p.row_before(step))

        @pl.when(p.matched)
        def _():
            whole = self.slot(p.row, 0, 2 * self.one + self.both)
            pltpu.make_async_copy(whole, whole, self.local).wait()

        @pl.when(jnp.logical_not(p.matched))
        def _():
            wait_other(p.row)

    def drain(self):
        p = self.place
        start, size = self.plane_part()
        piece = self.slot(p.row, start, size)
        for step in range(1, p.rows):
            self.send_pair(p.row, step).wait_send()

        @pl.when(p.matched)
        def _():
            for step in range(1, p.rows):
                remote(piece, piece, self.sem(0, step), self.sem(3, p.row), p.across()).wait_send()
            for step in range(p.rows):
                self.send_across(p.row, step).wait_send()

        @pl.when(jnp.logical_not(p.matched))
        def _():
            self.send_pair(p.row, 0).wait_send()


def add_rows(count, target, *parts):
    step = next(s for s in (64, 32, 16) if count % s == 0)

    @pl.loop(0, count // step)
    def _(i):
        cut = pl.ds(pl.multiple_of(i * step, step), step)
        total = parts[0][cut, :].astype(jnp.float32)
        for part in parts[1:]:
            total = total + part[cut, :].astype(jnp.float32)
        target[cut, :] = total.astype(target.dtype)


def first_share(count, share=5 / 16):
    return int(count * share) // 16 * 16


class Grad:
    def __init__(self, place, block, rows, bufs, sems, credits, index, stage=None, summed=None, share=5 / 16):
        self.p, self.block, self.m, self.index, self.sems, self.stage = place, block, rows, index, sems, stage
        self.credits, self.summed = credits, summed
        self.a = first_share(rows, share)
        self.b = rows - self.a
        self.recv_a, self.recv_b, self.acc, self.more, self.zbuf = bufs
        self.levels = (place.planes - 1).bit_length()
        self.full = self.acc.shape[0]

    def sem(self, kind, at=0):
        return self.sems.at[self.index, kind, at]

    def low(self):
        return self.acc.at[pl.ds(0, self.a), :]

    def high(self):
        return self.acc.at[pl.ds(self.a, self.b), :]

    def send(self, src, dst, kind, at, target):
        return remote(src, dst, self.sem(kind, at), self.sem(kind + 1, at), target)

    def landed(self, buf, kind, at=0):
        self.send(buf, buf, kind, at, self.p.sibling()).wait_recv()

    def left(self, buf, kind, at=0):
        self.send(buf, buf, kind, at, self.p.sibling()).wait_send()

    def copies_y(self):
        p = self.p
        return [
            self.send(self.block(p.row_after(s), 0, self.a), self.recv_a.at[s - 1], 0, s, p.at(row=p.row_after(s)))
            for s in range(1, p.rows)
        ]

    def copies_x(self):
        return [
            self.send(self.block(j, self.a, self.b), self.recv_b.at[j], 2, j, self.p.across())
            for j in range(self.p.rows)
        ]

    def begin_y(self):
        for copy in self.copies_y():
            copy.start()

    def begin_x(self):
        @pl.when(jnp.logical_not(self.p.matched))
        def _():
            for copy in self.copies_x():
                copy.start()

    def own(self, row, start, size, slot):
        piece = self.block(row, start, size)
        if self.stage is None:
            return piece, []
        buf, sem = self.stage
        buf = buf.at[slot, pl.ds(0, size), :]
        copy = pltpu.make_async_copy(piece, buf, sem.at[slot])
        copy.start()
        return buf, [copy]

    def sum_y(self):
        p = self.p
        own, copies = self.own(p.row, 0, self.a, 0)
        for s in range(1, p.rows):
            self.landed(self.recv_a.at[s - 1], 0, s)
        for copy in copies:
            copy.wait()
        add_rows(self.a, self.recv_a.at[0], own, *[self.recv_a.at[s - 1] for s in range(1, p.rows)])

        @pl.when(jnp.logical_not(p.matched))
        def _():
            self.send(self.recv_a.at[0], self.low(), 4, 0, p.across()).start()

    def sum_x(self):
        p = self.p

        @pl.when(p.matched)
        def _():
            steps = list(range(1, p.rows)) + [0]
            owns = [self.own(p.row_after(s), self.a, self.b, n) for n, s in enumerate(steps[:2])]
            for n, s in enumerate(steps):
                row = p.row_after(s)
                if n >= 2:
                    owns.append(self.own(row, self.a, self.b, n % 2))
                own, copies = owns[n]
                buf = self.recv_b.at[row]
                self.landed(buf, 2, row)
                for copy in copies:
                    copy.wait()
                add_rows(self.b, buf, own, buf)
                if s:
                    target = self.high() if s == 1 else self.more.at[s - 2]
                    self.send(buf, target, 6, s, p.at(row=row)).start()

    def span(self, level):
        start, size = 0, self.full
        for i in range(1, level + 1):
            size //= 2
            start = start + self.p.group_bit(i) * size
        return start, size

    def rows_of(self, start, size):
        return self.acc.at[pl.ds(pl.multiple_of(start, 16), size), :]

    def z_copy(self, level):
        if level == 0:
            return self.send(self.acc, self.zbuf[0], 8, 0, self.p.mate(0))
        start, size = self.span(level - 1)
        half = size // 2
        piece = self.rows_of(start + (1 - self.p.group_bit(level)) * half, half)
        return self.send(piece, self.zbuf[level], 8, level, self.p.mate(level))

    def z_back(self, level):
        piece = self.acc if level == 0 else self.rows_of(*self.span(level))
        return self.send(piece, piece, 10, level, self.p.mate(level))

    def z_free(self, level):
        self.z_copy(level).wait_send()
        pl.semaphore_signal(
            self.credits.at[self.index, level], inc=1, device_id=self.p.mate(level), device_id_type=MESH_ID
        )

    def z_return(self, level):
        pl.semaphore_wait(self.credits.at[self.index, level], 1)
        self.z_back(level).start()

    def plane_sum(self):
        p = self.p

        @pl.when(p.matched)
        def _():
            self.landed(self.low(), 4)
            add_rows(self.a, self.low(), self.low(), self.recv_a.at[0])
            others = []
            for s in range(1, p.rows):
                buf = self.high() if s == 1 else self.more.at[s - 2]
                self.landed(buf, 6, s)
                others.append(buf)
            add_rows(self.b, self.high(), self.recv_b.at[p.row], *others)

    def sum_both(self):
        p = self.p
        if self.summed is None:
            self.plane_sum()
        else:
            pl.when(p.matched)(self.summed.wait)

        @pl.when(jnp.logical_and(p.matched, jnp.logical_not(p.inner)))
        def _():
            self.z_copy(0).start()

    def z0(self):
        p = self.p

        @pl.when(jnp.logical_and(p.matched, p.inner))
        def _():
            self.landed(self.zbuf[0], 8, 0)
            add_rows(self.full, self.acc, self.acc, self.zbuf[0])
            if self.levels > 1:
                self.z_copy(1).start()
            else:
                self.z_return(0)
                self.final().start()

        @pl.when(jnp.logical_and(p.matched, jnp.logical_not(p.inner)))
        def _():
            self.z_free(0)

    def z1(self):
        @pl.when(jnp.logical_and(self.p.matched, self.p.inner))
        def _():
            for level in range(1, self.levels):
                start, size = self.span(level)
                self.landed(self.zbuf[level], 8, level)
                piece = self.rows_of(start, size)
                add_rows(size, piece, piece, self.zbuf[level])
                self.z_free(level)
                if level + 1 < self.levels:
                    self.z_copy(level + 1).start()
                else:
                    self.z_return(level)

    def g1(self):
        @pl.when(jnp.logical_and(self.p.matched, self.p.inner))
        def _():
            for level in range(self.levels - 1, 0, -1):
                start, size = self.span(level - 1)
                half = size // 2
                self.landed(self.rows_of(start + (1 - self.p.group_bit(level)) * half, half), 10, level)
                self.z_return(level - 1)
                if level == 1:
                    self.final().start()

    def g0(self):
        @pl.when(jnp.logical_and(self.p.matched, jnp.logical_not(self.p.inner)))
        def _():
            self.landed(self.acc, 10, 0)
            self.final().start()

    def final(self):
        return remote(self.acc, self.acc, self.sem(12), self.sem(13), self.p.sibling())

    def store(self, stores):
        @pl.when(jnp.logical_not(self.p.matched))
        def _():
            self.final().wait_recv()

        copies = [
            pltpu.make_async_copy(self.acc.at[pl.ds(row, rows), pl.ds(col, cols)], out, sem)
            for row, rows, col, cols, out, sem in stores
        ]
        for copy in copies:
            copy.start()
        return copies

    def drain_plane(self):
        p = self.p
        for copy in self.copies_y():
            copy.wait_send()

        @pl.when(jnp.logical_not(p.matched))
        def _():
            for copy in self.copies_x():
                copy.wait_send()
            self.left(self.recv_a.at[0], 4)

        @pl.when(p.matched)
        def _():
            for s in range(1, p.rows):
                self.left(self.recv_b.at[0], 6, s)

    def drain(self):
        p = self.p
        if self.summed is None:
            self.drain_plane()

        @pl.when(p.matched)
        def _():
            self.final().wait_send()

        @pl.when(jnp.logical_and(p.matched, p.inner))
        def _():
            for level in range(self.levels):
                self.z_back(level).wait_send()


def grad_rows(rows, planes):
    tile = 16 * max(1, planes // 2)
    return -(-rows // tile) * tile


def grad_bufs(rows, cols, blocks, planes, summed=False, share=5 / 16):
    a = first_share(rows, share)
    V = lambda *shape: pltpu.VMEM(shape, jnp.bfloat16)
    levels = (planes - 1).bit_length()
    full = grad_rows(rows, planes)
    none = V(16, 128)
    plane = [none, none] if summed else [V(blocks - 1, a, cols), V(blocks, rows - a, cols)]
    more = none if summed or blocks <= 2 else V(blocks - 2, rows - a, cols)
    return plane + [V(full, cols), more, [V(full >> i, cols) for i in range(levels)]]


def plane_bufs(rows, cols, blocks, planes):
    return grad_bufs(rows, cols, blocks, planes, False, 1 / 2)[:4]


def block_rows(i, size=BLOCK):
    return pl.ds(pl.multiple_of(i * size, size), size)


def gelu_parts(gate):
    phi = 0.5 * (1.0 + lax.erf(gate * (1.0 / math.sqrt(2.0))))
    return phi, jnp.exp(gate * gate * -0.5) * (1.0 / math.sqrt(2.0 * math.pi))


def forward_kernel(
    chunks,
    tokens_ref, cot_ref, lengths_ref, first_gain_ref, second_gain_ref, freq_ref, joined_ref, mixer_ref, expand_ref, shrink_ref,
    *rest,
):
    n_chunks = len(chunks)
    outs, scratch = rest[:20], rest[20:]
    (o_tokens, o_first, o_q, o_k, o_v, o_mixed, o_lse, o_xhat, o_inv, o_top, o_own, o_other, o_back,
     o_expand, o_shrink, o_joined, o_mixer, o_small, o_table, o_sum) = outs
    (tok, cot, meta_src, meta, gains_ref, gains, table, first, wj, wm, wg, wu, ws, q_s, k_s, v_s, v_t, out_t, lse, mixed, xhat, inv, second,
     top, shrunk, back, other_half, hid, dgate, dup, g_expand, g_shrink, sum_bufs, sum_sem,
     tok_send, tok_recv, cot_send, cot_recv, swap_send, meta_send, meta_recv, gain_send, gain_recv,
     w_y, w_x, w_z, w_recv, w_recv_z, w_local, mix_send, mix_recv, mixed_send, mixed_recv, out_sem) = scratch
    p = Place()
    rows, seqs = p.rows, p.seqs
    width = tokens_ref.shape[1]
    wide = q_s.shape[1]
    pairs = wide // PAIR
    sems = (w_y, w_x, w_z, w_recv, w_recv_z, w_local)

    def down(ref, buf, col, size):
        source = lambda start, n: ref.at[:, pl.ds(start, n), pl.ds(col, size)]
        slot = lambda row, start, n: buf.at[:, pl.ds(row * width + start, n), :]
        return source, slot

    def along(ref, buf, at):
        source = lambda start, n: ref.at[pl.ds(at + start, n), :]
        slot = lambda row, start, n: buf.at[pl.ds(start, n), pl.ds(pl.multiple_of(row * width, width), width)]
        return source, slot

    half = wide // 2
    joined = [Weight(p, *down(joined_ref, wj.at[h], half * h, half), width, sems, h, 0.25) for h in range(2)]
    mixer = Weight(p, *along(mixer_ref, wm.at[p.core], 0), wide, sems, 2, 0.41)
    groups, at = [], 0
    for i, count in enumerate(chunks):
        groups.append([
            Weight(p, *along(ref, buf, at), count, sems, 3 + 3 * i + n, 0.41)
            for n, (ref, buf) in enumerate(((expand_ref.at[0], wg[i]), (expand_ref.at[1], wu[i]), (shrink_ref, ws[i])))
        ])
        at += count

    place_row = lanes_of((1, LEN))
    for s in range(seqs):
        base = [lengths_ref[p.col * seqs + s, d] for d in range(DOCS)]
        segment = jnp.zeros((1, LEN), jnp.int32)
        start = jnp.zeros((1, LEN), jnp.int32)
        end = jnp.int32(0)
        for d in range(DOCS):
            end = end + base[d]
            past = place_row >= end
            segment = segment + past.astype(jnp.int32)
            start = jnp.where(past, end, start)
        meta_src[s, 0:1, :] = (place_row - start).astype(jnp.float32)
        meta_src[s, 1:2, :] = segment.astype(jnp.float32)
        meta_src[s, 2:3, :] = (segment < DOCS - 1).astype(jnp.float32)
        meta_src[s, 3:8, :] = jnp.zeros((5, LEN), jnp.float32)

    gains_ref[0:1, :] = first_gain_ref[...]
    gains_ref[1:2, :] = second_gain_ref[...]
    gains_ref[2:8, :] = jnp.zeros((6, width), jnp.float32)
    p.barrier([p.across(), p.pair()])

    is_here = p.core == p.row // seqs

    blocks = range(LEN // BLOCK)

    def send_seq(ref, buf, send, recv, block):
        for t in range(seqs):
            seq = lax.rem(p.row + t, seqs)
            piece = ref.at[pl.ds(pl.multiple_of(seq * LEN + block * BLOCK, BLOCK), BLOCK), :]
            place = buf.at[p.row, pl.ds(block * BLOCK, BLOCK), :]
            target = p.at(core=p.row // seqs, row=p.core * seqs + seq)

            def away():
                remote(piece, place, send.at[t, block], recv.at[p.row, block], target).start()

            if t:
                away()
            else:
                pl.when(jnp.logical_not(is_here))(away)

                @pl.when(is_here)
                def _():
                    pltpu.make_async_copy(piece, place, recv.at[p.row, block]).start()

    def swap_seq(buf, slot, recv, swap, u, block):
        piece = buf.at[slot, pl.ds(block * BLOCK, BLOCK), :]
        return remote(piece, piece, swap.at[u, block], recv.at[slot, block], p.sibling())

    def take_seq(buf, recv, swap, block):
        for u in range(seqs):
            slot = p.core * seqs + u
            piece = buf.at[slot, pl.ds(block * BLOCK, BLOCK), :]
            pltpu.make_async_copy(piece, piece, recv.at[slot, block]).wait()
            swap_seq(buf, slot, recv, swap, u, block).start()

    def finish_seq(buf, recv, swap, block):
        for u in range(seqs):
            swap_seq(buf, (1 - p.core) * seqs + u, recv, swap, u, block).wait_recv()

    def drain_seq(buf, send, recv, swap):
        for block in blocks:
            piece = buf.at[0, pl.ds(0, BLOCK), :]
            for u in range(seqs):
                swap_seq(buf, 0, recv, swap, u, block).wait_send()
                if u:
                    remote(piece, piece, send.at[u, block], recv.at[0, block], p.sibling()).wait_send()

            @pl.when(jnp.logical_not(is_here))
            def _():
                remote(piece, piece, send.at[0, block], recv.at[0, block], p.sibling()).wait_send()

    sends_meta = lax.rem(p.row, seqs) == 0

    @pl.when(sends_meta)
    def _():
        for t in range(seqs):
            target = p.at(core=p.row // seqs, row=p.core * seqs + t)

            def away():
                remote(meta_src.at[t], meta, meta_send.at[t], meta_recv, target).start()

            if t:
                away()
            else:
                pl.when(jnp.logical_not(is_here))(away)

                @pl.when(is_here)
                def _():
                    pltpu.make_async_copy(meta_src.at[t], meta, meta_recv).start()

    for step in range(1, rows):
        remote(gains_ref, gains.at[p.row], gain_send.at[step], gain_recv.at[p.row], p.at(row=p.row_after(step))).start()
    pltpu.make_async_copy(gains_ref, gains.at[p.row], gain_recv.at[p.row]).start()
    def service(matched, unmatched):
        for here, actions in ((p.matched, matched), (jnp.logical_not(p.matched), unmatched)):
            if actions:

                @pl.when(here)
                def _():
                    for action in actions:
                        action()

    tokens_of = [functools.partial(send_seq, tokens_ref, tok, tok_send, tok_recv, block) for block in blocks]
    cot_of = [functools.partial(send_seq, cot_ref, cot, cot_send, cot_recv, block) for block in blocks]
    j0, j1 = joined
    (g0, u0, s0), (g1, u1, s1), (g2, u2, s2) = groups

    def each(action, *weights):
        return [functools.partial(getattr(weight, action)) for weight in weights]

    service(
        [g0.own_x, tokens_of[3], j1.own_x, j0.own_x, j0.own_y, tokens_of[1], j0.pass_on, tokens_of[2], tokens_of[0], g0.own_y, j1.own_y],
        [g0.take_first, tokens_of[2], tokens_of[0], tokens_of[1], j0.take_first],
    )

    def gain_of(kind):
        return jnp.concatenate([gains[j, kind : kind + 1, :] for j in range(rows)], axis=1)

    def norm(values):
        center = jnp.mean(values, axis=-1, keepdims=True)
        values = values - center
        spread = jnp.mean(values * values, axis=-1, keepdims=True)
        scale = lax.rsqrt(spread + norm_eps)
        return values * scale, scale

    def tokens_at(cut):
        return jnp.concatenate([tok[j, cut, :] for j in range(rows)], axis=1).astype(jnp.float32)

    def first_norm(block):
        cut = slice(block * BLOCK, (block + 1) * BLOCK)
        finish_seq(tok, tok_recv, swap_send.at[0], block)
        first[cut, :] = (norm(tokens_at(cut))[0] * gain_a).astype(jnp.bfloat16)

    for step in range(1, rows):
        row = p.row_before(step)
        remote(gains.at[row], gains.at[row], gain_send.at[step], gain_recv.at[row], p.sibling()).wait_recv()
    pltpu.make_async_copy(gains.at[p.row], gains.at[p.row], gain_recv.at[p.row]).wait()
    gain_a, gain_b = gain_of(0), gain_of(1)
    pltpu.make_async_copy(meta, meta, meta_recv).wait()
    columns = meta[...].T
    angle = columns[:, 0:1] * freq_ref[0:1, :]
    sign = jnp.where(lanes_of((1, PAIR)) % HD < HD // 2, -1.0, 1.0)
    table[0] = jnp.cos(angle)
    table[1] = jnp.sin(angle) * sign
    segment_col, valid_col = columns[:, 1:2], columns[:, 2:3]
    take_seq(tok, tok_recv, swap_send.at[0], 0)
    service([], [tokens_of[3]])
    take_seq(tok, tok_recv, swap_send.at[0], 1)
    service(
        [mixer.own_y, u1.own_x, u0.own_x, u0.own_y, j1.pass_on, s0.own_x, s1.own_x, s0.own_y, g0.pass_on],
        [j1.take_first, j0.take_others],
    )
    take_seq(tok, tok_recv, swap_send.at[0], 2)
    service([s1.own_y], [])
    first_norm(0)
    service([g2.own_y], [])
    take_seq(tok, tok_recv, swap_send.at[0], 3)
    first_norm(1)
    service([mixer.own_x], [u1.take_first])
    first_norm(2)
    first_norm(3)
    service([mixer.pass_on], [u0.take_first])

    def project(h):
        cols = slice(h * half, (h + 1) * half)

        @pl.loop(0, LEN // BLOCK)
        def _(i):
            cut = block_rows(i)
            part = first[cut, :]
            cosine, sine = (jnp.concatenate([table[n, cut, :]] * (half // PAIR), axis=1) for n in range(2))
            for j, dst in ((0, q_s), (1, k_s)):
                raw = dot(part, wj[h, j])
                dst[cut, cols] = (raw * cosine + swap_halves(raw) * sine).astype(jnp.bfloat16)
            v_s[cut, cols] = dot(part, wj[h, 2]).astype(jnp.bfloat16)

    def attention(pair, between):
        cols = slice(pair * PAIR, (pair + 1) * PAIR)
        v_t[...] = v_s[:, cols].astype(jnp.float32).T.astype(jnp.bfloat16)
        for head in range(2):
            lanes = slice(head * HD, (head + 1) * HD)

            @pl.loop(0, LEN // BLOCK)
            def _(i):
                cut = block_rows(i)
                scores = dot(k_s[:, cols], only_head(q_s[cut, cols], head), NT)
                scores = jnp.where(segment_col == meta[1:2, cut], scores, masked_value)
                peak = jnp.max(scores, axis=0, keepdims=True)
                weights = jnp.exp2((scores - peak) * TO_EXP2)
                total = jnp.sum(weights, axis=0, keepdims=True)
                out_t[lanes, cut] = dot(v_t[lanes, :], weights.astype(jnp.bfloat16)) / total
                lse[pair, head : head + 1, cut] = peak * TO_EXP2 + jnp.log2(total)

            if head == 0:
                service(*between)

        mixed[p.core, :, cols] = out_t[...].T.astype(jnp.bfloat16)
        piece = mixed.at[p.core, :, cols]
        remote(piece, piece, mixed_send.at[pair], mixed_recv.at[pair], p.sibling()).start()

    def share_mixer():
        mixer.finish()
        piece = wm.at[p.core]
        remote(piece, piece, mix_send, mix_recv, p.sibling()).start()

    j0.finish()
    project(0)
    service([u1.own_y], [])
    attention(0, ([*cot_of], []))
    service([s0.pass_on, g1.own_y, s2.own_y, u0.pass_on], [j1.take_others])
    attention(1, ([], []))
    service([u2.own_x, g1.own_x], [s1.take_first, *cot_of, s0.take_first])
    j1.finish()
    project(1)
    service([], [g0.take_others])
    attention(2, ([], [mixer.take_first]))
    service([u1.pass_on, s1.pass_on], [mixer.take_others])
    attention(3, ([], []))
    service([s2.own_x], [])
    service([g2.own_x, g1.pass_on, g2.pass_on], [])
    share_mixer()
    service([], [s0.take_others, u0.take_others])
    for block in blocks:
        take_seq(cot, cot_recv, swap_send.at[1], block)

    for pair in range(pairs):
        piece = mixed.at[p.core, :, pair * PAIR : (pair + 1) * PAIR]
        remote(piece, piece, mixed_send.at[pair], mixed_recv.at[pair], p.sibling()).wait_recv()
    piece = wm.at[p.core]
    remote(piece, piece, mix_send, mix_recv, p.sibling()).wait_recv()
    for block in blocks:
        finish_seq(cot, cot_recv, swap_send.at[1], block)

    @pl.loop(0, LEN // BLOCK)
    def _(i):
        cut = block_rows(i)
        value = tokens_at(cut) + dot(mixed[0, cut, :], wm[0]) + dot(mixed[1, cut, :], wm[1])
        normed, scale = norm(value)
        xhat[cut, :] = normed.astype(jnp.bfloat16)
        inv[cut, :] = jnp.broadcast_to(scale, (BLOCK, PAIR))
        second[cut, :] = (normed * gain_b).astype(jnp.bfloat16)
        shrunk[cut, :] = jnp.where(lanes_of((1, D)) // (D // CORES) == p.core, value, 0.0)

    valid_16 = valid_col > 0.5
    top[...] = jnp.where(valid_16, jnp.concatenate([cot[j] for j in range(rows)], axis=1), jnp.zeros((), jnp.bfloat16))

    keep = []

    def store(src, dst):
        copy = pltpu.make_async_copy(src, dst, out_sem.at[len(keep)])
        keep.append(copy)
        copy.start()
        return copy

    for j in range(rows):
        store(tok.at[j], o_tokens.at[j])
    for src, dst in ((first, o_first), (q_s, o_q), (k_s, o_k), (v_s, o_v), (mixed.at[p.core], o_mixed), (lse, o_lse),
                     (inv, o_inv), (table, o_table), (top, o_top), (wj.at[0], o_joined.at[0]), (wj.at[1], o_joined.at[1]), (wm.at[p.core], o_mixer)):
        store(src, dst)
    xhat_copy = store(xhat, o_xhat)
    for j in range(rows):
        store(gains.at[j], o_small.at[:, pl.ds(j * width, width)])
    store(meta, o_small.at[:, pl.ds(D, LEN)])

    service([], [u1.take_others, g1.take_first])
    early = [
        ([], []),
        ([], [g2.take_others]),
        ([], []),
    ]
    middle = [
        ([u2.own_y, s2.pass_on], [g1.take_others, g2.take_first, s2.take_first]),
        ([], [u2.take_others]),
        ([], []),
    ]
    ready = [
        ([], [s1.take_others]),
        ([], []),
        ([], []),
    ]
    late = [
        ([u2.pass_on], [s2.take_others, u2.take_first]),
        ([], []),
        ([], []),
    ]

    def first_block(row, start, size):
        return g_expand[0].at[pl.ds(start, size), pl.ds(pl.multiple_of(row * width, width), width)]

    plane = Grad(p, first_block, 2 * chunks[0], (*sum_bufs, []), sum_sem, None, 0, share=1 / 2)
    then_early = [[], [], [plane.sum_x]]
    at = 0
    for i, lanes in enumerate(chunks):
        if i + 1 == n_chunks:
            xhat_copy.wait()
        for weight in groups[i]:
            weight.finish()
        service(*ready[i])

        @pl.loop(0, LEN // WIDE_BLOCK)
        def _(t):
            cut = block_rows(t, WIDE_BLOCK)
            part, grad = second[cut, :], top[cut, :]
            gate = dot(part, wg[i][...], NT)
            up = dot(part, wu[i][...], NT)
            hidden_grad = dot(grad, ws[i][...], NT).astype(jnp.bfloat16).astype(jnp.float32)
            phi, density = gelu_parts(gate)
            act = gate * phi
            hidden = (act * up).astype(jnp.bfloat16)
            d_gate = (hidden_grad * up * (phi + gate * density)).astype(jnp.bfloat16)
            d_up = (hidden_grad * act).astype(jnp.bfloat16)
            hid[cut, :lanes] = hidden
            dgate[cut, :lanes] = d_gate
            dup[cut, :lanes] = d_up
            value = shrunk[cut, :] + dot(hidden, ws[i][...])
            grad_sum = dot(d_gate, wg[i][...]) + dot(d_up, wu[i][...])
            if i:
                grad_sum = back[cut, :] + grad_sum
            if i + 1 < n_chunks:
                shrunk[cut, :] = value
                back[cut, :] = grad_sum
            else:
                xhat[cut, :] = grad_sum.astype(jnp.bfloat16)
                left, right = value[:, : D // 2], value[:, D // 2 :]
                shrunk[cut, : D // 2] = jnp.where(p.core == 0, left, right)
                other_half[cut, :] = jnp.where(p.core == 0, right, left).astype(jnp.bfloat16)

            @pl.when(t == LEN // WIDE_BLOCK // 2 - 1)
            def _():
                service(*early[i])
                for action in then_early[i]:
                    action()


        service(*middle[i])
        if i == 1:
            plane.sum_y()
        if i + 1 == n_chunks:
            store(xhat, o_back)
            store(shrunk.at[:, pl.ds(0, D // 2)], o_own)
            store(other_half, o_other)
        for n, (left, right) in enumerate(((dgate, second), (dup, second), (hid, top))):
            target = g_shrink[i] if n == 2 else g_expand[i]
            for start in range(0, lanes, BLOCK):
                size = min(BLOCK, lanes - start)
                spot = start if n == 2 else n * lanes + start
                target[spot : spot + size, :] = dot(left[:, start : start + size], right[...], TN).astype(jnp.bfloat16)
            if n == 1 and i == 0:
                plane.begin_y()
                plane.begin_x()

        if i:
            store(g_expand[i], o_expand.at[pl.ds(2 * at, 2 * lanes), :])
        store(g_shrink[i], o_shrink.at[pl.ds(at, lanes), :])
        service(*late[i])
        at += lanes

    plane.plane_sum()
    store(plane.acc, o_sum)

    plane.drain_plane()
    drain_seq(tok, tok_send, tok_recv, swap_send.at[0])
    drain_seq(cot, cot_send, cot_recv, swap_send.at[1])
    for step in range(1, rows):
        remote(gains_ref, gains.at[p.row], gain_send.at[step], gain_recv.at[p.row], p.sibling()).wait_send()

    @pl.when(sends_meta)
    def _():
        for t in range(1, seqs):
            remote(meta_src.at[t], meta, meta_send.at[t], meta_recv, p.sibling()).wait_send()

        @pl.when(jnp.logical_not(is_here))
        def _():
            remote(meta_src.at[0], meta, meta_send.at[0], meta_recv, p.sibling()).wait_send()

    for pair in range(pairs):
        piece = mixed.at[p.core, :, pair * PAIR : (pair + 1) * PAIR]
        remote(piece, piece, mixed_send.at[pair], mixed_recv.at[pair], p.sibling()).wait_send()
    piece = wm.at[p.core]
    remote(piece, piece, mix_send, mix_recv, p.sibling()).wait_send()
    for weight in joined + [mixer] + sum(groups, []):
        weight.drain()
    for copy in keep:
        if copy is not xhat_copy:
            copy.wait()


def forward(tokens, cot, lengths, first_gain, second_gain, joined, mixer, expand, shrink, chunks):
    rows = lax.axis_size("row")
    seqs = rows // CORES
    width = tokens.shape[1]
    wide = mixer.shape[0]
    pairs = wide // PAIR
    blocks = LEN // BLOCK
    n_chunks = len(chunks)
    hidden_here = sum(chunks)
    planes = lax.axis_size("dp") // CORES
    weights = 3 + 3 * n_chunks
    bf16, f32 = jnp.bfloat16, jnp.float32
    freq = np.tile((rope_base ** (-2.0 * np.arange(HD // 2) / HD)).astype(np.float32), (8, 4))
    outs = [
        ((rows, LEN, width), bf16), ((LEN, D), bf16), ((LEN, wide), bf16), ((LEN, wide), bf16), ((LEN, wide), bf16),
        ((LEN, wide), bf16), ((pairs, 2, LEN), f32), ((LEN, D), bf16), ((LEN, PAIR), f32), ((LEN, D), bf16),
        ((LEN, D // 2), f32), ((LEN, D // 2), bf16), ((LEN, D), bf16),
        ((2 * hidden_here, D), bf16), ((hidden_here, D), bf16), ((2, 3, D, wide // 2), bf16), ((wide, D), bf16),
        ((8, D + LEN), f32), ((2, LEN, PAIR), f32), ((grad_rows(2 * chunks[0], planes), width), bf16),
    ]
    V, dma = pltpu.VMEM, pltpu.SemaphoreType.DMA
    widest = max(chunks)
    scratch = [
        V((rows, LEN, width), bf16), V((rows, LEN, width), bf16), V((seqs, 8, LEN), f32), V((8, LEN), f32),
        V((8, width), f32), V((rows, 8, width), f32), V((2, LEN, PAIR), f32), V((LEN, D), bf16), V((2, 3, D, wide // 2), bf16), V((CORES, wide, D), bf16),
        [V((lanes, D), bf16) for lanes in chunks], [V((lanes, D), bf16) for lanes in chunks], [V((lanes, D), bf16) for lanes in chunks],
        V((LEN, wide), bf16), V((LEN, wide), bf16), V((LEN, wide), bf16), V((PAIR, LEN), bf16), V((PAIR, LEN), f32),
        V((pairs, 2, LEN), f32), V((CORES, LEN, wide), bf16), V((LEN, D), bf16), V((LEN, PAIR), f32), V((LEN, D), bf16),
        V((LEN, D), bf16), V((LEN, D), f32), V((LEN, D), f32), V((LEN, D // 2), bf16), V((LEN, widest), bf16), V((LEN, widest), bf16), V((LEN, widest), bf16),
        [V((2 * lanes, D), bf16) for lanes in chunks],
        [V((lanes, D), bf16) for lanes in chunks],
        plane_bufs(2 * chunks[0], width, rows, planes), dma((1, 14, rows)),
        dma((seqs, blocks)), dma((rows, blocks)), dma((seqs, blocks)), dma((rows, blocks)), dma((2, seqs, blocks)), dma((seqs,)), dma,
        dma((rows,)), dma((rows,)),
        dma((weights, rows)), dma((weights, rows)), dma((weights, rows)), dma((weights, rows)), dma((weights, rows)),
        dma((weights,)), dma, dma, dma((pairs,)), dma((pairs,)), dma((2 * rows + 17 + 3 * n_chunks,)),
    ]
    anywhere = pl.BlockSpec(memory_space=pl.ANY)
    in_specs = [anywhere] * 10
    in_specs[2] = pl.BlockSpec(memory_space=pltpu.SMEM)
    in_specs[3:6] = [pl.BlockSpec(memory_space=pltpu.VMEM)] * 3
    return pl.pallas_call(
        functools.partial(forward_kernel, chunks),
        in_specs=in_specs,
        out_specs=[anywhere] * len(outs),
        out_shape=[jax.ShapeDtypeStruct(*o) for o in outs],
        scratch_shapes=scratch,
        compiler_params=pltpu.CompilerParams(
            collective_id=0, has_side_effects=True, vmem_limit_bytes=62 * 1024 * 1024
        ),
        name="layer_forward",
    )(tokens, cot, lengths, first_gain[None, :], second_gain[None, :], freq, joined, mixer, expand, shrink)


def backward_kernel(
    chunks,
    tokens_ref, first_ref, q_ref, k_ref, v_ref, mixed_ref, lse_ref, xhat_ref, inv_ref, top_ref, own_ref, other_ref, back_ref,
    expand_ref, shrink_ref, joined_ref, mixer_ref, small_ref, table_ref, sum_ref,
    o_block, o_input, o_joined, o_mixer, o_expand, o_shrink, o_gains,
    q_s, k_s, v_s, mixed, xa, xb, xc, wj, wm, lse, inv, small, table, other, keep_grad, middle_low, mixed_grad, g_mixer, g_joined,
    dk, dv, dq_t, k_t, delta, own_half, block_half, gain_sum, gain_y, gain_x, gain_z, stage_lane, grad_scratch,
    load_sem, stage_sem, sum_sem, grad_sem, credit, swap_credit, back_send, back_recv, other_send, other_recv, first_send, first_recv,
    out_send, out_recv, in_send, in_recv, gain_send, gain_recv, out_sem,
):
    p = Place()
    rows, seqs, planes = p.rows, p.seqs, p.planes
    width = D // rows
    wide = q_s.shape[1]
    pairs = wide // PAIR
    levels = (planes - 1).bit_length()
    half = wide // 2

    def by_row(ref):
        return lambda j, start, size: ref.at[pl.ds(pl.multiple_of(j * width + start, 16), size), :]

    def by_lane(ref, at=0):
        return lambda j, start, size: ref.at[pl.ds(at + start, size), pl.ds(pl.multiple_of(j * width, width), width)]

    grads, places, at = {}, {}, 0
    stage = (stage_lane, stage_sem)

    def add_grad(name, block, count, stage, stores, summed=None):
        i = len(grads)
        grads[name] = Grad(p, block, count, grad_scratch[i], grad_sem, credit, i, stage, summed)
        places[name] = stores

    for i, count in enumerate(chunks):
        add_grad(("E", i), by_lane(expand_ref, 2 * at), 2 * count, stage,
                 [(j * count, count, 0, width, o_expand.at[j, pl.ds(at, count), :]) for j in range(2)],
                 None if i else pltpu.make_async_copy(sum_ref, grad_scratch[0][2], sum_sem))
        add_grad(("S", i), by_lane(shrink_ref, at), count, stage, [(0, count, 0, width, o_shrink.at[pl.ds(at, count), :])])
        at += count
    for h in range(2):
        add_grad(("J", h), by_row(g_joined.at[h]), width, None,
                 [(0, width, j * half, half, o_joined.at[j, :, pl.ds(h * half, half)]) for j in range(3)])
    add_grad(("M", 0), by_lane(g_mixer), wide, None, [(0, wide, 0, width, o_mixer)])

    loads = {}

    def load(name, src, dst):
        copy = pltpu.make_async_copy(src, dst, load_sem.at[len(loads)])
        copy.start()
        loads[name] = copy

    load("small", small_ref, small)
    load("back", back_ref, xc)
    load("xhat", xhat_ref, xa)
    load("inv", inv_ref, inv)
    load("top", top_ref, xb)
    load("mixer", mixer_ref, wm)
    load("mixed", mixed_ref, mixed)
    load("q", q_ref, q_s)
    load("k", k_ref, k_s)
    load("v", v_ref, v_s)
    load("lse", lse_ref, lse)
    load("table", table_ref, table)
    load("joined", joined_ref, wj)
    load("own", own_ref, own_half)
    pl.when(p.matched)(grads["E", 0].summed.start)
    p.barrier([p.across()] + [p.mate(level) for level in range(levels)])

    def swap_block(i, src, dst, send, recv):
        cut = pl.ds(i * BLOCK, BLOCK)
        return remote(src.at[cut, :], dst.at[cut, :], send.at[i], recv.at[i], p.sibling())

    blocks_n = LEN // BLOCK
    for i in range(blocks_n):
        swap_block(i, back_ref, other, back_send, back_recv).start()

    stores = []

    def run(*todo):
        for step in todo:
            if callable(step):
                step()
                continue
            action, kind, i = step
            grad = grads[kind, i]
            if action == "store":
                spots = [spot + (out_sem.at[len(stores) + n],) for n, spot in enumerate(places[kind, i])]
                stores.extend(grad.store(spots))
            elif action == "begin":
                grad.begin_y()
                grad.begin_x()
            else:
                getattr(grad, action)()

    run(("begin_x", "E", 1), ("begin_y", "E", 2), ("begin_x", "S", 0), ("begin_y", "S", 2), ("begin_y", "E", 1))
    other_copy = remote(other_ref, block_half, other_send, other_recv, p.sibling())
    other_copy.start()

    for name in ("small", "back", "xhat", "inv", "top", "mixer", "mixed"):
        loads[name].wait()
    gain_a, gain_b = small[0:1, :D], small[1:2, :D]
    gain_sum[...] = jnp.zeros_like(gain_sum)
    for grad in grads.values():
        if grad.full != grad.m and grad.summed is None:
            grad.acc[grad.m :, :] = jnp.zeros((grad.full - grad.m, grad.acc.shape[1]), jnp.bfloat16)

    def norm_back(grad, normed, scale, gain):
        scaled = grad * gain
        mean_a = jnp.mean(scaled, axis=-1, keepdims=True)
        mean_b = jnp.mean(scaled * normed, axis=-1, keepdims=True)
        return scale * (scaled - mean_a - normed * mean_b)

    def own_of(value):
        return jnp.where(p.core == 0, value[:, : D // 2], value[:, D // 2 :])

    def second_norm(i):
        cut = slice(i * BLOCK, (i + 1) * BLOCK)
        swap_block(i, back_ref, other, back_send, back_recv).wait_recv()
        grad = xc[cut, :].astype(jnp.float32) + other[cut, :].astype(jnp.float32)
        normed = xa[cut, :].astype(jnp.float32)
        gain_sum[1:2, :] += jnp.sum(grad * normed, axis=0, keepdims=True)
        value = xb[cut, :].astype(jnp.float32) + norm_back(grad, normed, inv[cut, 0:1], gain_b)
        keep_grad[cut, :] = own_of(value)
        value = value.astype(jnp.bfloat16)
        middle_low[cut, :] = value
        mixed_grad[cut, :] = dot(value, wm[...], NT).astype(jnp.bfloat16)
    second_norm(0)
    second_norm(1)
    run(("begin_y", "S", 0))
    second_norm(2)
    second_norm(3)
    pl.semaphore_signal(swap_credit, inc=1, device_id=p.sibling(), device_id_type=MESH_ID)
    run(("begin_x", "S", 2))
    @pl.loop(0, D // BLOCK)
    def _(d):
        cut = block_rows(d)
        g_mixer[:, cut] = dot(mixed[...], middle_low[:, cut], TN).astype(jnp.bfloat16)

    load("first", first_ref, xa)
    for j in range(rows):
        load(f"tokens{j}", tokens_ref.at[j], xb.at[:, pl.ds(j * width, width)])

    def leave(src, dst, send, recv):
        core, seq = p.row // seqs, lax.rem(p.row, seqs)
        copies = []
        for u in range(seqs):
            row = p.core * seqs + u
            is_self = jnp.logical_and(core == p.core, row == p.row)
            piece = src.at[:, pl.ds(u * width, width)]
            copies.append((is_self, piece, dst(seq), send.at[u], recv.at[seq], p.at(core=core, row=row)))
        return copies

    def leave_start(copies):
        for is_self, piece, place, send, recv, target in copies:
            @pl.when(is_self)
            def _():
                pltpu.make_async_copy(piece, place, recv).start()

            @pl.when(jnp.logical_not(is_self))
            def _():
                remote(piece, place, send, recv, target).start()

    def leave_wait(copies, dst, recv):
        for s in range(seqs):
            pltpu.make_async_copy(dst(s), dst(s), recv.at[s]).wait()
        for is_self, piece, place, send, recv_sem, target in copies:
            @pl.when(jnp.logical_not(is_self))
            def _():
                remote(piece, place, send, recv_sem, target).wait_send()

    out_at = lambda s: o_block.at[pl.ds(pl.multiple_of(s * LEN, LEN), LEN), :]
    in_at = lambda s: o_input.at[pl.ds(pl.multiple_of(s * LEN, LEN), LEN), :]
    out_copies = leave(block_half, out_at, out_send, out_recv)
    in_copies = leave(mixed_grad, in_at, in_send, in_recv)

    def block_output():
        loads["own"].wait()
        other_copy.wait()
        add_rows(LEN, block_half, own_half, block_half)
        leave_start(out_copies)

    for name in ("q", "k", "v", "lse", "table"):
        loads[name].wait()
    columns = small[:, D:].T
    segment_col = columns[:, 1:2]

    def attention_start(pair):
        cols = slice(pair * PAIR, (pair + 1) * PAIR)
        product = mixed[:, cols].astype(jnp.float32) * mixed_grad[:, cols].astype(jnp.float32)
        chooser = lax.broadcasted_iota(jnp.int32, (8, PAIR), 0) == lanes_of((8, PAIR)) // HD
        delta[...] = dot(chooser.astype(jnp.float32), product, NT, precision=lax.Precision.HIGHEST)
        k_t[...] = k_s[:, cols].astype(jnp.float32).T.astype(jnp.bfloat16)
        dk[...] = jnp.zeros_like(dk)
        dv[...] = jnp.zeros_like(dv)

    def attention_head(pair, head):
        cols = slice(pair * PAIR, (pair + 1) * PAIR)
        keys, values = k_s[:, cols], v_s[:, cols]
        lanes = slice(head * HD, (head + 1) * HD)
        for i in range(LEN // BLOCK):
            cut = slice(i * BLOCK, (i + 1) * BLOCK)
            q_part, g_part = only_head(q_s[cut, cols], head), only_head(mixed_grad[cut, cols], head)
            scores = dot(keys, q_part, NT)
            probs = jnp.exp2(scores * TO_EXP2 - lse[pair, head : head + 1, cut])
            probs = jnp.where(segment_col == small[1:2, D + i * BLOCK : D + (i + 1) * BLOCK], probs, 0.0)
            probs_grad = dot(values, g_part, NT)
            scores_grad = (probs * (probs_grad - delta[head : head + 1, cut])).astype(jnp.bfloat16)
            dv[...] += dot(probs.astype(jnp.bfloat16), g_part)
            dk[...] += dot(scores_grad, q_part)
            dq_t[lanes, cut] = dot(k_t[lanes, :], scores_grad)

    def attention_end(pair):
        cols = slice(pair * PAIR, (pair + 1) * PAIR)
        cosine, sine = table[0], table[1]
        scale = 1.0 / math.sqrt(HD)
        dqs = dq_t[...].T * scale
        q_s[:, cols] = (dqs * cosine - swap_halves(dqs) * sine).astype(jnp.bfloat16)
        dks = dk[...] * scale
        k_s[:, cols] = (dks * cosine - swap_halves(dks) * sine).astype(jnp.bfloat16)
        v_s[:, cols] = dv[...].astype(jnp.bfloat16)

    def joined_weight_grad(h):
        @pl.loop(0, D // BLOCK)
        def _(d):
            cut = block_rows(d)
            part = xa[:, cut]
            for j, back in enumerate((q_s, k_s, v_s)):
                g_joined[h, cut, j * half : (j + 1) * half] = dot(
                    part, back[:, h * half : (h + 1) * half], TN
                ).astype(jnp.bfloat16)

    run(("sum_both", "E", 0))
    attention_start(0)
    attention_head(0, 0)
    attention_head(0, 1)
    attention_end(0)
    attention_start(1)
    attention_head(1, 0)
    attention_head(1, 1)
    attention_end(1)
    run(("z0", "E", 0), ("sum_x", "E", 1), ("sum_y", "E", 1))
    loads["first"].wait()
    joined_weight_grad(0)
    attention_start(2)
    attention_head(2, 0)
    run(
        ("begin_y", "M", 0), ("begin_x", "J", 0), ("sum_y", "S", 2), ("sum_x", "S", 2), ("begin_y", "J", 0),
        ("z1", "E", 0), ("sum_x", "S", 0), ("sum_both", "E", 1),
    )
    attention_head(2, 1)
    attention_end(2)
    attention_start(3)
    attention_head(3, 0)
    attention_head(3, 1)
    attention_end(3)
    run(
        ("sum_both", "S", 2), ("sum_x", "J", 0), ("z0", "E", 1), ("sum_y", "S", 0), ("z0", "S", 2),
        ("sum_both", "S", 0), ("g1", "E", 0), ("begin_x", "E", 2), ("sum_x", "E", 2), ("sum_y", "J", 0),
        ("sum_y", "E", 2), ("z1", "E", 1), ("sum_both", "J", 0), ("sum_both", "E", 2),
    )
    joined_weight_grad(1)
    run(
        ("begin_x", "J", 1), ("begin_y", "J", 1), ("z1", "S", 2), ("z0", "S", 0), ("begin_y", "S", 1),
        ("z0", "J", 0), ("g1", "E", 1), ("sum_x", "J", 1), ("sum_y", "J", 1), ("z1", "S", 0), ("begin_x", "M", 0),
    )
    loads["joined"].wait()
    pl.semaphore_wait(swap_credit, 1)

    def first_back(i):
        cut = slice(i * BLOCK, (i + 1) * BLOCK)
        value = jnp.zeros((BLOCK, D), jnp.float32)
        for h in range(2):
            for j, part in enumerate((q_s, k_s, v_s)):
                value = value + dot(part[cut, h * half : (h + 1) * half], wj[h, j], NT)
        xc[cut, :] = value.astype(jnp.bfloat16)
        swap_block(i, xc, other, first_send, first_recv).start()

    first_back(0)
    first_back(1)

    run(
        ("g0", "E", 0), ("g1", "S", 2), ("z0", "E", 2), ("sum_both", "J", 1), ("z1", "J", 0), ("g1", "S", 0),
        ("begin_x", "S", 1), ("sum_x", "M", 0), ("sum_y", "M", 0), ("sum_y", "S", 1), ("z1", "E", 2), ("g1", "J", 0),
        ("g0", "S", 2), ("sum_x", "S", 1), ("z0", "J", 1), ("sum_both", "M", 0),
    )
    first_back(2)
    first_back(3)
    run(("store", "E", 0), ("sum_both", "S", 1), ("g0", "E", 1), ("g1", "E", 2), ("z1", "J", 1))
    for j in range(rows):
        loads[f"tokens{j}"].wait()
    for i in range(blocks_n):
        cut = slice(i * BLOCK, (i + 1) * BLOCK)
        swap_block(i, xc, other, first_send, first_recv).wait_recv()
        grad = xc[cut, :].astype(jnp.float32) + other[cut, :].astype(jnp.float32)
        values = xb[cut, :].astype(jnp.float32)
        values = values - jnp.mean(values, axis=-1, keepdims=True)
        scale = lax.rsqrt(jnp.mean(values * values, axis=-1, keepdims=True) + norm_eps)
        normed = values * scale
        gain_sum[0:1, :] += jnp.sum(grad * normed, axis=0, keepdims=True)
        total = keep_grad[cut, :] + own_of(norm_back(grad, normed, scale, gain_a))
        mixed_grad[cut, :] = total.astype(jnp.bfloat16)

    def gain_copies():
        return [
            remote(gain_sum.at[:, pl.ds(pl.multiple_of(p.row_after(s) * width, width), width)], gain_y.at[s],
                   gain_send.at[s], gain_recv.at[s], p.at(row=p.row_after(s)))
            for s in range(1, rows)
        ]

    gain_across = remote(gain_x.at[0], gain_x.at[1], gain_send.at[rows], gain_recv.at[rows], p.across())
    gain_total = gain_z.at[2 * levels]
    gain_back = remote(gain_total, gain_total, gain_send.at[rows + 1 + levels], gain_recv.at[rows + 1 + levels], p.sibling())

    def gain_plane(level):
        return remote(gain_z.at[2 * level], gain_z.at[2 * level + 1], gain_send.at[rows + 1 + level],
                      gain_recv.at[rows + 1 + level], p.mate(level))

    def gains_y():
        for s in range(1, rows):
            remote(gain_y.at[s], gain_y.at[s], gain_send.at[s], gain_recv.at[s], p.sibling()).wait_recv()
        total = gain_sum[:, pl.ds(pl.multiple_of(p.row * width, width), width)]
        for s in range(1, rows):
            total = total + gain_y[s]
        gain_x[0] = total
        pl.when(p.matched)(gain_across.start)

    def gains_x():
        @pl.when(jnp.logical_not(p.matched))
        def _():
            gain_across.wait_recv()
            gain_z[0] = gain_x[0] + gain_x[1]
            gain_plane(0).start()

    def gains_z():
        @pl.when(jnp.logical_not(p.matched))
        def _():
            for level in range(levels):
                gain_plane(level).wait()
                gain_z[2 * level + 2] = gain_z[2 * level] + gain_z[2 * level + 1]
                if level + 1 < levels:
                    gain_plane(level + 1).start()
            gain_back.start()
            gain_back.wait_send()

    def gains_end():
        @pl.when(p.matched)
        def _():
            gain_back.wait_recv()
            gain_across.wait_send()

    for copy in gain_copies():
        copy.start()
    leave_start(in_copies)

    run(
        ("z0", "S", 1), ("g1", "J", 1), ("z0", "M", 0), ("g0", "J", 1), gains_y, ("store", "S", 2), ("z1", "S", 1),
        ("store", "E", 1), ("z1", "M", 0), ("g1", "S", 1), gains_x, ("g0", "E", 2), block_output, ("g0", "S", 1),
        ("g0", "S", 0), ("store", "J", 1), ("g0", "J", 0), gains_z, ("store", "S", 0), ("store", "J", 0),
        ("g1", "M", 0), ("store", "E", 2), ("store", "S", 1), ("g0", "M", 0), ("store", "M", 0),
    )
    gains_end()
    gains_out = pltpu.make_async_copy(gain_z.at[2 * levels], o_gains, out_sem.at[len(stores)])
    gains_out.start()

    leave_wait(out_copies, out_at, out_recv)
    leave_wait(in_copies, in_at, in_recv)
    for i in range(blocks_n):
        swap_block(i, back_ref, other, back_send, back_recv).wait_send()
        swap_block(i, xc, other, first_send, first_recv).wait_send()
    for copy in gain_copies():
        copy.wait_send()
    for grad in grads.values():
        grad.drain()
    for copy in stores:
        copy.wait()
    gains_out.wait()


def backward(saved, chunks):
    (tokens, first, queries, keys, values, mixed, lse, xhat, inv, top, own, other, back, expand, shrink, joined, mixer,
     small, table, plane_sum) = saved
    rows = lax.axis_size("row")
    planes = lax.axis_size("dp") // CORES
    seqs = rows // CORES
    width = D // rows
    wide = queries.shape[1]
    pairs = wide // PAIR
    hidden_here = sum(chunks)
    widest = 2 * max(chunks)
    levels = (planes - 1).bit_length()
    bf16, f32 = jnp.bfloat16, jnp.float32
    V, dma = pltpu.VMEM, pltpu.SemaphoreType.DMA
    outs = [
        ((seqs * LEN, width), bf16), ((seqs * LEN, width), bf16), ((3, width, wide), bf16), ((wide, width), bf16),
        ((2, hidden_here, width), bf16), ((hidden_here, width), bf16), ((8, width), f32),
    ]
    grad_shapes = []
    for lanes in chunks:
        grad_shapes += [(2 * lanes, width), (lanes, width)]
    grad_shapes += [(width, 3 * wide // 2)] * 2 + [(wide, width)]
    count = len(grad_shapes)
    scratch = [
        V((LEN, wide), bf16), V((LEN, wide), bf16), V((LEN, wide), bf16), V((LEN, wide), bf16),
        V((LEN, D), bf16), V((LEN, D), bf16), V((LEN, D), bf16), V((2, 3, D, wide // 2), bf16), V((wide, D), bf16),
        V((pairs, 2, LEN), f32), V((LEN, PAIR), f32), V((8, D + LEN), f32), V((2, LEN, PAIR), f32), V((LEN, D), bf16),
        V((LEN, D // 2), f32), V((LEN, D), bf16), V((LEN, wide), bf16), V((wide, D), bf16), V((2, D, 3 * wide // 2), bf16),
        V((LEN, PAIR), f32), V((LEN, PAIR), f32), V((PAIR, LEN), f32), V((PAIR, LEN), bf16), V((8, LEN), f32),
        V((LEN, D // 2), f32), V((LEN, D // 2), bf16),
        V((8, D), f32), V((rows, 8, width), f32), V((2, 8, width), f32), V((2 * levels + 1, 8, width), f32),
        V((2, widest - first_share(widest), width), bf16),
        [grad_bufs(*shape, rows, planes, i == 0) for i, shape in enumerate(grad_shapes)],
        dma((15 + rows,)), dma((2,)), dma, dma((count, 14, max(rows, levels))), pltpu.SemaphoreType.REGULAR((count, levels)),
        pltpu.SemaphoreType.REGULAR,
        dma((4,)), dma((4,)), dma, dma, dma((4,)), dma((4,)),
        dma((seqs,)), dma((seqs,)), dma((seqs,)), dma((seqs,)), dma((rows + 2 + levels,)), dma((rows + 2 + levels,)),
        dma((3 * len(chunks) + 8,)),
    ]
    anywhere = pl.BlockSpec(memory_space=pl.ANY)
    return pl.pallas_call(
        functools.partial(backward_kernel, chunks),
        in_specs=[anywhere] * len(saved),
        out_specs=[anywhere] * len(outs),
        out_shape=[jax.ShapeDtypeStruct(*o) for o in outs],
        scratch_shapes=scratch,
        compiler_params=pltpu.CompilerParams(
            collective_id=1, has_side_effects=True, vmem_limit_bytes=62 * 1024 * 1024
        ),
        name="layer_backward",
    )(*saved)


def finish_kernel(*refs):
    count = len(refs) // 2
    gains_ref, firsts, seconds = refs[count - 1], *refs[-2:]
    for src, dst in zip(refs[: count - 1], refs[count:]):
        dst[...] = src[...].astype(dst.dtype)
    firsts[...] = gains_ref[0:1, :]
    seconds[...] = gains_ref[1:2, :]


def finish(block, *rest):
    steps = 8
    *grads, gains = rest
    arrays = [x.reshape(-1, x.shape[-1]) for x in (block, *grads)]

    def spec(x):
        parts = next(n for n in (steps, steps // 2, steps // 4, 1) if x.shape[0] % (16 * n) == 0)
        return pl.BlockSpec((x.shape[0] // parts, x.shape[1]), lambda i: (i * parts // steps, 0))

    whole = lambda rows: pl.BlockSpec((rows, gains.shape[1]), lambda i: (0, 0))
    shape = jax.ShapeDtypeStruct
    outs = pl.pallas_call(
        finish_kernel,
        grid=(steps,),
        in_specs=[spec(x) for x in arrays] + [whole(8)],
        out_specs=[spec(x) for x in arrays] + [whole(1)] * 2,
        out_shape=[shape(arrays[0].shape, block.dtype)]
        + [shape(x.shape, jnp.float32) for x in arrays[1:]]
        + [shape((1, gains.shape[1]), jnp.float32)] * 2,
        compiler_params=pltpu.CompilerParams(vmem_limit_bytes=60 * 1024 * 1024),
        name="layer_finish",
    )(*arrays, gains)
    return [out.reshape(x.shape) for out, x in zip(outs, (block, *grads))] + [outs[-2][0], outs[-1][0]]


def shards(
    tokens_in, lengths, first_gain, joined_weight, mixer_weight, second_gain, expand_weight, shrink_weight, cotangent
):
    rows, cols = lax.axis_size("row"), lax.axis_size("col")
    hidden_here = shrink_weight.shape[0]
    assert tokens_in.shape[0] * CORES == LEN * rows and cols == CORES
    chunks = (512, 512, hidden_here - 1024)
    joined_here = joined_weight.transpose(1, 0, 2)
    expand_here = expand_weight.transpose(1, 2, 0)
    saved = forward(
        tokens_in, cotangent, lengths, first_gain, second_gain, joined_here, mixer_weight, expand_here, shrink_weight, chunks
    )
    block_output, input_grad, joined_grad, mixer_grad, expand_grad, shrink_grad, *gains = finish(*backward(saved, chunks))
    return (
        block_output,
        input_grad,
        joined_grad.transpose(1, 0, 2),
        mixer_grad,
        expand_grad.transpose(2, 0, 1),
        shrink_grad,
        gains[0],
        gains[1],
    )


def solution(mesh):
    placed = (
        P(("dp", "col"), "row"),
        P("dp", None),
        P("row"),
        P("row", None, "col"),
        P("col", "row"),
        P("row"),
        P("row", None, "col"),
        P("col", "row"),
        P(("dp", "col"), "row"),
    )
    return jax.shard_map(
        shards,
        mesh=mesh,
        in_specs=placed,
        out_specs=(
            P(("dp", "col"), "row"),
            P(("dp", "col"), "row"),
            P("row", None, "col"),
            P("col", "row"),
            P("row", None, "col"),
            P("col", "row"),
            P("row"),
            P("row"),
        ),
        check_vma=False,
    )
```
